32 devices in a mesh: group: 2 (over y), obs: 4 (over z), node: 2 (over x), mp: 2 (over core).
Axes of the slice: x: 2, y: 2, z: 4, core: 2. Of those that a mesh axis runs over, the one named last changes fastest.
Arguments:
- obs_feat: bfloat16 [2048, 512], P(('group', 'obs', 'node')), parts along dimension 0, may hold values from -6 to 6
- node_state: bfloat16 [5120, 512], P(('group', 'obs', 'node')), parts along dimension 0, may hold values from -6 to 6
- grad_agg: bfloat16 [5120, 512], P(('group', 'obs', 'node')), parts along dimension 0, may hold values from -6 to 6
- owner: int32 [2048, 2], P(('group', 'obs', 'node')), parts along dimension 0, may hold values from 0 to 7, all different within a row; in each aligned block of 128 rows (0 to 127, 128 to 255, ...) at most 64 rows name the same one
- local_idx: int32 [2048, 2], P(('group', 'obs', 'node')), parts along dimension 0, may hold values from 0 to 319
- slot: int32 [2048], P(('group', 'obs', 'node')), parts along dimension 0, may hold values from 0 to 5
- w_obs: bfloat16 [512, 512], P(None, 'mp'), may hold values from -0.25 to 0.25
- w_node: bfloat16 [512, 512], P(None, 'mp'), may hold values from -0.25 to 0.25
- slot_bias: float32 [6, 512], P(None, 'mp'), may hold values from -4 to 4
- w_out: bfloat16 [512, 512], P('mp'), may hold values from -0.25 to 0.25
Outputs:
- grad_obs: bfloat16 [2048, 512], P(('group', 'obs', 'node'), 'mp'), parts along dimension 0
- grad_node: float32 [5120, 512], P(('group', 'obs', 'node'), 'mp'), parts along dimension 0
- grad_w_obs: float32 [1024, 512], P('group', 'mp'), parts along dimension 0
- grad_w_node: float32 [1024, 512], P('group', 'mp'), parts along dimension 0
- grad_w_out: float32 [1024, 512], P(('group', 'mp')), parts along dimension 0
- grad_slot_bias: float32 [12, 512], P('group', 'mp'), parts along dimension 0
The draws below stay inside these ranges and needn't reach their ends.
There are 2 independent parts, one for each index of `group`. The reference program is written for one: setup_inputs(seed, part) draws one part's arguments, and reference() takes and returns one part's arrays. A program takes and returns all parts, laid end to end along the dimension named above; an argument that names none is the same for every part. Nothing has to cross between parts.
Inputs may be any that keep to these rules, and one draw needn't show every extreme that they name: `owner`: each row names 2 different regions; among the rows of one device no region is named more than 64 times, a bound that some block reaches.
All inputs are finite; a program needn't handle non-finite values.
Results may differ from the reference program's by a relative error of at most 0.011.
Values may be sent and summed in bfloat16 or wider, within the bound.
No kernel may reach another device: no remote copies, remote signals or barrier semaphores. Data moves between devices by JAX's collectives and lax.ppermute only.
A program may use at most 64 MiB of HBM per device.

```python
import math
import jax
import jax.numpy as jnp
import numpy as np
from jax import lax

L = 512
H = 512
K = 2
SLOTS = 6
OBS_DEV = 128
NODE_DEV = 320
OWNERS = 8
CAP = 64
OBS = 1024
NODES = 2560


def set_ends(array, stream_key, least, high):
    extent = array.shape
    index_at = [jax.random.randint(jax.random.fold_in(stream_key, axis), (), 0, extent[axis]) for axis in range(len(extent))]
    array = array.at[tuple(index_at)].set(least)
    longest = extent.index(max(extent))
    index_at[longest] = (index_at[longest] + 1) % extent[longest]
    return array.at[tuple(index_at)].set(high)


def levels(rng, shape, pieces, low, top_value):
    def one(axis_at, shards_of):
        draws = jax.random.uniform(jax.random.fold_in(jax.random.fold_in(rng, 6), axis_at), (shards_of,), jnp.float32, low / len(pieces), top_value / len(pieces))
        return jnp.repeat(jnp.exp(draws), shape[axis_at] // shards_of).reshape((-1,) + (1,) * (len(shape) - axis_at - 1))

    factor_of = one(*pieces[0])
    for cut in pieces[1:]:
        factor_of = factor_of * one(*cut)
    return factor_of


def routed_block(own_key, own, number, rows, count, top, limit, lean):
    sequence = jax.random.permutation(own_key, count)
    heavy_load, common = portions_of(count, rows * top, limit, lean, True), portions_of(count, rows * top, limit, lean, False)
    places = jnp.arange(count)

    def named(tallies, rotation):
        used = int((tallies > 0).sum())
        fixed = max(1, used // 4)
        moved = fixed + (places - fixed + rotation * (used - fixed)) % max(1, count - fixed)
        return jnp.zeros((count,), jnp.int32).at[sequence[jnp.where(places < fixed, places, moved)]].set(jnp.asarray(tallies, jnp.int32))

    tallies = jnp.where(number % 4 == 0, named(heavy_load, number // 4), named(common, number - number // 4 - 1))
    mixed = jax.random.permutation(jax.random.fold_in(own, 3), count)
    source_of, sink = mixed[0:count // 2 * 2:2], mixed[1:count // 2 * 2:2]
    room = jnp.minimum(tallies[source_of] - 1, limit - tallies[sink]) // 2
    room = jnp.where((source_of == sequence[0]) | (sink == sequence[0]) | (tallies[sink] == 0), 0, jnp.maximum(room, 0))
    moved = jax.random.randint(jax.random.fold_in(own, 4), (count // 2,), 0, 1 << 20) % (room + 1)
    tallies = tallies.at[source_of].add(-moved).at[sink].add(moved)
    items = jnp.searchsorted(jnp.cumsum(tallies), jnp.arange(rows * top), side="right").astype(jnp.int32)
    grid = items.reshape(top, rows).T
    grid = grid[jax.random.permutation(jax.random.fold_in(own, 1), rows)]
    rotation = jax.random.randint(jax.random.fold_in(own, 2), (rows, 1), 0, top)
    return jnp.take_along_axis(grid, (jnp.arange(top)[None, :] + rotation) % top, axis=1)


def portions_of(number_of, total, bound, lean, full):
    loads = [(1 << 20) // math.isqrt(rank ** lean) + 1 for rank in range(1, number_of + 1)]
    largest = bound if full else min(bound, max(-(-total // number_of), total * loads[0] // sum(loads)))
    least = 1 if total - largest >= number_of - 1 else 0
    holding, rest = [largest] + [least] * (number_of - 1), total - largest - least * (number_of - 1)
    while rest > 0:
        movable = [i for i in range(1, number_of) if holding[i] < largest] or [i for i in range(1, number_of) if holding[i] < bound]
        whole, left = sum([loads[i] for i in movable]), rest
        for i in movable:
            extra = min(bound - holding[i], max(1, left * loads[i] // whole), rest)
            holding[i] = holding[i] + extra
            rest = rest - extra
    return np.array(holding)


def gaussian(key, extent, spread, reach, cuts=(), kind=jnp.bfloat16):
    level = levels(key, extent, cuts, -0.22, 0.18) if cuts else 1.0
    values = jax.random.normal(key, extent, jnp.float32) * spread * level
    return jnp.minimum(jnp.maximum(values, -reach), reach).astype(kind)


def setup_inputs(seed: int = 0, part: int = 0) -> dict:
    streams_of = jax.random.split(jax.random.key(seed), 11)
    part_splits = jax.random.split(jax.random.fold_in(streams_of[10], part), 11)
    obs_feat = gaussian(part_splits[0], (OBS, L), 1.0, 6.0, ((0, 8),))
    node_state = gaussian(part_splits[1], (NODES, L), 1.0, 6.0, ((0, 8),))
    grad_agg = gaussian(part_splits[2], (NODES, L), 1.0, 6.0, ((0, 8),))
    owner_keys = jax.random.split(jax.random.fold_in(part_splits[3], 1), OBS // OBS_DEV)
    owner_turns = jax.random.permutation(jax.random.fold_in(part_splits[3], 3), OBS // OBS_DEV)
    owner = jax.vmap(lambda own, number: routed_block(jax.random.fold_in(part_splits[3], 2), own, number, OBS_DEV, OWNERS, K, CAP, 2))(owner_keys, owner_turns).reshape((OBS, K))
    local_idx = set_ends(jax.random.randint(part_splits[4], (OBS, K), 0, NODE_DEV), jax.random.fold_in(part_splits[4], 1), 0, NODE_DEV - 1).astype(jnp.int32)
    slot = set_ends(jax.random.randint(part_splits[5], (OBS,), 0, SLOTS), jax.random.fold_in(part_splits[5], 1), 0, SLOTS - 1).astype(jnp.int32)
    w_obs = gaussian(streams_of[6], (L, H), L ** -0.5, 0.25, ((1, 2),))
    w_node = gaussian(streams_of[7], (L, H), L ** -0.5, 0.25, ((1, 2),))
    slot_bias = gaussian(streams_of[8], (SLOTS, H), 1.0, 4.0, ((1, 2),), jnp.float32)
    w_out = gaussian(streams_of[9], (H, L), H ** -0.5, 0.25, ((0, 2),))
    return dict(obs_feat=obs_feat, node_state=node_state, grad_agg=grad_agg, owner=owner, local_idx=local_idx, slot=slot, w_obs=w_obs, w_node=w_node, slot_bias=slot_bias, w_out=w_out)


def reference(obs_feat, node_state, grad_agg, owner, local_idx, slot, w_obs, w_node, slot_bias, w_out):
    flat = (owner * NODE_DEV + local_idx).reshape(-1).astype(jnp.int32)
    edge_state = jnp.take(node_state, flat, axis=0)
    edge_grad = jnp.take(grad_agg, flat, axis=0)
    slot_hot = (slot[:, None] == jnp.arange(SLOTS, dtype=jnp.int32)[None, :]).astype(jnp.float32)
    bias = jnp.dot(slot_hot, slot_bias, precision=lax.Precision.HIGHEST)
    obs_part = jnp.dot(obs_feat, w_obs, preferred_element_type=jnp.float32) + bias
    node_part = jnp.dot(edge_state, w_node, preferred_element_type=jnp.float32)
    pre = (obs_part[:, None, :] + node_part.reshape(OBS, K, H)).reshape(OBS * K, H)
    sig = jax.nn.sigmoid(pre)
    zvals = (pre * sig).astype(jnp.bfloat16)
    g_z = jnp.dot(edge_grad, w_out.T, preferred_element_type=jnp.float32)
    g_a = (g_z * sig * (1.0 + pre * (1.0 - sig))).astype(jnp.bfloat16)
    obs_hidden = jnp.sum(g_a.astype(jnp.float32).reshape(OBS, K, H), axis=1).astype(jnp.bfloat16)
    grad_obs = jnp.dot(obs_hidden, w_obs.T, preferred_element_type=jnp.float32).astype(jnp.bfloat16)
    node_hidden = jax.ops.segment_sum(g_a.astype(jnp.float32), flat, num_segments=NODES)
    grad_node = jnp.dot(node_hidden, w_node.astype(jnp.float32).T, precision=lax.Precision.HIGHEST)
    grad_w_obs = jnp.dot(obs_feat.T, obs_hidden, preferred_element_type=jnp.float32)
    grad_w_node = jnp.dot(edge_state.T, g_a, preferred_element_type=jnp.float32)
    grad_w_out = jnp.dot(zvals.T, edge_grad, preferred_element_type=jnp.float32)
    grad_slot = jnp.dot(slot_hot.T, obs_hidden.astype(jnp.float32), precision=lax.Precision.HIGHEST)
    return grad_obs, grad_node, grad_w_obs, grad_w_node, grad_w_out, grad_slot
```

```python
import functools

import jax
import jax.numpy as jnp
from jax import lax
from jax.experimental import pallas as pl
from jax.experimental.pallas import tpu as pltpu
from jax.sharding import PartitionSpec as P

OWNER_AXES = ("obs", "node")
SUBLANES = 16
BF16 = jnp.bfloat16
F32 = jnp.float32


def dot(left, right, left_dim=1, right_dim=0):
    return lax.dot_general(
        left, right, (((left_dim,), (right_dim,)), ((), ())), preferred_element_type=F32
    )


def iota(shape, dim):
    return lax.broadcasted_iota(jnp.int32, shape, dim)


def call(kernel, outs, *args):
    vmem = pl.BlockSpec(memory_space=pltpu.VMEM)
    return pl.pallas_call(
        kernel,
        out_shape=[jax.ShapeDtypeStruct(shape, dtype) for shape, dtype in outs],
        in_specs=[vmem] * len(args),
        out_specs=[vmem] * len(outs),
        compiler_params=pltpu.CompilerParams(vmem_limit_bytes=40 << 20),
    )(*args)


def exchange(blocks):
    return lax.all_to_all(blocks, OWNER_AXES, split_axis=0, concat_axis=0, tiled=True)


def swap_cores(value):
    return lax.ppermute(value, "mp", [(0, 1), (1, 0)])


def other_half(ref):
    half = ref.shape[0] // 2
    me = lax.axis_index("mp")
    mine = ref[pl.ds(pl.multiple_of(me * half, half), half), :]
    theirs = ref[pl.ds(pl.multiple_of((1 - me) * half, half), half), :]
    return mine, theirs


def slot_one_hot(slot_ref, slots):
    obs = slot_ref.shape[1]
    return (iota((slots, obs), 0) == slot_ref[...]).astype(F32)


def pack_kernel(obs_ref, owner_ref, index_ref, slot_ref, w_ref, bias_ref, out_ref, place_ref):
    owners, chunk, lanes = out_ref.shape
    fanout, obs = owner_ref.shape
    cap = (chunk - SUBLANES) * lanes // w_ref.shape[1]
    owner, index = owner_ref[...], index_ref[...]
    hits = [iota((owners, obs), 0) == owner[k : k + 1] for k in range(fanout)]
    count = functools.reduce(jnp.add, [h.astype(F32) for h in hits])
    before = dot(count, (iota((obs, obs), 0) < iota((obs, obs), 1)).astype(F32))
    header = jnp.zeros((SUBLANES, obs), F32)
    pick = None
    for k in range(fanout):
        rank = jnp.sum(jnp.where(hits[k], before, 0.0), axis=0, keepdims=True)
        place = owner[k : k + 1] * cap + rank.astype(jnp.int32)
        place_ref[k : k + 1, :] = place
        mine = iota((owners * cap, obs), 0) == place
        pick = mine if pick is None else pick | mine
        plus = index[k : k + 1] + 1
        fields = (owner[k : k + 1].astype(F32), rank, (plus // 16).astype(F32), (plus % 16).astype(F32))
        for j, row in enumerate(fields):
            header = jnp.where(iota(header.shape, 0) == 4 * k + j, row, header)
    bias = lax.dot_general(
        slot_one_hot(slot_ref, bias_ref.shape[0]),
        bias_ref[...],
        (((0,), (0,)), ((), ())),
        precision=lax.Precision.HIGHEST,
        preferred_element_type=F32,
    )
    part = (dot(obs_ref[...], w_ref[...]) + bias).astype(BF16)
    packed = dot(pick.astype(BF16), part).astype(BF16)
    header = header.astype(BF16)
    for d in range(owners):
        for c in range(part.shape[1] // lanes):
            out_ref[d, c * cap : (c + 1) * cap, :] = packed[
                d * cap : (d + 1) * cap, c * lanes : (c + 1) * lanes
            ]
        out_ref[d, chunk - SUBLANES :, :] = header


def table_kernel(state_ref, agg_ref, w_node_ref, w_out_ref, table_ref):
    hidden = w_node_ref.shape[1]
    parts = (dot(state_ref[...], w_node_ref[...]), dot(agg_ref[...], w_out_ref[...], 1, 1))
    for j, part in enumerate(parts):
        high = part.astype(BF16)
        table_ref[:, 2 * j * hidden : (2 * j + 1) * hidden] = high
        table_ref[:, (2 * j + 1) * hidden : (2 * j + 2) * hidden] = (
            part - high.astype(F32)
        ).astype(BF16)


def edge_kernel(recv_ref, table_ref, act_ref, hot_ref):
    owners, chunk, lanes = recv_ref.shape
    hidden = table_ref.shape[1] // 4
    cap = (chunk - SUBLANES) * lanes // hidden
    me = lax.axis_index(OWNER_AXES).astype(F32)
    columns = []
    parts = []
    for s in range(owners):
        header = recv_ref[s, chunk - SUBLANES :, :].astype(F32)
        plus = jnp.zeros((cap, lanes), F32)
        for k in range(2):
            row = header[4 * k : 4 * k + 4]
            rank = jnp.where(row[0:1] == me, row[1:2], -1.0).astype(jnp.int32)
            plus = plus + jnp.where(iota((cap, lanes), 0) == rank, row[2:3] * 16.0 + row[3:4], 0.0)
        columns.append(jnp.sum(plus, axis=1, keepdims=True).astype(jnp.int32) - 1)
        parts.append(
            jnp.concatenate(
                [recv_ref[s, c * cap : (c + 1) * cap, :] for c in range(hidden // lanes)], axis=1
            ).astype(F32)
        )
    column = jnp.concatenate(columns, axis=0)
    hot = (column == iota(hot_ref.shape, 1)).astype(BF16)
    hot_ref[...] = hot
    rows = dot(hot, table_ref[...])
    pre = jnp.concatenate(parts, axis=0) + (rows[:, :hidden] + rows[:, hidden : 2 * hidden])
    g_z = rows[:, 2 * hidden : 3 * hidden] + rows[:, 3 * hidden :]
    sig = jax.nn.sigmoid(pre)
    act_ref[:, :hidden] = (g_z * sig * (1.0 + pre * (1.0 - sig))).astype(BF16)
    act_ref[:, hidden:] = (pre * sig).astype(BF16)


def put_rows(out_ref, start, rows, value):
    value = value.astype(BF16)
    width = out_ref.shape[2]
    for d in range(out_ref.shape[0]):
        for c in range(value.shape[1] // width):
            at = start + c * rows
            if (d + 1) * rows <= value.shape[0]:
                block = value[d * rows : (d + 1) * rows, c * width : (c + 1) * width]
            else:
                block = jnp.zeros((rows, width), BF16)
            out_ref[d, at : at + rows, :] = block


def chunk_rows(total, owners):
    return max(SUBLANES, total // owners)


def node_kernel(hot_ref, act_ref, state_ref, agg_ref, w_node_ref, sums_ref, keep_ref, send_ref):
    owners = sums_ref.shape[0]
    width = state_ref.shape[1]
    hidden = w_node_ref.shape[1]
    by_node = dot(hot_ref[...], act_ref[...], 0, 0).astype(BF16)
    node_hidden, z_sum = by_node[:, :hidden], by_node[:, hidden:]
    mine, theirs = other_half(w_node_ref)
    send_ref[...] = dot(node_hidden, theirs, 1, 1).astype(BF16)
    keep_ref[...] = dot(node_hidden, mine, 1, 1)
    rows = chunk_rows(width, owners)
    put_rows(sums_ref, 0, rows, dot(state_ref[...], node_hidden, 0, 0))
    put_rows(sums_ref, rows, chunk_rows(hidden, owners), dot(z_sum, agg_ref[...], 0, 0))


def obs_kernel(back_ref, place_ref, slot_ref, obs_ref, w_ref, sums_ref, keep_ref, send_ref, *, slots):
    owners = sums_ref.shape[0]
    width, hidden = w_ref.shape
    fanout, obs = place_ref.shape
    pick = None
    for k in range(fanout):
        mine = iota((back_ref.shape[0], obs), 0) == place_ref[k : k + 1, :]
        pick = mine if pick is None else pick | mine
    obs_hidden = dot(pick.astype(BF16), back_ref[...], 0, 0).astype(BF16)
    mine, theirs = other_half(w_ref)
    send_ref[...] = dot(obs_hidden, theirs, 1, 1).astype(BF16)
    keep_ref[...] = dot(obs_hidden, mine, 1, 1)
    rows = chunk_rows(width, owners)
    put_rows(sums_ref, 0, rows, dot(obs_ref[...], obs_hidden, 0, 0))
    slot_sum = dot(slot_one_hot(slot_ref, slots).astype(BF16), obs_hidden).astype(BF16)
    for d in range(owners):
        sums_ref[d, rows:, :] = slot_sum


def sum_kernel(first_ref, second_ref, out_ref, slot_ref):
    owners, rows, _ = first_ref.shape
    more = out_ref.shape[1] - rows
    first = jnp.sum(first_ref[...].astype(F32), axis=0).astype(BF16)
    second = jnp.sum(second_ref[...].astype(F32), axis=0)
    slot_ref[...] = second[more : more + slot_ref.shape[0]]
    second = second[:more].astype(BF16)
    for d in range(owners):
        out_ref[d, :rows, :] = first
        out_ref[d, rows:, :] = second


def finish_kernel(
    all_ref, node_keep_ref, node_got_ref, obs_keep_ref, obs_got_ref,
    grad_obs_ref, grad_node_ref, w_obs_ref, w_node_ref, w_out_ref,
):
    owners, _, hidden = all_ref.shape
    width = w_obs_ref.shape[0]
    rows, out_rows = chunk_rows(width, owners), chunk_rows(w_out_ref.shape[0], owners)
    pieces = w_out_ref.shape[1] // hidden
    for d in range(owners):
        at = d * rows
        if at < width:
            w_node_ref[at : at + rows, :] = all_ref[d, :rows, :].astype(F32)
            w_obs_ref[at : at + rows, :] = all_ref[d, rows + pieces * out_rows :, :].astype(F32)
        at = d * out_rows
        if at < w_out_ref.shape[0]:
            for c in range(pieces):
                begin = rows + c * out_rows
                w_out_ref[at : at + out_rows, c * hidden : (c + 1) * hidden] = all_ref[
                    d, begin : begin + out_rows, :
                ].astype(F32)
    grad_node_ref[...] = node_keep_ref[...] + node_got_ref[...].astype(F32)
    grad_obs_ref[...] = (obs_keep_ref[...] + obs_got_ref[...].astype(F32)).astype(BF16)


def local(obs_feat, node_state, grad_agg, owner, local_idx, slot, w_obs, w_node, slot_bias, w_out):
    owners = lax.axis_size(OWNER_AXES)
    obs, fanout = owner.shape
    nodes, width = node_state.shape
    hidden = w_obs.shape[1]
    slots = slot_bias.shape[0]
    cap = max(2, 2 * obs * fanout // owners)
    cap = -(-cap // SUBLANES) * SUBLANES
    edges = owners * cap
    half = width // 2
    slot_row = slot.reshape(1, obs)

    chunk = cap * hidden // obs + SUBLANES
    packed, place = call(
        pack_kernel,
        [((owners, chunk, obs), BF16), ((fanout, obs), jnp.int32)],
        obs_feat, owner.T, local_idx.T, slot_row, w_obs, slot_bias,
    )
    (table,) = call(
        table_kernel, [((nodes, 4 * hidden), BF16)], node_state, grad_agg, w_node, w_out
    )
    received = exchange(packed)
    act, hot = call(
        edge_kernel, [((edges, 2 * hidden), BF16), ((edges, nodes), BF16)], received, table
    )
    back = exchange(act[:, :hidden].reshape(owners, cap, hidden)).reshape(edges, hidden)

    rows = chunk_rows(width, owners)
    first = rows + width // hidden * chunk_rows(hidden, owners)
    node_sums, node_keep, node_send = call(
        node_kernel,
        [((owners, first, hidden), BF16), ((nodes, half), F32), ((nodes, half), BF16)],
        hot, act, node_state, grad_agg, w_node,
    )
    node_got = swap_cores(node_send)
    node_sums = exchange(node_sums)
    padded = -(-slots // SUBLANES) * SUBLANES
    obs_sums, obs_keep, obs_send = call(
        functools.partial(obs_kernel, slots=padded),
        [((owners, rows + padded, hidden), BF16), ((obs, half), F32), ((obs, half), BF16)],
        back, place, slot_row, obs_feat, w_obs,
    )
    obs_got = swap_cores(obs_send)
    obs_sums = exchange(obs_sums)
    totals, grad_slot = call(
        sum_kernel,
        [((owners, first + rows, hidden), BF16), ((slots, hidden), F32)],
        node_sums, obs_sums,
    )
    totals = exchange(totals)
    grad_obs, grad_node, grad_w_obs, grad_w_node, grad_w_out = call(
        finish_kernel,
        [
            ((obs, half), BF16),
            ((nodes, half), F32),
            ((width, hidden), F32),
            ((width, hidden), F32),
            ((hidden, width), F32),
        ],
        totals, node_keep, node_got, obs_keep, obs_got,
    )
    return grad_obs, grad_node, grad_w_obs, grad_w_node, grad_w_out, grad_slot


def solution(mesh):
    rows = P(("group", "obs", "node"), None)
    return jax.shard_map(
        local,
        mesh=mesh,
        in_specs=(
            rows, rows, rows, rows, rows,
            P(("group", "obs", "node")),
            P(None, "mp"), P(None, "mp"), P(None, "mp"), P("mp", None),
        ),
        out_specs=(
            P(("group", "obs", "node"), "mp"),
            P(("group", "obs", "node"), "mp"),
            P("group", "mp"),
            P("group", "mp"),
            P(("group", "mp"), None),
            P("group", "mp"),
        ),
        check_vma=False,
    )
```

```python
import functools

import jax
import jax.numpy as jnp
from jax import lax
from jax.experimental import pallas as pl
from jax.experimental.pallas import tpu as pltpu
from jax.sharding import PartitionSpec as P

OWNER_AXES = ("obs", "node")
SUBLANES = 16
BF16 = jnp.bfloat16
F32 = jnp.float32


def dot(left, right, left_dim=1, right_dim=0):
    return lax.dot_general(
        left, right, (((left_dim,), (right_dim,)), ((), ())), preferred_element_type=F32
    )


def iota(shape, dim):
    return lax.broadcasted_iota(jnp.int32, shape, dim)


def call(kernel, outs, *args, scratch=(), in_hbm=False):
    vmem = pl.BlockSpec(memory_space=pltpu.VMEM)
    return pl.pallas_call(
        kernel,
        out_shape=[jax.ShapeDtypeStruct(shape, dtype) for shape, dtype in outs],
        in_specs=[pl.BlockSpec(memory_space=pl.ANY) if in_hbm else vmem] * len(args),
        out_specs=[vmem] * len(outs),
        scratch_shapes=list(scratch),
        compiler_params=pltpu.CompilerParams(vmem_limit_bytes=40 << 20),
    )(*args)


def shift(value, axis, step):
    size = lax.axis_size(axis)
    return lax.ppermute(value, axis, [(i, (i + step) % size) for i in range(size)])


def other_half(ref):
    half = ref.shape[0] // 2
    me = lax.axis_index("mp")
    mine = ref[pl.ds(pl.multiple_of(me * half, half), half), :]
    theirs = ref[pl.ds(pl.multiple_of((1 - me) * half, half), half), :]
    return mine, theirs


def slot_one_hot(slot_ref, slots):
    obs = slot_ref.shape[1]
    return (iota((slots, obs), 0) == slot_ref[...]).astype(F32)


def pack_kernel(cap, *refs):
    hbm, outs, local_refs, sems = refs[:6], refs[6:-7], refs[-7:-1], refs[-1]
    place_ref, outs = outs[0], outs[1:]
    copies = [
        pltpu.make_async_copy(src, dst, sems.at[i]) for i, (src, dst) in enumerate(zip(hbm, local_refs))
    ]
    for copy in copies:
        copy.start()
    for copy in copies:
        copy.wait()
    obs_ref, owner_ref, index_ref, slot_ref, w_ref, bias_ref = local_refs
    owners = len(outs)
    chunk, lanes = outs[0].shape
    fanout, obs = owner_ref.shape
    owner, index = owner_ref[...], index_ref[...]
    hits = [iota((owners, obs), 0) == owner[k : k + 1] for k in range(fanout)]
    count = functools.reduce(jnp.add, [h.astype(F32) for h in hits])
    before = dot(count, (iota((obs, obs), 0) < iota((obs, obs), 1)).astype(F32))
    header = jnp.zeros((SUBLANES, obs), F32)
    places = []
    for k in range(fanout):
        rank = jnp.sum(jnp.where(hits[k], before, 0.0), axis=0, keepdims=True)
        places.append(owner[k : k + 1] * cap + rank.astype(jnp.int32))
        place_ref[k : k + 1, :] = places[k]
        plus = index[k : k + 1] + 1
        fields = (owner[k : k + 1].astype(F32), rank, (plus // 16).astype(F32), (plus % 16).astype(F32))
        for j, row in enumerate(fields):
            header = jnp.where(iota(header.shape, 0) == 4 * k + j, row, header)
    bias = lax.dot_general(
        slot_one_hot(slot_ref, bias_ref.shape[0]),
        bias_ref[...],
        (((0,), (0,)), ((), ())),
        precision=lax.Precision.HIGHEST,
        preferred_element_type=F32,
    )
    part = (dot(obs_ref[...], w_ref[...]) + bias).astype(BF16)
    header = header.astype(BF16)
    me = lax.axis_index(OWNER_AXES)
    for j, out_ref in enumerate(outs):
        slots = iota((cap, obs), 0) + lax.rem(me + j, owners) * cap
        pick = functools.reduce(jnp.logical_or, [slots == place for place in places])
        packed = dot(pick.astype(BF16), part).astype(BF16)
        for c in range(part.shape[1] // lanes):
            out_ref[c * cap : (c + 1) * cap, :] = packed[:, c * lanes : (c + 1) * lanes]
        out_ref[chunk - SUBLANES :, :] = header


def table_kernel(state_ref, agg_ref, w_node_ref, w_out_ref, table_ref):
    hidden = w_node_ref.shape[1]
    parts = (dot(state_ref[...], w_node_ref[...]), dot(agg_ref[...], w_out_ref[...], 1, 1))
    for j, part in enumerate(parts):
        high = part.astype(BF16)
        table_ref[:, 2 * j * hidden : (2 * j + 1) * hidden] = high
        table_ref[:, (2 * j + 1) * hidden : (2 * j + 2) * hidden] = (
            part - high.astype(F32)
        ).astype(BF16)


def edge_kernel(owners, fanout, *refs):
    recv_refs, table_ref = refs[:owners], refs[owners]
    back_refs, act_ref, hot_ref = refs[owners + 1 : 2 * owners + 1], refs[-2], refs[-1]
    chunk, lanes = recv_refs[0].shape
    cap, hidden = back_refs[0].shape
    me = lax.axis_index(OWNER_AXES).astype(F32)
    columns = []
    parts = []
    for recv_ref in recv_refs:
        header = recv_ref[chunk - SUBLANES :, :].astype(F32)
        plus = jnp.zeros((cap, lanes), F32)
        for k in range(fanout):
            row = header[4 * k : 4 * k + 4]
            rank = jnp.where(row[0:1] == me, row[1:2], -1.0).astype(jnp.int32)
            plus = plus + jnp.where(iota((cap, lanes), 0) == rank, row[2:3] * 16.0 + row[3:4], 0.0)
        columns.append(jnp.sum(plus, axis=1, keepdims=True).astype(jnp.int32) - 1)
        parts.append(
            jnp.concatenate(
                [recv_ref[c * cap : (c + 1) * cap, :] for c in range(hidden // lanes)], axis=1
            ).astype(F32)
        )
    column = jnp.concatenate(columns, axis=0)
    hot = (column == iota(hot_ref.shape, 1)).astype(BF16)
    hot_ref[...] = hot
    rows = dot(hot, table_ref[...])
    pre = jnp.concatenate(parts, axis=0) + (rows[:, :hidden] + rows[:, hidden : 2 * hidden])
    g_z = rows[:, 2 * hidden : 3 * hidden] + rows[:, 3 * hidden :]
    sig = jax.nn.sigmoid(pre)
    g_a = (g_z * sig * (1.0 + pre * (1.0 - sig))).astype(BF16)
    act_ref[:, :hidden] = g_a
    act_ref[:, hidden:] = (pre * sig).astype(BF16)
    for j, back_ref in enumerate(back_refs):
        back_ref[...] = g_a[j * cap : (j + 1) * cap]


def split_x(total_ref, lines, tail, keep_ref, send_refs):
    shares = len(send_refs) + 1
    me = lax.axis_index("node")
    for j in range(shares):
        to = lax.rem(me + j, shares)
        out_ref = send_refs[j - 1] if j else keep_ref
        at = begin = 0
        for count in lines:
            part = count // shares
            rows = total_ref[pl.ds(pl.multiple_of(begin + to * part, SUBLANES), part), :]
            out_ref[at : at + part, :] = rows.astype(out_ref.dtype)
            at, begin = at + part, begin + count
        if tail:
            out_ref[at : at + tail, :] = total_ref[begin : begin + tail, :].astype(out_ref.dtype)


def node_kernel(
    lines, hot_ref, act_ref, state_ref, agg_ref, w_node_ref, mine_ref, theirs_ref, keep_ref, *refs
):
    send_refs, total_ref = refs[:-1], refs[-1]
    hidden = w_node_ref.shape[1]
    by_node = dot(hot_ref[...], act_ref[...], 0, 0).astype(BF16)
    node_hidden, z_sum = by_node[:, :hidden], by_node[:, hidden:]
    total_ref[: lines[0], :] = dot(state_ref[...], node_hidden, 0, 0)
    begin = lines[0]
    for c, count in enumerate(lines[1:]):
        total_ref[begin : begin + count, :] = dot(
            z_sum, agg_ref[:, c * hidden : (c + 1) * hidden], 0, 0
        )
        begin += count
    split_x(total_ref, lines, 0, keep_ref, send_refs)
    mine, theirs = other_half(w_node_ref)
    theirs_ref[...] = dot(node_hidden, theirs, 1, 1).astype(BF16)
    mine_ref[...] = dot(node_hidden, mine, 1, 1)


def obs_kernel(
    owners, lines, tail, place_ref, slot_ref, obs_ref, w_ref, *refs
):
    back_refs, mine_ref, theirs_ref, keep_ref = refs[:owners], refs[owners], refs[owners + 1], refs[owners + 2]
    send_refs, total_ref = refs[owners + 3 : -1], refs[-1]
    fanout, obs = place_ref.shape
    cap = back_refs[0].shape[0]
    me = lax.axis_index(OWNER_AXES)
    obs_hidden = None
    for j, back_ref in enumerate(back_refs):
        slots = iota((cap, obs), 0) + lax.rem(me + j, owners) * cap
        pick = functools.reduce(
            jnp.logical_or, [slots == place_ref[k : k + 1, :] for k in range(fanout)]
        )
        part = dot(pick.astype(BF16), back_ref[...], 0, 0)
        obs_hidden = part if obs_hidden is None else obs_hidden + part
    obs_hidden = obs_hidden.astype(BF16)
    total_ref[: lines[0], :] = dot(obs_ref[...], obs_hidden, 0, 0)
    total_ref[lines[0] :, :] = dot(slot_one_hot(slot_ref, tail).astype(BF16), obs_hidden)
    split_x(total_ref, lines, tail, keep_ref, send_refs)
    mine, theirs = other_half(w_ref)
    theirs_ref[...] = dot(obs_hidden, theirs, 1, 1).astype(BF16)
    mine_ref[...] = dot(obs_hidden, mine, 1, 1)


def piece_rows(part, shares):
    return max(SUBLANES, part // shares)


def sum_x_kernel(parts, tail, others, *refs):
    keep_ref, recv_refs = refs[0], refs[1 : others + 1]
    out_ref, send_refs, total_ref = refs[others + 1], refs[others + 2 : -1], refs[-1]
    shares = len(send_refs) + 1
    total = keep_ref[...]
    for recv_ref in recv_refs:
        total = total + recv_ref[...].astype(F32)
    total_ref[...] = total
    me = lax.axis_index("obs")
    for j in range(shares):
        to = lax.rem(me + j, shares)
        ref = send_refs[j - 1] if j else out_ref
        at = begin = 0
        for part in parts:
            piece = piece_rows(part, shares)
            begin_at = begin + jnp.minimum(to, part // piece - 1) * piece
            rows = total_ref[pl.ds(pl.multiple_of(begin_at, SUBLANES), piece), :]
            ref[at : at + piece, :] = rows.astype(ref.dtype)
            at, begin = at + piece, begin + part
        if tail:
            ref[at : at + tail, :] = total_ref[begin : begin + tail, :].astype(ref.dtype)


def sum_z_kernel(others, *refs):
    total = refs[0][...]
    for recv_ref in refs[1 : others + 1]:
        total = total + recv_ref[...].astype(F32)
    out_ref = refs[others + 1]
    rows = out_ref.shape[0]
    out_ref[...] = total[:rows].astype(BF16)
    if len(refs) > others + 2:
        slot_ref = refs[others + 2]
        slot_ref[...] = total[rows : rows + slot_ref.shape[0]]


def spread_kernel(x_shares, z_shares, targets, *refs):
    blocks, out_refs = refs[: x_shares * z_shares], refs[x_shares * z_shares :]
    me_x, me_z = lax.axis_index("node"), lax.axis_index("obs")
    for i, block_ref in enumerate(blocks):
        from_x = lax.rem(me_x - i // z_shares + x_shares, x_shares)
        from_z = lax.rem(me_z - i % z_shares + z_shares, z_shares)
        hidden = block_ref.shape[1]
        at = 0
        for out, count, column in targets:
            part = count // x_shares
            piece = piece_rows(part, z_shares)
            out_ref = out_refs[out]

            def write(out_ref=out_ref, part=part, piece=piece, column=column, at=at, block_ref=block_ref):
                begin = pl.multiple_of(from_x * part + from_z * piece, SUBLANES)
                out_ref[pl.ds(begin, piece), column : column + hidden] = block_ref[
                    at : at + piece, :
                ].astype(F32)

            if part // piece == z_shares:
                write()
            else:
                pl.when(from_z < part // piece)(write)
            at += piece


def merge_kernel(node_ref, node_got_ref, obs_ref, obs_got_ref, grad_node_ref, grad_obs_ref):
    grad_node_ref[...] = node_ref[...] + node_got_ref[...].astype(F32)
    grad_obs_ref[...] = (obs_ref[...] + obs_got_ref[...].astype(F32)).astype(BF16)


def reduce_shares(lines, tail, slots, keep, sends):
    x_shares, z_shares = lax.axis_size("node"), lax.axis_size("obs")
    hidden = keep.shape[1]
    parts = [count // x_shares for count in lines]
    rows = sum(piece_rows(part, z_shares) for part in parts)
    got = [shift(send, "node", j + 1) for j, send in enumerate(sends)]
    keep, *sends = call(
        functools.partial(sum_x_kernel, parts, tail, len(got)),
        [((rows + tail, hidden), F32)] + [((rows + tail, hidden), BF16)] * (z_shares - 1),
        keep, *got,
        scratch=[pltpu.VMEM(keep.shape, F32)],
    )
    got = [shift(send, "obs", j + 1) for j, send in enumerate(sends)]
    return call(
        functools.partial(sum_z_kernel, len(got)),
        [((rows, hidden), BF16)] + ([((slots, hidden), F32)] if tail else []),
        keep, *got,
    )


def gather_pieces(piece):
    x_shares, z_shares = lax.axis_size("node"), lax.axis_size("obs")
    along_z = [piece] + [shift(piece, "obs", j) for j in range(1, z_shares)]
    blocks = list(along_z)
    for j in range(1, x_shares):
        blocks += [shift(block, "node", j) for block in along_z]
    return blocks


def local(obs_feat, node_state, grad_agg, owner, local_idx, slot, w_obs, w_node, slot_bias, w_out):
    owners = lax.axis_size(OWNER_AXES)
    x_shares, z_shares = lax.axis_size("node"), lax.axis_size("obs")
    obs, fanout = owner.shape
    nodes, width = node_state.shape
    hidden = w_obs.shape[1]
    slots = slot_bias.shape[0]
    cap = max(2, 2 * obs * fanout // owners)
    cap = -(-cap // SUBLANES) * SUBLANES
    edges = owners * cap
    half = width // 2
    slot_row = slot.reshape(1, obs)

    chunk = cap * hidden // obs + SUBLANES
    inputs = (obs_feat, owner.T, local_idx.T, slot_row, w_obs, slot_bias)
    place, *packed = call(
        functools.partial(pack_kernel, cap),
        [((fanout, obs), jnp.int32)] + [((chunk, obs), BF16)] * owners,
        *inputs,
        scratch=[pltpu.VMEM(a.shape, a.dtype) for a in inputs] + [pltpu.SemaphoreType.DMA((len(inputs),))],
        in_hbm=True,
    )
    received = packed[:1] + [shift(packed[j], OWNER_AXES, j) for j in range(1, owners)]
    (table,) = call(
        table_kernel, [((nodes, 4 * hidden), BF16)], node_state, grad_agg, w_node, w_out
    )
    *back, act, hot = call(
        functools.partial(edge_kernel, owners, fanout),
        [((cap, hidden), BF16)] * owners + [((edges, 2 * hidden), BF16), ((edges, nodes), BF16)],
        *received, table,
    )
    back = back[:1] + [shift(back[j], OWNER_AXES, -j) for j in range(1, owners)]

    node_lines = [width] + [hidden] * (width // hidden)
    share = sum(node_lines) // x_shares
    node_mine, node_theirs, keep, *sends = call(
        functools.partial(node_kernel, node_lines),
        [((nodes, half), F32), ((nodes, half), BF16), ((share, hidden), F32)]
        + [((share, hidden), BF16)] * (x_shares - 1),
        hot, act, node_state, grad_agg, w_node,
        scratch=[pltpu.VMEM((sum(node_lines), hidden), F32)],
    )
    (node_piece,) = reduce_shares(node_lines, 0, 0, keep, sends)
    node_got = shift(node_theirs, "mp", 1)

    tail = -(-slots // SUBLANES) * SUBLANES
    share = width // x_shares + tail
    obs_mine, obs_theirs, keep, *sends = call(
        functools.partial(obs_kernel, owners, [width], tail),
        [((obs, half), F32), ((obs, half), BF16), ((share, hidden), F32)]
        + [((share, hidden), BF16)] * (x_shares - 1),
        place, slot_row, obs_feat, w_obs, *back,
        scratch=[pltpu.VMEM((width + tail, hidden), F32)],
    )
    obs_piece, grad_slot = reduce_shares([width], tail, slots, keep, sends)
    obs_got = shift(obs_theirs, "mp", 1)

    node_blocks = gather_pieces(node_piece)
    obs_blocks = gather_pieces(obs_piece)
    grad_node, grad_obs = call(
        merge_kernel, [((nodes, half), F32), ((obs, half), BF16)],
        node_mine, node_got, obs_mine, obs_got,
    )
    node_targets = [(0, width, 0)] + [(1, hidden, c * hidden) for c in range(width // hidden)]
    grad_w_node, grad_w_out = call(
        functools.partial(spread_kernel, x_shares, z_shares, node_targets),
        [((width, hidden), F32), ((hidden, width), F32)],
        *node_blocks,
    )
    (grad_w_obs,) = call(
        functools.partial(spread_kernel, x_shares, z_shares, [(0, width, 0)]),
        [((width, hidden), F32)],
        *obs_blocks,
    )
    return grad_obs, grad_node, grad_w_obs, grad_w_node, grad_w_out, grad_slot


def solution(mesh):
    rows = P(("group", "obs", "node"), None)
    return jax.shard_map(
        local,
        mesh=mesh,
        in_specs=(
            rows, rows, rows, rows, rows,
            P(("group", "obs", "node")),
            P(None, "mp"), P(None, "mp"), P(None, "mp"), P("mp", None),
        ),
        out_specs=(
            P(("group", "obs", "node"), "mp"),
            P(("group", "obs", "node"), "mp"),
            P("group", "mp"),
            P("group", "mp"),
            P(("group", "mp"), None),
            P("group", "mp"),
        ),
        check_vma=False,
    )
```

```python
import functools

import jax
import jax.numpy as jnp
from jax import lax
from jax.experimental import pallas as pl
from jax.experimental.pallas import tpu as pltpu
from jax.sharding import PartitionSpec as P

OWNER_AXES = ("obs", "node")
SUBLANES = 16
BF16 = jnp.bfloat16
F32 = jnp.float32


def dot(left, right, left_dim=1, right_dim=0):
    return lax.dot_general(
        left, right, (((left_dim,), (right_dim,)), ((), ())), preferred_element_type=F32
    )


def iota(shape, dim):
    return lax.broadcasted_iota(jnp.int32, shape, dim)


def call(kernel, outs, *args, scratch=(), in_hbm=False):
    vmem = pl.BlockSpec(memory_space=pltpu.VMEM)
    return pl.pallas_call(
        kernel,
        out_shape=[jax.ShapeDtypeStruct(shape, dtype) for shape, dtype in outs],
        in_specs=[pl.BlockSpec(memory_space=pl.ANY) if in_hbm else vmem] * len(args),
        out_specs=[vmem] * len(outs),
        scratch_shapes=list(scratch),
        compiler_params=pltpu.CompilerParams(vmem_limit_bytes=(60 if in_hbm else 40) << 20),
    )(*args)


def exchange(blocks, axes):
    return lax.all_to_all(blocks, axes, split_axis=0, concat_axis=0, tiled=True)


def shift(value, axis, step):
    size = lax.axis_size(axis)
    return lax.ppermute(value, axis, [(i, (i + step) % size) for i in range(size)])


def other_half(ref):
    half = ref.shape[0] // 2
    me = lax.axis_index("mp")
    mine = ref[pl.ds(pl.multiple_of(me * half, half), half), :]
    theirs = ref[pl.ds(pl.multiple_of((1 - me) * half, half), half), :]
    return mine, theirs


def slot_one_hot(slot_ref, slots):
    obs = slot_ref.shape[1]
    return (iota((slots, obs), 0) == slot_ref[...]).astype(F32)


def pack_kernel(cap, *refs):
    hbm, outs, local_refs, sems = refs[:6], refs[6:8], refs[8:14], refs[14]
    place_ref, out_ref = outs
    copies = [
        pltpu.make_async_copy(src, dst, sems.at[i]) for i, (src, dst) in enumerate(zip(hbm, local_refs))
    ]
    for copy in copies:
        copy.start()
    for copy in copies:
        copy.wait()
    obs_ref, owner_ref, index_ref, slot_ref, w_ref, bias_ref = local_refs
    owners, chunk, lanes = out_ref.shape
    fanout, obs = owner_ref.shape
    owner, index = owner_ref[...], index_ref[...]
    hits = [iota((owners, obs), 0) == owner[k : k + 1] for k in range(fanout)]
    count = functools.reduce(jnp.add, [h.astype(F32) for h in hits])
    before = dot(count, (iota((obs, obs), 0) < iota((obs, obs), 1)).astype(F32))
    header = jnp.zeros((SUBLANES, obs), F32)
    places = []
    for k in range(fanout):
        rank = jnp.sum(jnp.where(hits[k], before, 0.0), axis=0, keepdims=True)
        places.append(owner[k : k + 1] * cap + rank.astype(jnp.int32))
        place_ref[k : k + 1, :] = places[k]
        plus = index[k : k + 1] + 1
        fields = (owner[k : k + 1].astype(F32), rank, (plus // 16).astype(F32), (plus % 16).astype(F32))
        for j, row in enumerate(fields):
            header = jnp.where(iota(header.shape, 0) == 4 * k + j, row, header)
    bias = lax.dot_general(
        slot_one_hot(slot_ref, bias_ref.shape[0]),
        bias_ref[...],
        (((0,), (0,)), ((), ())),
        precision=lax.Precision.HIGHEST,
        preferred_element_type=F32,
    )
    part = (dot(obs_ref[...], w_ref[...]) + bias).astype(BF16)
    header = header.astype(BF16)
    slots = iota((owners * cap, obs), 0)
    pick = functools.reduce(jnp.logical_or, [slots == place for place in places])
    packed = dot(pick.astype(BF16), part).astype(BF16)
    for d in range(owners):
        for c in range(part.shape[1] // lanes):
            out_ref[d, c * cap : (c + 1) * cap, :] = packed[
                d * cap : (d + 1) * cap, c * lanes : (c + 1) * lanes
            ]
        out_ref[d, chunk - SUBLANES :, :] = header


def table_kernel(state_ref, agg_ref, w_node_ref, w_out_ref, table_ref):
    hidden = w_node_ref.shape[1]
    parts = (dot(state_ref[...], w_node_ref[...]), dot(agg_ref[...], w_out_ref[...], 1, 1))
    for j, part in enumerate(parts):
        high = part.astype(BF16)
        table_ref[:, 2 * j * hidden : (2 * j + 1) * hidden] = high
        table_ref[:, (2 * j + 1) * hidden : (2 * j + 2) * hidden] = (
            part - high.astype(F32)
        ).astype(BF16)


def edge_kernel(fanout, recv_ref, table_ref, back_ref, act_ref, hot_ref):
    owners, chunk, lanes = recv_ref.shape
    _, cap, hidden = back_ref.shape
    me = lax.axis_index(OWNER_AXES).astype(F32)
    columns = []
    parts = []
    for s in range(owners):
        header = recv_ref[s, chunk - SUBLANES :, :].astype(F32)
        plus = jnp.zeros((cap, lanes), F32)
        for k in range(fanout):
            row = header[4 * k : 4 * k + 4]
            rank = jnp.where(row[0:1] == me, row[1:2], -1.0).astype(jnp.int32)
            plus = plus + jnp.where(iota((cap, lanes), 0) == rank, row[2:3] * 16.0 + row[3:4], 0.0)
        columns.append(jnp.sum(plus, axis=1, keepdims=True).astype(jnp.int32) - 1)
        parts.append(
            jnp.concatenate(
                [recv_ref[s, c * cap : (c + 1) * cap, :] for c in range(hidden // lanes)], axis=1
            ).astype(F32)
        )
    column = jnp.concatenate(columns, axis=0)
    hot = (column == iota(hot_ref.shape, 1)).astype(BF16)
    hot_ref[...] = hot
    rows = dot(hot, table_ref[...])
    pre = jnp.concatenate(parts, axis=0) + (rows[:, :hidden] + rows[:, hidden : 2 * hidden])
    g_z = rows[:, 2 * hidden : 3 * hidden] + rows[:, 3 * hidden :]
    sig = jax.nn.sigmoid(pre)
    g_a = (g_z * sig * (1.0 + pre * (1.0 - sig))).astype(BF16)
    act_ref[:, :hidden] = g_a
    act_ref[:, hidden:] = (pre * sig).astype(BF16)
    for s in range(owners):
        back_ref[s] = g_a[s * cap : (s + 1) * cap]


def split_x(total_ref, lines, tail, keep_ref, send_refs):
    shares = len(send_refs) + 1
    me = lax.axis_index("node")
    for j in range(shares):
        to = lax.rem(me + j, shares)
        out_ref = send_refs[j - 1] if j else keep_ref
        at = begin = 0
        for count in lines:
            part = count // shares
            rows = total_ref[pl.ds(pl.multiple_of(begin + to * part, SUBLANES), part), :]
            out_ref[at : at + part, :] = rows.astype(out_ref.dtype)
            at, begin = at + part, begin + count
        if tail:
            out_ref[at : at + tail, :] = total_ref[begin : begin + tail, :].astype(out_ref.dtype)


def node_kernel(
    lines, hot_ref, act_ref, state_ref, agg_ref, w_node_ref, mine_ref, theirs_ref, keep_ref, *refs
):
    send_refs, total_ref = refs[:-1], refs[-1]
    hidden = w_node_ref.shape[1]
    by_node = dot(hot_ref[...], act_ref[...], 0, 0).astype(BF16)
    node_hidden, z_sum = by_node[:, :hidden], by_node[:, hidden:]
    total_ref[: lines[0], :] = dot(state_ref[...], node_hidden, 0, 0)
    begin = lines[0]
    for c, count in enumerate(lines[1:]):
        total_ref[begin : begin + count, :] = dot(
            z_sum, agg_ref[:, c * hidden : (c + 1) * hidden], 0, 0
        )
        begin += count
    split_x(total_ref, lines, 0, keep_ref, send_refs)
    mine, theirs = other_half(w_node_ref)
    theirs_ref[...] = dot(node_hidden, theirs, 1, 1).astype(BF16)
    mine_ref[...] = dot(node_hidden, mine, 1, 1)


def obs_kernel(
    lines, tail, back_ref, place_ref, slot_ref, obs_ref, w_ref, mine_ref, theirs_ref, keep_ref, *refs
):
    send_refs, total_ref = refs[:-1], refs[-1]
    fanout, obs = place_ref.shape
    slots = iota((back_ref.shape[0], obs), 0)
    pick = functools.reduce(
        jnp.logical_or, [slots == place_ref[k : k + 1, :] for k in range(fanout)]
    )
    obs_hidden = dot(pick.astype(BF16), back_ref[...], 0, 0)
    obs_hidden = obs_hidden.astype(BF16)
    total_ref[: lines[0], :] = dot(obs_ref[...], obs_hidden, 0, 0)
    total_ref[lines[0] :, :] = dot(slot_one_hot(slot_ref, tail).astype(BF16), obs_hidden)
    split_x(total_ref, lines, tail, keep_ref, send_refs)
    mine, theirs = other_half(w_ref)
    theirs_ref[...] = dot(obs_hidden, theirs, 1, 1).astype(BF16)
    mine_ref[...] = dot(obs_hidden, mine, 1, 1)


def piece_rows(part, shares):
    return max(SUBLANES, part // shares)


def sum_x_kernel(parts, tail, others, *refs):
    keep_ref, recv_refs, out_ref = refs[0], refs[1 : others + 1], refs[others + 1]
    shares = out_ref.shape[0]
    total = keep_ref[...]
    for recv_ref in recv_refs:
        total = total + recv_ref[...].astype(F32)
    total = total.astype(BF16)
    for to in range(shares):
        at = begin = 0
        for part in parts:
            piece = piece_rows(part, shares)
            if (to + 1) * piece <= part:
                rows = total[begin + to * piece : begin + (to + 1) * piece]
            else:
                rows = jnp.zeros((piece, total.shape[1]), BF16)
            out_ref[to, at : at + piece, :] = rows
            at, begin = at + piece, begin + part
        if tail:
            out_ref[to, at : at + tail, :] = total[begin : begin + tail]


def sum_z_kernel(got_ref, out_ref, *slot_refs):
    total = jnp.sum(got_ref[...].astype(F32), axis=0)
    shares, rows, _ = out_ref.shape
    piece = total[:rows].astype(BF16)
    for to in range(shares):
        out_ref[to] = piece
    for slot_ref in slot_refs:
        slot_ref[...] = total[rows : rows + slot_ref.shape[0]]


def spread_kernel(targets, blocks, *out_refs):
    x_shares = len(blocks)
    z_shares, _, hidden = blocks[0].shape
    me = lax.axis_index("node")
    for j, block_ref in enumerate(blocks):
        share = lax.rem(me - j + x_shares, x_shares)
        at = 0
        for out, count, column in targets:
            part = count // x_shares
            piece = piece_rows(part, z_shares)
            for z in range(part // piece):
                begin = pl.multiple_of(share * part + z * piece, SUBLANES)
                out_refs[out][pl.ds(begin, piece), column : column + hidden] = block_ref[
                    z, at : at + piece, :
                ].astype(F32)
            at += piece


def merge_kernel(node_ref, node_got_ref, obs_ref, obs_got_ref, grad_node_ref, grad_obs_ref):
    grad_node_ref[...] = node_ref[...] + node_got_ref[...].astype(F32)
    grad_obs_ref[...] = (obs_ref[...] + obs_got_ref[...].astype(F32)).astype(BF16)


def reduce_shares(lines, tail, slots, keep, sends):
    x_shares, z_shares = lax.axis_size("node"), lax.axis_size("obs")
    hidden = keep.shape[1]
    parts = [count // x_shares for count in lines]
    rows = sum(piece_rows(part, z_shares) for part in parts)
    got = [shift(send, "node", j + 1) for j, send in enumerate(sends)]
    (sums,) = call(
        functools.partial(sum_x_kernel, parts, tail, len(got)),
        [((z_shares, rows + tail, hidden), BF16)],
        keep, *got,
    )
    return call(
        sum_z_kernel,
        [((z_shares, rows, hidden), BF16)] + ([((slots, hidden), F32)] if tail else []),
        exchange(sums, "obs"),
    )


def gather_pieces(copies):
    along_z = exchange(copies, "obs")
    return [along_z] + [shift(along_z, "node", j) for j in range(1, lax.axis_size("node"))]


def spread(targets, blocks, outs):
    def kernel(*refs):
        spread_kernel(targets, refs[: len(blocks)], *refs[len(blocks) :])

    return call(kernel, outs, *blocks)


def local(obs_feat, node_state, grad_agg, owner, local_idx, slot, w_obs, w_node, slot_bias, w_out):
    owners = lax.axis_size(OWNER_AXES)
    x_shares = lax.axis_size("node")
    obs, fanout = owner.shape
    nodes, width = node_state.shape
    hidden = w_obs.shape[1]
    slots = slot_bias.shape[0]
    cap = max(2, 2 * obs * fanout // owners)
    cap = -(-cap // SUBLANES) * SUBLANES
    edges = owners * cap
    half = width // 2
    slot_row = slot.reshape(1, obs)

    chunk = cap * hidden // obs + SUBLANES
    inputs = (obs_feat, owner.T, local_idx.T, slot_row, w_obs, slot_bias)
    place, packed = call(
        functools.partial(pack_kernel, cap),
        [((fanout, obs), jnp.int32), ((owners, chunk, obs), BF16)],
        *inputs,
        scratch=[pltpu.VMEM(a.shape, a.dtype) for a in inputs] + [pltpu.SemaphoreType.DMA((len(inputs),))],
        in_hbm=True,
    )
    received = exchange(packed, OWNER_AXES)
    (table,) = call(
        table_kernel, [((nodes, 4 * hidden), BF16)], node_state, grad_agg, w_node, w_out
    )
    back, act, hot = call(
        functools.partial(edge_kernel, fanout),
        [((owners, cap, hidden), BF16), ((edges, 2 * hidden), BF16), ((edges, nodes), BF16)],
        received, table,
    )
    back = exchange(back, OWNER_AXES).reshape(edges, hidden)

    node_lines = [width] + [hidden] * (width // hidden)
    share = sum(node_lines) // x_shares
    node_mine, node_theirs, keep, *sends = call(
        functools.partial(node_kernel, node_lines),
        [((nodes, half), F32), ((nodes, half), BF16), ((share, hidden), F32)]
        + [((share, hidden), BF16)] * (x_shares - 1),
        hot, act, node_state, grad_agg, w_node,
        scratch=[pltpu.VMEM((sum(node_lines), hidden), F32)],
    )
    (node_piece,) = reduce_shares(node_lines, 0, 0, keep, sends)
    node_got = shift(node_theirs, "mp", 1)

    tail = -(-slots // SUBLANES) * SUBLANES
    share = width // x_shares + tail
    obs_mine, obs_theirs, keep, *sends = call(
        functools.partial(obs_kernel, [width], tail),
        [((obs, half), F32), ((obs, half), BF16), ((share, hidden), F32)]
        + [((share, hidden), BF16)] * (x_shares - 1),
        back, place, slot_row, obs_feat, w_obs,
        scratch=[pltpu.VMEM((width + tail, hidden), F32)],
    )
    obs_piece, grad_slot = reduce_shares([width], tail, slots, keep, sends)
    obs_got = shift(obs_theirs, "mp", 1)

    node_blocks = gather_pieces(node_piece)
    obs_blocks = gather_pieces(obs_piece)
    grad_node, grad_obs = call(
        merge_kernel, [((nodes, half), F32), ((obs, half), BF16)],
        node_mine, node_got, obs_mine, obs_got,
    )
    node_targets = [(0, width, 0)] + [(1, hidden, c * hidden) for c in range(width // hidden)]
    grad_w_node, grad_w_out = spread(
        node_targets, node_blocks, [((width, hidden), F32), ((hidden, width), F32)]
    )
    (grad_w_obs,) = spread([(0, width, 0)], obs_blocks, [((width, hidden), F32)])
    return grad_obs, grad_node, grad_w_obs, grad_w_node, grad_w_out, grad_slot


def solution(mesh):
    rows = P(("group", "obs", "node"), None)
    return jax.shard_map(
        local,
        mesh=mesh,
        in_specs=(
            rows, rows, rows, rows, rows,
            P(("group", "obs", "node")),
            P(None, "mp"), P(None, "mp"), P(None, "mp"), P("mp", None),
        ),
        out_specs=(
            P(("group", "obs", "node"), "mp"),
            P(("group", "obs", "node"), "mp"),
            P("group", "mp"),
            P("group", "mp"),
            P(("group", "mp"), None),
            P("group", "mp"),
        ),
        check_vma=False,
    )
```

```python
import functools

import jax
import jax.numpy as jnp
from jax import lax
from jax.experimental import pallas as pl
from jax.experimental.pallas import tpu as pltpu
from jax.sharding import PartitionSpec as P

OWNER_AXES = ("obs", "node")
SUBLANES = 16
BF16 = jnp.bfloat16
F32 = jnp.float32


def dot(left, right, left_dim=1, right_dim=0):
    return lax.dot_general(
        left, right, (((left_dim,), (right_dim,)), ((), ())), preferred_element_type=F32
    )


def iota(shape, dim):
    return lax.broadcasted_iota(jnp.int32, shape, dim)


def call(kernel, outs, *args, scratch=()):
    vmem = pl.BlockSpec(memory_space=pltpu.VMEM)
    return pl.pallas_call(
        kernel,
        out_shape=[jax.ShapeDtypeStruct(shape, dtype) for shape, dtype in outs],
        in_specs=[vmem] * len(args),
        out_specs=[vmem] * len(outs),
        scratch_shapes=list(scratch),
        compiler_params=pltpu.CompilerParams(vmem_limit_bytes=40 << 20),
    )(*args)


def call_staged(kernel, outs, *args):
    count = len(args)

    def staged(*refs):
        hbm, out_refs, held, sems = refs[:count], refs[count : -count - 1], refs[-count - 1 : -1], refs[-1]
        copies = [pltpu.make_async_copy(hbm[i], held[i], sems.at[i]) for i in range(count)]
        for copy in copies:
            copy.start()
        for copy in copies:
            copy.wait()
        kernel(*held, *out_refs)

    return pl.pallas_call(
        staged,
        out_shape=[jax.ShapeDtypeStruct(shape, dtype) for shape, dtype in outs],
        in_specs=[pl.BlockSpec(memory_space=pl.ANY)] * count,
        out_specs=[pl.BlockSpec(memory_space=pltpu.VMEM)] * len(outs),
        scratch_shapes=[pltpu.VMEM(a.shape, a.dtype) for a in args]
        + [pltpu.SemaphoreType.DMA((count,))],
        compiler_params=pltpu.CompilerParams(vmem_limit_bytes=60 << 20),
    )(*args)


def exchange(blocks, axes):
    return lax.all_to_all(blocks, axes, split_axis=0, concat_axis=0, tiled=True)


def shift(value, axis, step):
    size = lax.axis_size(axis)
    return lax.ppermute(value, axis, [(i, (i + step) % size) for i in range(size)])


def other_half(ref):
    half = ref.shape[0] // 2
    me = lax.axis_index("mp")
    mine = ref[pl.ds(pl.multiple_of(me * half, half), half), :]
    theirs = ref[pl.ds(pl.multiple_of((1 - me) * half, half), half), :]
    return mine, theirs


def slot_one_hot(slot_ref, slots):
    obs = slot_ref.shape[1]
    return (iota((slots, obs), 0) == slot_ref[...]).astype(F32)


def pack_kernel(cap, *refs):
    obs_ref, owner_ref, index_ref, slot_ref, w_ref, bias_ref, place_ref, *outs = refs
    owners = len(outs)
    chunk, lanes = outs[0].shape
    fanout, obs = owner_ref.shape
    owner, index = owner_ref[...], index_ref[...]
    hits = [iota((owners, obs), 0) == owner[k : k + 1] for k in range(fanout)]
    count = functools.reduce(jnp.add, [h.astype(F32) for h in hits])
    before = dot(count, (iota((obs, obs), 0) < iota((obs, obs), 1)).astype(F32))
    header = jnp.zeros((SUBLANES, obs), F32)
    places = []
    for k in range(fanout):
        rank = jnp.sum(jnp.where(hits[k], before, 0.0), axis=0, keepdims=True)
        places.append(owner[k : k + 1] * cap + rank.astype(jnp.int32))
        place_ref[k : k + 1, :] = places[k]
        plus = index[k : k + 1] + 1
        fields = (owner[k : k + 1].astype(F32), rank, (plus // 16).astype(F32), (plus % 16).astype(F32))
        for j, row in enumerate(fields):
            header = jnp.where(iota(header.shape, 0) == 4 * k + j, row, header)
    bias = lax.dot_general(
        slot_one_hot(slot_ref, bias_ref.shape[0]),
        bias_ref[...],
        (((0,), (0,)), ((), ())),
        precision=lax.Precision.HIGHEST,
        preferred_element_type=F32,
    )
    part = (dot(obs_ref[...], w_ref[...]) + bias).astype(BF16)
    header = header.astype(BF16)
    me = lax.axis_index(OWNER_AXES)
    for j, out_ref in enumerate(outs):
        slots = iota((cap, obs), 0) + lax.rem(me + j, owners) * cap
        pick = functools.reduce(jnp.logical_or, [slots == place for place in places])
        packed = dot(pick.astype(BF16), part).astype(BF16)
        for c in range(part.shape[1] // lanes):
            out_ref[c * cap : (c + 1) * cap, :] = packed[:, c * lanes : (c + 1) * lanes]
        out_ref[chunk - SUBLANES :, :] = header


def table_kernel(state_ref, agg_ref, w_node_ref, w_out_ref, table_ref):
    hidden = w_node_ref.shape[1]
    parts = (dot(state_ref[...], w_node_ref[...]), dot(agg_ref[...], w_out_ref[...], 1, 1))
    for j, part in enumerate(parts):
        high = part.astype(BF16)
        table_ref[:, 2 * j * hidden : (2 * j + 1) * hidden] = high
        table_ref[:, (2 * j + 1) * hidden : (2 * j + 2) * hidden] = (
            part - high.astype(F32)
        ).astype(BF16)


def edge_kernel(owners, fanout, *refs):
    recv_refs, (table_ref, back_ref, act_ref, hot_ref) = refs[:owners], refs[owners:]
    chunk, lanes = recv_refs[0].shape
    _, cap, hidden = back_ref.shape
    me = lax.axis_index(OWNER_AXES)
    me_float = me.astype(F32)
    columns = []
    parts = []
    for recv_ref in recv_refs:
        header = recv_ref[chunk - SUBLANES :, :].astype(F32)
        plus = jnp.zeros((cap, lanes), F32)
        for k in range(fanout):
            row = header[4 * k : 4 * k + 4]
            rank = jnp.where(row[0:1] == me_float, row[1:2], -1.0).astype(jnp.int32)
            plus = plus + jnp.where(iota((cap, lanes), 0) == rank, row[2:3] * 16.0 + row[3:4], 0.0)
        columns.append(jnp.sum(plus, axis=1, keepdims=True).astype(jnp.int32) - 1)
        parts.append(
            jnp.concatenate(
                [recv_ref[c * cap : (c + 1) * cap, :] for c in range(hidden // lanes)], axis=1
            ).astype(F32)
        )
    column = jnp.concatenate(columns, axis=0)
    hot = (column == iota(hot_ref.shape, 1)).astype(BF16)
    hot_ref[...] = hot
    rows = dot(hot, table_ref[...])
    pre = jnp.concatenate(parts, axis=0) + (rows[:, :hidden] + rows[:, hidden : 2 * hidden])
    g_z = rows[:, 2 * hidden : 3 * hidden] + rows[:, 3 * hidden :]
    sig = jax.nn.sigmoid(pre)
    g_a = (g_z * sig * (1.0 + pre * (1.0 - sig))).astype(BF16)
    act_ref[:, :hidden] = g_a
    act_ref[:, hidden:] = (pre * sig).astype(BF16)
    for j in range(owners):
        back_ref[lax.rem(me - j + owners, owners)] = g_a[j * cap : (j + 1) * cap]


def halving_steps():
    bits = [
        [(axis, k) for k in range(lax.axis_size(axis).bit_length() - 1)] for axis in ("node", "obs")
    ]
    steps = []
    for k in range(max(map(len, bits))):
        both = [line[k] for line in bits if k < len(line)]
        steps += [(both[0], both[-1])] + ([(both[1], both[0])] if len(both) > 1 else [])
    return steps


def flip(value, step):
    axes = ("obs", "node", "mp")
    sizes = [lax.axis_size(axis) for axis in axes]
    pairs = []
    for index in range(sizes[0] * sizes[1] * sizes[2]):
        place = [index // (sizes[1] * sizes[2]), index // sizes[2] % sizes[1], index % sizes[2]]
        axis, k = step[place[2] % 2]
        place[axes.index(axis)] ^= 1 << k
        pairs.append((index, (place[0] * sizes[1] + place[1]) * sizes[2] + place[2]))
    return lax.ppermute(value, axes, pairs)


def own_bit(step):
    bits = [(lax.axis_index(axis) >> k) & 1 for axis, k in step]
    return jnp.where(lax.axis_index("mp") % 2 == 0, bits[0], bits[1])


def halves(rows):
    return rows % (2 * SUBLANES) == 0


def split_half(total_ref, step, tail, keep_ref, send_ref):
    rows = total_ref.shape[0] - tail
    if halves(rows):
        rows //= 2
        bit = own_bit(step)
        kept, sent = [pl.ds(pl.multiple_of(b * rows, SUBLANES), rows) for b in (bit, 1 - bit)]
    else:
        kept = sent = pl.ds(0, rows)
    keep_ref[:rows, :] = total_ref[kept, :]
    send_ref[:rows, :] = total_ref[sent, :].astype(BF16)
    if tail:
        both = total_ref[total_ref.shape[0] - tail :, :]
        keep_ref[rows:, :] = both
        send_ref[rows:, :] = both.astype(BF16)


def node_kernel(
    step, hot_ref, act_ref, state_ref, agg_ref, w_node_ref, mine_ref, theirs_ref, keep_ref, send_ref, total_ref
):
    width, hidden = w_node_ref.shape
    by_node = dot(hot_ref[...], act_ref[...], 0, 0).astype(BF16)
    node_hidden, z_sum = by_node[:, :hidden], by_node[:, hidden:]
    total_ref[:width, :] = dot(state_ref[...], node_hidden, 0, 0)
    for c in range(width // hidden):
        begin = width + c * hidden
        total_ref[begin : begin + hidden, :] = dot(
            z_sum, agg_ref[:, c * hidden : (c + 1) * hidden], 0, 0
        )
    split_half(total_ref, step, 0, keep_ref, send_ref)
    mine, theirs = other_half(w_node_ref)
    theirs_ref[...] = dot(node_hidden, theirs, 1, 1).astype(BF16)
    mine_ref[...] = dot(node_hidden, mine, 1, 1)


def obs_kernel(
    step, tail, back_ref, place_ref, slot_ref, obs_ref, w_ref, mine_ref, theirs_ref, keep_ref, send_ref, total_ref
):
    width = w_ref.shape[0]
    fanout, obs = place_ref.shape
    slots = iota((back_ref.shape[0], obs), 0)
    pick = functools.reduce(
        jnp.logical_or, [slots == place_ref[k : k + 1, :] for k in range(fanout)]
    )
    obs_hidden = dot(pick.astype(BF16), back_ref[...], 0, 0)
    obs_hidden = obs_hidden.astype(BF16)
    total_ref[:width, :] = dot(obs_ref[...], obs_hidden, 0, 0)
    total_ref[width:, :] = dot(slot_one_hot(slot_ref, tail).astype(BF16), obs_hidden)
    split_half(total_ref, step, tail, keep_ref, send_ref)
    mine, theirs = other_half(w_ref)
    theirs_ref[...] = dot(obs_hidden, theirs, 1, 1).astype(BF16)
    mine_ref[...] = dot(obs_hidden, mine, 1, 1)


def add_kernel(step, tail, keep_ref, got_ref, next_ref, send_ref, total_ref):
    total_ref[...] = keep_ref[...] + got_ref[...].astype(F32)
    split_half(total_ref, step, tail, next_ref, send_ref)


def last_kernel(keep_ref, got_ref, piece_ref, *slot_refs):
    total = keep_ref[...] + got_ref[...].astype(F32)
    rows = piece_ref.shape[0]
    piece_ref[...] = total[:rows].astype(BF16)
    for slot_ref in slot_refs:
        slot_ref[...] = total[rows : rows + slot_ref.shape[0]]


def join_kernel(step, mine_ref, got_ref, out_ref):
    rows = mine_ref.shape[0]
    bit = own_bit(step)
    out_ref[pl.ds(pl.multiple_of(bit * rows, SUBLANES), rows), :] = mine_ref[...]
    out_ref[pl.ds(pl.multiple_of((1 - bit) * rows, SUBLANES), rows), :] = got_ref[...]


def spread_kernel(step, mine_ref, got_ref, *out_refs):
    mine, got = mine_ref[...], got_ref[...]
    low = own_bit(step) == 0
    joined = [jnp.where(low, mine, got), jnp.where(low, got, mine)]
    half, hidden = mine.shape
    at = 0
    for out_ref in out_refs:
        rows = out_ref.shape[0]
        for c in range(out_ref.shape[1] // hidden):
            for begin in range(0, rows, min(rows, half)):
                count = min(rows, half)
                offset = at % half
                out_ref[begin : begin + count, c * hidden : (c + 1) * hidden] = joined[at // half][
                    offset : offset + count
                ].astype(F32)
                at += count


def merge_kernel(node_ref, node_got_ref, obs_ref, obs_got_ref, grad_node_ref, grad_obs_ref):
    grad_node_ref[...] = node_ref[...] + node_got_ref[...].astype(F32)
    grad_obs_ref[...] = (obs_ref[...] + obs_got_ref[...].astype(F32)).astype(BF16)


def reduce_halving(steps, tail, slots, keep, send):
    hidden = keep.shape[1]
    for done, nxt in zip(steps[:-1], steps[1:]):
        rows = keep.shape[0] - tail
        rows = (rows // 2 if halves(rows) else rows) + tail
        keep, send = call(
            functools.partial(add_kernel, nxt, tail),
            [((rows, hidden), F32), ((rows, hidden), BF16)],
            keep, flip(send, done),
            scratch=[pltpu.VMEM(keep.shape, F32)],
        )
    rows = keep.shape[0] - tail
    return call(
        last_kernel,
        [((rows, hidden), BF16)] + ([((slots, hidden), F32)] if tail else []),
        keep, flip(send, steps[-1]),
    )


def gather_doubling(steps, rows, piece, outs):
    used = []
    for step in steps:
        if halves(rows):
            used.append(step)
            rows //= 2
    for step in used[:0:-1]:
        (piece,) = call(
            functools.partial(join_kernel, step),
            [((2 * piece.shape[0], piece.shape[1]), BF16)],
            piece, flip(piece, step),
        )
    return call(functools.partial(spread_kernel, used[0]), outs, piece, flip(piece, used[0]))


def local(obs_feat, node_state, grad_agg, owner, local_idx, slot, w_obs, w_node, slot_bias, w_out):
    owners = lax.axis_size(OWNER_AXES)
    obs, fanout = owner.shape
    nodes, width = node_state.shape
    hidden = w_obs.shape[1]
    slots = slot_bias.shape[0]
    cap = max(2, 2 * obs * fanout // owners)
    cap = -(-cap // SUBLANES) * SUBLANES
    edges = owners * cap
    half = width // 2
    slot_row = slot.reshape(1, obs)

    chunk = cap * hidden // obs + SUBLANES
    place, *packed = call_staged(
        functools.partial(pack_kernel, cap),
        [((fanout, obs), jnp.int32)] + [((chunk, obs), BF16)] * owners,
        obs_feat, owner.T, local_idx.T, slot_row, w_obs, slot_bias,
    )
    received = packed[:1] + [shift(packed[j], OWNER_AXES, j) for j in range(1, owners)]
    (table,) = call_staged(
        table_kernel, [((nodes, 4 * hidden), BF16)], node_state, grad_agg, w_node, w_out
    )
    back, act, hot = call(
        functools.partial(edge_kernel, owners, fanout),
        [((owners, cap, hidden), BF16), ((edges, 2 * hidden), BF16), ((edges, nodes), BF16)],
        *received, table,
    )
    back = exchange(back, OWNER_AXES).reshape(edges, hidden)

    steps = halving_steps()
    stack = width + width // hidden * hidden
    node_mine, node_theirs, keep, send = call(
        functools.partial(node_kernel, steps[0]),
        [((nodes, half), F32), ((nodes, half), BF16), ((stack // 2, hidden), F32), ((stack // 2, hidden), BF16)],
        hot, act, node_state, grad_agg, w_node,
        scratch=[pltpu.VMEM((stack, hidden), F32)],
    )
    (node_piece,) = reduce_halving(steps, 0, 0, keep, send)
    node_got = shift(node_theirs, "mp", 1)

    tail = -(-slots // SUBLANES) * SUBLANES
    share = width // 2 + tail
    obs_mine, obs_theirs, keep, send = call(
        functools.partial(obs_kernel, steps[0], tail),
        [((obs, half), F32), ((obs, half), BF16), ((share, hidden), F32), ((share, hidden), BF16)],
        back, place, slot_row, obs_feat, w_obs,
        scratch=[pltpu.VMEM((width + tail, hidden), F32)],
    )
    obs_piece, grad_slot = reduce_halving(steps, tail, slots, keep, send)
    obs_got = shift(obs_theirs, "mp", 1)

    grad_node, grad_obs = call(
        merge_kernel, [((nodes, half), F32), ((obs, half), BF16)],
        node_mine, node_got, obs_mine, obs_got,
    )
    grad_w_node, grad_w_out = gather_doubling(
        steps, stack, node_piece, [((width, hidden), F32), ((hidden, width), F32)]
    )
    (grad_w_obs,) = gather_doubling(steps, width, obs_piece, [((width, hidden), F32)])
    return grad_obs, grad_node, grad_w_obs, grad_w_node, grad_w_out, grad_slot


def solution(mesh):
    rows = P(("group", "obs", "node"), None)
    return jax.shard_map(
        local,
        mesh=mesh,
        in_specs=(
            rows, rows, rows, rows, rows,
            P(("group", "obs", "node")),
            P(None, "mp"), P(None, "mp"), P(None, "mp"), P("mp", None),
        ),
        out_specs=(
            P(("group", "obs", "node"), "mp"),
            P(("group", "obs", "node"), "mp"),
            P("group", "mp"),
            P("group", "mp"),
            P(("group", "mp"), None),
            P("group", "mp"),
        ),
        check_vma=False,
    )
```

```python
import functools

import jax
import jax.numpy as jnp
from jax import lax
from jax.experimental import pallas as pl
from jax.experimental.pallas import tpu as pltpu
from jax.sharding import PartitionSpec as P

OWNER_AXES = ("obs", "node")
SUBLANES = 16
BUNDLES = 1
BF16 = jnp.bfloat16
F32 = jnp.float32


def dot(left, right, left_dim=1, right_dim=0):
    return lax.dot_general(
        left, right, (((left_dim,), (right_dim,)), ((), ())), preferred_element_type=F32
    )


def iota(shape, dim):
    return lax.broadcasted_iota(jnp.int32, shape, dim)


def call(kernel, outs, *args, scratch=(), after=()):
    vmem = pl.BlockSpec(memory_space=pltpu.VMEM)
    count = len(args)
    specs = [vmem] * count + [pl.BlockSpec(memory_space=pl.ANY)] * len(after)
    args += tuple(after)
    return pl.pallas_call(
        lambda *refs: kernel(*refs[:count], *refs[len(args) :]),
        out_shape=[jax.ShapeDtypeStruct(shape, dtype) for shape, dtype in outs],
        in_specs=specs,
        out_specs=[vmem] * len(outs),
        scratch_shapes=list(scratch),
        compiler_params=pltpu.CompilerParams(vmem_limit_bytes=40 << 20),
    )(*args)


def call_staged(kernel, outs, *args, held=()):
    count = len(args)
    sources = list(args) + [a for a in held if not any(a is b for b in args)]
    kept = [next(i for i, b in enumerate(sources) if a is b) for a in held]
    rest = [i for i in range(len(sources)) if i not in kept]

    def staged(*refs):
        hbm, refs = refs[: len(sources)], refs[len(sources) :]
        out_refs, refs = refs[: len(outs)], refs[len(outs) :]
        buffers = dict(zip(kept, refs[: len(kept)])) | dict(zip(rest, refs[len(kept) : -1]))
        copies = [
            pltpu.make_async_copy(hbm[i], buffers[i], refs[-1].at[i]) for i in range(len(sources))
        ]
        for copy in copies:
            copy.start()
        for copy in copies:
            copy.wait()
        kernel(*[buffers[i] for i in range(count)], *out_refs)

    return pl.pallas_call(
        staged,
        out_shape=[jax.ShapeDtypeStruct(shape, dtype) for shape, dtype in outs]
        + [jax.ShapeDtypeStruct(a.shape, a.dtype) for a in held],
        in_specs=[pl.BlockSpec(memory_space=pltpu.HBM)] * len(sources),
        out_specs=[pl.BlockSpec(memory_space=pltpu.VMEM)] * (len(outs) + len(held)),
        scratch_shapes=[pltpu.VMEM(sources[i].shape, sources[i].dtype) for i in rest]
        + [pltpu.SemaphoreType.DMA((len(sources),))],
        compiler_params=pltpu.CompilerParams(vmem_limit_bytes=40 << 20),
    )(*[pltpu.with_memory_space_constraint(a, pltpu.HBM) for a in sources])


def exchange(blocks, axes):
    return lax.all_to_all(blocks, axes, split_axis=0, concat_axis=0, tiled=True)


def shift(value, axis, step):
    size = lax.axis_size(axis)
    return lax.ppermute(value, axis, [(i, (i + step) % size) for i in range(size)])


def other_half(ref):
    half = ref.shape[0] // 2
    me = lax.axis_index("mp")
    mine = ref[pl.ds(pl.multiple_of(me * half, half), half), :]
    theirs = ref[pl.ds(pl.multiple_of((1 - me) * half, half), half), :]
    return mine, theirs


def column_half(ref, which):
    half = ref.shape[1] // 2
    return ref[:, pl.ds(pl.multiple_of(which * half, 128), half)]


def pack_kernel(cap, obs_ref, owner_ref, index_ref, slot_ref, place_ref, other_ref, *outs):
    owners = len(outs)
    chunk, lanes = outs[0].shape
    fanout, obs = owner_ref.shape
    owner, index = owner_ref[...], index_ref[...]
    hits = [iota((owners, obs), 0) == owner[k : k + 1] for k in range(fanout)]
    count = functools.reduce(jnp.add, [h.astype(F32) for h in hits])
    before = dot(count, (iota((obs, obs), 0) < iota((obs, obs), 1)).astype(F32))
    header = jnp.where(iota((SUBLANES, obs), 0) == 4 * fanout, slot_ref[...].astype(F32), 0.0)
    places = []
    for k in range(fanout):
        rank = jnp.sum(jnp.where(hits[k], before, 0.0), axis=0, keepdims=True)
        places.append(owner[k : k + 1] * cap + rank.astype(jnp.int32))
        place_ref[k : k + 1, :] = places[k]
        plus = index[k : k + 1] + 1
        fields = (owner[k : k + 1].astype(F32), rank, (plus // 16).astype(F32), (plus % 16).astype(F32))
        for j, row in enumerate(fields):
            header = jnp.where(iota(header.shape, 0) == 4 * k + j, row, header)
    header = header.astype(BF16)
    me, core = lax.axis_index(OWNER_AXES), lax.axis_index("mp")
    mine, other = column_half(obs_ref, core), column_half(obs_ref, 1 - core)

    def write(ref, pick, rows):
        packed = dot(pick, rows).astype(BF16)
        for c in range(rows.shape[1] // lanes):
            ref[c * cap : (c + 1) * cap, :] = packed[:, c * lanes : (c + 1) * lanes]
        ref[chunk - SUBLANES :, :] = header

    for j, out_ref in enumerate(outs):
        slots = iota((cap, obs), 0) + lax.rem(me + j, owners) * cap
        pick = functools.reduce(jnp.logical_or, [slots == place for place in places]).astype(BF16)
        write(out_ref, pick, mine)
        if j == 0:
            write(other_ref, pick, other)


def table_kernel(state_ref, agg_ref, w_node_ref, w_out_ref, bias_ref, table_ref):
    hidden = w_node_ref.shape[1]
    nodes, slots = state_ref.shape[0], bias_ref.shape[0]
    table_ref[nodes:, :] = jnp.zeros((table_ref.shape[0] - nodes, table_ref.shape[1]), BF16)

    def put(begin, column, part):
        high = part.astype(BF16)
        table_ref[begin : begin + part.shape[0], column : column + hidden] = high
        table_ref[begin : begin + part.shape[0], column + hidden : column + 2 * hidden] = (
            part - high.astype(F32)
        ).astype(BF16)

    put(0, 0, dot(state_ref[...], w_node_ref[...]))
    put(0, 2 * hidden, dot(agg_ref[...], w_out_ref[...], 1, 1))
    put(nodes, 0, bias_ref[...])


def join_blocks_kernel(*refs):
    out_ref = refs[-1]
    for j, ref in enumerate(refs[:-1]):
        out_ref[j] = ref[...]


def edge_kernel(
    fanout, nodes, own_ref, mine_ref, other_ref, theirs_ref, table_ref, w_obs_ref, act_ref, hot_ref, rows_mine_ref, rows_theirs_ref, *back_refs
):
    owners = len(back_refs)
    chunk, lanes = own_ref.shape
    half = w_obs_ref.shape[0] // 2
    hidden = w_obs_ref.shape[1]
    cap = (chunk - SUBLANES) * lanes // half
    me = lax.axis_index(OWNER_AXES).astype(F32)
    base = 1 << nodes.bit_length()
    columns = []
    for j in range(owners):
        block, other = (mine_ref.at[j - 1], theirs_ref.at[j - 1]) if j else (own_ref, other_ref)
        header = block[chunk - SUBLANES :, :].astype(F32)
        slot = header[4 * fanout : 4 * fanout + 1] * base
        code = jnp.zeros((cap, lanes), F32)
        for k in range(fanout):
            row = header[4 * k : 4 * k + 4]
            rank = jnp.where(row[0:1] == me, row[1:2], -1.0).astype(jnp.int32)
            code = code + jnp.where(
                iota((cap, lanes), 0) == rank, row[2:3] * 16.0 + row[3:4] + slot, 0.0
            )
        columns.append(jnp.sum(code, axis=1, keepdims=True).astype(jnp.int32))
        for c in range(half // lanes):
            rows = slice(j * cap, (j + 1) * cap)
            place = slice(c * lanes, (c + 1) * lanes)
            rows_mine_ref[rows, place] = block[c * cap : (c + 1) * cap, :]
            rows_theirs_ref[rows, place] = other[c * cap : (c + 1) * cap, :]
    code = jnp.concatenate(columns, axis=0)
    index, slot = (code & (base - 1)) - 1, (code >> (base.bit_length() - 1)) + nodes
    column = iota(hot_ref.shape, 1)
    hot = ((column == index) | ((column == slot) & (index >= 0))).astype(BF16)
    hot_ref[...] = hot
    rows = dot(hot, table_ref[...])
    w_mine, w_theirs = other_half(w_obs_ref)
    pre = dot(rows_mine_ref[...], w_mine) + dot(rows_theirs_ref[...], w_theirs)
    pre = pre + (rows[:, :hidden] + rows[:, hidden : 2 * hidden])
    g_z = rows[:, 2 * hidden : 3 * hidden] + rows[:, 3 * hidden :]
    sig = jax.nn.sigmoid(pre)
    g_a = (g_z * sig * (1.0 + pre * (1.0 - sig))).astype(BF16)
    act_ref[:, :hidden] = g_a
    act_ref[:, hidden:] = (pre * sig).astype(BF16)
    for j, back_ref in enumerate(back_refs):
        back_ref[...] = g_a[j * cap : (j + 1) * cap]


def halving_steps():
    bits = [
        [(axis, k) for k in range(lax.axis_size(axis).bit_length() - 1)] for axis in ("node", "obs")
    ]
    steps = []
    for k in range(max(map(len, bits))):
        both = [line[k] for line in bits if k < len(line)]
        steps += [(both[0], both[-1])] + ([(both[1], both[0])] if len(both) > 1 else [])
    return steps


def flip(value, step):
    axes = ("obs", "node", "mp")
    sizes = [lax.axis_size(axis) for axis in axes]
    pairs = []
    for index in range(sizes[0] * sizes[1] * sizes[2]):
        place = [index // (sizes[1] * sizes[2]), index // sizes[2] % sizes[1], index % sizes[2]]
        axis, k = step[place[2] % 2]
        place[axes.index(axis)] ^= 1 << k
        pairs.append((index, (place[0] * sizes[1] + place[1]) * sizes[2] + place[2]))
    return lax.ppermute(value, axes, pairs)


def own_bit(step):
    bits = [(lax.axis_index(axis) >> k) & 1 for axis, k in step]
    return jnp.where(lax.axis_index("mp") % 2 == 0, bits[0], bits[1])


def halves(rows):
    return rows % (2 * SUBLANES) == 0


def split_half(total_ref, start, rows, step, tail, keep_ref, send_ref):
    end = start + rows
    if halves(rows):
        rows //= 2
        bit = own_bit(step)
        kept, sent = [pl.ds(pl.multiple_of(start + b * rows, SUBLANES), rows) for b in (bit, 1 - bit)]
    else:
        kept = sent = pl.ds(start, rows)
    keep_ref[:rows, :] = total_ref[kept, :]
    send_ref[:rows, :] = total_ref[sent, :].astype(BF16)
    if tail:
        both = total_ref[end : end + tail, :]
        keep_ref[rows:, :] = both
        send_ref[rows:, :] = both.astype(BF16)


def weight_kernel(
    step, bundles, tail, hot_ref, act_ref, rows_mine_ref, rows_theirs_ref, state_ref, agg_ref, w_node_ref,
    mine_ref, theirs_ref, *refs
):
    halves_refs, total_ref = refs[:-1], refs[-1]
    width, hidden = w_node_ref.shape
    nodes = state_ref.shape[0]
    sums = dot(hot_ref[...], act_ref[...], 0, 0)
    by_node = sums[:nodes].astype(BF16)
    node_hidden, z_sum = by_node[:, :hidden], by_node[:, hidden:]
    total_ref[:width, :] = dot(state_ref[...], node_hidden, 0, 0)
    begin = width
    for c in range(width // hidden):
        total_ref[begin : begin + hidden, :] = dot(
            z_sum, agg_ref[:, c * hidden : (c + 1) * hidden], 0, 0
        )
        begin += hidden
    g_a = act_ref[:, :hidden]
    core, half = lax.axis_index("mp"), width // 2
    for which, ref in ((core, rows_mine_ref), (1 - core, rows_theirs_ref)):
        total_ref[pl.ds(pl.multiple_of(begin + which * half, SUBLANES), half), :] = dot(ref[...], g_a, 0, 0)
    begin += width
    total_ref[begin:, :] = sums[nodes:, :hidden]
    rows = begin // bundles
    for i in range(bundles):
        split_half(
            total_ref, i * rows, rows, step, tail if i == bundles - 1 else 0,
            halves_refs[2 * i], halves_refs[2 * i + 1],
        )
    mine, theirs = other_half(w_node_ref)
    theirs_ref[...] = dot(node_hidden, theirs, 1, 1).astype(BF16)
    mine_ref[...] = dot(node_hidden, mine, 1, 1)


def obs_kernel(owners, *refs):
    back_refs, (place_ref, w_ref, mine_ref, theirs_ref) = refs[:owners], refs[owners:]
    fanout, obs = place_ref.shape
    cap = back_refs[0].shape[0]
    me = lax.axis_index(OWNER_AXES)
    obs_hidden = None
    for j, back_ref in enumerate(back_refs):
        slots = iota((cap, obs), 0) + lax.rem(me + j, owners) * cap
        pick = functools.reduce(
            jnp.logical_or, [slots == place_ref[k : k + 1, :] for k in range(fanout)]
        )
        part = dot(pick.astype(BF16), back_ref[...], 0, 0)
        obs_hidden = part if obs_hidden is None else obs_hidden + part
    obs_hidden = obs_hidden.astype(BF16)
    mine, theirs = other_half(w_ref)
    theirs_ref[...] = dot(obs_hidden, theirs, 1, 1).astype(BF16)
    mine_ref[...] = dot(obs_hidden, mine, 1, 1)


def add_kernel(step, tail, keep_ref, got_ref, next_ref, send_ref, total_ref):
    total_ref[...] = keep_ref[...] + got_ref[...].astype(F32)
    split_half(total_ref, 0, total_ref.shape[0] - tail, step, tail, next_ref, send_ref)


def last_kernel(keep_ref, got_ref, piece_ref, *slot_refs):
    total = keep_ref[...] + got_ref[...].astype(F32)
    rows = piece_ref.shape[0]
    piece_ref[...] = total[:rows].astype(BF16)
    for slot_ref in slot_refs:
        slot_ref[...] = total[rows : rows + slot_ref.shape[0]]


def join_kernel(step, mine_ref, got_ref, out_ref):
    rows = mine_ref.shape[0]
    bit = own_bit(step)
    out_ref[pl.ds(pl.multiple_of(bit * rows, SUBLANES), rows), :] = mine_ref[...]
    out_ref[pl.ds(pl.multiple_of((1 - bit) * rows, SUBLANES), rows), :] = got_ref[...]


def spread_kernel(step, bundles, *refs):
    low = own_bit(step) == 0
    joined = []
    for i in range(bundles):
        mine, got = refs[2 * i][...], refs[2 * i + 1][...]
        joined += [jnp.where(low, mine, got), jnp.where(low, got, mine)]
    half, hidden = joined[0].shape
    at = 0
    for out_ref in refs[2 * bundles :]:
        for c in range(out_ref.shape[1] // hidden):
            begin = 0
            while begin < out_ref.shape[0]:
                offset = at % half
                count = min(out_ref.shape[0] - begin, half - offset)
                out_ref[begin : begin + count, c * hidden : (c + 1) * hidden] = joined[at // half][
                    offset : offset + count
                ].astype(F32)
                at, begin = at + count, begin + count


def merge_kernel(node_ref, node_got_ref, obs_ref, obs_got_ref, grad_node_ref, grad_obs_ref):
    grad_node_ref[...] = node_ref[...] + node_got_ref[...].astype(F32)
    grad_obs_ref[...] = (obs_ref[...] + obs_got_ref[...].astype(F32)).astype(BF16)


def reduce_halving(steps, tail, slots, keep, send, after):
    hidden = keep.shape[1]
    for done, nxt, wait in zip(steps[:-1], steps[1:], after):
        rows = keep.shape[0] - tail
        rows = (rows // 2 if halves(rows) else rows) + tail
        keep, send = call(
            functools.partial(add_kernel, nxt, tail),
            [((rows, hidden), F32), ((rows, hidden), BF16)],
            keep, flip(send, done),
            scratch=[pltpu.VMEM(keep.shape, F32)],
            after=wait,
        )
    rows = keep.shape[0] - tail
    return call(
        last_kernel,
        [((rows, hidden), BF16)] + ([((slots, hidden), F32)] if tail else []),
        keep, flip(send, steps[-1]),
        after=after[len(steps) - 1],
    )


def gather_doubling(steps, rows, piece, after):
    used = []
    for step in steps:
        if halves(rows):
            used.append(step)
            rows //= 2
    for step in used[:0:-1]:
        (piece,) = call(
            functools.partial(join_kernel, step),
            [((2 * piece.shape[0], piece.shape[1]), BF16)],
            piece, flip(piece, step),
            after=after if step == used[1] else (),
        )
    return piece, flip(piece, used[0])


def local(obs_feat, node_state, grad_agg, owner, local_idx, slot, w_obs, w_node, slot_bias, w_out):
    owners = lax.axis_size(OWNER_AXES)
    obs, fanout = owner.shape
    nodes, width = node_state.shape
    hidden = w_obs.shape[1]
    slots = slot_bias.shape[0]
    cap = max(2, 2 * obs * fanout // owners)
    cap = -(-cap // SUBLANES) * SUBLANES
    edges = owners * cap
    half = width // 2
    slot_row = slot.reshape(1, obs)

    chunk = cap * half // obs + SUBLANES
    place, other, *packed = call_staged(
        functools.partial(pack_kernel, cap),
        [((fanout, obs), jnp.int32)] + [((chunk, obs), BF16)] * (owners + 1),
        obs_feat, owner.T, local_idx.T, slot_row,
    )
    received = [shift(packed[j], OWNER_AXES, j) for j in range(1, owners)]
    tail = -(-slots // SUBLANES) * SUBLANES
    table, state_held, agg_held, w_node_held, w_obs_held = call_staged(
        table_kernel,
        [((nodes + tail, 4 * hidden), BF16)],
        node_state, grad_agg, w_node, w_out, slot_bias,
        held=(node_state, grad_agg, w_node, w_obs),
    )
    (mine,) = call(
        join_blocks_kernel, [((owners - 1, chunk, obs), BF16)], *received,
        after=(w_obs_held,),
    )
    theirs = shift(mine, "mp", 1)
    act, hot, rows_mine, rows_theirs, *back = call(
        functools.partial(edge_kernel, fanout, nodes),
        [((edges, 2 * hidden), BF16), ((edges, nodes + tail), BF16)]
        + [((edges, half), BF16)] * 2
        + [((cap, hidden), BF16)] * owners,
        packed[0], mine, other, theirs, table, w_obs_held,
    )

    steps = halving_steps()
    stack = 2 * width + width // hidden * hidden
    bundles = BUNDLES
    rows = stack // bundles
    shapes = []
    for i in range(bundles):
        share = rows // 2 + (tail if i == bundles - 1 else 0)
        shapes += [((share, hidden), F32), ((share, hidden), BF16)]
    node_mine, node_theirs, *shares = call(
        functools.partial(weight_kernel, steps[0], bundles, tail),
        [((nodes, half), F32), ((nodes, half), BF16)] + shapes,
        hot, act, rows_mine, rows_theirs, state_held, agg_held, w_node_held,
        scratch=[pltpu.VMEM((stack + tail, hidden), F32)],
    )
    node_got = shift(node_theirs, "mp", 1)

    back = back[:1] + [shift(back[j], OWNER_AXES, -j) for j in range(1, owners)]
    obs_mine, obs_theirs = call(
        functools.partial(obs_kernel, owners),
        [((obs, half), F32), ((obs, half), BF16)],
        *back, place, w_obs_held,
    )
    obs_got = shift(obs_theirs, "mp", 1)
    grad_node, grad_obs = call(
        merge_kernel, [((nodes, half), F32), ((obs, half), BF16)],
        node_mine, node_got, obs_mine, obs_got,
    )

    waits = [back[1 + i * (owners - 1) // len(steps) : 1 + (i + 1) * (owners - 1) // len(steps)] for i in range(len(steps))]
    held_back = [pltpu.with_memory_space_constraint(grad_obs, pltpu.HBM)]
    ends = []
    for i in range(bundles):
        last = i == bundles - 1
        piece, *grad_slot = reduce_halving(
            steps, tail if last else 0, slots, shares[2 * i], shares[2 * i + 1], waits
        )
        ends += gather_doubling(steps, rows, piece, held_back)
    grad_w_node, grad_w_out, grad_w_obs = call(
        functools.partial(spread_kernel, steps[0], bundles),
        [((width, hidden), F32), ((hidden, width), F32), ((width, hidden), F32)],
        *ends,
    )
    (grad_slot,) = grad_slot
    return grad_obs, grad_node, grad_w_obs, grad_w_node, grad_w_out, grad_slot


def solution(mesh):
    rows = P(("group", "obs", "node"), None)
    return jax.shard_map(
        local,
        mesh=mesh,
        in_specs=(
            rows, rows, rows, rows, rows,
            P(("group", "obs", "node")),
            P(None, "mp"), P(None, "mp"), P(None, "mp"), P("mp", None),
        ),
        out_specs=(
            P(("group", "obs", "node"), "mp"),
            P(("group", "obs", "node"), "mp"),
            P("group", "mp"),
            P("group", "mp"),
            P(("group", "mp"), None),
            P("group", "mp"),
        ),
        check_vma=False,
    )
```

```python
import functools

import jax
import jax.numpy as jnp
from jax import lax
from jax.experimental import pallas as pl
from jax.experimental.pallas import tpu as pltpu
from jax.sharding import PartitionSpec as P

OWNER_AXES = ("obs", "node")
SUBLANES = 16
BUNDLES = 1
BF16 = jnp.bfloat16
F32 = jnp.float32


def dot(left, right, left_dim=1, right_dim=0):
    return lax.dot_general(
        left, right, (((left_dim,), (right_dim,)), ((), ())), preferred_element_type=F32
    )


def iota(shape, dim):
    return lax.broadcasted_iota(jnp.int32, shape, dim)


def call(kernel, outs, *args, scratch=(), after=()):
    vmem = pl.BlockSpec(memory_space=pltpu.VMEM)
    count = len(args)
    specs = [vmem] * count + [pl.BlockSpec(memory_space=pl.ANY)] * len(after)
    args += tuple(after)
    return pl.pallas_call(
        lambda *refs: kernel(*refs[:count], *refs[len(args) :]),
        out_shape=[jax.ShapeDtypeStruct(shape, dtype) for shape, dtype in outs],
        in_specs=specs,
        out_specs=[vmem] * len(outs),
        scratch_shapes=list(scratch),
        compiler_params=pltpu.CompilerParams(vmem_limit_bytes=40 << 20),
    )(*args)


def call_staged(kernel, outs, *args, held=()):
    count = len(args)
    sources = list(args) + [a for a in held if not any(a is b for b in args)]
    kept = [next(i for i, b in enumerate(sources) if a is b) for a in held]
    rest = [i for i in range(len(sources)) if i not in kept]

    def staged(*refs):
        hbm, refs = refs[: len(sources)], refs[len(sources) :]
        out_refs, refs = refs[: len(outs)], refs[len(outs) :]
        buffers = dict(zip(kept, refs[: len(kept)])) | dict(zip(rest, refs[len(kept) : -1]))
        copies = [
            pltpu.make_async_copy(hbm[i], buffers[i], refs[-1].at[i]) for i in range(len(sources))
        ]
        for copy in copies:
            copy.start()
        for copy in copies:
            copy.wait()
        kernel(*[buffers[i] for i in range(count)], *out_refs)

    return pl.pallas_call(
        staged,
        out_shape=[jax.ShapeDtypeStruct(shape, dtype) for shape, dtype in outs]
        + [jax.ShapeDtypeStruct(a.shape, a.dtype) for a in held],
        in_specs=[pl.BlockSpec(memory_space=pltpu.HBM)] * len(sources),
        out_specs=[pl.BlockSpec(memory_space=pltpu.VMEM)] * (len(outs) + len(held)),
        scratch_shapes=[pltpu.VMEM(sources[i].shape, sources[i].dtype) for i in rest]
        + [pltpu.SemaphoreType.DMA((len(sources),))],
        compiler_params=pltpu.CompilerParams(vmem_limit_bytes=40 << 20),
    )(*[pltpu.with_memory_space_constraint(a, pltpu.HBM) for a in sources])


def exchange(blocks, axes):
    return lax.all_to_all(blocks, axes, split_axis=0, concat_axis=0, tiled=True)


def shift(value, axis, step):
    size = lax.axis_size(axis)
    return lax.ppermute(value, axis, [(i, (i + step) % size) for i in range(size)])


def other_half(ref):
    half = ref.shape[0] // 2
    me = lax.axis_index("mp")
    mine = ref[pl.ds(pl.multiple_of(me * half, half), half), :]
    theirs = ref[pl.ds(pl.multiple_of((1 - me) * half, half), half), :]
    return mine, theirs


def column_half(ref, which):
    half = ref.shape[1] // 2
    return ref[:, pl.ds(pl.multiple_of(which * half, 128), half)]


def pack_kernel(cap, obs_ref, owner_ref, index_ref, slot_ref, other_ref, *outs):
    owners = len(outs)
    chunk, lanes = outs[0].shape
    fanout, obs = owner_ref.shape
    owner, index = owner_ref[...], index_ref[...]
    hits = [iota((owners, obs), 0) == owner[k : k + 1] for k in range(fanout)]
    count = functools.reduce(jnp.add, [h.astype(F32) for h in hits])
    before = dot(count, (iota((obs, obs), 0) < iota((obs, obs), 1)).astype(F32))
    header = jnp.where(iota((SUBLANES, obs), 0) == 4 * fanout, slot_ref[...].astype(F32), 0.0)
    places = []
    for k in range(fanout):
        rank = jnp.sum(jnp.where(hits[k], before, 0.0), axis=0, keepdims=True)
        places.append(owner[k : k + 1] * cap + rank.astype(jnp.int32))
        plus = index[k : k + 1] + 1
        fields = (owner[k : k + 1].astype(F32), rank, (plus // 16).astype(F32), (plus % 16).astype(F32))
        for j, row in enumerate(fields):
            header = jnp.where(iota(header.shape, 0) == 4 * k + j, row, header)
    header = header.astype(BF16)
    me, core = lax.axis_index(OWNER_AXES), lax.axis_index("mp")
    mine, other = column_half(obs_ref, core), column_half(obs_ref, 1 - core)

    def write(ref, pick, rows):
        packed = dot(pick, rows).astype(BF16)
        for c in range(rows.shape[1] // lanes):
            ref[c * cap : (c + 1) * cap, :] = packed[:, c * lanes : (c + 1) * lanes]
        ref[chunk - SUBLANES :, :] = header

    for j, out_ref in enumerate(outs):
        slots = iota((cap, obs), 0) + lax.rem(me + j, owners) * cap
        pick = functools.reduce(jnp.logical_or, [slots == place for place in places]).astype(BF16)
        write(out_ref, pick, mine)
        if j == 0:
            write(other_ref, pick, other)


def table_kernel(state_ref, agg_ref, w_node_ref, w_out_ref, bias_ref, table_ref):
    hidden = w_node_ref.shape[1]
    nodes, slots = state_ref.shape[0], bias_ref.shape[0]
    table_ref[nodes:, :] = jnp.zeros((table_ref.shape[0] - nodes, table_ref.shape[1]), BF16)

    def put(begin, column, part):
        high = part.astype(BF16)
        table_ref[begin : begin + part.shape[0], column : column + hidden] = high
        table_ref[begin : begin + part.shape[0], column + hidden : column + 2 * hidden] = (
            part - high.astype(F32)
        ).astype(BF16)

    put(0, 0, dot(state_ref[...], w_node_ref[...]))
    put(0, 2 * hidden, dot(agg_ref[...], w_out_ref[...], 1, 1))
    put(nodes, 0, bias_ref[...])


def join_blocks_kernel(*refs):
    out_ref = refs[-1]
    for j, ref in enumerate(refs[:-1]):
        out_ref[j] = ref[...]


def edge_kernel(
    fanout, nodes, steps, own_ref, mine_ref, other_ref, theirs_ref, table_ref, w_obs_ref,
    act_ref, hot_ref, rows_mine_ref, rows_theirs_ref, keep_ref, send_ref, total_ref,
):
    owners = mine_ref.shape[0] + 1
    chunk, lanes = own_ref.shape
    half = w_obs_ref.shape[0] // 2
    hidden = w_obs_ref.shape[1]
    cap = (chunk - SUBLANES) * lanes // half
    me = lax.axis_index(OWNER_AXES)
    base = 1 << nodes.bit_length()
    columns = []
    picks = []
    for j in range(owners):
        block, other = (mine_ref.at[j - 1], theirs_ref.at[j - 1]) if j else (own_ref, other_ref)
        header = block[chunk - SUBLANES :, :].astype(F32)
        slot = header[4 * fanout : 4 * fanout + 1] * base
        code = jnp.zeros((cap, lanes), F32)
        pick = jnp.zeros((cap, lanes), jnp.bool_)
        for k in range(fanout):
            row = header[4 * k : 4 * k + 4]
            rank = jnp.where(row[0:1] == me.astype(F32), row[1:2], -1.0).astype(jnp.int32)
            hit = iota((cap, lanes), 0) == rank
            pick = pick | hit
            code = code + jnp.where(hit, row[2:3] * 16.0 + row[3:4] + slot, 0.0)
        picks.append(pick.astype(BF16))
        columns.append(jnp.sum(code, axis=1, keepdims=True).astype(jnp.int32))
        for c in range(half // lanes):
            rows = slice(j * cap, (j + 1) * cap)
            place = slice(c * lanes, (c + 1) * lanes)
            rows_mine_ref[rows, place] = block[c * cap : (c + 1) * cap, :]
            rows_theirs_ref[rows, place] = other[c * cap : (c + 1) * cap, :]
    code = jnp.concatenate(columns, axis=0)
    index, slot = (code & (base - 1)) - 1, (code >> (base.bit_length() - 1)) + nodes
    column = iota(hot_ref.shape, 1)
    hot = ((column == index) | ((column == slot) & (index >= 0))).astype(BF16)
    hot_ref[...] = hot
    rows = dot(hot, table_ref[...])
    w_mine, w_theirs = other_half(w_obs_ref)
    pre = dot(rows_mine_ref[...], w_mine) + dot(rows_theirs_ref[...], w_theirs)
    pre = pre + (rows[:, :hidden] + rows[:, hidden : 2 * hidden])
    g_z = rows[:, 2 * hidden : 3 * hidden] + rows[:, 3 * hidden :]
    sig = jax.nn.sigmoid(pre)
    g_a = (g_z * sig * (1.0 + pre * (1.0 - sig))).astype(BF16)
    act_ref[:, :hidden] = g_a
    act_ref[:, hidden:] = (pre * sig).astype(BF16)
    for j, pick in enumerate(picks):
        source = lax.rem(me - j + owners, owners)
        begin = pl.multiple_of(place_of(source, steps) * lanes, SUBLANES)
        total_ref[pl.ds(begin, lanes), :] = dot(pick, g_a[j * cap : (j + 1) * cap], 0, 0).astype(BF16)
    split_half(total_ref, 0, owners * lanes, steps[0], 0, keep_ref, send_ref)


def halving_steps():
    bits = [
        [(axis, k) for k in range(lax.axis_size(axis).bit_length() - 1)] for axis in ("node", "obs")
    ]
    steps = []
    for k in range(max(map(len, bits))):
        both = [line[k] for line in bits if k < len(line)]
        steps += [(both[0], both[-1])] + ([(both[1], both[0])] if len(both) > 1 else [])
    return steps


def flip(value, step):
    axes = ("obs", "node", "mp")
    sizes = [lax.axis_size(axis) for axis in axes]
    pairs = []
    for index in range(sizes[0] * sizes[1] * sizes[2]):
        place = [index // (sizes[1] * sizes[2]), index // sizes[2] % sizes[1], index % sizes[2]]
        axis, k = step[place[2] % 2]
        place[axes.index(axis)] ^= 1 << k
        pairs.append((index, (place[0] * sizes[1] + place[1]) * sizes[2] + place[2]))
    return lax.ppermute(value, axes, pairs)


def bit_of(step, node, obs):
    bits = [({"node": node, "obs": obs}[axis] >> k) & 1 for axis, k in step]
    return jnp.where(lax.axis_index("mp") % 2 == 0, bits[0], bits[1])


def own_bit(step):
    return bit_of(step, lax.axis_index("node"), lax.axis_index("obs"))


def place_of(owner, steps):
    shares = lax.axis_size("node")
    place = 0
    for step in steps:
        place = 2 * place + bit_of(step, lax.rem(owner, shares), lax.div(owner, shares))
    return place


def halves(rows):
    return rows % (2 * SUBLANES) == 0


def split_half(total_ref, start, rows, step, tail, keep_ref, send_ref):
    end = start + rows
    if halves(rows):
        rows //= 2
        bit = own_bit(step)
        kept, sent = [pl.ds(pl.multiple_of(start + b * rows, SUBLANES), rows) for b in (bit, 1 - bit)]
    else:
        kept = sent = pl.ds(start, rows)
    keep_ref[:rows, :] = total_ref[kept, :]
    send_ref[:rows, :] = total_ref[sent, :].astype(BF16)
    if tail:
        both = total_ref[end : end + tail, :]
        keep_ref[rows:, :] = both
        send_ref[rows:, :] = both.astype(BF16)


def weight_kernel(
    step, bundles, tail, hot_ref, act_ref, rows_mine_ref, rows_theirs_ref, state_ref, agg_ref, w_node_ref,
    mine_ref, theirs_ref, *refs
):
    halves_refs, total_ref = refs[:-1], refs[-1]
    width, hidden = w_node_ref.shape
    nodes = state_ref.shape[0]
    sums = dot(hot_ref[...], act_ref[...], 0, 0)
    by_node = sums[:nodes].astype(BF16)
    node_hidden, z_sum = by_node[:, :hidden], by_node[:, hidden:]
    total_ref[:width, :] = dot(state_ref[...], node_hidden, 0, 0)
    begin = width
    for c in range(width // hidden):
        total_ref[begin : begin + hidden, :] = dot(
            z_sum, agg_ref[:, c * hidden : (c + 1) * hidden], 0, 0
        )
        begin += hidden
    g_a = act_ref[:, :hidden]
    core, half = lax.axis_index("mp"), width // 2
    for which, ref in ((core, rows_mine_ref), (1 - core, rows_theirs_ref)):
        total_ref[pl.ds(pl.multiple_of(begin + which * half, SUBLANES), half), :] = dot(ref[...], g_a, 0, 0)
    begin += width
    total_ref[begin:, :] = sums[nodes:, :hidden]
    rows = begin // bundles
    for i in range(bundles):
        split_half(
            total_ref, i * rows, rows, step, tail if i == bundles - 1 else 0,
            halves_refs[2 * i], halves_refs[2 * i + 1],
        )
    mine, theirs = other_half(w_node_ref)
    theirs_ref[...] = dot(node_hidden, theirs, 1, 1).astype(BF16)
    mine_ref[...] = dot(node_hidden, mine, 1, 1)


def obs_kernel(keep_ref, got_ref, w_ref, mine_ref, theirs_ref):
    obs_hidden = (keep_ref[...].astype(F32) + got_ref[...].astype(F32)).astype(BF16)
    mine, theirs = other_half(w_ref)
    theirs_ref[...] = dot(obs_hidden, theirs, 1, 1).astype(BF16)
    mine_ref[...] = dot(obs_hidden, mine, 1, 1)


def add_kernel(step, tail, keep_ref, got_ref, next_ref, send_ref, total_ref):
    total = keep_ref[...].astype(F32) + got_ref[...].astype(F32)
    total_ref[...] = total.astype(total_ref.dtype)
    split_half(total_ref, 0, total_ref.shape[0] - tail, step, tail, next_ref, send_ref)


def last_kernel(keep_ref, got_ref, piece_ref, *slot_refs):
    total = keep_ref[...] + got_ref[...].astype(F32)
    rows = piece_ref.shape[0]
    piece_ref[...] = total[:rows].astype(BF16)
    for slot_ref in slot_refs:
        slot_ref[...] = total[rows : rows + slot_ref.shape[0]]


def join_kernel(step, mine_ref, got_ref, out_ref):
    rows = mine_ref.shape[0]
    bit = own_bit(step)
    out_ref[pl.ds(pl.multiple_of(bit * rows, SUBLANES), rows), :] = mine_ref[...]
    out_ref[pl.ds(pl.multiple_of((1 - bit) * rows, SUBLANES), rows), :] = got_ref[...]


def spread_kernel(step, bundles, *refs):
    low = own_bit(step) == 0
    joined = []
    for i in range(bundles):
        mine, got = refs[2 * i][...], refs[2 * i + 1][...]
        joined += [jnp.where(low, mine, got), jnp.where(low, got, mine)]
    half, hidden = joined[0].shape
    at = 0
    for out_ref in refs[2 * bundles :]:
        for c in range(out_ref.shape[1] // hidden):
            begin = 0
            while begin < out_ref.shape[0]:
                offset = at % half
                count = min(out_ref.shape[0] - begin, half - offset)
                out_ref[begin : begin + count, c * hidden : (c + 1) * hidden] = joined[at // half][
                    offset : offset + count
                ].astype(F32)
                at, begin = at + count, begin + count


def merge_kernel(node_ref, node_got_ref, obs_ref, obs_got_ref, grad_node_ref, grad_obs_ref):
    grad_node_ref[...] = node_ref[...] + node_got_ref[...].astype(F32)
    grad_obs_ref[...] = (obs_ref[...] + obs_got_ref[...].astype(F32)).astype(BF16)


def half_rows(rows):
    return rows // 2 if halves(rows) else rows


def summing(steps, tail, keep, send, after):
    hidden = keep.shape[1]
    for done, nxt in zip(steps[:-1], steps[1:]):
        rows = half_rows(keep.shape[0] - tail) + tail
        keep, send = call(
            functools.partial(add_kernel, nxt, tail),
            [((rows, hidden), keep.dtype), ((rows, hidden), BF16)],
            keep, flip(send, done),
            scratch=[pltpu.VMEM(keep.shape, keep.dtype)],
            after=after,
        )
        after[:] = [send]
        yield
    return keep, flip(send, steps[-1])


def weight_chain(steps, rows, tail, slots, keep, send, after):
    used = []
    for step in steps:
        if halves(rows):
            used.append(step)
            rows //= 2
    keep, got = yield from summing(steps, tail, keep, send, after)
    piece, *sums = call(
        last_kernel,
        [((rows, keep.shape[1]), BF16)] + ([((slots, keep.shape[1]), F32)] if tail else []),
        keep, got,
        after=after,
    )
    after[:] = [piece]
    yield
    for step in used[:0:-1]:
        (piece,) = call(
            functools.partial(join_kernel, step),
            [((2 * piece.shape[0], piece.shape[1]), BF16)],
            piece, flip(piece, step),
            after=after,
        )
        after[:] = [piece]
        yield
    return [piece, flip(piece, used[0])], sums


def obs_chain(steps, w_obs, node_mine, node_theirs, keep, send, after):
    keep, got = yield from summing(steps, 0, keep, send, after)
    half = w_obs.shape[0] // 2
    obs_mine, obs_theirs = call(
        obs_kernel, [((keep.shape[0], half), F32), ((keep.shape[0], half), BF16)], keep, got, w_obs,
        after=after,
    )
    after[:] = [obs_theirs]
    yield
    grad_node, grad_obs = call(
        merge_kernel, [(node_mine.shape, F32), (obs_mine.shape, BF16)],
        node_mine, shift(node_theirs, "mp", 1), obs_mine, shift(obs_theirs, "mp", 1),
        after=after,
    )
    after[:] = [pltpu.with_memory_space_constraint(grad_obs, pltpu.HBM)]
    yield
    return grad_node, grad_obs


def in_turns(chains):
    results = [None] * len(chains)
    running = list(enumerate(chains))
    while running:
        for item in list(running):
            try:
                next(item[1])
            except StopIteration as stop:
                results[item[0]] = stop.value
                running.remove(item)
    return results


def local(obs_feat, node_state, grad_agg, owner, local_idx, slot, w_obs, w_node, slot_bias, w_out):
    owners = lax.axis_size(OWNER_AXES)
    obs, fanout = owner.shape
    nodes, width = node_state.shape
    hidden = w_obs.shape[1]
    slots = slot_bias.shape[0]
    cap = max(2, 2 * obs * fanout // owners)
    cap = -(-cap // SUBLANES) * SUBLANES
    edges = owners * cap
    half = width // 2
    slot_row = slot.reshape(1, obs)

    steps = halving_steps()
    chunk = cap * half // obs + SUBLANES
    other, *packed = call_staged(
        functools.partial(pack_kernel, cap),
        [((chunk, obs), BF16)] * (owners + 1),
        obs_feat, owner.T, local_idx.T, slot_row,
    )
    received = [shift(packed[j], OWNER_AXES, j) for j in range(1, owners)]
    tail = -(-slots // SUBLANES) * SUBLANES
    table, state_held, agg_held, w_node_held, w_obs_held = call_staged(
        table_kernel,
        [((nodes + tail, 4 * hidden), BF16)],
        node_state, grad_agg, w_node, w_out, slot_bias,
        held=(node_state, grad_agg, w_node, w_obs),
    )
    (mine,) = call(
        join_blocks_kernel, [((owners - 1, chunk, obs), BF16)], *received,
        after=(w_obs_held,),
    )
    theirs = shift(mine, "mp", 1)
    act, hot, rows_mine, rows_theirs, obs_keep, obs_send = call(
        functools.partial(edge_kernel, fanout, nodes, steps),
        [((edges, 2 * hidden), BF16), ((edges, nodes + tail), BF16)]
        + [((edges, half), BF16)] * 2
        + [((owners * obs // 2, hidden), BF16)] * 2,
        packed[0], mine, other, theirs, table, w_obs_held,
        scratch=[pltpu.VMEM((owners * obs, hidden), BF16)],
    )

    stack = 2 * width + width // hidden * hidden
    bundles = BUNDLES
    rows = stack // bundles
    shapes = []
    for i in range(bundles):
        share = rows // 2 + (tail if i == bundles - 1 else 0)
        shapes += [((share, hidden), F32), ((share, hidden), BF16)]
    node_mine, node_theirs, *shares = call(
        functools.partial(weight_kernel, steps[0], bundles, tail),
        [((nodes, half), F32), ((nodes, half), BF16)] + shapes,
        hot, act, rows_mine, rows_theirs, state_held, agg_held, w_node_held,
        scratch=[pltpu.VMEM((stack + tail, hidden), F32)],
    )
    after = []
    chains = [
        weight_chain(
            steps, rows, tail if i == bundles - 1 else 0, slots, shares[2 * i], shares[2 * i + 1], after
        )
        for i in range(bundles)
    ]
    chains.append(obs_chain(steps, w_obs_held, node_mine, node_theirs, obs_keep, obs_send, after))
    *weights, (grad_node, grad_obs) = in_turns(chains)
    ends = [end for pair, _ in weights for end in pair]
    (grad_slot,) = weights[-1][1]
    grad_w_node, grad_w_out, grad_w_obs = call(
        functools.partial(spread_kernel, steps[0], bundles),
        [((width, hidden), F32), ((hidden, width), F32), ((width, hidden), F32)],
        *ends,
    )
    return grad_obs, grad_node, grad_w_obs, grad_w_node, grad_w_out, grad_slot


def solution(mesh):
    rows = P(("group", "obs", "node"), None)
    return jax.shard_map(
        local,
        mesh=mesh,
        in_specs=(
            rows, rows, rows, rows, rows,
            P(("group", "obs", "node")),
            P(None, "mp"), P(None, "mp"), P(None, "mp"), P("mp", None),
        ),
        out_specs=(
            P(("group", "obs", "node"), "mp"),
            P(("group", "obs", "node"), "mp"),
            P("group", "mp"),
            P("group", "mp"),
            P(("group", "mp"), None),
            P("group", "mp"),
        ),
        check_vma=False,
    )
```

```python
import functools

import jax
import jax.numpy as jnp
from jax import lax
from jax.experimental import pallas as pl
from jax.experimental.pallas import tpu as pltpu
from jax.sharding import PartitionSpec as P

OWNER_AXES = ("obs", "node")
SUBLANES = 16
BUNDLES = 2
BF16 = jnp.bfloat16
F32 = jnp.float32


def dot(left, right, left_dim=1, right_dim=0):
    return lax.dot_general(
        left, right, (((left_dim,), (right_dim,)), ((), ())), preferred_element_type=F32
    )


def iota(shape, dim):
    return lax.broadcasted_iota(jnp.int32, shape, dim)


def call(kernel, outs, *args, scratch=(), after=()):
    vmem = pl.BlockSpec(memory_space=pltpu.VMEM)
    count = len(args)
    specs = [vmem] * count + [pl.BlockSpec(memory_space=pl.ANY)] * len(after)
    args += tuple(after)
    return pl.pallas_call(
        lambda *refs: kernel(*refs[:count], *refs[len(args) :]),
        out_shape=[jax.ShapeDtypeStruct(shape, dtype) for shape, dtype in outs],
        in_specs=specs,
        out_specs=[vmem] * len(outs),
        scratch_shapes=list(scratch),
        compiler_params=pltpu.CompilerParams(vmem_limit_bytes=40 << 20),
    )(*args)


def call_staged(kernel, outs, *args, held=()):
    count = len(args)
    sources = list(args) + [a for a in held if not any(a is b for b in args)]
    kept = [next(i for i, b in enumerate(sources) if a is b) for a in held]
    rest = [i for i in range(len(sources)) if i not in kept]

    def staged(*refs):
        hbm, refs = refs[: len(sources)], refs[len(sources) :]
        out_refs, refs = refs[: len(outs)], refs[len(outs) :]
        buffers = dict(zip(kept, refs[: len(kept)])) | dict(zip(rest, refs[len(kept) : -1]))
        copies = [
            pltpu.make_async_copy(hbm[i], buffers[i], refs[-1].at[i]) for i in range(len(sources))
        ]
        for copy in copies:
            copy.start()
        for copy in copies:
            copy.wait()
        kernel(*[buffers[i] for i in range(count)], *out_refs)

    return pl.pallas_call(
        staged,
        out_shape=[jax.ShapeDtypeStruct(shape, dtype) for shape, dtype in outs]
        + [jax.ShapeDtypeStruct(a.shape, a.dtype) for a in held],
        in_specs=[pl.BlockSpec(memory_space=pltpu.HBM)] * len(sources),
        out_specs=[pl.BlockSpec(memory_space=pltpu.VMEM)] * (len(outs) + len(held)),
        scratch_shapes=[pltpu.VMEM(sources[i].shape, sources[i].dtype) for i in rest]
        + [pltpu.SemaphoreType.DMA((len(sources),))],
        compiler_params=pltpu.CompilerParams(vmem_limit_bytes=40 << 20),
    )(*[pltpu.with_memory_space_constraint(a, pltpu.HBM) for a in sources])


def exchange(blocks, axes):
    return lax.all_to_all(blocks, axes, split_axis=0, concat_axis=0, tiled=True)


def shift(value, axis, step):
    size = lax.axis_size(axis)
    return lax.ppermute(value, axis, [(i, (i + step) % size) for i in range(size)])


def other_half(ref):
    half = ref.shape[0] // 2
    me = lax.axis_index("mp")
    mine = ref[pl.ds(pl.multiple_of(me * half, half), half), :]
    theirs = ref[pl.ds(pl.multiple_of((1 - me) * half, half), half), :]
    return mine, theirs


def column_half(ref, which):
    half = ref.shape[1] // 2
    return ref[:, pl.ds(pl.multiple_of(which * half, 128), half)]


def pack_kernel(cap, obs_ref, owner_ref, index_ref, slot_ref, other_ref, *outs):
    owners = len(outs)
    chunk, lanes = outs[0].shape
    fanout, obs = owner_ref.shape
    owner, index = owner_ref[...], index_ref[...]
    hits = [iota((owners, obs), 0) == owner[k : k + 1] for k in range(fanout)]
    count = functools.reduce(jnp.add, [h.astype(F32) for h in hits])
    before = dot(count, (iota((obs, obs), 0) < iota((obs, obs), 1)).astype(F32))
    header = jnp.where(iota((SUBLANES, obs), 0) == 4 * fanout, slot_ref[...].astype(F32), 0.0)
    places = []
    for k in range(fanout):
        rank = jnp.sum(jnp.where(hits[k], before, 0.0), axis=0, keepdims=True)
        places.append(owner[k : k + 1] * cap + rank.astype(jnp.int32))
        plus = index[k : k + 1] + 1
        fields = (owner[k : k + 1].astype(F32), rank, (plus // 16).astype(F32), (plus % 16).astype(F32))
        for j, row in enumerate(fields):
            header = jnp.where(iota(header.shape, 0) == 4 * k + j, row, header)
    header = header.astype(BF16)
    me, core = lax.axis_index(OWNER_AXES), lax.axis_index("mp")
    mine, other = column_half(obs_ref, core), column_half(obs_ref, 1 - core)

    def write(ref, pick, rows):
        packed = dot(pick, rows).astype(BF16)
        for c in range(rows.shape[1] // lanes):
            ref[c * cap : (c + 1) * cap, :] = packed[:, c * lanes : (c + 1) * lanes]
        ref[chunk - SUBLANES :, :] = header

    for j, out_ref in enumerate(outs):
        slots = iota((cap, obs), 0) + lax.rem(me + j, owners) * cap
        pick = functools.reduce(jnp.logical_or, [slots == place for place in places]).astype(BF16)
        write(out_ref, pick, mine)
        if j == 0:
            write(other_ref, pick, other)


def table_kernel(state_ref, agg_ref, w_node_ref, w_out_ref, bias_ref, table_ref):
    hidden = w_node_ref.shape[1]
    nodes, slots = state_ref.shape[0], bias_ref.shape[0]
    table_ref[nodes:, :] = jnp.zeros((table_ref.shape[0] - nodes, table_ref.shape[1]), BF16)

    def put(begin, column, part):
        high = part.astype(BF16)
        table_ref[begin : begin + part.shape[0], column : column + hidden] = high
        table_ref[begin : begin + part.shape[0], column + hidden : column + 2 * hidden] = (
            part - high.astype(F32)
        ).astype(BF16)

    put(0, 0, dot(state_ref[...], w_node_ref[...]))
    put(0, 2 * hidden, dot(agg_ref[...], w_out_ref[...], 1, 1))
    put(nodes, 0, bias_ref[...])


def join_blocks_kernel(*refs):
    out_ref = refs[-1]
    for j, ref in enumerate(refs[:-1]):
        out_ref[j] = ref[...]


def edge_kernel(
    fanout, nodes, steps, own_ref, mine_ref, other_ref, theirs_ref, table_ref, w_obs_ref,
    act_ref, hot_ref, rows_mine_ref, rows_theirs_ref, keep_ref, send_ref, total_ref,
):
    owners = mine_ref.shape[0] + 1
    chunk, lanes = own_ref.shape
    half = w_obs_ref.shape[0] // 2
    hidden = w_obs_ref.shape[1]
    cap = (chunk - SUBLANES) * lanes // half
    me = lax.axis_index(OWNER_AXES)
    base = 1 << nodes.bit_length()
    columns = []
    picks = []
    for j in range(owners):
        block, other = (mine_ref.at[j - 1], theirs_ref.at[j - 1]) if j else (own_ref, other_ref)
        header = block[chunk - SUBLANES :, :].astype(F32)
        slot = header[4 * fanout : 4 * fanout + 1] * base
        code = jnp.zeros((cap, lanes), F32)
        pick = jnp.zeros((cap, lanes), jnp.bool_)
        for k in range(fanout):
            row = header[4 * k : 4 * k + 4]
            rank = jnp.where(row[0:1] == me.astype(F32), row[1:2], -1.0).astype(jnp.int32)
            hit = iota((cap, lanes), 0) == rank
            pick = pick | hit
            code = code + jnp.where(hit, row[2:3] * 16.0 + row[3:4] + slot, 0.0)
        picks.append(pick.astype(BF16))
        columns.append(jnp.sum(code, axis=1, keepdims=True).astype(jnp.int32))
        for c in range(half // lanes):
            rows = slice(j * cap, (j + 1) * cap)
            place = slice(c * lanes, (c + 1) * lanes)
            rows_mine_ref[rows, place] = block[c * cap : (c + 1) * cap, :]
            rows_theirs_ref[rows, place] = other[c * cap : (c + 1) * cap, :]
    code = jnp.concatenate(columns, axis=0)
    index, slot = (code & (base - 1)) - 1, (code >> (base.bit_length() - 1)) + nodes
    column = iota(hot_ref.shape, 1)
    hot = ((column == index) | ((column == slot) & (index >= 0))).astype(BF16)
    hot_ref[...] = hot
    rows = dot(hot, table_ref[...])
    w_mine, w_theirs = other_half(w_obs_ref)
    pre = dot(rows_mine_ref[...], w_mine) + dot(rows_theirs_ref[...], w_theirs)
    pre = pre + (rows[:, :hidden] + rows[:, hidden : 2 * hidden])
    g_z = rows[:, 2 * hidden : 3 * hidden] + rows[:, 3 * hidden :]
    sig = jax.nn.sigmoid(pre)
    g_a = (g_z * sig * (1.0 + pre * (1.0 - sig))).astype(BF16)
    act_ref[:, :hidden] = g_a
    act_ref[:, hidden:] = (pre * sig).astype(BF16)
    for j, pick in enumerate(picks):
        source = lax.rem(me - j + owners, owners)
        begin = pl.multiple_of(place_of(source, steps) * lanes, SUBLANES)
        total_ref[pl.ds(begin, lanes), :] = dot(pick, g_a[j * cap : (j + 1) * cap], 0, 0).astype(BF16)
    split_half(total_ref, 0, owners * lanes, steps[0], 0, keep_ref, send_ref)


def halving_steps():
    bits = [
        [(axis, k) for k in range(lax.axis_size(axis).bit_length() - 1)] for axis in ("node", "obs")
    ]
    steps = []
    for k in range(max(map(len, bits))):
        both = [line[k] for line in bits if k < len(line)]
        steps += [(both[0], both[-1])] + ([(both[1], both[0])] if len(both) > 1 else [])
    return steps


def flip(value, step):
    axes = ("obs", "node", "mp")
    sizes = [lax.axis_size(axis) for axis in axes]
    pairs = []
    for index in range(sizes[0] * sizes[1] * sizes[2]):
        place = [index // (sizes[1] * sizes[2]), index // sizes[2] % sizes[1], index % sizes[2]]
        axis, k = step[place[2] % 2]
        place[axes.index(axis)] ^= 1 << k
        pairs.append((index, (place[0] * sizes[1] + place[1]) * sizes[2] + place[2]))
    return lax.ppermute(value, axes, pairs)


def bit_of(step, node, obs):
    bits = [({"node": node, "obs": obs}[axis] >> k) & 1 for axis, k in step]
    return jnp.where(lax.axis_index("mp") % 2 == 0, bits[0], bits[1])


def own_bit(step):
    return bit_of(step, lax.axis_index("node"), lax.axis_index("obs"))


def place_of(owner, steps):
    shares = lax.axis_size("node")
    place = 0
    for step in steps:
        place = 2 * place + bit_of(step, lax.rem(owner, shares), lax.div(owner, shares))
    return place


def halves(rows):
    return rows % (2 * SUBLANES) == 0


def split_half(total_ref, start, rows, step, tail, keep_ref, send_ref):
    end = start + rows
    if halves(rows):
        rows //= 2
        bit = own_bit(step)
        kept, sent = [pl.ds(pl.multiple_of(start + b * rows, SUBLANES), rows) for b in (bit, 1 - bit)]
    else:
        kept = sent = pl.ds(start, rows)
    keep_ref[:rows, :] = total_ref[kept, :]
    send_ref[:rows, :] = total_ref[sent, :].astype(BF16)
    if tail:
        both = total_ref[end : end + tail, :]
        keep_ref[rows:, :] = both
        send_ref[rows:, :] = both.astype(BF16)


def weight_kernel(
    step, bundles, tail, hot_ref, act_ref, rows_mine_ref, rows_theirs_ref, state_ref, agg_ref, w_node_ref,
    mine_ref, theirs_ref, *refs
):
    halves_refs, total_ref = refs[:-1], refs[-1]
    width, hidden = w_node_ref.shape
    nodes = state_ref.shape[0]
    sums = dot(hot_ref[...], act_ref[...], 0, 0)
    by_node = sums[:nodes].astype(BF16)
    node_hidden, z_sum = by_node[:, :hidden], by_node[:, hidden:]
    total_ref[:width, :] = dot(state_ref[...], node_hidden, 0, 0)
    begin = width
    for c in range(width // hidden):
        total_ref[begin : begin + hidden, :] = dot(
            z_sum, agg_ref[:, c * hidden : (c + 1) * hidden], 0, 0
        )
        begin += hidden
    g_a = act_ref[:, :hidden]
    core, half = lax.axis_index("mp"), width // 2
    for which, ref in ((core, rows_mine_ref), (1 - core, rows_theirs_ref)):
        total_ref[pl.ds(pl.multiple_of(begin + which * half, SUBLANES), half), :] = dot(ref[...], g_a, 0, 0)
    begin += width
    total_ref[begin:, :] = sums[nodes:, :hidden]
    rows = begin // bundles
    for i in range(bundles):
        split_half(
            total_ref, i * rows, rows, step, tail if i == bundles - 1 else 0,
            halves_refs[2 * i], halves_refs[2 * i + 1],
        )
    mine, theirs = other_half(w_node_ref)
    theirs_ref[...] = dot(node_hidden, theirs, 1, 1).astype(BF16)
    mine_ref[...] = dot(node_hidden, mine, 1, 1)


def obs_kernel(keep_ref, got_ref, w_ref, mine_ref, theirs_ref):
    obs_hidden = (keep_ref[...].astype(F32) + got_ref[...].astype(F32)).astype(BF16)
    mine, theirs = other_half(w_ref)
    theirs_ref[...] = dot(obs_hidden, theirs, 1, 1).astype(BF16)
    mine_ref[...] = dot(obs_hidden, mine, 1, 1)


def add_kernel(step, tail, keep_ref, got_ref, next_ref, send_ref, total_ref):
    total = keep_ref[...].astype(F32) + got_ref[...].astype(F32)
    total_ref[...] = total.astype(total_ref.dtype)
    split_half(total_ref, 0, total_ref.shape[0] - tail, step, tail, next_ref, send_ref)


def last_kernel(keep_ref, got_ref, piece_ref, *slot_refs):
    total = keep_ref[...] + got_ref[...].astype(F32)
    rows = piece_ref.shape[0]
    piece_ref[...] = total[:rows].astype(BF16)
    for slot_ref in slot_refs:
        slot_ref[...] = total[rows : rows + slot_ref.shape[0]]


def join_kernel(step, mine_ref, got_ref, out_ref):
    rows = mine_ref.shape[0]
    bit = own_bit(step)
    out_ref[pl.ds(pl.multiple_of(bit * rows, SUBLANES), rows), :] = mine_ref[...]
    out_ref[pl.ds(pl.multiple_of((1 - bit) * rows, SUBLANES), rows), :] = got_ref[...]


def spread_kernel(step, bundles, *refs):
    low = own_bit(step) == 0
    joined = []
    for i in range(bundles):
        mine, got = refs[2 * i][...], refs[2 * i + 1][...]
        joined += [jnp.where(low, mine, got), jnp.where(low, got, mine)]
    half, hidden = joined[0].shape
    at = 0
    for out_ref in refs[2 * bundles :]:
        for c in range(out_ref.shape[1] // hidden):
            begin = 0
            while begin < out_ref.shape[0]:
                offset = at % half
                count = min(out_ref.shape[0] - begin, half - offset)
                out_ref[begin : begin + count, c * hidden : (c + 1) * hidden] = joined[at // half][
                    offset : offset + count
                ].astype(F32)
                at, begin = at + count, begin + count


def merge_kernel(node_ref, node_got_ref, obs_ref, obs_got_ref, grad_node_ref, grad_obs_ref):
    grad_node_ref[...] = node_ref[...] + node_got_ref[...].astype(F32)
    grad_obs_ref[...] = (obs_ref[...] + obs_got_ref[...].astype(F32)).astype(BF16)


def half_rows(rows):
    return rows // 2 if halves(rows) else rows


def summing(steps, tail, keep, send, after):
    hidden = keep.shape[1]
    for done, nxt in zip(steps[:-1], steps[1:]):
        rows = half_rows(keep.shape[0] - tail) + tail
        keep, send = call(
            functools.partial(add_kernel, nxt, tail),
            [((rows, hidden), keep.dtype), ((rows, hidden), BF16)],
            keep, flip(send, done),
            scratch=[pltpu.VMEM(keep.shape, keep.dtype)],
            after=after,
        )
        after[:] = [send]
        yield
    return keep, flip(send, steps[-1])


def weight_chain(steps, rows, tail, slots, keep, send, after):
    used = []
    for step in steps:
        if halves(rows):
            used.append(step)
            rows //= 2
    keep, got = yield from summing(steps, tail, keep, send, after)
    piece, *sums = call(
        last_kernel,
        [((rows, keep.shape[1]), BF16)] + ([((slots, keep.shape[1]), F32)] if tail else []),
        keep, got,
        after=after,
    )
    after[:] = [piece]
    yield
    for step in used[:0:-1]:
        (piece,) = call(
            functools.partial(join_kernel, step),
            [((2 * piece.shape[0], piece.shape[1]), BF16)],
            piece, flip(piece, step),
            after=after,
        )
        after[:] = [piece]
        yield
    return [piece, flip(piece, used[0])], sums


def obs_chain(steps, w_obs, node_mine, node_theirs, keep, send, after):
    keep, got = yield from summing(steps, 0, keep, send, after)
    half = w_obs.shape[0] // 2
    obs_mine, obs_theirs = call(
        obs_kernel, [((keep.shape[0], half), F32), ((keep.shape[0], half), BF16)], keep, got, w_obs,
        after=after,
    )
    after[:] = [obs_theirs]
    yield
    grad_node, grad_obs = call(
        merge_kernel, [(node_mine.shape, F32), (obs_mine.shape, BF16)],
        node_mine, shift(node_theirs, "mp", 1), obs_mine, shift(obs_theirs, "mp", 1),
        after=after,
    )
    after[:] = [pltpu.with_memory_space_constraint(grad_obs, pltpu.HBM)]
    yield
    return grad_node, grad_obs


def in_turns(chains):
    results = [None] * len(chains)
    running = list(enumerate(chains))
    while running:
        for item in list(running):
            try:
                next(item[1])
            except StopIteration as stop:
                results[item[0]] = stop.value
                running.remove(item)
    return results


def local(obs_feat, node_state, grad_agg, owner, local_idx, slot, w_obs, w_node, slot_bias, w_out):
    owners = lax.axis_size(OWNER_AXES)
    obs, fanout = owner.shape
    nodes, width = node_state.shape
    hidden = w_obs.shape[1]
    slots = slot_bias.shape[0]
    cap = max(2, 2 * obs * fanout // owners)
    cap = -(-cap // SUBLANES) * SUBLANES
    edges = owners * cap
    half = width // 2
    slot_row = slot.reshape(1, obs)

    steps = halving_steps()
    chunk = cap * half // obs + SUBLANES
    other, *packed = call_staged(
        functools.partial(pack_kernel, cap),
        [((chunk, obs), BF16)] * (owners + 1),
        obs_feat, owner.T, local_idx.T, slot_row,
    )
    received = [shift(packed[j], OWNER_AXES, j) for j in range(1, owners)]
    tail = -(-slots // SUBLANES) * SUBLANES
    table, state_held, agg_held, w_node_held, w_obs_held = call_staged(
        table_kernel,
        [((nodes + tail, 4 * hidden), BF16)],
        node_state, grad_agg, w_node, w_out, slot_bias,
        held=(node_state, grad_agg, w_node, w_obs),
    )
    (mine,) = call(
        join_blocks_kernel, [((owners - 1, chunk, obs), BF16)], *received,
        after=(w_obs_held,),
    )
    theirs = shift(mine, "mp", 1)
    act, hot, rows_mine, rows_theirs, obs_keep, obs_send = call(
        functools.partial(edge_kernel, fanout, nodes, steps),
        [((edges, 2 * hidden), BF16), ((edges, nodes + tail), BF16)]
        + [((edges, half), BF16)] * 2
        + [((owners * obs // 2, hidden), BF16)] * 2,
        packed[0], mine, other, theirs, table, w_obs_held,
        scratch=[pltpu.VMEM((owners * obs, hidden), BF16)],
    )

    stack = 2 * width + width // hidden * hidden
    bundles = BUNDLES
    rows = stack // bundles
    shapes = []
    for i in range(bundles):
        share = rows // 2 + (tail if i == bundles - 1 else 0)
        shapes += [((share, hidden), F32), ((share, hidden), BF16)]
    node_mine, node_theirs, *shares = call(
        functools.partial(weight_kernel, steps[0], bundles, tail),
        [((nodes, half), F32), ((nodes, half), BF16)] + shapes,
        hot, act, rows_mine, rows_theirs, state_held, agg_held, w_node_held,
        scratch=[pltpu.VMEM((stack + tail, hidden), F32)],
    )
    after = []
    chains = [
        weight_chain(
            steps, rows, tail if i == bundles - 1 else 0, slots, shares[2 * i], shares[2 * i + 1], after
        )
        for i in range(bundles)
    ]
    chains.append(obs_chain(steps, w_obs_held, node_mine, node_theirs, obs_keep, obs_send, after))
    *weights, (grad_node, grad_obs) = in_turns(chains)
    ends = [end for pair, _ in weights for end in pair]
    (grad_slot,) = weights[-1][1]
    grad_w_node, grad_w_out, grad_w_obs = call(
        functools.partial(spread_kernel, steps[0], bundles),
        [((width, hidden), F32), ((hidden, width), F32), ((width, hidden), F32)],
        *ends,
    )
    return grad_obs, grad_node, grad_w_obs, grad_w_node, grad_w_out, grad_slot


def solution(mesh):
    rows = P(("group", "obs", "node"), None)
    return jax.shard_map(
        local,
        mesh=mesh,
        in_specs=(
            rows, rows, rows, rows, rows,
            P(("group", "obs", "node")),
            P(None, "mp"), P(None, "mp"), P(None, "mp"), P("mp", None),
        ),
        out_specs=(
            P(("group", "obs", "node"), "mp"),
            P(("group", "obs", "node"), "mp"),
            P("group", "mp"),
            P("group", "mp"),
            P(("group", "mp"), None),
            P("group", "mp"),
        ),
        check_vma=False,
    )
```

```python
import functools

import jax
import jax.numpy as jnp
from jax import lax
from jax.experimental import pallas as pl
from jax.experimental.pallas import tpu as pltpu
from jax.sharding import PartitionSpec as P

OWNER_AXES = ("obs", "node")
SUBLANES = 16
BF16 = jnp.bfloat16
F32 = jnp.float32


def dot(left, right, left_dim=1, right_dim=0):
    return lax.dot_general(
        left, right, (((left_dim,), (right_dim,)), ((), ())), preferred_element_type=F32
    )


def iota(shape, dim):
    return lax.broadcasted_iota(jnp.int32, shape, dim)


def call(kernel, outs, *args, scratch=(), after=()):
    vmem = pl.BlockSpec(memory_space=pltpu.VMEM)
    count = len(args)
    specs = [vmem] * count + [pl.BlockSpec(memory_space=pl.ANY)] * len(after)
    args += tuple(after)
    return pl.pallas_call(
        lambda *refs: kernel(*refs[:count], *refs[len(args) :]),
        out_shape=[jax.ShapeDtypeStruct(shape, dtype) for shape, dtype in outs],
        in_specs=specs,
        out_specs=[vmem] * len(outs),
        scratch_shapes=list(scratch),
        compiler_params=pltpu.CompilerParams(vmem_limit_bytes=40 << 20),
    )(*args)


def call_staged(kernel, outs, *args, held=()):
    count = len(args)
    sources = list(args) + [a for a in held if not any(a is b for b in args)]
    kept = [next(i for i, b in enumerate(sources) if a is b) for a in held]
    rest = [i for i in range(len(sources)) if i not in kept]

    def staged(*refs):
        hbm, refs = refs[: len(sources)], refs[len(sources) :]
        out_refs, refs = refs[: len(outs)], refs[len(outs) :]
        buffers = dict(zip(kept, refs[: len(kept)])) | dict(zip(rest, refs[len(kept) : -1]))
        copies = [
            pltpu.make_async_copy(hbm[i], buffers[i], refs[-1].at[i]) for i in range(len(sources))
        ]
        for copy in copies:
            copy.start()
        for copy in copies:
            copy.wait()
        kernel(*[buffers[i] for i in range(count)], *out_refs)

    return pl.pallas_call(
        staged,
        out_shape=[jax.ShapeDtypeStruct(shape, dtype) for shape, dtype in outs]
        + [jax.ShapeDtypeStruct(a.shape, a.dtype) for a in held],
        in_specs=[pl.BlockSpec(memory_space=pltpu.HBM)] * len(sources),
        out_specs=[pl.BlockSpec(memory_space=pltpu.VMEM)] * (len(outs) + len(held)),
        scratch_shapes=[pltpu.VMEM(sources[i].shape, sources[i].dtype) for i in rest]
        + [pltpu.SemaphoreType.DMA((len(sources),))],
        compiler_params=pltpu.CompilerParams(vmem_limit_bytes=40 << 20),
    )(*[pltpu.with_memory_space_constraint(a, pltpu.HBM) for a in sources])


def exchange(blocks, axes):
    return lax.all_to_all(blocks, axes, split_axis=0, concat_axis=0, tiled=True)


def shift(value, axis, step):
    size = lax.axis_size(axis)
    return lax.ppermute(value, axis, [(i, (i + step) % size) for i in range(size)])


def other_half(ref):
    half = ref.shape[0] // 2
    me = lax.axis_index("mp")
    mine = ref[pl.ds(pl.multiple_of(me * half, half), half), :]
    theirs = ref[pl.ds(pl.multiple_of((1 - me) * half, half), half), :]
    return mine, theirs


def column_half(ref, which):
    half = ref.shape[1] // 2
    return ref[:, pl.ds(pl.multiple_of(which * half, 128), half)]


def pack_kernel(cap, obs_ref, owner_ref, index_ref, slot_ref, other_ref, *outs):
    owners = len(outs)
    chunk, lanes = outs[0].shape
    fanout, obs = owner_ref.shape
    owner, index = owner_ref[...], index_ref[...]
    hits = [iota((owners, obs), 0) == owner[k : k + 1] for k in range(fanout)]
    count = functools.reduce(jnp.add, [h.astype(F32) for h in hits])
    before = dot(count, (iota((obs, obs), 0) < iota((obs, obs), 1)).astype(F32))
    header = jnp.where(iota((SUBLANES, obs), 0) == 4 * fanout, slot_ref[...].astype(F32), 0.0)
    places = []
    for k in range(fanout):
        rank = jnp.sum(jnp.where(hits[k], before, 0.0), axis=0, keepdims=True)
        places.append(owner[k : k + 1] * cap + rank.astype(jnp.int32))
        plus = index[k : k + 1] + 1
        fields = (owner[k : k + 1].astype(F32), rank, (plus // 16).astype(F32), (plus % 16).astype(F32))
        for j, row in enumerate(fields):
            header = jnp.where(iota(header.shape, 0) == 4 * k + j, row, header)
    header = header.astype(BF16)
    me, core = lax.axis_index(OWNER_AXES), lax.axis_index("mp")
    mine, other = column_half(obs_ref, core), column_half(obs_ref, 1 - core)

    def write(ref, pick, rows):
        packed = dot(pick, rows).astype(BF16)
        for c in range(rows.shape[1] // lanes):
            ref[c * cap : (c + 1) * cap, :] = packed[:, c * lanes : (c + 1) * lanes]
        ref[chunk - SUBLANES :, :] = header

    for j, out_ref in enumerate(outs):
        slots = iota((cap, obs), 0) + lax.rem(me + j, owners) * cap
        pick = functools.reduce(jnp.logical_or, [slots == place for place in places]).astype(BF16)
        write(out_ref, pick, mine)
        if j == 0:
            write(other_ref, pick, other)


def table_kernel(state_ref, agg_ref, w_node_ref, w_out_ref, bias_ref, table_ref):
    hidden = w_node_ref.shape[1]
    nodes, slots = state_ref.shape[0], bias_ref.shape[0]
    table_ref[nodes:, :] = jnp.zeros((table_ref.shape[0] - nodes, table_ref.shape[1]), BF16)

    def put(begin, column, part):
        high = part.astype(BF16)
        table_ref[begin : begin + part.shape[0], column : column + hidden] = high
        table_ref[begin : begin + part.shape[0], column + hidden : column + 2 * hidden] = (
            part - high.astype(F32)
        ).astype(BF16)

    put(0, 0, dot(state_ref[...], w_node_ref[...]))
    put(0, 2 * hidden, dot(agg_ref[...], w_out_ref[...], 1, 1))
    put(nodes, 0, bias_ref[...])


def join_blocks_kernel(*refs):
    out_ref = refs[-1]
    for j, ref in enumerate(refs[:-1]):
        out_ref[j] = ref[...]


def edge_kernel(
    fanout, nodes, own_ref, mine_ref, other_ref, theirs_ref, table_ref, w_obs_ref,
    act_ref, hot_ref, rows_mine_ref, rows_theirs_ref, pick_ref,
):
    owners = mine_ref.shape[0] + 1
    chunk, lanes = own_ref.shape
    half = w_obs_ref.shape[0] // 2
    hidden = w_obs_ref.shape[1]
    cap = (chunk - SUBLANES) * lanes // half
    me = lax.axis_index(OWNER_AXES)
    base = 1 << nodes.bit_length()
    columns = []
    for j in range(owners):
        block, other = (mine_ref.at[j - 1], theirs_ref.at[j - 1]) if j else (own_ref, other_ref)
        header = block[chunk - SUBLANES :, :].astype(F32)
        slot = header[4 * fanout : 4 * fanout + 1] * base
        code = jnp.zeros((cap, lanes), F32)
        pick = jnp.zeros((cap, lanes), jnp.bool_)
        for k in range(fanout):
            row = header[4 * k : 4 * k + 4]
            rank = jnp.where(row[0:1] == me.astype(F32), row[1:2], -1.0).astype(jnp.int32)
            hit = iota((cap, lanes), 0) == rank
            pick = pick | hit
            code = code + jnp.where(hit, row[2:3] * 16.0 + row[3:4] + slot, 0.0)
        pick_ref[j * cap : (j + 1) * cap, :] = pick.astype(BF16)
        columns.append(jnp.sum(code, axis=1, keepdims=True).astype(jnp.int32))
        for c in range(half // lanes):
            rows = slice(j * cap, (j + 1) * cap)
            place = slice(c * lanes, (c + 1) * lanes)
            rows_mine_ref[rows, place] = block[c * cap : (c + 1) * cap, :]
            rows_theirs_ref[rows, place] = other[c * cap : (c + 1) * cap, :]
    code = jnp.concatenate(columns, axis=0)
    index, slot = (code & (base - 1)) - 1, (code >> (base.bit_length() - 1)) + nodes
    column = iota(hot_ref.shape, 1)
    hot = ((column == index) | ((column == slot) & (index >= 0))).astype(BF16)
    hot_ref[...] = hot
    rows = dot(hot, table_ref[...])
    w_mine, w_theirs = other_half(w_obs_ref)
    pre = dot(rows_mine_ref[...], w_mine) + dot(rows_theirs_ref[...], w_theirs)
    pre = pre + (rows[:, :hidden] + rows[:, hidden : 2 * hidden])
    g_z = rows[:, 2 * hidden : 3 * hidden] + rows[:, 3 * hidden :]
    sig = jax.nn.sigmoid(pre)
    act_ref[:, :hidden] = (g_z * sig * (1.0 + pre * (1.0 - sig))).astype(BF16)
    act_ref[:, hidden:] = (pre * sig).astype(BF16)


def halving_steps():
    bits = [
        [(axis, k) for k in range(lax.axis_size(axis).bit_length() - 1)] for axis in ("node", "obs")
    ]
    steps = []
    for k in range(max(map(len, bits))):
        both = [line[k] for line in bits if k < len(line)]
        steps += [(both[0], both[-1])] + ([(both[1], both[0])] if len(both) > 1 else [])
    return steps


def flip(value, step):
    axes = ("obs", "node", "mp")
    sizes = [lax.axis_size(axis) for axis in axes]
    pairs = []
    for index in range(sizes[0] * sizes[1] * sizes[2]):
        place = [index // (sizes[1] * sizes[2]), index // sizes[2] % sizes[1], index % sizes[2]]
        axis, k = step[place[2] % 2]
        place[axes.index(axis)] ^= 1 << k
        pairs.append((index, (place[0] * sizes[1] + place[1]) * sizes[2] + place[2]))
    return lax.ppermute(value, axes, pairs)


def bit_of(step, node, obs):
    bits = [({"node": node, "obs": obs}[axis] >> k) & 1 for axis, k in step]
    return jnp.where(lax.axis_index("mp") % 2 == 0, bits[0], bits[1])


def own_bit(step):
    return bit_of(step, lax.axis_index("node"), lax.axis_index("obs"))


def place_of(owner, steps):
    shares = lax.axis_size("node")
    place = 0
    for step in steps:
        place = 2 * place + bit_of(step, lax.rem(owner, shares), lax.div(owner, shares))
    return place


def halves(rows):
    return rows % (2 * SUBLANES) == 0


def half_rows(rows):
    return rows // 2 if halves(rows) else rows


def split_half(total_ref, parts, tail, step, keep_ref, send_ref):
    begin = at = 0
    for rows in parts:
        half = half_rows(rows)
        kept = sent = pl.ds(begin, rows)
        if half < rows:
            bit = own_bit(step)
            kept, sent = [
                pl.ds(pl.multiple_of(begin + b * half, SUBLANES), half) for b in (bit, 1 - bit)
            ]
        keep_ref[at : at + half, :] = total_ref[kept, :]
        send_ref[at : at + half, :] = total_ref[sent, :].astype(BF16)
        begin, at = begin + rows, at + half
    if tail:
        both = total_ref[begin:, :]
        keep_ref[at:, :] = both
        send_ref[at:, :] = both.astype(BF16)


def node_kernel(step, hot_ref, act_ref, state_ref, agg_ref, hidden_ref, slot_ref, keep_ref, send_ref, total_ref):
    nodes, width = state_ref.shape
    hidden = total_ref.shape[1]
    sums = dot(hot_ref[...], act_ref[...], 0, 0)
    by_node = sums[:nodes].astype(BF16)
    node_hidden, z_sum = by_node[:, :hidden], by_node[:, hidden:]
    hidden_ref[...] = node_hidden
    slot_ref[...] = sums[nodes:, :hidden]
    total_ref[:width, :] = dot(state_ref[...], node_hidden, 0, 0)
    for begin in range(0, width, hidden):
        total_ref[width + begin : width + begin + hidden, :] = dot(
            z_sum, agg_ref[:, begin : begin + hidden], 0, 0
        )
    split_half(total_ref, [total_ref.shape[0]], 0, step, keep_ref, send_ref)


def rows_kernel(
    steps, owners, act_ref, rows_mine_ref, rows_theirs_ref, pick_ref, slot_ref, keep_ref, send_ref, total_ref
):
    edges, obs = pick_ref.shape
    half, hidden = rows_mine_ref.shape[1], total_ref.shape[1]
    g_a = act_ref[:, :hidden]
    core = lax.axis_index("mp")
    for which, ref in ((core, rows_mine_ref), (1 - core, rows_theirs_ref)):
        total_ref[pl.ds(pl.multiple_of(which * half, SUBLANES), half), :] = dot(ref[...], g_a, 0, 0)
    me, cap, begin = lax.axis_index(OWNER_AXES), edges // owners, 2 * half
    for j in range(owners):
        source = lax.rem(me - j + owners, owners)
        place = pl.multiple_of(begin + place_of(source, steps) * obs, SUBLANES)
        edges_of = slice(j * cap, (j + 1) * cap)
        total_ref[pl.ds(place, obs), :] = dot(pick_ref[edges_of, :], g_a[edges_of], 0, 0)
    total_ref[begin + owners * obs :, :] = slot_ref[...]
    split_half(
        total_ref, [begin, owners * obs], slot_ref.shape[0], steps[0], keep_ref, send_ref
    )


def grad_node_kernel(hidden_ref, w_node_ref, mine_ref, theirs_ref):
    mine, theirs = other_half(w_node_ref)
    theirs_ref[...] = dot(hidden_ref[...], theirs, 1, 1).astype(BF16)
    mine_ref[...] = dot(hidden_ref[...], mine, 1, 1)


def add_kernel(parts, tail, step, keep_ref, got_ref, next_ref, send_ref, total_ref):
    total_ref[...] = keep_ref[...] + got_ref[...].astype(F32)
    split_half(total_ref, parts, tail, step, next_ref, send_ref)


def piece_kernel(keep_ref, got_ref, piece_ref):
    piece_ref[...] = (keep_ref[...] + got_ref[...].astype(F32)).astype(BF16)


def obs_kernel(keep_ref, got_ref, w_ref, piece_ref, slot_ref, mine_ref, theirs_ref):
    total = keep_ref[...] + got_ref[...].astype(F32)
    rows, obs = piece_ref.shape[0], mine_ref.shape[0]
    piece_ref[...] = total[:rows].astype(BF16)
    slot_ref[...] = total[rows + obs : rows + obs + slot_ref.shape[0]]
    obs_hidden = total[rows : rows + obs].astype(BF16)
    mine, theirs = other_half(w_ref)
    theirs_ref[...] = dot(obs_hidden, theirs, 1, 1).astype(BF16)
    mine_ref[...] = dot(obs_hidden, mine, 1, 1)


def join_kernel(step, mine_ref, got_ref, out_ref):
    rows = mine_ref.shape[0]
    bit = own_bit(step)
    out_ref[pl.ds(pl.multiple_of(bit * rows, SUBLANES), rows), :] = mine_ref[...]
    out_ref[pl.ds(pl.multiple_of((1 - bit) * rows, SUBLANES), rows), :] = got_ref[...]


def spread(step, mine_ref, got_ref, out_refs):
    low = own_bit(step) == 0
    mine, got = mine_ref[...], got_ref[...]
    joined = [jnp.where(low, mine, got), jnp.where(low, got, mine)]
    half, hidden = mine.shape
    at = 0
    for out_ref in out_refs:
        for c in range(out_ref.shape[1] // hidden):
            begin = 0
            while begin < out_ref.shape[0]:
                offset = at % half
                count = min(out_ref.shape[0] - begin, half - offset)
                out_ref[begin : begin + count, c * hidden : (c + 1) * hidden] = joined[at // half][
                    offset : offset + count
                ].astype(F32)
                at, begin = at + count, begin + count


def node_out_kernel(
    step, mine_ref, got_ref, node_ref, node_got_ref, obs_ref, obs_got_ref, w_node_ref, w_out_ref, grad_node_ref, grad_obs_ref
):
    spread(step, mine_ref, got_ref, (w_node_ref, w_out_ref))
    grad_node_ref[...] = node_ref[...] + node_got_ref[...].astype(F32)
    grad_obs_ref[...] = (obs_ref[...] + obs_got_ref[...].astype(F32)).astype(BF16)


def obs_out_kernel(step, mine_ref, got_ref, w_obs_ref):
    spread(step, mine_ref, got_ref, (w_obs_ref,))


def summing(steps, parts, tail, keep, send, after):
    hidden = keep.shape[1]
    for done, nxt in zip(steps[:-1], steps[1:]):
        parts = [half_rows(rows) for rows in parts]
        share = sum(map(half_rows, parts)) + tail
        keep, send = call(
            functools.partial(add_kernel, parts, tail, nxt),
            [((share, hidden), F32), ((share, hidden), BF16)],
            keep, flip(send, done),
            scratch=[pltpu.VMEM(keep.shape, F32)],
            after=after,
        )
        after[:] = [send]
        yield
    return keep, flip(send, steps[-1])


def gathering(steps, rows, piece, after):
    used = []
    for step in steps:
        if halves(rows):
            used.append(step)
            rows //= 2
    for step in used[:0:-1]:
        (piece,) = call(
            functools.partial(join_kernel, step),
            [((2 * piece.shape[0], piece.shape[1]), BF16)],
            piece, flip(piece, step),
            after=after,
        )
        after[:] = [piece]
        yield
    return piece, flip(piece, used[0])


def final_rows(steps, rows):
    for _ in steps:
        rows = half_rows(rows)
    return rows


def node_chain(steps, rows, keep, send, after):
    keep, got = yield from summing(steps, [rows], 0, keep, send, after)
    (piece,) = call(piece_kernel, [(keep.shape, BF16)], keep, got, after=after)
    after[:] = [piece]
    yield
    return (yield from gathering(steps, rows, piece, after))


def obs_chain(steps, w_obs, parts, tail, slots, keep, send, after):
    keep, got = yield from summing(steps, parts, tail, keep, send, after)
    half, hidden = w_obs.shape[0] // 2, w_obs.shape[1]
    rows, obs = [final_rows(steps, count) for count in parts]
    piece, grad_slot, obs_mine, obs_theirs = call(
        obs_kernel,
        [((rows, hidden), BF16), ((slots, hidden), F32), ((obs, half), F32), ((obs, half), BF16)],
        keep, got, w_obs,
        after=after,
    )
    after[:] = [piece]
    yield
    ends = yield from gathering(steps, parts[0], piece, after)
    return ends, grad_slot, obs_mine, obs_theirs


def in_turns(chains):
    results = [None] * len(chains)
    running = list(enumerate(chains))
    while running:
        for item in list(running):
            try:
                next(item[1])
            except StopIteration as stop:
                results[item[0]] = stop.value
                running.remove(item)
    return results


def local(obs_feat, node_state, grad_agg, owner, local_idx, slot, w_obs, w_node, slot_bias, w_out):
    owners = lax.axis_size(OWNER_AXES)
    obs, fanout = owner.shape
    nodes, width = node_state.shape
    hidden = w_obs.shape[1]
    slots = slot_bias.shape[0]
    cap = max(2, 2 * obs * fanout // owners)
    cap = -(-cap // SUBLANES) * SUBLANES
    edges = owners * cap
    half = width // 2
    slot_row = slot.reshape(1, obs)

    steps = halving_steps()
    chunk = cap * half // obs + SUBLANES
    other, *packed = call_staged(
        functools.partial(pack_kernel, cap),
        [((chunk, obs), BF16)] * (owners + 1),
        obs_feat, owner.T, local_idx.T, slot_row,
    )
    received = [shift(packed[j], OWNER_AXES, j) for j in range(1, owners)]
    tail = -(-slots // SUBLANES) * SUBLANES
    table, state_held, agg_held, w_node_held, w_obs_held = call_staged(
        table_kernel,
        [((nodes + tail, 4 * hidden), BF16)],
        node_state, grad_agg, w_node, w_out, slot_bias,
        held=(node_state, grad_agg, w_node, w_obs),
    )
    (mine,) = call(
        join_blocks_kernel, [((owners - 1, chunk, obs), BF16)], *received,
        after=(w_obs_held,),
    )
    theirs = shift(mine, "mp", 1)
    act, hot, rows_mine, rows_theirs, pick = call(
        functools.partial(edge_kernel, fanout, nodes),
        [((edges, 2 * hidden), BF16), ((edges, nodes + tail), BF16)]
        + [((edges, half), BF16)] * 2
        + [((edges, obs), BF16)],
        packed[0], mine, other, theirs, table, w_obs_held,
    )

    after = []
    stack = width + width // hidden * hidden
    share = half_rows(stack)
    node_hidden, slot_sums, keep, send = call(
        functools.partial(node_kernel, steps[0]),
        [((nodes, hidden), BF16), ((tail, hidden), F32), ((share, hidden), F32), ((share, hidden), BF16)],
        hot, act, state_held, agg_held,
        scratch=[pltpu.VMEM((stack, hidden), F32)],
    )
    first = node_chain(steps, stack, keep, send, after)
    parts = [width, owners * obs]
    share = sum(map(half_rows, parts)) + tail
    keep, send = call(
        functools.partial(rows_kernel, steps, owners),
        [((share, hidden), F32), ((share, hidden), BF16)],
        act, rows_mine, rows_theirs, pick, slot_sums,
        scratch=[pltpu.VMEM((sum(parts) + tail, hidden), F32)],
    )
    second = obs_chain(steps, w_obs_held, parts, tail, slots, keep, send, after)
    node_mine, node_theirs = call(
        grad_node_kernel, [((nodes, half), F32), ((nodes, half), BF16)], node_hidden, w_node_held
    )
    after[:] = [node_theirs]
    node_ends, (obs_ends, grad_slot, obs_mine, obs_theirs) = in_turns([first, second])
    grad_w_node, grad_w_out, grad_node, grad_obs = call(
        functools.partial(node_out_kernel, steps[0]),
        [
            ((width, hidden), F32),
            ((hidden, width), F32),
            ((nodes, half), F32),
            ((obs, half), BF16),
        ],
        *node_ends, node_mine, shift(node_theirs, "mp", 1), obs_mine, shift(obs_theirs, "mp", 1),
        after=after,
    )
    (grad_w_obs,) = call(
        functools.partial(obs_out_kernel, steps[0]), [((width, hidden), F32)], *obs_ends,
        after=[pltpu.with_memory_space_constraint(grad_obs, pltpu.HBM)],
    )
    return grad_obs, grad_node, grad_w_obs, grad_w_node, grad_w_out, grad_slot


def solution(mesh):
    rows = P(("group", "obs", "node"), None)
    return jax.shard_map(
        local,
        mesh=mesh,
        in_specs=(
            rows, rows, rows, rows, rows,
            P(("group", "obs", "node")),
            P(None, "mp"), P(None, "mp"), P(None, "mp"), P("mp", None),
        ),
        out_specs=(
            P(("group", "obs", "node"), "mp"),
            P(("group", "obs", "node"), "mp"),
            P("group", "mp"),
            P("group", "mp"),
            P(("group", "mp"), None),
            P("group", "mp"),
        ),
        check_vma=False,
    )
```

```python
import functools

import jax
import jax.numpy as jnp
from jax import lax
from jax.experimental import pallas as pl
from jax.experimental.pallas import tpu as pltpu
from jax.sharding import PartitionSpec as P

OWNER_AXES = ("obs", "node")
SUBLANES = 16
BUNDLES = 2
BF16 = jnp.bfloat16
F32 = jnp.float32


def dot(left, right, left_dim=1, right_dim=0):
    return lax.dot_general(
        left, right, (((left_dim,), (right_dim,)), ((), ())), preferred_element_type=F32
    )


def iota(shape, dim):
    return lax.broadcasted_iota(jnp.int32, shape, dim)


def call(kernel, outs, *args, scratch=(), after=()):
    vmem = pl.BlockSpec(memory_space=pltpu.VMEM)
    count = len(args)
    specs = [vmem] * count + [pl.BlockSpec(memory_space=pl.ANY)] * len(after)
    args += tuple(after)
    return pl.pallas_call(
        lambda *refs: kernel(*refs[:count], *refs[len(args) :]),
        out_shape=[jax.ShapeDtypeStruct(shape, dtype) for shape, dtype in outs],
        in_specs=specs,
        out_specs=[vmem] * len(outs),
        scratch_shapes=list(scratch),
        compiler_params=pltpu.CompilerParams(vmem_limit_bytes=40 << 20),
    )(*args)


def call_staged(kernel, outs, *args, held=()):
    count = len(args)
    sources = list(args) + [a for a in held if not any(a is b for b in args)]
    kept = [next(i for i, b in enumerate(sources) if a is b) for a in held]
    rest = [i for i in range(len(sources)) if i not in kept]

    def staged(*refs):
        hbm, refs = refs[: len(sources)], refs[len(sources) :]
        out_refs, refs = refs[: len(outs)], refs[len(outs) :]
        buffers = dict(zip(kept, refs[: len(kept)])) | dict(zip(rest, refs[len(kept) : -1]))
        copies = [
            pltpu.make_async_copy(hbm[i], buffers[i], refs[-1].at[i]) for i in range(len(sources))
        ]
        for copy in copies:
            copy.start()
        for copy in copies:
            copy.wait()
        kernel(*[buffers[i] for i in range(count)], *out_refs)

    return pl.pallas_call(
        staged,
        out_shape=[jax.ShapeDtypeStruct(shape, dtype) for shape, dtype in outs]
        + [jax.ShapeDtypeStruct(a.shape, a.dtype) for a in held],
        in_specs=[pl.BlockSpec(memory_space=pltpu.HBM)] * len(sources),
        out_specs=[pl.BlockSpec(memory_space=pltpu.VMEM)] * (len(outs) + len(held)),
        scratch_shapes=[pltpu.VMEM(sources[i].shape, sources[i].dtype) for i in rest]
        + [pltpu.SemaphoreType.DMA((len(sources),))],
        compiler_params=pltpu.CompilerParams(vmem_limit_bytes=40 << 20),
    )(*[pltpu.with_memory_space_constraint(a, pltpu.HBM) for a in sources])


def exchange(blocks, axes):
    return lax.all_to_all(blocks, axes, split_axis=0, concat_axis=0, tiled=True)


def shift(value, axis, step):
    size = lax.axis_size(axis)
    return lax.ppermute(value, axis, [(i, (i + step) % size) for i in range(size)])


def other_half(ref):
    half = ref.shape[0] // 2
    me = lax.axis_index("mp")
    mine = ref[pl.ds(pl.multiple_of(me * half, half), half), :]
    theirs = ref[pl.ds(pl.multiple_of((1 - me) * half, half), half), :]
    return mine, theirs


def column_half(ref, which):
    half = ref.shape[1] // 2
    return ref[:, pl.ds(pl.multiple_of(which * half, 128), half)]


def pack_kernel(cap, obs_ref, owner_ref, index_ref, slot_ref, other_ref, *outs):
    owners = len(outs)
    chunk, lanes = outs[0].shape
    fanout, obs = owner_ref.shape
    owner, index = owner_ref[...], index_ref[...]
    hits = [iota((owners, obs), 0) == owner[k : k + 1] for k in range(fanout)]
    count = functools.reduce(jnp.add, [h.astype(F32) for h in hits])
    before = dot(count, (iota((obs, obs), 0) < iota((obs, obs), 1)).astype(F32))
    header = jnp.where(iota((SUBLANES, obs), 0) == 4 * fanout, slot_ref[...].astype(F32), 0.0)
    places = []
    for k in range(fanout):
        rank = jnp.sum(jnp.where(hits[k], before, 0.0), axis=0, keepdims=True)
        places.append(owner[k : k + 1] * cap + rank.astype(jnp.int32))
        plus = index[k : k + 1] + 1
        fields = (owner[k : k + 1].astype(F32), rank, (plus // 16).astype(F32), (plus % 16).astype(F32))
        for j, row in enumerate(fields):
            header = jnp.where(iota(header.shape, 0) == 4 * k + j, row, header)
    header = header.astype(BF16)
    me, core = lax.axis_index(OWNER_AXES), lax.axis_index("mp")
    mine, other = column_half(obs_ref, core), column_half(obs_ref, 1 - core)

    def write(ref, pick, rows):
        packed = dot(pick, rows).astype(BF16)
        for c in range(rows.shape[1] // lanes):
            ref[c * cap : (c + 1) * cap, :] = packed[:, c * lanes : (c + 1) * lanes]
        ref[chunk - SUBLANES :, :] = header

    for j, out_ref in enumerate(outs):
        slots = iota((cap, obs), 0) + lax.rem(me + j, owners) * cap
        pick = functools.reduce(jnp.logical_or, [slots == place for place in places]).astype(BF16)
        write(out_ref, pick, mine)
        if j == 0:
            write(other_ref, pick, other)


def table_kernel(state_ref, agg_ref, w_node_ref, w_out_ref, bias_ref, table_ref):
    hidden = w_node_ref.shape[1]
    nodes, slots = state_ref.shape[0], bias_ref.shape[0]
    table_ref[nodes:, :] = jnp.zeros((table_ref.shape[0] - nodes, table_ref.shape[1]), BF16)

    def put(begin, column, part):
        high = part.astype(BF16)
        table_ref[begin : begin + part.shape[0], column : column + hidden] = high
        table_ref[begin : begin + part.shape[0], column + hidden : column + 2 * hidden] = (
            part - high.astype(F32)
        ).astype(BF16)

    put(0, 0, dot(state_ref[...], w_node_ref[...]))
    put(0, 2 * hidden, dot(agg_ref[...], w_out_ref[...], 1, 1))
    put(nodes, 0, bias_ref[...])


def join_blocks_kernel(*refs):
    out_ref = refs[-1]
    for j, ref in enumerate(refs[:-1]):
        out_ref[j] = ref[...]


def edge_kernel(
    fanout, nodes, steps, own_ref, mine_ref, other_ref, theirs_ref, table_ref, w_obs_ref,
    act_ref, hot_ref, rows_mine_ref, rows_theirs_ref, keep_ref, send_ref, total_ref,
):
    owners = mine_ref.shape[0] + 1
    chunk, lanes = own_ref.shape
    half = w_obs_ref.shape[0] // 2
    hidden = w_obs_ref.shape[1]
    cap = (chunk - SUBLANES) * lanes // half
    me = lax.axis_index(OWNER_AXES)
    base = 1 << nodes.bit_length()
    columns = []
    picks = []
    for j in range(owners):
        block, other = (mine_ref.at[j - 1], theirs_ref.at[j - 1]) if j else (own_ref, other_ref)
        header = block[chunk - SUBLANES :, :].astype(F32)
        slot = header[4 * fanout : 4 * fanout + 1] * base
        code = jnp.zeros((cap, lanes), F32)
        pick = jnp.zeros((cap, lanes), jnp.bool_)
        for k in range(fanout):
            row = header[4 * k : 4 * k + 4]
            rank = jnp.where(row[0:1] == me.astype(F32), row[1:2], -1.0).astype(jnp.int32)
            hit = iota((cap, lanes), 0) == rank
            pick = pick | hit
            code = code + jnp.where(hit, row[2:3] * 16.0 + row[3:4] + slot, 0.0)
        picks.append(pick.astype(BF16))
        columns.append(jnp.sum(code, axis=1, keepdims=True).astype(jnp.int32))
        for c in range(half // lanes):
            rows = slice(j * cap, (j + 1) * cap)
            place = slice(c * lanes, (c + 1) * lanes)
            rows_mine_ref[rows, place] = block[c * cap : (c + 1) * cap, :]
            rows_theirs_ref[rows, place] = other[c * cap : (c + 1) * cap, :]
    code = jnp.concatenate(columns, axis=0)
    index, slot = (code & (base - 1)) - 1, (code >> (base.bit_length() - 1)) + nodes
    column = iota(hot_ref.shape, 1)
    hot = ((column == index) | ((column == slot) & (index >= 0))).astype(BF16)
    hot_ref[...] = hot
    rows = dot(hot, table_ref[...])
    w_mine, w_theirs = other_half(w_obs_ref)
    pre = dot(rows_mine_ref[...], w_mine) + dot(rows_theirs_ref[...], w_theirs)
    pre = pre + (rows[:, :hidden] + rows[:, hidden : 2 * hidden])
    g_z = rows[:, 2 * hidden : 3 * hidden] + rows[:, 3 * hidden :]
    sig = jax.nn.sigmoid(pre)
    g_a = (g_z * sig * (1.0 + pre * (1.0 - sig))).astype(BF16)
    act_ref[:, :hidden] = g_a
    act_ref[:, hidden:] = (pre * sig).astype(BF16)
    for j, pick in enumerate(picks):
        source = lax.rem(me - j + owners, owners)
        begin = pl.multiple_of(place_of(source, steps) * lanes, SUBLANES)
        total_ref[pl.ds(begin, lanes), :] = dot(pick, g_a[j * cap : (j + 1) * cap], 0, 0).astype(BF16)
    split_half(total_ref, 0, owners * lanes, steps[0], 0, keep_ref, send_ref)


def halving_steps():
    bits = [
        [(axis, k) for k in range(lax.axis_size(axis).bit_length() - 1)] for axis in ("node", "obs")
    ]
    steps = []
    for k in range(max(map(len, bits))):
        both = [line[k] for line in bits if k < len(line)]
        steps += [(both[0], both[-1])] + ([(both[1], both[0])] if len(both) > 1 else [])
    return steps


def flip(value, step):
    axes = ("obs", "node", "mp")
    sizes = [lax.axis_size(axis) for axis in axes]
    pairs = []
    for index in range(sizes[0] * sizes[1] * sizes[2]):
        place = [index // (sizes[1] * sizes[2]), index // sizes[2] % sizes[1], index % sizes[2]]
        axis, k = step[place[2] % 2]
        place[axes.index(axis)] ^= 1 << k
        pairs.append((index, (place[0] * sizes[1] + place[1]) * sizes[2] + place[2]))
    return lax.ppermute(value, axes, pairs)


def bit_of(step, node, obs):
    bits = [({"node": node, "obs": obs}[axis] >> k) & 1 for axis, k in step]
    return jnp.where(lax.axis_index("mp") % 2 == 0, bits[0], bits[1])


def own_bit(step):
    return bit_of(step, lax.axis_index("node"), lax.axis_index("obs"))


def place_of(owner, steps):
    shares = lax.axis_size("node")
    place = 0
    for step in steps:
        place = 2 * place + bit_of(step, lax.rem(owner, shares), lax.div(owner, shares))
    return place


def halves(rows):
    return rows % (2 * SUBLANES) == 0


def split_half(total_ref, start, rows, step, tail, keep_ref, send_ref):
    end = start + rows
    if halves(rows):
        rows //= 2
        bit = own_bit(step)
        kept, sent = [pl.ds(pl.multiple_of(start + b * rows, SUBLANES), rows) for b in (bit, 1 - bit)]
    else:
        kept = sent = pl.ds(start, rows)
    keep_ref[:rows, :] = total_ref[kept, :]
    send_ref[:rows, :] = total_ref[sent, :].astype(BF16)
    if tail:
        both = total_ref[end : end + tail, :]
        keep_ref[rows:, :] = both
        send_ref[rows:, :] = both.astype(BF16)


def weight_kernel(
    step, bundles, tail, hot_ref, act_ref, rows_mine_ref, rows_theirs_ref, state_ref, agg_ref, w_node_ref,
    mine_ref, theirs_ref, *refs
):
    halves_refs, total_ref = refs[:-1], refs[-1]
    width, hidden = w_node_ref.shape
    nodes = state_ref.shape[0]
    sums = dot(hot_ref[...], act_ref[...], 0, 0)
    by_node = sums[:nodes].astype(BF16)
    node_hidden, z_sum = by_node[:, :hidden], by_node[:, hidden:]
    total_ref[:width, :] = dot(state_ref[...], node_hidden, 0, 0)
    begin = width
    for c in range(width // hidden):
        total_ref[begin : begin + hidden, :] = dot(
            z_sum, agg_ref[:, c * hidden : (c + 1) * hidden], 0, 0
        )
        begin += hidden
    g_a = act_ref[:, :hidden]
    core, half = lax.axis_index("mp"), width // 2
    for which, ref in ((core, rows_mine_ref), (1 - core, rows_theirs_ref)):
        total_ref[pl.ds(pl.multiple_of(begin + which * half, SUBLANES), half), :] = dot(ref[...], g_a, 0, 0)
    begin += width
    total_ref[begin:, :] = sums[nodes:, :hidden]
    rows = begin // bundles
    for i in range(bundles):
        split_half(
            total_ref, i * rows, rows, step, tail if i == bundles - 1 else 0,
            halves_refs[2 * i], halves_refs[2 * i + 1],
        )
    mine, theirs = other_half(w_node_ref)
    theirs_ref[...] = dot(node_hidden, theirs, 1, 1).astype(BF16)
    mine_ref[...] = dot(node_hidden, mine, 1, 1)


def obs_kernel(keep_ref, got_ref, w_ref, mine_ref, theirs_ref):
    obs_hidden = (keep_ref[...].astype(F32) + got_ref[...].astype(F32)).astype(BF16)
    mine, theirs = other_half(w_ref)
    theirs_ref[...] = dot(obs_hidden, theirs, 1, 1).astype(BF16)
    mine_ref[...] = dot(obs_hidden, mine, 1, 1)


def add_kernel(step, tail, keep_ref, got_ref, next_ref, send_ref, total_ref):
    total = keep_ref[...].astype(F32) + got_ref[...].astype(F32)
    total_ref[...] = total.astype(total_ref.dtype)
    split_half(total_ref, 0, total_ref.shape[0] - tail, step, tail, next_ref, send_ref)


def last_kernel(keep_ref, got_ref, piece_ref, *slot_refs):
    total = keep_ref[...] + got_ref[...].astype(F32)
    rows = piece_ref.shape[0]
    piece_ref[...] = total[:rows].astype(BF16)
    for slot_ref in slot_refs:
        slot_ref[...] = total[rows : rows + slot_ref.shape[0]]


def join_kernel(step, mine_ref, got_ref, out_ref):
    rows = mine_ref.shape[0]
    bit = own_bit(step)
    out_ref[pl.ds(pl.multiple_of(bit * rows, SUBLANES), rows), :] = mine_ref[...]
    out_ref[pl.ds(pl.multiple_of((1 - bit) * rows, SUBLANES), rows), :] = got_ref[...]


def spread_kernel(step, bundles, *refs):
    low = own_bit(step) == 0
    joined = []
    for i in range(bundles):
        mine, got = refs[2 * i][...], refs[2 * i + 1][...]
        joined += [jnp.where(low, mine, got), jnp.where(low, got, mine)]
    half, hidden = joined[0].shape
    at = 0
    for out_ref in refs[2 * bundles :]:
        for c in range(out_ref.shape[1] // hidden):
            begin = 0
            while begin < out_ref.shape[0]:
                offset = at % half
                count = min(out_ref.shape[0] - begin, half - offset)
                out_ref[begin : begin + count, c * hidden : (c + 1) * hidden] = joined[at // half][
                    offset : offset + count
                ].astype(F32)
                at, begin = at + count, begin + count


def merge_kernel(node_ref, node_got_ref, obs_ref, obs_got_ref, grad_node_ref, grad_obs_ref):
    grad_node_ref[...] = node_ref[...] + node_got_ref[...].astype(F32)
    grad_obs_ref[...] = (obs_ref[...] + obs_got_ref[...].astype(F32)).astype(BF16)


def half_rows(rows):
    return rows // 2 if halves(rows) else rows


def summing(steps, tail, keep, send, after):
    hidden = keep.shape[1]
    for done, nxt in zip(steps[:-1], steps[1:]):
        rows = half_rows(keep.shape[0] - tail) + tail
        keep, send = call(
            functools.partial(add_kernel, nxt, tail),
            [((rows, hidden), keep.dtype), ((rows, hidden), BF16)],
            keep, flip(send, done),
            scratch=[pltpu.VMEM(keep.shape, keep.dtype)],
            after=after,
        )
        after[:] = [send]
        yield
    return keep, flip(send, steps[-1])


def final_halvings(steps, rows):
    count = 0
    for _ in steps:
        count += halves(rows)
        rows = half_rows(rows)
    return count


def weight_chain(steps, rows, tail, slots, keep, send, after):
    used = []
    for step in steps:
        if halves(rows):
            used.append(step)
            rows //= 2
    keep, got = yield from summing(steps, tail, keep, send, after)
    piece, *sums = call(
        last_kernel,
        [((rows, keep.shape[1]), BF16)] + ([((slots, keep.shape[1]), F32)] if tail else []),
        keep, got,
        after=after,
    )
    after[:] = [piece]
    yield
    for step in used[:0:-1]:
        (piece,) = call(
            functools.partial(join_kernel, step),
            [((2 * piece.shape[0], piece.shape[1]), BF16)],
            piece, flip(piece, step),
            after=after,
        )
        after[:] = [piece]
        yield
    return [piece, flip(piece, used[0])], sums


def obs_chain(steps, w_obs, keep, send, after):
    keep, got = yield from summing(steps, 0, keep, send, after)
    half = w_obs.shape[0] // 2
    obs_mine, obs_theirs = call(
        obs_kernel, [((keep.shape[0], half), F32), ((keep.shape[0], half), BF16)], keep, got, w_obs,
        after=after,
    )
    after[:] = [obs_theirs]
    yield
    return obs_mine, obs_theirs


def in_turns(chains, other, rounds, turns):
    def finish(chain):
        try:
            next(chain)
        except StopIteration as stop:
            return stop.value

    taken = 0
    for done in range(1, rounds + 1):
        for chain in chains:
            next(chain)
        while taken < turns and -(-(taken + 1) * rounds // turns) <= done:
            next(other)
            taken += 1
    return [finish(chain) for chain in chains], finish(other)


def local(obs_feat, node_state, grad_agg, owner, local_idx, slot, w_obs, w_node, slot_bias, w_out):
    owners = lax.axis_size(OWNER_AXES)
    obs, fanout = owner.shape
    nodes, width = node_state.shape
    hidden = w_obs.shape[1]
    slots = slot_bias.shape[0]
    cap = max(2, 2 * obs * fanout // owners)
    cap = -(-cap // SUBLANES) * SUBLANES
    edges = owners * cap
    half = width // 2
    slot_row = slot.reshape(1, obs)

    steps = halving_steps()
    chunk = cap * half // obs + SUBLANES
    other, *packed = call_staged(
        functools.partial(pack_kernel, cap),
        [((chunk, obs), BF16)] * (owners + 1),
        obs_feat, owner.T, local_idx.T, slot_row,
    )
    received = [shift(packed[j], OWNER_AXES, j) for j in range(1, owners)]
    tail = -(-slots // SUBLANES) * SUBLANES
    table, state_held, agg_held, w_node_held, w_obs_held = call_staged(
        table_kernel,
        [((nodes + tail, 4 * hidden), BF16)],
        node_state, grad_agg, w_node, w_out, slot_bias,
        held=(node_state, grad_agg, w_node, w_obs),
    )
    (mine,) = call(
        join_blocks_kernel, [((owners - 1, chunk, obs), BF16)], *received,
        after=(w_obs_held,),
    )
    theirs = shift(mine, "mp", 1)
    act, hot, rows_mine, rows_theirs, obs_keep, obs_send = call(
        functools.partial(edge_kernel, fanout, nodes, steps),
        [((edges, 2 * hidden), BF16), ((edges, nodes + tail), BF16)]
        + [((edges, half), BF16)] * 2
        + [((owners * obs // 2, hidden), BF16)] * 2,
        packed[0], mine, other, theirs, table, w_obs_held,
        scratch=[pltpu.VMEM((owners * obs, hidden), BF16)],
    )

    stack = 2 * width + width // hidden * hidden
    bundles = BUNDLES
    rows = stack // bundles
    shapes = []
    for i in range(bundles):
        share = rows // 2 + (tail if i == bundles - 1 else 0)
        shapes += [((share, hidden), F32), ((share, hidden), BF16)]
    node_mine, node_theirs, *shares = call(
        functools.partial(weight_kernel, steps[0], bundles, tail),
        [((nodes, half), F32), ((nodes, half), BF16)] + shapes,
        hot, act, rows_mine, rows_theirs, state_held, agg_held, w_node_held,
        scratch=[pltpu.VMEM((stack + tail, hidden), F32)],
    )
    after = []
    chains = [
        weight_chain(
            steps, rows, tail if i == bundles - 1 else 0, slots, shares[2 * i], shares[2 * i + 1], after
        )
        for i in range(bundles)
    ]
    rounds = len(steps) + final_halvings(steps, rows) - 1
    weights, (obs_mine, obs_theirs) = in_turns(
        chains, obs_chain(steps, w_obs_held, obs_keep, obs_send, after), rounds, len(steps)
    )
    grad_node, grad_obs = call(
        merge_kernel, [((nodes, half), F32), ((obs, half), BF16)],
        node_mine, shift(node_theirs, "mp", 1), obs_mine, shift(obs_theirs, "mp", 1),
    )
    ends = [end for pair, _ in weights for end in pair]
    (grad_slot,) = weights[-1][1]
    grad_w_node, grad_w_out, grad_w_obs = call(
        functools.partial(spread_kernel, steps[0], bundles),
        [((width, hidden), F32), ((hidden, width), F32), ((width, hidden), F32)],
        *ends,
        after=[pltpu.with_memory_space_constraint(grad_obs, pltpu.HBM)],
    )
    return grad_obs, grad_node, grad_w_obs, grad_w_node, grad_w_out, grad_slot


def solution(mesh):
    rows = P(("group", "obs", "node"), None)
    return jax.shard_map(
        local,
        mesh=mesh,
        in_specs=(
            rows, rows, rows, rows, rows,
            P(("group", "obs", "node")),
            P(None, "mp"), P(None, "mp"), P(None, "mp"), P("mp", None),
        ),
        out_specs=(
            P(("group", "obs", "node"), "mp"),
            P(("group", "obs", "node"), "mp"),
            P("group", "mp"),
            P("group", "mp"),
            P(("group", "mp"), None),
            P("group", "mp"),
        ),
        check_vma=False,
    )
```

```python
import functools

import jax
import jax.numpy as jnp
from jax import lax
from jax.experimental import pallas as pl
from jax.experimental.pallas import tpu as pltpu
from jax.sharding import PartitionSpec as P

OWNER_AXES = ("obs", "node")
SUBLANES = 16
BUNDLES = 2
BF16 = jnp.bfloat16
F32 = jnp.float32


def dot(left, right, left_dim=1, right_dim=0):
    return lax.dot_general(
        left, right, (((left_dim,), (right_dim,)), ((), ())), preferred_element_type=F32
    )


def iota(shape, dim):
    return lax.broadcasted_iota(jnp.int32, shape, dim)


def call(kernel, outs, *args, scratch=(), after=()):
    vmem = pl.BlockSpec(memory_space=pltpu.VMEM)
    count = len(args)
    specs = [vmem] * count + [pl.BlockSpec(memory_space=pl.ANY)] * len(after)
    args += tuple(after)
    return pl.pallas_call(
        lambda *refs: kernel(*refs[:count], *refs[len(args) :]),
        out_shape=[jax.ShapeDtypeStruct(shape, dtype) for shape, dtype in outs],
        in_specs=specs,
        out_specs=[vmem] * len(outs),
        scratch_shapes=list(scratch),
        compiler_params=pltpu.CompilerParams(vmem_limit_bytes=40 << 20),
    )(*args)


def call_staged(kernel, outs, *args, held=()):
    count = len(args)
    sources = list(args) + [a for a in held if not any(a is b for b in args)]
    kept = [next(i for i, b in enumerate(sources) if a is b) for a in held]
    rest = [i for i in range(len(sources)) if i not in kept]

    def staged(*refs):
        hbm, refs = refs[: len(sources)], refs[len(sources) :]
        out_refs, refs = refs[: len(outs)], refs[len(outs) :]
        buffers = dict(zip(kept, refs[: len(kept)])) | dict(zip(rest, refs[len(kept) : -1]))
        copies = [
            pltpu.make_async_copy(hbm[i], buffers[i], refs[-1].at[i]) for i in range(len(sources))
        ]
        for copy in copies:
            copy.start()
        for copy in copies:
            copy.wait()
        kernel(*[buffers[i] for i in range(count)], *out_refs)

    return pl.pallas_call(
        staged,
        out_shape=[jax.ShapeDtypeStruct(shape, dtype) for shape, dtype in outs]
        + [jax.ShapeDtypeStruct(a.shape, a.dtype) for a in held],
        in_specs=[pl.BlockSpec(memory_space=pltpu.HBM)] * len(sources),
        out_specs=[pl.BlockSpec(memory_space=pltpu.VMEM)] * (len(outs) + len(held)),
        scratch_shapes=[pltpu.VMEM(sources[i].shape, sources[i].dtype) for i in rest]
        + [pltpu.SemaphoreType.DMA((len(sources),))],
        compiler_params=pltpu.CompilerParams(vmem_limit_bytes=40 << 20),
    )(*[pltpu.with_memory_space_constraint(a, pltpu.HBM) for a in sources])


def exchange(blocks, axes):
    return lax.all_to_all(blocks, axes, split_axis=0, concat_axis=0, tiled=True)


def shift(value, axis, step):
    size = lax.axis_size(axis)
    return lax.ppermute(value, axis, [(i, (i + step) % size) for i in range(size)])


def other_half(ref):
    half = ref.shape[0] // 2
    me = lax.axis_index("mp")
    mine = ref[pl.ds(pl.multiple_of(me * half, half), half), :]
    theirs = ref[pl.ds(pl.multiple_of((1 - me) * half, half), half), :]
    return mine, theirs


def column_half(ref, which):
    half = ref.shape[1] // 2
    return ref[:, pl.ds(pl.multiple_of(which * half, 128), half)]


def pack_kernel(cap, obs_ref, owner_ref, index_ref, slot_ref, other_ref, *outs):
    owners = len(outs)
    chunk, lanes = outs[0].shape
    fanout, obs = owner_ref.shape
    owner, index = owner_ref[...], index_ref[...]
    hits = [iota((owners, obs), 0) == owner[k : k + 1] for k in range(fanout)]
    count = functools.reduce(jnp.add, [h.astype(F32) for h in hits])
    before = dot(count, (iota((obs, obs), 0) < iota((obs, obs), 1)).astype(F32))
    header = jnp.where(iota((SUBLANES, obs), 0) == 4 * fanout, slot_ref[...].astype(F32), 0.0)
    places = []
    for k in range(fanout):
        rank = jnp.sum(jnp.where(hits[k], before, 0.0), axis=0, keepdims=True)
        places.append(owner[k : k + 1] * cap + rank.astype(jnp.int32))
        plus = index[k : k + 1] + 1
        fields = (owner[k : k + 1].astype(F32), rank, (plus // 16).astype(F32), (plus % 16).astype(F32))
        for j, row in enumerate(fields):
            header = jnp.where(iota(header.shape, 0) == 4 * k + j, row, header)
    header = header.astype(BF16)
    me, core = lax.axis_index(OWNER_AXES), lax.axis_index("mp")
    mine, other = column_half(obs_ref, core), column_half(obs_ref, 1 - core)

    def write(ref, pick, rows):
        packed = dot(pick, rows).astype(BF16)
        for c in range(rows.shape[1] // lanes):
            ref[c * cap : (c + 1) * cap, :] = packed[:, c * lanes : (c + 1) * lanes]
        ref[chunk - SUBLANES :, :] = header

    for j, out_ref in enumerate(outs):
        slots = iota((cap, obs), 0) + lax.rem(me + j, owners) * cap
        pick = functools.reduce(jnp.logical_or, [slots == place for place in places]).astype(BF16)
        write(out_ref, pick, mine)
        if j == 0:
            write(other_ref, pick, other)


def table_kernel(state_ref, agg_ref, w_node_ref, w_out_ref, bias_ref, table_ref):
    hidden = w_node_ref.shape[1]
    nodes, slots = state_ref.shape[0], bias_ref.shape[0]
    table_ref[nodes:, :] = jnp.zeros((table_ref.shape[0] - nodes, table_ref.shape[1]), BF16)

    def put(begin, column, part):
        high = part.astype(BF16)
        table_ref[begin : begin + part.shape[0], column : column + hidden] = high
        table_ref[begin : begin + part.shape[0], column + hidden : column + 2 * hidden] = (
            part - high.astype(F32)
        ).astype(BF16)

    put(0, 0, dot(state_ref[...], w_node_ref[...]))
    put(0, 2 * hidden, dot(agg_ref[...], w_out_ref[...], 1, 1))
    put(nodes, 0, bias_ref[...])


def join_blocks_kernel(*refs):
    out_ref = refs[-1]
    for j, ref in enumerate(refs[:-1]):
        out_ref[j] = ref[...]


def edge_kernel(
    fanout, nodes, steps, own_ref, mine_ref, other_ref, theirs_ref, table_ref, w_obs_ref,
    act_ref, hot_ref, rows_mine_ref, rows_theirs_ref, keep_ref, send_ref, total_ref,
):
    owners = mine_ref.shape[0] + 1
    chunk, lanes = own_ref.shape
    half = w_obs_ref.shape[0] // 2
    hidden = w_obs_ref.shape[1]
    cap = (chunk - SUBLANES) * lanes // half
    me = lax.axis_index(OWNER_AXES)
    base = 1 << nodes.bit_length()
    columns = []
    picks = []
    for j in range(owners):
        block, other = (mine_ref.at[j - 1], theirs_ref.at[j - 1]) if j else (own_ref, other_ref)
        header = block[chunk - SUBLANES :, :].astype(F32)
        slot = header[4 * fanout : 4 * fanout + 1] * base
        code = jnp.zeros((cap, lanes), F32)
        pick = jnp.zeros((cap, lanes), jnp.bool_)
        for k in range(fanout):
            row = header[4 * k : 4 * k + 4]
            rank = jnp.where(row[0:1] == me.astype(F32), row[1:2], -1.0).astype(jnp.int32)
            hit = iota((cap, lanes), 0) == rank
            pick = pick | hit
            code = code + jnp.where(hit, row[2:3] * 16.0 + row[3:4] + slot, 0.0)
        picks.append(pick.astype(BF16))
        columns.append(jnp.sum(code, axis=1, keepdims=True).astype(jnp.int32))
        for c in range(half // lanes):
            rows = slice(j * cap, (j + 1) * cap)
            place = slice(c * lanes, (c + 1) * lanes)
            rows_mine_ref[rows, place] = block[c * cap : (c + 1) * cap, :]
            rows_theirs_ref[rows, place] = other[c * cap : (c + 1) * cap, :]
    code = jnp.concatenate(columns, axis=0)
    index, slot = (code & (base - 1)) - 1, (code >> (base.bit_length() - 1)) + nodes
    column = iota(hot_ref.shape, 1)
    hot = ((column == index) | ((column == slot) & (index >= 0))).astype(BF16)
    hot_ref[...] = hot
    rows = dot(hot, table_ref[...])
    w_mine, w_theirs = other_half(w_obs_ref)
    pre = dot(rows_mine_ref[...], w_mine) + dot(rows_theirs_ref[...], w_theirs)
    pre = pre + (rows[:, :hidden] + rows[:, hidden : 2 * hidden])
    g_z = rows[:, 2 * hidden : 3 * hidden] + rows[:, 3 * hidden :]
    sig = jax.nn.sigmoid(pre)
    g_a = (g_z * sig * (1.0 + pre * (1.0 - sig))).astype(BF16)
    act_ref[:, :hidden] = g_a
    act_ref[:, hidden:] = (pre * sig).astype(BF16)
    for j, pick in enumerate(picks):
        source = lax.rem(me - j + owners, owners)
        begin = pl.multiple_of(place_of(source, steps) * lanes, SUBLANES)
        total_ref[pl.ds(begin, lanes), :] = dot(pick, g_a[j * cap : (j + 1) * cap], 0, 0).astype(BF16)
    split_half(total_ref, 0, owners * lanes, steps[0], 0, keep_ref, send_ref)


def halving_steps():
    bits = [
        [(axis, k) for k in range(lax.axis_size(axis).bit_length() - 1)] for axis in ("node", "obs")
    ]
    steps = []
    for k in range(max(map(len, bits))):
        both = [line[k] for line in bits if k < len(line)]
        steps += [(both[0], both[-1])] + ([(both[1], both[0])] if len(both) > 1 else [])
    return steps


def flip(value, step):
    axes = ("obs", "node", "mp")
    sizes = [lax.axis_size(axis) for axis in axes]
    pairs = []
    for index in range(sizes[0] * sizes[1] * sizes[2]):
        place = [index // (sizes[1] * sizes[2]), index // sizes[2] % sizes[1], index % sizes[2]]
        axis, k = step[place[2] % 2]
        place[axes.index(axis)] ^= 1 << k
        pairs.append((index, (place[0] * sizes[1] + place[1]) * sizes[2] + place[2]))
    return lax.ppermute(value, axes, pairs)


def bit_of(step, node, obs):
    bits = [({"node": node, "obs": obs}[axis] >> k) & 1 for axis, k in step]
    return jnp.where(lax.axis_index("mp") % 2 == 0, bits[0], bits[1])


def own_bit(step):
    return bit_of(step, lax.axis_index("node"), lax.axis_index("obs"))


def place_of(owner, steps):
    shares = lax.axis_size("node")
    place = 0
    for step in steps:
        place = 2 * place + bit_of(step, lax.rem(owner, shares), lax.div(owner, shares))
    return place


def halves(rows):
    return rows % (2 * SUBLANES) == 0


def half_rows(rows):
    return rows // 2 if halves(rows) else rows


def split_half(total_ref, start, rows, step, tail, keep_ref, send_ref):
    end = start + rows
    half = half_rows(rows) if step else rows
    if half < rows:
        bit = own_bit(step)
        kept, sent = [pl.ds(pl.multiple_of(start + b * half, SUBLANES), half) for b in (bit, 1 - bit)]
        keep_ref[:half, :] = total_ref[kept, :]
        send_ref[:half, :] = total_ref[sent, :].astype(BF16)
    else:
        both = total_ref[start:end, :].astype(BF16)
        keep_ref[:half, :] = both.astype(keep_ref.dtype)
        send_ref[:half, :] = both
    if tail:
        both = total_ref[end : end + tail, :].astype(BF16)
        keep_ref[half:, :] = both.astype(keep_ref.dtype)
        send_ref[half:, :] = both


def weight_kernel(
    step, bundles, tail, hot_ref, act_ref, rows_mine_ref, rows_theirs_ref, state_ref, agg_ref, w_node_ref,
    mine_ref, theirs_ref, *refs
):
    halves_refs, total_ref = refs[:-1], refs[-1]
    width, hidden = w_node_ref.shape
    nodes = state_ref.shape[0]
    sums = dot(hot_ref[...], act_ref[...], 0, 0)
    by_node = sums[:nodes].astype(BF16)
    node_hidden, z_sum = by_node[:, :hidden], by_node[:, hidden:]
    total_ref[:width, :] = dot(state_ref[...], node_hidden, 0, 0)
    begin = width
    for c in range(width // hidden):
        total_ref[begin : begin + hidden, :] = dot(
            z_sum, agg_ref[:, c * hidden : (c + 1) * hidden], 0, 0
        )
        begin += hidden
    g_a = act_ref[:, :hidden]
    core, half = lax.axis_index("mp"), width // 2
    for which, ref in ((core, rows_mine_ref), (1 - core, rows_theirs_ref)):
        total_ref[pl.ds(pl.multiple_of(begin + which * half, SUBLANES), half), :] = dot(ref[...], g_a, 0, 0)
    begin += width
    total_ref[begin:, :] = sums[nodes:, :hidden]
    rows = begin // bundles
    for i in range(bundles):
        split_half(
            total_ref, i * rows, rows, step, tail if i == bundles - 1 else 0,
            halves_refs[2 * i], halves_refs[2 * i + 1],
        )
    mine, theirs = other_half(w_node_ref)
    theirs_ref[...] = dot(node_hidden, theirs, 1, 1).astype(BF16)
    mine_ref[...] = dot(node_hidden, mine, 1, 1)


def obs_kernel(keep_ref, got_ref, w_ref, mine_ref, theirs_ref):
    obs_hidden = (keep_ref[...].astype(F32) + got_ref[...].astype(F32)).astype(BF16)
    mine, theirs = other_half(w_ref)
    theirs_ref[...] = dot(obs_hidden, theirs, 1, 1).astype(BF16)
    mine_ref[...] = dot(obs_hidden, mine, 1, 1)


def add_kernel(step, tail, keep_ref, got_ref, next_ref, send_ref, total_ref):
    total = keep_ref[...].astype(F32) + got_ref[...].astype(F32)
    total_ref[...] = total.astype(total_ref.dtype)
    split_half(total_ref, 0, total_ref.shape[0] - tail, step, tail, next_ref, send_ref)


def last_kernel(keep_ref, got_ref, piece_ref, *slot_refs):
    total = keep_ref[...] + got_ref[...].astype(F32)
    rows = piece_ref.shape[0]
    piece_ref[...] = total[:rows].astype(BF16)
    for slot_ref in slot_refs:
        slot_ref[...] = total[rows : rows + slot_ref.shape[0]]


def join_kernel(step, mine_ref, got_ref, out_ref):
    rows = mine_ref.shape[0]
    bit = own_bit(step)
    out_ref[pl.ds(pl.multiple_of(bit * rows, SUBLANES), rows), :] = mine_ref[...]
    out_ref[pl.ds(pl.multiple_of((1 - bit) * rows, SUBLANES), rows), :] = got_ref[...]


def spread_kernel(step, bundles, *refs):
    low = own_bit(step) == 0
    joined = []
    for i in range(bundles):
        mine, got = refs[2 * i][...], refs[2 * i + 1][...]
        joined += [jnp.where(low, mine, got), jnp.where(low, got, mine)]
    half, hidden = joined[0].shape
    at = 0
    for out_ref in refs[2 * bundles :]:
        for c in range(out_ref.shape[1] // hidden):
            begin = 0
            while begin < out_ref.shape[0]:
                offset = at % half
                count = min(out_ref.shape[0] - begin, half - offset)
                out_ref[begin : begin + count, c * hidden : (c + 1) * hidden] = joined[at // half][
                    offset : offset + count
                ].astype(F32)
                at, begin = at + count, begin + count


def merge_kernel(node_ref, node_got_ref, obs_ref, obs_got_ref, grad_node_ref, grad_obs_ref):
    grad_node_ref[...] = node_ref[...] + node_got_ref[...].astype(F32)
    grad_obs_ref[...] = (obs_ref[...] + obs_got_ref[...].astype(F32)).astype(BF16)


def summing(steps, halved, tail, keep, got, after):
    hidden = keep.shape[1]
    for at, following in enumerate(steps[1:], 1):
        step = following if at < halved else None
        rows = keep.shape[0] - tail
        rows = (half_rows(rows) if step else rows) + tail
        keep, send = call(
            functools.partial(add_kernel, step, tail),
            [((rows, hidden), keep.dtype), ((rows, hidden), BF16)],
            keep, got,
            scratch=[pltpu.VMEM(keep.shape, keep.dtype)],
            after=after,
        )
        after[:] = [send]
        got = flip(send, following)
        yield
    return keep, got


def halving_used(steps, rows):
    used = []
    for step in steps[:-1]:
        if halves(rows):
            used.append(step)
            rows //= 2
    return used


def weight_chain(steps, rows, tail, slots, keep, got, after):
    used = halving_used(steps, rows)
    keep, got = yield from summing(steps, len(steps) - 1, tail, keep, got, after)
    piece, *sums = call(
        last_kernel,
        [((keep.shape[0] - tail, keep.shape[1]), BF16)]
        + ([((slots, keep.shape[1]), F32)] if tail else []),
        keep, got,
        after=after,
    )
    after[:] = [piece]
    got = flip(piece, used[-1])
    yield
    for step, following in zip(used[:0:-1], used[-2::-1]):
        (piece,) = call(
            functools.partial(join_kernel, step),
            [((2 * piece.shape[0], piece.shape[1]), BF16)],
            piece, got,
            after=after,
        )
        after[:] = [piece]
        got = flip(piece, following)
        yield
    return [piece, got], sums


def obs_chain(steps, w_obs, keep, got, after):
    keep, got = yield from summing(steps, len(steps), 0, keep, got, after)
    half = w_obs.shape[0] // 2
    obs_mine, obs_theirs = call(
        obs_kernel, [((keep.shape[0], half), F32), ((keep.shape[0], half), BF16)], keep, got, w_obs,
        after=after,
    )
    after[:] = [obs_theirs]
    obs_got = shift(obs_theirs, "mp", 1)
    yield
    return obs_mine, obs_got


def in_turns(chains, turns):
    results = {}
    for key in turns + [key for key in range(len(chains))]:
        try:
            next(chains[key])
        except StopIteration as stop:
            results[key] = stop.value
    return [results[key] for key in range(len(chains))]


def local(obs_feat, node_state, grad_agg, owner, local_idx, slot, w_obs, w_node, slot_bias, w_out):
    owners = lax.axis_size(OWNER_AXES)
    obs, fanout = owner.shape
    nodes, width = node_state.shape
    hidden = w_obs.shape[1]
    slots = slot_bias.shape[0]
    cap = max(2, 2 * obs * fanout // owners)
    cap = -(-cap // SUBLANES) * SUBLANES
    edges = owners * cap
    half = width // 2
    slot_row = slot.reshape(1, obs)

    steps = halving_steps()
    chunk = cap * half // obs + SUBLANES
    other, *packed = call_staged(
        functools.partial(pack_kernel, cap),
        [((chunk, obs), BF16)] * (owners + 1),
        obs_feat, owner.T, local_idx.T, slot_row,
    )
    received = [shift(packed[j], OWNER_AXES, j) for j in range(1, owners)]
    tail = -(-slots // SUBLANES) * SUBLANES
    table, state_held, agg_held, w_node_held, w_obs_held = call_staged(
        table_kernel,
        [((nodes + tail, 4 * hidden), BF16)],
        node_state, grad_agg, w_node, w_out, slot_bias,
        held=(node_state, grad_agg, w_node, w_obs),
    )
    (mine,) = call(
        join_blocks_kernel, [((owners - 1, chunk, obs), BF16)], *received,
        after=(w_obs_held,),
    )
    theirs = shift(mine, "mp", 1)
    act, hot, rows_mine, rows_theirs, obs_keep, obs_send = call(
        functools.partial(edge_kernel, fanout, nodes, steps),
        [((edges, 2 * hidden), BF16), ((edges, nodes + tail), BF16)]
        + [((edges, half), BF16)] * 2
        + [((owners * obs // 2, hidden), BF16)] * 2,
        packed[0], mine, other, theirs, table, w_obs_held,
        scratch=[pltpu.VMEM((owners * obs, hidden), BF16)],
    )

    stack = 2 * width + width // hidden * hidden
    bundles = BUNDLES
    rows = stack // bundles
    obs_got = flip(obs_send, steps[0])
    shapes = []
    for i in range(bundles):
        share = rows // 2 + (tail if i == bundles - 1 else 0)
        shapes += [((share, hidden), F32), ((share, hidden), BF16)]
    node_mine, node_theirs, *shares = call(
        functools.partial(weight_kernel, steps[0], bundles, tail),
        [((nodes, half), F32), ((nodes, half), BF16)] + shapes,
        hot, act, rows_mine, rows_theirs, state_held, agg_held, w_node_held,
        scratch=[pltpu.VMEM((stack + tail, hidden), F32)],
    )
    after = []
    got = [flip(send, steps[0]) for send in shares[1::2]]
    chains = [
        weight_chain(
            steps, rows, tail if i == bundles - 1 else 0, slots, shares[2 * i], got[i], after
        )
        for i in range(bundles)
    ]
    node_got = shift(node_theirs, "mp", 1)
    everyone = list(range(1, bundles + 1))
    turns = ([0] + everyone) * (len(steps) - 1) + everyone + [0] + everyone * (len(halving_used(steps, rows)) - 1)
    (obs_mine, obs_got), *weights = in_turns(
        [obs_chain(steps, w_obs_held, obs_keep, obs_got, after)] + chains, turns
    )
    grad_node, grad_obs = call(
        merge_kernel, [((nodes, half), F32), ((obs, half), BF16)],
        node_mine, node_got, obs_mine, obs_got,
    )
    ends = [end for pair, _ in weights for end in pair]
    (grad_slot,) = weights[-1][1]
    grad_w_node, grad_w_out, grad_w_obs = call(
        functools.partial(spread_kernel, steps[0], bundles),
        [((width, hidden), F32), ((hidden, width), F32), ((width, hidden), F32)],
        *ends,
        after=[pltpu.with_memory_space_constraint(grad_obs, pltpu.HBM)],
    )
    return grad_obs, grad_node, grad_w_obs, grad_w_node, grad_w_out, grad_slot


def solution(mesh):
    rows = P(("group", "obs", "node"), None)
    return jax.shard_map(
        local,
        mesh=mesh,
        in_specs=(
            rows, rows, rows, rows, rows,
            P(("group", "obs", "node")),
            P(None, "mp"), P(None, "mp"), P(None, "mp"), P("mp", None),
        ),
        out_specs=(
            P(("group", "obs", "node"), "mp"),
            P(("group", "obs", "node"), "mp"),
            P("group", "mp"),
            P("group", "mp"),
            P(("group", "mp"), None),
            P("group", "mp"),
        ),
        check_vma=False,
    )
```

```python
import functools

import jax
import jax.numpy as jnp
from jax import lax
from jax.experimental import pallas as pl
from jax.experimental.pallas import tpu as pltpu
from jax.sharding import PartitionSpec as P

OWNER_AXES = ("obs", "node")
SUBLANES = 16
BUNDLES = 2
BF16 = jnp.bfloat16
F32 = jnp.float32


def dot(left, right, left_dim=1, right_dim=0):
    return lax.dot_general(
        left, right, (((left_dim,), (right_dim,)), ((), ())), preferred_element_type=F32
    )


def iota(shape, dim):
    return lax.broadcasted_iota(jnp.int32, shape, dim)


def call(kernel, outs, *args, scratch=(), after=()):
    vmem = pl.BlockSpec(memory_space=pltpu.VMEM)
    count = len(args)
    specs = [vmem] * count + [pl.BlockSpec(memory_space=pl.ANY)] * len(after)
    args += tuple(after)
    return pl.pallas_call(
        lambda *refs: kernel(*refs[:count], *refs[len(args) :]),
        out_shape=[jax.ShapeDtypeStruct(shape, dtype) for shape, dtype in outs],
        in_specs=specs,
        out_specs=[vmem] * len(outs),
        scratch_shapes=list(scratch),
        compiler_params=pltpu.CompilerParams(vmem_limit_bytes=40 << 20),
    )(*args)


def call_staged(kernel, outs, *args, held=()):
    count = len(args)
    sources = list(args) + [a for a in held if not any(a is b for b in args)]
    kept = [next(i for i, b in enumerate(sources) if a is b) for a in held]
    rest = [i for i in range(len(sources)) if i not in kept]

    def staged(*refs):
        hbm, refs = refs[: len(sources)], refs[len(sources) :]
        out_refs, refs = refs[: len(outs)], refs[len(outs) :]
        buffers = dict(zip(kept, refs[: len(kept)])) | dict(zip(rest, refs[len(kept) : -1]))
        copies = [
            pltpu.make_async_copy(hbm[i], buffers[i], refs[-1].at[i]) for i in range(len(sources))
        ]
        for copy in copies:
            copy.start()
        for copy in copies:
            copy.wait()
        kernel(*[buffers[i] for i in range(count)], *out_refs)

    return pl.pallas_call(
        staged,
        out_shape=[jax.ShapeDtypeStruct(shape, dtype) for shape, dtype in outs]
        + [jax.ShapeDtypeStruct(a.shape, a.dtype) for a in held],
        in_specs=[pl.BlockSpec(memory_space=pltpu.HBM)] * len(sources),
        out_specs=[pl.BlockSpec(memory_space=pltpu.VMEM)] * (len(outs) + len(held)),
        scratch_shapes=[pltpu.VMEM(sources[i].shape, sources[i].dtype) for i in rest]
        + [pltpu.SemaphoreType.DMA((len(sources),))],
        compiler_params=pltpu.CompilerParams(vmem_limit_bytes=40 << 20),
    )(*[pltpu.with_memory_space_constraint(a, pltpu.HBM) for a in sources])


def exchange(blocks, axes):
    return lax.all_to_all(blocks, axes, split_axis=0, concat_axis=0, tiled=True)


def shift(value, axis, step):
    size = lax.axis_size(axis)
    return lax.ppermute(value, axis, [(i, (i + step) % size) for i in range(size)])


def other_half(ref):
    half = ref.shape[0] // 2
    me = lax.axis_index("mp")
    mine = ref[pl.ds(pl.multiple_of(me * half, half), half), :]
    theirs = ref[pl.ds(pl.multiple_of((1 - me) * half, half), half), :]
    return mine, theirs


def column_half(ref, which):
    half = ref.shape[1] // 2
    return ref[:, pl.ds(pl.multiple_of(which * half, 128), half)]


def pack_kernel(cap, obs_ref, owner_ref, index_ref, slot_ref, other_ref, *outs):
    owners = len(outs)
    chunk, lanes = outs[0].shape
    fanout, obs = owner_ref.shape
    owner, index = owner_ref[...], index_ref[...]
    hits = [iota((owners, obs), 0) == owner[k : k + 1] for k in range(fanout)]
    count = functools.reduce(jnp.add, [h.astype(F32) for h in hits])
    before = dot(count, (iota((obs, obs), 0) < iota((obs, obs), 1)).astype(F32))
    header = jnp.where(iota((SUBLANES, obs), 0) == 4 * fanout, slot_ref[...].astype(F32), 0.0)
    places = []
    for k in range(fanout):
        rank = jnp.sum(jnp.where(hits[k], before, 0.0), axis=0, keepdims=True)
        places.append(owner[k : k + 1] * cap + rank.astype(jnp.int32))
        plus = index[k : k + 1] + 1
        fields = (owner[k : k + 1].astype(F32), rank, (plus // 16).astype(F32), (plus % 16).astype(F32))
        for j, row in enumerate(fields):
            header = jnp.where(iota(header.shape, 0) == 4 * k + j, row, header)
    header = header.astype(BF16)
    me, core = lax.axis_index(OWNER_AXES), lax.axis_index("mp")
    mine, other = column_half(obs_ref, core), column_half(obs_ref, 1 - core)

    def write(ref, pick, rows):
        packed = dot(pick, rows).astype(BF16)
        for c in range(rows.shape[1] // lanes):
            ref[c * cap : (c + 1) * cap, :] = packed[:, c * lanes : (c + 1) * lanes]
        ref[chunk - SUBLANES :, :] = header

    for j, out_ref in enumerate(outs):
        slots = iota((cap, obs), 0) + lax.rem(me + j, owners) * cap
        pick = functools.reduce(jnp.logical_or, [slots == place for place in places]).astype(BF16)
        write(out_ref, pick, mine)
        if j == 0:
            write(other_ref, pick, other)


def table_kernel(state_ref, agg_ref, w_node_ref, w_out_ref, bias_ref, table_ref):
    hidden = w_node_ref.shape[1]
    nodes, slots = state_ref.shape[0], bias_ref.shape[0]
    table_ref[nodes:, :] = jnp.zeros((table_ref.shape[0] - nodes, table_ref.shape[1]), BF16)

    def put(begin, column, part):
        high = part.astype(BF16)
        table_ref[begin : begin + part.shape[0], column : column + hidden] = high
        table_ref[begin : begin + part.shape[0], column + hidden : column + 2 * hidden] = (
            part - high.astype(F32)
        ).astype(BF16)

    put(0, 0, dot(state_ref[...], w_node_ref[...]))
    put(0, 2 * hidden, dot(agg_ref[...], w_out_ref[...], 1, 1))
    put(nodes, 0, bias_ref[...])


def join_blocks_kernel(*refs):
    out_ref = refs[-1]
    for j, ref in enumerate(refs[:-1]):
        out_ref[j] = ref[...]


def edge_kernel(
    fanout, nodes, steps, own_ref, mine_ref, other_ref, theirs_ref, table_ref, w_obs_ref,
    act_ref, hot_ref, rows_mine_ref, rows_theirs_ref, keep_ref, send_ref, total_ref,
):
    owners = mine_ref.shape[0] + 1
    chunk, lanes = own_ref.shape
    half = w_obs_ref.shape[0] // 2
    hidden = w_obs_ref.shape[1]
    cap = (chunk - SUBLANES) * lanes // half
    me = lax.axis_index(OWNER_AXES)
    base = 1 << nodes.bit_length()
    columns = []
    picks = []
    for j in range(owners):
        block, other = (mine_ref.at[j - 1], theirs_ref.at[j - 1]) if j else (own_ref, other_ref)
        header = block[chunk - SUBLANES :, :].astype(F32)
        slot = header[4 * fanout : 4 * fanout + 1] * base
        code = jnp.zeros((cap, lanes), F32)
        pick = jnp.zeros((cap, lanes), jnp.bool_)
        for k in range(fanout):
            row = header[4 * k : 4 * k + 4]
            rank = jnp.where(row[0:1] == me.astype(F32), row[1:2], -1.0).astype(jnp.int32)
            hit = iota((cap, lanes), 0) == rank
            pick = pick | hit
            code = code + jnp.where(hit, row[2:3] * 16.0 + row[3:4] + slot, 0.0)
        picks.append(pick.astype(BF16))
        columns.append(jnp.sum(code, axis=1, keepdims=True).astype(jnp.int32))
        for c in range(half // lanes):
            rows = slice(j * cap, (j + 1) * cap)
            place = slice(c * lanes, (c + 1) * lanes)
            rows_mine_ref[rows, place] = block[c * cap : (c + 1) * cap, :]
            rows_theirs_ref[rows, place] = other[c * cap : (c + 1) * cap, :]
    code = jnp.concatenate(columns, axis=0)
    index, slot = (code & (base - 1)) - 1, (code >> (base.bit_length() - 1)) + nodes
    column = iota(hot_ref.shape, 1)
    hot = ((column == index) | ((column == slot) & (index >= 0))).astype(BF16)
    hot_ref[...] = hot
    rows = dot(hot, table_ref[...])
    w_mine, w_theirs = other_half(w_obs_ref)
    pre = dot(rows_mine_ref[...], w_mine) + dot(rows_theirs_ref[...], w_theirs)
    pre = pre + (rows[:, :hidden] + rows[:, hidden : 2 * hidden])
    g_z = rows[:, 2 * hidden : 3 * hidden] + rows[:, 3 * hidden :]
    sig = jax.nn.sigmoid(pre)
    g_a = (g_z * sig * (1.0 + pre * (1.0 - sig))).astype(BF16)
    act_ref[:, :hidden] = g_a
    act_ref[:, hidden:] = (pre * sig).astype(BF16)
    for j, pick in enumerate(picks):
        source = lax.rem(me - j + owners, owners)
        begin = pl.multiple_of(place_of(source, steps) * lanes, SUBLANES)
        total_ref[pl.ds(begin, lanes), :] = dot(pick, g_a[j * cap : (j + 1) * cap], 0, 0).astype(BF16)
    split_half(total_ref, 0, owners * lanes, steps[0], 0, keep_ref, send_ref)


def halving_steps():
    bits = [
        [(axis, k) for k in range(lax.axis_size(axis).bit_length() - 1)] for axis in ("node", "obs")
    ]
    steps = []
    for k in range(max(map(len, bits))):
        both = [line[k] for line in bits if k < len(line)]
        steps += [(both[0], both[-1])] + ([(both[1], both[0])] if len(both) > 1 else [])
    return steps


def flip(value, step):
    axes = ("obs", "node", "mp")
    sizes = [lax.axis_size(axis) for axis in axes]
    pairs = []
    for index in range(sizes[0] * sizes[1] * sizes[2]):
        place = [index // (sizes[1] * sizes[2]), index // sizes[2] % sizes[1], index % sizes[2]]
        axis, k = step[place[2] % 2]
        place[axes.index(axis)] ^= (2 << k) - 1
        pairs.append((index, (place[0] * sizes[1] + place[1]) * sizes[2] + place[2]))
    return lax.ppermute(value, axes, pairs)


def bit_of(step, node, obs):
    codes = {"node": node ^ (node >> 1), "obs": obs ^ (obs >> 1)}
    bits = [(codes[axis] >> k) & 1 for axis, k in step]
    return jnp.where(lax.axis_index("mp") % 2 == 0, bits[0], bits[1])


def own_bit(step):
    return bit_of(step, lax.axis_index("node"), lax.axis_index("obs"))


def place_of(owner, steps):
    shares = lax.axis_size("node")
    place = 0
    for step in steps:
        place = 2 * place + bit_of(step, lax.rem(owner, shares), lax.div(owner, shares))
    return place


def halves(rows):
    return rows % (2 * SUBLANES) == 0


def half_rows(rows):
    return rows // 2 if halves(rows) else rows


def split_half(total_ref, start, rows, step, tail, keep_ref, send_ref):
    end = start + rows
    half = half_rows(rows) if step else rows
    if half < rows:
        bit = own_bit(step)
        kept, sent = [pl.ds(pl.multiple_of(start + b * half, SUBLANES), half) for b in (bit, 1 - bit)]
        keep_ref[:half, :] = total_ref[kept, :]
        send_ref[:half, :] = total_ref[sent, :].astype(BF16)
    else:
        both = total_ref[start:end, :].astype(BF16)
        keep_ref[:half, :] = both.astype(keep_ref.dtype)
        send_ref[:half, :] = both
    if tail:
        both = total_ref[end : end + tail, :].astype(BF16)
        keep_ref[half:, :] = both.astype(keep_ref.dtype)
        send_ref[half:, :] = both


def weight_kernel(
    step, bundles, tail, hot_ref, act_ref, rows_mine_ref, rows_theirs_ref, state_ref, agg_ref, w_node_ref,
    mine_ref, theirs_ref, *refs
):
    halves_refs, total_ref = refs[:-1], refs[-1]
    width, hidden = w_node_ref.shape
    nodes = state_ref.shape[0]
    sums = dot(hot_ref[...], act_ref[...], 0, 0)
    by_node = sums[:nodes].astype(BF16)
    node_hidden, z_sum = by_node[:, :hidden], by_node[:, hidden:]
    total_ref[:width, :] = dot(state_ref[...], node_hidden, 0, 0)
    begin = width
    for c in range(width // hidden):
        total_ref[begin : begin + hidden, :] = dot(
            z_sum, agg_ref[:, c * hidden : (c + 1) * hidden], 0, 0
        )
        begin += hidden
    g_a = act_ref[:, :hidden]
    core, half = lax.axis_index("mp"), width // 2
    for which, ref in ((core, rows_mine_ref), (1 - core, rows_theirs_ref)):
        total_ref[pl.ds(pl.multiple_of(begin + which * half, SUBLANES), half), :] = dot(ref[...], g_a, 0, 0)
    begin += width
    total_ref[begin:, :] = sums[nodes:, :hidden]
    rows = begin // bundles
    for i in range(bundles):
        split_half(
            total_ref, i * rows, rows, step, tail if i == bundles - 1 else 0,
            halves_refs[2 * i], halves_refs[2 * i + 1],
        )
    mine, theirs = other_half(w_node_ref)
    theirs_ref[...] = dot(node_hidden, theirs, 1, 1).astype(BF16)
    mine_ref[...] = dot(node_hidden, mine, 1, 1)


def obs_kernel(keep_ref, got_ref, w_ref, mine_ref, theirs_ref):
    obs_hidden = (keep_ref[...].astype(F32) + got_ref[...].astype(F32)).astype(BF16)
    mine, theirs = other_half(w_ref)
    theirs_ref[...] = dot(obs_hidden, theirs, 1, 1).astype(BF16)
    mine_ref[...] = dot(obs_hidden, mine, 1, 1)


def add_kernel(step, tail, keep_ref, got_ref, next_ref, send_ref, total_ref):
    total = keep_ref[...].astype(F32) + got_ref[...].astype(F32)
    total_ref[...] = total.astype(total_ref.dtype)
    split_half(total_ref, 0, total_ref.shape[0] - tail, step, tail, next_ref, send_ref)


def last_kernel(keep_ref, got_ref, piece_ref, *slot_refs):
    total = keep_ref[...] + got_ref[...].astype(F32)
    rows = piece_ref.shape[0]
    piece_ref[...] = total[:rows].astype(BF16)
    for slot_ref in slot_refs:
        slot_ref[...] = total[rows : rows + slot_ref.shape[0]]


def join_kernel(step, mine_ref, got_ref, out_ref):
    rows = mine_ref.shape[0]
    bit = own_bit(step)
    out_ref[pl.ds(pl.multiple_of(bit * rows, SUBLANES), rows), :] = mine_ref[...]
    out_ref[pl.ds(pl.multiple_of((1 - bit) * rows, SUBLANES), rows), :] = got_ref[...]


def spread_kernel(step, bundles, *refs):
    low = own_bit(step) == 0
    joined = []
    for i in range(bundles):
        mine, got = refs[2 * i][...], refs[2 * i + 1][...]
        joined += [jnp.where(low, mine, got), jnp.where(low, got, mine)]
    half, hidden = joined[0].shape
    at = 0
    for out_ref in refs[2 * bundles :]:
        for c in range(out_ref.shape[1] // hidden):
            begin = 0
            while begin < out_ref.shape[0]:
                offset = at % half
                count = min(out_ref.shape[0] - begin, half - offset)
                out_ref[begin : begin + count, c * hidden : (c + 1) * hidden] = joined[at // half][
                    offset : offset + count
                ].astype(F32)
                at, begin = at + count, begin + count


def merge_kernel(node_ref, node_got_ref, obs_ref, obs_got_ref, grad_node_ref, grad_obs_ref):
    grad_node_ref[...] = node_ref[...] + node_got_ref[...].astype(F32)
    grad_obs_ref[...] = (obs_ref[...] + obs_got_ref[...].astype(F32)).astype(BF16)


def summing(steps, halved, tail, keep, got, after):
    hidden = keep.shape[1]
    for at, following in enumerate(steps[1:], 1):
        step = following if at < halved else None
        rows = keep.shape[0] - tail
        rows = (half_rows(rows) if step else rows) + tail
        keep, send = call(
            functools.partial(add_kernel, step, tail),
            [((rows, hidden), keep.dtype), ((rows, hidden), BF16)],
            keep, got,
            scratch=[pltpu.VMEM(keep.shape, keep.dtype)],
            after=after,
        )
        after[:] = [send]
        got = flip(send, following)
        yield
    return keep, got


def halving_used(steps, rows):
    used = []
    for step in steps[:-1]:
        if halves(rows):
            used.append(step)
            rows //= 2
    return used


def weight_chain(steps, rows, tail, slots, keep, got, after):
    used = halving_used(steps, rows)
    keep, got = yield from summing(steps, len(steps) - 1, tail, keep, got, after)
    piece, *sums = call(
        last_kernel,
        [((keep.shape[0] - tail, keep.shape[1]), BF16)]
        + ([((slots, keep.shape[1]), F32)] if tail else []),
        keep, got,
        after=after,
    )
    after[:] = [piece]
    got = flip(piece, used[-1])
    yield
    for step, following in zip(used[:0:-1], used[-2::-1]):
        (piece,) = call(
            functools.partial(join_kernel, step),
            [((2 * piece.shape[0], piece.shape[1]), BF16)],
            piece, got,
            after=after,
        )
        after[:] = [piece]
        got = flip(piece, following)
        yield
    return [piece, got], sums


def obs_chain(steps, w_obs, keep, got, after):
    keep, got = yield from summing(steps, len(steps), 0, keep, got, after)
    half = w_obs.shape[0] // 2
    obs_mine, obs_theirs = call(
        obs_kernel, [((keep.shape[0], half), F32), ((keep.shape[0], half), BF16)], keep, got, w_obs,
        after=after,
    )
    after[:] = [obs_theirs]
    obs_got = shift(obs_theirs, "mp", 1)
    yield
    return obs_mine, obs_got


def in_turns(chains, turns):
    results = {}
    for key in turns + [key for key in range(len(chains))]:
        try:
            next(chains[key])
        except StopIteration as stop:
            results[key] = stop.value
    return [results[key] for key in range(len(chains))]


def local(obs_feat, node_state, grad_agg, owner, local_idx, slot, w_obs, w_node, slot_bias, w_out):
    owners = lax.axis_size(OWNER_AXES)
    obs, fanout = owner.shape
    nodes, width = node_state.shape
    hidden = w_obs.shape[1]
    slots = slot_bias.shape[0]
    cap = max(2, 2 * obs * fanout // owners)
    cap = -(-cap // SUBLANES) * SUBLANES
    edges = owners * cap
    half = width // 2
    slot_row = slot.reshape(1, obs)

    steps = halving_steps()
    chunk = cap * half // obs + SUBLANES
    other, *packed = call_staged(
        functools.partial(pack_kernel, cap),
        [((chunk, obs), BF16)] * (owners + 1),
        obs_feat, owner.T, local_idx.T, slot_row,
    )
    received = [shift(packed[j], OWNER_AXES, j) for j in range(1, owners)]
    tail = -(-slots // SUBLANES) * SUBLANES
    table, state_held, agg_held, w_node_held, w_obs_held = call_staged(
        table_kernel,
        [((nodes + tail, 4 * hidden), BF16)],
        node_state, grad_agg, w_node, w_out, slot_bias,
        held=(node_state, grad_agg, w_node, w_obs),
    )
    (mine,) = call(
        join_blocks_kernel, [((owners - 1, chunk, obs), BF16)], *received,
        after=(w_obs_held,),
    )
    theirs = shift(mine, "mp", 1)
    act, hot, rows_mine, rows_theirs, obs_keep, obs_send = call(
        functools.partial(edge_kernel, fanout, nodes, steps),
        [((edges, 2 * hidden), BF16), ((edges, nodes + tail), BF16)]
        + [((edges, half), BF16)] * 2
        + [((owners * obs // 2, hidden), BF16)] * 2,
        packed[0], mine, other, theirs, table, w_obs_held,
        scratch=[pltpu.VMEM((owners * obs, hidden), BF16)],
    )

    stack = 2 * width + width // hidden * hidden
    bundles = BUNDLES
    rows = stack // bundles
    obs_got = flip(obs_send, steps[0])
    shapes = []
    for i in range(bundles):
        share = rows // 2 + (tail if i == bundles - 1 else 0)
        shapes += [((share, hidden), F32), ((share, hidden), BF16)]
    node_mine, node_theirs, *shares = call(
        functools.partial(weight_kernel, steps[0], bundles, tail),
        [((nodes, half), F32), ((nodes, half), BF16)] + shapes,
        hot, act, rows_mine, rows_theirs, state_held, agg_held, w_node_held,
        scratch=[pltpu.VMEM((stack + tail, hidden), F32)],
    )
    after = []
    got = [flip(send, steps[0]) for send in shares[1::2]]
    chains = [
        weight_chain(
            steps, rows, tail if i == bundles - 1 else 0, slots, shares[2 * i], got[i], after
        )
        for i in range(bundles)
    ]
    node_got = shift(node_theirs, "mp", 1)
    everyone = list(range(1, bundles + 1))
    turns = ([0] + everyone) * (len(steps) - 1) + everyone + [0] + everyone * (len(halving_used(steps, rows)) - 1)
    (obs_mine, obs_got), *weights = in_turns(
        [obs_chain(steps, w_obs_held, obs_keep, obs_got, after)] + chains, turns
    )
    grad_node, grad_obs = call(
        merge_kernel, [((nodes, half), F32), ((obs, half), BF16)],
        node_mine, node_got, obs_mine, obs_got,
    )
    ends = [end for pair, _ in weights for end in pair]
    (grad_slot,) = weights[-1][1]
    grad_w_node, grad_w_out, grad_w_obs = call(
        functools.partial(spread_kernel, steps[0], bundles),
        [((width, hidden), F32), ((hidden, width), F32), ((width, hidden), F32)],
        *ends,
        after=[pltpu.with_memory_space_constraint(grad_obs, pltpu.HBM)],
    )
    return grad_obs, grad_node, grad_w_obs, grad_w_node, grad_w_out, grad_slot


def solution(mesh):
    rows = P(("group", "obs", "node"), None)
    return jax.shard_map(
        local,
        mesh=mesh,
        in_specs=(
            rows, rows, rows, rows, rows,
            P(("group", "obs", "node")),
            P(None, "mp"), P(None, "mp"), P(None, "mp"), P("mp", None),
        ),
        out_specs=(
            P(("group", "obs", "node"), "mp"),
            P(("group", "obs", "node"), "mp"),
            P("group", "mp"),
            P("group", "mp"),
            P(("group", "mp"), None),
            P("group", "mp"),
        ),
        check_vma=False,
    )
```

```python
import functools

import jax
import jax.numpy as jnp
from jax import lax
from jax.experimental import pallas as pl
from jax.experimental.pallas import tpu as pltpu
from jax.sharding import PartitionSpec as P

OWNER_AXES = ("obs", "node")
SUBLANES = 16
BUNDLES = 2
BF16 = jnp.bfloat16
F32 = jnp.float32


def dot(left, right, left_dim=1, right_dim=0):
    return lax.dot_general(
        left, right, (((left_dim,), (right_dim,)), ((), ())), preferred_element_type=F32
    )


def iota(shape, dim):
    return lax.broadcasted_iota(jnp.int32, shape, dim)


def call(kernel, outs, *args, scratch=(), after=()):
    vmem = pl.BlockSpec(memory_space=pltpu.VMEM)
    count = len(args)
    specs = [vmem] * count + [pl.BlockSpec(memory_space=pl.ANY)] * len(after)
    args += tuple(after)
    return pl.pallas_call(
        lambda *refs: kernel(*refs[:count], *refs[len(args) :]),
        out_shape=[jax.ShapeDtypeStruct(shape, dtype) for shape, dtype in outs],
        in_specs=specs,
        out_specs=[vmem] * len(outs),
        scratch_shapes=list(scratch),
        compiler_params=pltpu.CompilerParams(vmem_limit_bytes=40 << 20),
    )(*args)


def call_staged(kernel, outs, *args, held=()):
    count = len(args)
    sources = list(args) + [a for a in held if not any(a is b for b in args)]
    kept = [next(i for i, b in enumerate(sources) if a is b) for a in held]
    rest = [i for i in range(len(sources)) if i not in kept]

    def staged(*refs):
        hbm, refs = refs[: len(sources)], refs[len(sources) :]
        out_refs, refs = refs[: len(outs)], refs[len(outs) :]
        buffers = dict(zip(kept, refs[: len(kept)])) | dict(zip(rest, refs[len(kept) : -1]))
        copies = [
            pltpu.make_async_copy(hbm[i], buffers[i], refs[-1].at[i]) for i in range(len(sources))
        ]
        for copy in copies:
            copy.start()
        for copy in copies:
            copy.wait()
        kernel(*[buffers[i] for i in range(count)], *out_refs)

    return pl.pallas_call(
        staged,
        out_shape=[jax.ShapeDtypeStruct(shape, dtype) for shape, dtype in outs]
        + [jax.ShapeDtypeStruct(a.shape, a.dtype) for a in held],
        in_specs=[pl.BlockSpec(memory_space=pltpu.HBM)] * len(sources),
        out_specs=[pl.BlockSpec(memory_space=pltpu.VMEM)] * (len(outs) + len(held)),
        scratch_shapes=[pltpu.VMEM(sources[i].shape, sources[i].dtype) for i in rest]
        + [pltpu.SemaphoreType.DMA((len(sources),))],
        compiler_params=pltpu.CompilerParams(vmem_limit_bytes=40 << 20),
    )(*[pltpu.with_memory_space_constraint(a, pltpu.HBM) for a in sources])


def exchange(blocks, axes):
    return lax.all_to_all(blocks, axes, split_axis=0, concat_axis=0, tiled=True)


def shift(value, axis, step):
    size = lax.axis_size(axis)
    return lax.ppermute(value, axis, [(i, (i + step) % size) for i in range(size)])


def other_half(ref):
    half = ref.shape[0] // 2
    me = lax.axis_index("mp")
    mine = ref[pl.ds(pl.multiple_of(me * half, half), half), :]
    theirs = ref[pl.ds(pl.multiple_of((1 - me) * half, half), half), :]
    return mine, theirs


def column_half(ref, which):
    half = ref.shape[1] // 2
    return ref[:, pl.ds(pl.multiple_of(which * half, 128), half)]


def pack_kernel(cap, obs_ref, owner_ref, index_ref, slot_ref, other_ref, *outs):
    owners = len(outs)
    chunk, lanes = outs[0].shape
    fanout, obs = owner_ref.shape
    owner, index = owner_ref[...], index_ref[...]
    hits = [iota((owners, obs), 0) == owner[k : k + 1] for k in range(fanout)]
    count = functools.reduce(jnp.add, [h.astype(F32) for h in hits])
    before = dot(count, (iota((obs, obs), 0) < iota((obs, obs), 1)).astype(F32))
    header = jnp.where(iota((SUBLANES, obs), 0) == 4 * fanout, slot_ref[...].astype(F32), 0.0)
    places = []
    for k in range(fanout):
        rank = jnp.sum(jnp.where(hits[k], before, 0.0), axis=0, keepdims=True)
        places.append(owner[k : k + 1] * cap + rank.astype(jnp.int32))
        plus = index[k : k + 1] + 1
        fields = (owner[k : k + 1].astype(F32), rank, (plus // 16).astype(F32), (plus % 16).astype(F32))
        for j, row in enumerate(fields):
            header = jnp.where(iota(header.shape, 0) == 4 * k + j, row, header)
    header = header.astype(BF16)
    me, core = lax.axis_index(OWNER_AXES), lax.axis_index("mp")
    mine, other = column_half(obs_ref, core), column_half(obs_ref, 1 - core)

    def write(ref, pick, rows):
        packed = dot(pick, rows).astype(BF16)
        for c in range(rows.shape[1] // lanes):
            ref[c * cap : (c + 1) * cap, :] = packed[:, c * lanes : (c + 1) * lanes]
        ref[chunk - SUBLANES :, :] = header

    for j, out_ref in enumerate(outs):
        slots = iota((cap, obs), 0) + lax.rem(me + j, owners) * cap
        pick = functools.reduce(jnp.logical_or, [slots == place for place in places]).astype(BF16)
        write(out_ref, pick, mine)
        if j == 0:
            write(other_ref, pick, other)


def table_kernel(state_ref, agg_ref, w_node_ref, w_out_ref, bias_ref, table_ref):
    hidden = w_node_ref.shape[1]
    nodes, slots = state_ref.shape[0], bias_ref.shape[0]
    table_ref[nodes:, :] = jnp.zeros((table_ref.shape[0] - nodes, table_ref.shape[1]), BF16)

    def put(begin, column, part):
        high = part.astype(BF16)
        table_ref[begin : begin + part.shape[0], column : column + hidden] = high
        table_ref[begin : begin + part.shape[0], column + hidden : column + 2 * hidden] = (
            part - high.astype(F32)
        ).astype(BF16)

    put(0, 0, dot(state_ref[...], w_node_ref[...]))
    put(0, 2 * hidden, dot(agg_ref[...], w_out_ref[...], 1, 1))
    put(nodes, 0, bias_ref[...])


def join_blocks_kernel(*refs):
    out_ref = refs[-1]
    for j, ref in enumerate(refs[:-1]):
        out_ref[j] = ref[...]


def edge_kernel(
    fanout, nodes, steps, own_ref, mine_ref, other_ref, theirs_ref, table_ref, w_obs_ref,
    act_ref, hot_ref, rows_mine_ref, rows_theirs_ref, keep_ref, send_ref, total_ref,
):
    owners = mine_ref.shape[0] + 1
    chunk, lanes = own_ref.shape
    half = w_obs_ref.shape[0] // 2
    hidden = w_obs_ref.shape[1]
    cap = (chunk - SUBLANES) * lanes // half
    me = lax.axis_index(OWNER_AXES)
    base = 1 << nodes.bit_length()
    columns = []
    picks = []
    for j in range(owners):
        block, other = (mine_ref.at[j - 1], theirs_ref.at[j - 1]) if j else (own_ref, other_ref)
        header = block[chunk - SUBLANES :, :].astype(F32)
        slot = header[4 * fanout : 4 * fanout + 1] * base
        code = jnp.zeros((cap, lanes), F32)
        pick = jnp.zeros((cap, lanes), jnp.bool_)
        for k in range(fanout):
            row = header[4 * k : 4 * k + 4]
            rank = jnp.where(row[0:1] == me.astype(F32), row[1:2], -1.0).astype(jnp.int32)
            hit = iota((cap, lanes), 0) == rank
            pick = pick | hit
            code = code + jnp.where(hit, row[2:3] * 16.0 + row[3:4] + slot, 0.0)
        picks.append(pick.astype(BF16))
        columns.append(jnp.sum(code, axis=1, keepdims=True).astype(jnp.int32))
        for c in range(half // lanes):
            rows = slice(j * cap, (j + 1) * cap)
            place = slice(c * lanes, (c + 1) * lanes)
            rows_mine_ref[rows, place] = block[c * cap : (c + 1) * cap, :]
            rows_theirs_ref[rows, place] = other[c * cap : (c + 1) * cap, :]
    code = jnp.concatenate(columns, axis=0)
    index, slot = (code & (base - 1)) - 1, (code >> (base.bit_length() - 1)) + nodes
    column = iota(hot_ref.shape, 1)
    hot = ((column == index) | ((column == slot) & (index >= 0))).astype(BF16)
    hot_ref[...] = hot
    rows = dot(hot, table_ref[...])
    w_mine, w_theirs = other_half(w_obs_ref)
    pre = dot(rows_mine_ref[...], w_mine) + dot(rows_theirs_ref[...], w_theirs)
    pre = pre + (rows[:, :hidden] + rows[:, hidden : 2 * hidden])
    g_z = rows[:, 2 * hidden : 3 * hidden] + rows[:, 3 * hidden :]
    sig = jax.nn.sigmoid(pre)
    g_a = (g_z * sig * (1.0 + pre * (1.0 - sig))).astype(BF16)
    act_ref[:, :hidden] = g_a
    act_ref[:, hidden:] = (pre * sig).astype(BF16)
    for j, pick in enumerate(picks):
        source = lax.rem(me - j + owners, owners)
        begin = pl.multiple_of(place_of(source, steps) * lanes, SUBLANES)
        total_ref[pl.ds(begin, lanes), :] = dot(pick, g_a[j * cap : (j + 1) * cap], 0, 0).astype(BF16)
    split_half(total_ref, 0, owners * lanes, steps[0], 0, keep_ref, send_ref)


def halving_steps():
    bits = [
        [(axis, k) for k in range(lax.axis_size(axis).bit_length() - 1)] for axis in ("node", "obs")
    ]
    steps = []
    for k in range(max(map(len, bits))):
        both = [line[k] for line in bits if k < len(line)]
        steps += [(both[0], both[-1])] + ([(both[1], both[0])] if len(both) > 1 else [])
    return steps


def flip(value, step):
    axes = ("obs", "node", "mp")
    sizes = [lax.axis_size(axis) for axis in axes]
    pairs = []
    for index in range(sizes[0] * sizes[1] * sizes[2]):
        place = [index // (sizes[1] * sizes[2]), index // sizes[2] % sizes[1], index % sizes[2]]
        axis, k = step[place[2] % 2]
        place[axes.index(axis)] ^= (2 << k) - 1
        pairs.append((index, (place[0] * sizes[1] + place[1]) * sizes[2] + place[2]))
    return lax.ppermute(value, axes, pairs)


def bit_of(step, node, obs):
    codes = {"node": node ^ (node >> 1), "obs": obs ^ (obs >> 1)}
    bits = [(codes[axis] >> k) & 1 for axis, k in step]
    return jnp.where(lax.axis_index("mp") % 2 == 0, bits[0], bits[1])


def own_bit(step):
    return bit_of(step, lax.axis_index("node"), lax.axis_index("obs"))


def place_of(owner, steps):
    shares = lax.axis_size("node")
    place = 0
    for step in steps:
        place = 2 * place + bit_of(step, lax.rem(owner, shares), lax.div(owner, shares))
    return place


def halves(rows):
    return rows % (2 * SUBLANES) == 0


def half_rows(rows):
    return rows // 2 if halves(rows) else rows


def split_half(total_ref, start, rows, step, tail, keep_ref, send_ref):
    end = start + rows
    half = half_rows(rows) if step else rows
    if half < rows:
        bit = own_bit(step)
        kept, sent = [pl.ds(pl.multiple_of(start + b * half, SUBLANES), half) for b in (bit, 1 - bit)]
        keep_ref[:half, :] = total_ref[kept, :]
        send_ref[:half, :] = total_ref[sent, :].astype(BF16)
    else:
        both = total_ref[start:end, :].astype(BF16)
        keep_ref[:half, :] = both.astype(keep_ref.dtype)
        send_ref[:half, :] = both
    if tail:
        both = total_ref[end : end + tail, :].astype(BF16)
        keep_ref[half:, :] = both.astype(keep_ref.dtype)
        send_ref[half:, :] = both


def weight_kernel(
    step, bundles, tail, hot_ref, act_ref, rows_mine_ref, rows_theirs_ref, state_ref, agg_ref, w_node_ref,
    mine_ref, theirs_ref, *refs
):
    halves_refs, total_ref = refs[:-1], refs[-1]
    width, hidden = w_node_ref.shape
    nodes = state_ref.shape[0]
    sums = dot(hot_ref[...], act_ref[...], 0, 0)
    by_node = sums[:nodes].astype(BF16)
    node_hidden, z_sum = by_node[:, :hidden], by_node[:, hidden:]
    total_ref[:width, :] = dot(state_ref[...], node_hidden, 0, 0)
    begin = width
    for c in range(width // hidden):
        total_ref[begin : begin + hidden, :] = dot(
            z_sum, agg_ref[:, c * hidden : (c + 1) * hidden], 0, 0
        )
        begin += hidden
    g_a = act_ref[:, :hidden]
    core, half = lax.axis_index("mp"), width // 2
    for which, ref in ((core, rows_mine_ref), (1 - core, rows_theirs_ref)):
        total_ref[pl.ds(pl.multiple_of(begin + which * half, SUBLANES), half), :] = dot(ref[...], g_a, 0, 0)
    begin += width
    total_ref[begin:, :] = sums[nodes:, :hidden]
    rows = begin // bundles
    for i in range(bundles):
        split_half(
            total_ref, i * rows, rows, step, tail if i == bundles - 1 else 0,
            halves_refs[2 * i], halves_refs[2 * i + 1],
        )
    mine, theirs = other_half(w_node_ref)
    theirs_ref[...] = dot(node_hidden, theirs, 1, 1).astype(BF16)
    mine_ref[...] = dot(node_hidden, mine, 1, 1)


def obs_kernel(keep_ref, got_ref, w_ref, mine_ref, theirs_ref):
    got = got_ref[got_ref.shape[0] - keep_ref.shape[0] :, :]
    obs_hidden = (keep_ref[...].astype(F32) + got.astype(F32)).astype(BF16)
    mine, theirs = other_half(w_ref)
    theirs_ref[...] = dot(obs_hidden, theirs, 1, 1).astype(BF16)
    mine_ref[...] = dot(obs_hidden, mine, 1, 1)


def add_kernel(step, tail, keep_ref, got_ref, next_ref, send_ref, total_ref):
    total = keep_ref[...].astype(F32) + got_ref[...].astype(F32)
    total_ref[...] = total.astype(total_ref.dtype)
    split_half(total_ref, 0, total_ref.shape[0] - tail, step, tail, next_ref, send_ref)


def add_with_rows_kernel(
    step, tail, keep_ref, got_ref, rows_ref, rows_got_ref, next_ref, send_ref, rows_next_ref, total_ref, rows_total_ref
):
    share = next_ref.shape[0]
    total_ref[...] = keep_ref[...] + got_ref[...].astype(F32)
    split_half(total_ref, 0, share - tail, None, tail, next_ref, send_ref.at[:share])
    rows_total_ref[...] = (rows_ref[...].astype(F32) + rows_got_ref[...].astype(F32)).astype(BF16)
    split_half(
        rows_total_ref, 0, rows_total_ref.shape[0], step, 0, rows_next_ref, send_ref.at[share:]
    )


def last_kernel(keep_ref, got_ref, piece_ref, *slot_refs):
    total = keep_ref[...] + got_ref[: keep_ref.shape[0], :].astype(F32)
    rows = piece_ref.shape[0]
    piece_ref[...] = total[:rows].astype(BF16)
    for slot_ref in slot_refs:
        slot_ref[...] = total[rows : rows + slot_ref.shape[0]]


def join_kernel(step, mine_ref, got_ref, out_ref):
    rows = mine_ref.shape[0]
    bit = own_bit(step)
    out_ref[pl.ds(pl.multiple_of(bit * rows, SUBLANES), rows), :] = mine_ref[...]
    out_ref[pl.ds(pl.multiple_of((1 - bit) * rows, SUBLANES), rows), :] = got_ref[...]


def spread_kernel(step, bundles, *refs):
    low = own_bit(step) == 0
    joined = []
    for i in range(bundles):
        mine, got = refs[2 * i][...], refs[2 * i + 1][...]
        joined += [jnp.where(low, mine, got), jnp.where(low, got, mine)]
    half, hidden = joined[0].shape
    at = 0
    for out_ref in refs[2 * bundles :]:
        for c in range(out_ref.shape[1] // hidden):
            begin = 0
            while begin < out_ref.shape[0]:
                offset = at % half
                count = min(out_ref.shape[0] - begin, half - offset)
                out_ref[begin : begin + count, c * hidden : (c + 1) * hidden] = joined[at // half][
                    offset : offset + count
                ].astype(F32)
                at, begin = at + count, begin + count


def merge_kernel(node_ref, node_got_ref, obs_ref, obs_got_ref, grad_node_ref, grad_obs_ref):
    grad_node_ref[...] = node_ref[...] + node_got_ref[...].astype(F32)
    grad_obs_ref[...] = (obs_ref[...] + obs_got_ref[...].astype(F32)).astype(BF16)


def summing(steps, halved, tail, keep, got, after):
    hidden = keep.shape[1]
    for at, following in enumerate(steps[1:], 1):
        step = following if at < halved else None
        rows = keep.shape[0] - tail
        rows = (half_rows(rows) if step else rows) + tail
        keep, send = call(
            functools.partial(add_kernel, step, tail),
            [((rows, hidden), keep.dtype), ((rows, hidden), BF16)],
            keep, got,
            scratch=[pltpu.VMEM(keep.shape, keep.dtype)],
            after=after,
        )
        after[:] = [send]
        got = flip(send, following)
        yield
    return keep, got


def halving_used(steps, rows):
    used = []
    for step in steps[:-1]:
        if halves(rows):
            used.append(step)
            rows //= 2
    return used


def weight_chain(steps, rows, tail, slots, keep, got, after, returned=None):
    used = halving_used(steps, rows)
    keep, got = yield from summing(steps[:-1], len(steps) - 1, tail, keep, got, after)
    if returned:
        rows_keep, rows_got = returned
        shape = (half_rows(rows_keep.shape[0]), keep.shape[1])
        keep, send, rows_keep = call(
            functools.partial(add_with_rows_kernel, steps[-1], tail),
            [(keep.shape, F32), ((keep.shape[0] + shape[0], shape[1]), BF16), (shape, BF16)],
            keep, got, rows_keep, rows_got,
            scratch=[pltpu.VMEM(keep.shape, F32), pltpu.VMEM(rows_keep.shape, BF16)],
            after=after,
        )
    else:
        keep, send = call(
            functools.partial(add_kernel, None, tail),
            [(keep.shape, F32), (keep.shape, BF16)],
            keep, got,
            scratch=[pltpu.VMEM(keep.shape, F32)],
            after=after,
        )
    after[:] = [send]
    arrived = got = flip(send, steps[-1])
    yield
    piece, *sums = call(
        last_kernel,
        [((keep.shape[0] - tail, keep.shape[1]), BF16)]
        + ([((slots, keep.shape[1]), F32)] if tail else []),
        keep, got,
        after=after,
    )
    after[:] = [piece]
    got = flip(piece, used[-1])
    yield
    for step, following in zip(used[:0:-1], used[-2::-1]):
        (piece,) = call(
            functools.partial(join_kernel, step),
            [((2 * piece.shape[0], piece.shape[1]), BF16)],
            piece, got,
            after=after,
        )
        after[:] = [piece]
        got = flip(piece, following)
        yield
    return [piece, got], sums, (rows_keep, arrived) if returned else ()


def rows_chain(steps, keep, got, after, out):
    out += yield from summing(steps[:-1], len(steps), 0, keep, got, after)


def in_turns(chains, turns):
    results = {}
    for key in turns + list(range(len(chains))):
        try:
            next(chains[key])
        except StopIteration as stop:
            results.setdefault(key, stop.value)
    return [results[key] for key in range(len(chains))]


def local(obs_feat, node_state, grad_agg, owner, local_idx, slot, w_obs, w_node, slot_bias, w_out):
    owners = lax.axis_size(OWNER_AXES)
    obs, fanout = owner.shape
    nodes, width = node_state.shape
    hidden = w_obs.shape[1]
    slots = slot_bias.shape[0]
    cap = max(2, 2 * obs * fanout // owners)
    cap = -(-cap // SUBLANES) * SUBLANES
    edges = owners * cap
    half = width // 2
    slot_row = slot.reshape(1, obs)

    steps = halving_steps()
    chunk = cap * half // obs + SUBLANES
    other, *packed = call_staged(
        functools.partial(pack_kernel, cap),
        [((chunk, obs), BF16)] * (owners + 1),
        obs_feat, owner.T, local_idx.T, slot_row,
    )
    received = [shift(packed[j], OWNER_AXES, j) for j in range(1, owners)]
    tail = -(-slots // SUBLANES) * SUBLANES
    table, state_held, agg_held, w_node_held, w_obs_held = call_staged(
        table_kernel,
        [((nodes + tail, 4 * hidden), BF16)],
        node_state, grad_agg, w_node, w_out, slot_bias,
        held=(node_state, grad_agg, w_node, w_obs),
    )
    (mine,) = call(
        join_blocks_kernel, [((owners - 1, chunk, obs), BF16)], *received,
        after=(w_obs_held,),
    )
    theirs = shift(mine, "mp", 1)
    act, hot, rows_mine, rows_theirs, obs_keep, obs_send = call(
        functools.partial(edge_kernel, fanout, nodes, steps),
        [((edges, 2 * hidden), BF16), ((edges, nodes + tail), BF16)]
        + [((edges, half), BF16)] * 2
        + [((owners * obs // 2, hidden), BF16)] * 2,
        packed[0], mine, other, theirs, table, w_obs_held,
        scratch=[pltpu.VMEM((owners * obs, hidden), BF16)],
    )

    stack = 2 * width + width // hidden * hidden
    bundles = BUNDLES
    rows = stack // bundles
    obs_got = flip(obs_send, steps[0])
    shapes = []
    for i in range(bundles):
        share = rows // 2 + (tail if i == bundles - 1 else 0)
        shapes += [((share, hidden), F32), ((share, hidden), BF16)]
    node_mine, node_theirs, *shares = call(
        functools.partial(weight_kernel, steps[0], bundles, tail),
        [((nodes, half), F32), ((nodes, half), BF16)] + shapes,
        hot, act, rows_mine, rows_theirs, state_held, agg_held, w_node_held,
        scratch=[pltpu.VMEM((stack + tail, hidden), F32)],
    )
    after = []
    returned = []
    chains = [rows_chain(steps, obs_keep, obs_got, after, returned)]
    got = [flip(send, steps[0]) for send in shares[1::2]]
    for i in range(bundles):
        last = i == bundles - 1
        chains.append(
            weight_chain(
                steps, rows, tail if last else 0, slots, shares[2 * i], got[i], after, returned if last else None
            )
        )
    node_got = shift(node_theirs, "mp", 1)
    everyone = list(range(len(chains)))
    turns = everyone * (len(steps) - 2) + [0] + everyone[1:] * (2 + len(halving_used(steps, rows)) - 1)
    _, *weights = in_turns(chains, turns)
    obs_keep, arrived = weights[-1][2]
    obs_mine, obs_theirs = call(
        obs_kernel, [((obs, half), F32), ((obs, half), BF16)], obs_keep, arrived, w_obs_held
    )
    grad_node, grad_obs = call(
        merge_kernel, [((nodes, half), F32), ((obs, half), BF16)],
        node_mine, node_got, obs_mine, shift(obs_theirs, "mp", 1),
    )
    ends = [end for pair, *_ in weights for end in pair]
    (grad_slot,) = weights[-1][1]
    grad_w_node, grad_w_out, grad_w_obs = call(
        functools.partial(spread_kernel, steps[0], bundles),
        [((width, hidden), F32), ((hidden, width), F32), ((width, hidden), F32)],
        *ends,
        after=[pltpu.with_memory_space_constraint(grad_obs, pltpu.HBM)],
    )
    return grad_obs, grad_node, grad_w_obs, grad_w_node, grad_w_out, grad_slot


def solution(mesh):
    rows = P(("group", "obs", "node"), None)
    return jax.shard_map(
        local,
        mesh=mesh,
        in_specs=(
            rows, rows, rows, rows, rows,
            P(("group", "obs", "node")),
            P(None, "mp"), P(None, "mp"), P(None, "mp"), P("mp", None),
        ),
        out_specs=(
            P(("group", "obs", "node"), "mp"),
            P(("group", "obs", "node"), "mp"),
            P("group", "mp"),
            P("group", "mp"),
            P(("group", "mp"), None),
            P("group", "mp"),
        ),
        check_vma=False,
    )
```

```python
import functools

import jax
import jax.numpy as jnp
from jax import lax
from jax.experimental import pallas as pl
from jax.experimental.pallas import tpu as pltpu
from jax.sharding import PartitionSpec as P

OWNER_AXES = ("obs", "node")
SUBLANES = 16
BUNDLES = 2
BF16 = jnp.bfloat16
F32 = jnp.float32


def dot(left, right, left_dim=1, right_dim=0):
    return lax.dot_general(
        left, right, (((left_dim,), (right_dim,)), ((), ())), preferred_element_type=F32
    )


def iota(shape, dim):
    return lax.broadcasted_iota(jnp.int32, shape, dim)


def call(kernel, outs, *args, scratch=(), after=()):
    vmem = pl.BlockSpec(memory_space=pltpu.VMEM)
    count = len(args)
    specs = [vmem] * count + [pl.BlockSpec(memory_space=pl.ANY)] * len(after)
    args += tuple(after)
    return pl.pallas_call(
        lambda *refs: kernel(*refs[:count], *refs[len(args) :]),
        out_shape=[jax.ShapeDtypeStruct(shape, dtype) for shape, dtype in outs],
        in_specs=specs,
        out_specs=[vmem] * len(outs),
        scratch_shapes=list(scratch),
        compiler_params=pltpu.CompilerParams(vmem_limit_bytes=40 << 20),
    )(*args)


def call_staged(kernel, outs, *args, held=()):
    count = len(args)
    sources = list(args) + [a for a in held if not any(a is b for b in args)]
    kept = [next(i for i, b in enumerate(sources) if a is b) for a in held]
    rest = [i for i in range(len(sources)) if i not in kept]

    def staged(*refs):
        hbm, refs = refs[: len(sources)], refs[len(sources) :]
        out_refs, refs = refs[: len(outs)], refs[len(outs) :]
        buffers = dict(zip(kept, refs[: len(kept)])) | dict(zip(rest, refs[len(kept) : -1]))
        copies = [
            pltpu.make_async_copy(hbm[i], buffers[i], refs[-1].at[i]) for i in range(len(sources))
        ]
        for copy in copies:
            copy.start()
        for copy in copies:
            copy.wait()
        kernel(*[buffers[i] for i in range(count)], *out_refs)

    return pl.pallas_call(
        staged,
        out_shape=[jax.ShapeDtypeStruct(shape, dtype) for shape, dtype in outs]
        + [jax.ShapeDtypeStruct(a.shape, a.dtype) for a in held],
        in_specs=[pl.BlockSpec(memory_space=pltpu.HBM)] * len(sources),
        out_specs=[pl.BlockSpec(memory_space=pltpu.VMEM)] * (len(outs) + len(held)),
        scratch_shapes=[pltpu.VMEM(sources[i].shape, sources[i].dtype) for i in rest]
        + [pltpu.SemaphoreType.DMA((len(sources),))],
        compiler_params=pltpu.CompilerParams(vmem_limit_bytes=40 << 20),
    )(*[pltpu.with_memory_space_constraint(a, pltpu.HBM) for a in sources])


def exchange(blocks, axes):
    return lax.all_to_all(blocks, axes, split_axis=0, concat_axis=0, tiled=True)


def shift(value, axis, step):
    size = lax.axis_size(axis)
    return lax.ppermute(value, axis, [(i, (i + step) % size) for i in range(size)])


def other_half(ref):
    half = ref.shape[0] // 2
    me = lax.axis_index("mp")
    mine = ref[pl.ds(pl.multiple_of(me * half, half), half), :]
    theirs = ref[pl.ds(pl.multiple_of((1 - me) * half, half), half), :]
    return mine, theirs


def column_half(ref, which):
    half = ref.shape[1] // 2
    return ref[:, pl.ds(pl.multiple_of(which * half, 128), half)]


def pack_kernel(cap, obs_ref, owner_ref, index_ref, slot_ref, other_ref, *outs):
    owners = len(outs)
    chunk, lanes = outs[0].shape
    fanout, obs = owner_ref.shape
    owner, index = owner_ref[...], index_ref[...]
    hits = [iota((owners, obs), 0) == owner[k : k + 1] for k in range(fanout)]
    count = functools.reduce(jnp.add, [h.astype(F32) for h in hits])
    before = dot(count, (iota((obs, obs), 0) < iota((obs, obs), 1)).astype(F32))
    header = jnp.where(iota((SUBLANES, obs), 0) == 4 * fanout, slot_ref[...].astype(F32), 0.0)
    places = []
    for k in range(fanout):
        rank = jnp.sum(jnp.where(hits[k], before, 0.0), axis=0, keepdims=True)
        places.append(owner[k : k + 1] * cap + rank.astype(jnp.int32))
        plus = index[k : k + 1] + 1
        fields = (owner[k : k + 1].astype(F32), rank, (plus // 16).astype(F32), (plus % 16).astype(F32))
        for j, row in enumerate(fields):
            header = jnp.where(iota(header.shape, 0) == 4 * k + j, row, header)
    header = header.astype(BF16)
    me, core = lax.axis_index(OWNER_AXES), lax.axis_index("mp")
    mine, other = column_half(obs_ref, core), column_half(obs_ref, 1 - core)

    def write(ref, pick, rows):
        packed = dot(pick, rows).astype(BF16)
        for c in range(rows.shape[1] // lanes):
            ref[c * cap : (c + 1) * cap, :] = packed[:, c * lanes : (c + 1) * lanes]
        ref[chunk - SUBLANES :, :] = header

    for j, out_ref in enumerate(outs):
        slots = iota((cap, obs), 0) + lax.rem(me + j, owners) * cap
        pick = functools.reduce(jnp.logical_or, [slots == place for place in places]).astype(BF16)
        write(out_ref, pick, mine)
        if j == 0:
            write(other_ref, pick, other)


def table_kernel(state_ref, agg_ref, w_node_ref, w_out_ref, bias_ref, table_ref):
    hidden = w_node_ref.shape[1]
    nodes, slots = state_ref.shape[0], bias_ref.shape[0]
    table_ref[nodes:, :] = jnp.zeros((table_ref.shape[0] - nodes, table_ref.shape[1]), BF16)

    def put(begin, column, part):
        high = part.astype(BF16)
        table_ref[begin : begin + part.shape[0], column : column + hidden] = high
        table_ref[begin : begin + part.shape[0], column + hidden : column + 2 * hidden] = (
            part - high.astype(F32)
        ).astype(BF16)

    put(0, 0, dot(state_ref[...], w_node_ref[...]))
    put(0, 2 * hidden, dot(agg_ref[...], w_out_ref[...], 1, 1))
    put(nodes, 0, bias_ref[...])


def join_blocks_kernel(*refs):
    out_ref = refs[-1]
    for j, ref in enumerate(refs[:-1]):
        out_ref[j] = ref[...]


def edge_kernel(
    fanout, nodes, steps, own_ref, mine_ref, other_ref, theirs_ref, table_ref, w_obs_ref,
    act_ref, hot_ref, rows_mine_ref, rows_theirs_ref, keep_ref, send_ref, pick_ref, total_ref, packed_ref, picks_ref,
):
    owners = mine_ref.shape[0] + 1
    chunk, lanes = own_ref.shape
    half = w_obs_ref.shape[0] // 2
    hidden = w_obs_ref.shape[1]
    cap = (chunk - SUBLANES) * lanes // half
    me = lax.axis_index(OWNER_AXES)
    base = 1 << nodes.bit_length()
    partner = partner_of(steps[0]).astype(F32)
    columns = []
    picks = []
    places = []
    for j in range(owners):
        block, other = (mine_ref.at[j - 1], theirs_ref.at[j - 1]) if j else (own_ref, other_ref)
        header = block[chunk - SUBLANES :, :].astype(F32)
        slot = header[4 * fanout : 4 * fanout + 1] * base
        code = jnp.zeros((cap, lanes), F32)
        pick = partner_pick = jnp.zeros((cap, lanes), jnp.bool_)
        for k in range(fanout):
            row = header[4 * k : 4 * k + 4]
            rank = jnp.where(row[0:1] == me.astype(F32), row[1:2], -1.0).astype(jnp.int32)
            hit = iota((cap, lanes), 0) == rank
            pick = pick | hit
            rank = jnp.where(row[0:1] == partner, row[1:2], -1.0).astype(jnp.int32)
            partner_pick = partner_pick | (iota((cap, lanes), 0) == rank)
            code = code + jnp.where(hit, row[2:3] * 16.0 + row[3:4] + slot, 0.0)
        picks.append(pick.astype(BF16))
        places.append(place_of(lax.rem(me - j + owners, owners), steps))
        begin = pl.multiple_of(places[j] * cap, SUBLANES)
        picks_ref[pl.ds(begin, cap), :] = partner_pick.astype(BF16)
        columns.append(jnp.sum(code, axis=1, keepdims=True).astype(jnp.int32))
        for c in range(half // lanes):
            rows = slice(j * cap, (j + 1) * cap)
            place = slice(c * lanes, (c + 1) * lanes)
            rows_mine_ref[rows, place] = block[c * cap : (c + 1) * cap, :]
            rows_theirs_ref[rows, place] = other[c * cap : (c + 1) * cap, :]
    code = jnp.concatenate(columns, axis=0)
    index, slot = (code & (base - 1)) - 1, (code >> (base.bit_length() - 1)) + nodes
    column = iota(hot_ref.shape, 1)
    hot = ((column == index) | ((column == slot) & (index >= 0))).astype(BF16)
    hot_ref[...] = hot
    rows = dot(hot, table_ref[...])
    w_mine, w_theirs = other_half(w_obs_ref)
    pre = dot(rows_mine_ref[...], w_mine) + dot(rows_theirs_ref[...], w_theirs)
    pre = pre + (rows[:, :hidden] + rows[:, hidden : 2 * hidden])
    g_z = rows[:, 2 * hidden : 3 * hidden] + rows[:, 3 * hidden :]
    sig = jax.nn.sigmoid(pre)
    g_a = (g_z * sig * (1.0 + pre * (1.0 - sig))).astype(BF16)
    act_ref[:, :hidden] = g_a
    act_ref[:, hidden:] = (pre * sig).astype(BF16)
    for j, pick in enumerate(picks):
        rows = g_a[j * cap : (j + 1) * cap]
        begin = pl.multiple_of(places[j] * lanes, SUBLANES)
        total_ref[pl.ds(begin, lanes), :] = dot(pick, rows, 0, 0).astype(BF16)
        packed_ref[pl.ds(pl.multiple_of(places[j] * cap, SUBLANES), cap), :] = rows
    bit = own_bit(steps[0])
    for out_ref, ref, which in (
        (keep_ref, total_ref, bit), (send_ref, packed_ref, 1 - bit), (pick_ref, picks_ref, bit)
    ):
        count = out_ref.shape[0]
        out_ref[...] = ref[pl.ds(pl.multiple_of(which * count, SUBLANES), count), :]


def halving_steps():
    bits = [
        [(axis, k) for k in range(lax.axis_size(axis).bit_length() - 1)] for axis in ("node", "obs")
    ]
    steps = []
    for k in range(max(map(len, bits))):
        both = [line[k] for line in bits if k < len(line)]
        steps += [(both[0], both[-1])] + ([(both[1], both[0])] if len(both) > 1 else [])
    return steps


def flip(value, step):
    axes = ("obs", "node", "mp")
    sizes = [lax.axis_size(axis) for axis in axes]
    pairs = []
    for index in range(sizes[0] * sizes[1] * sizes[2]):
        place = [index // (sizes[1] * sizes[2]), index // sizes[2] % sizes[1], index % sizes[2]]
        axis, k = step[place[2] % 2]
        place[axes.index(axis)] ^= (2 << k) - 1
        pairs.append((index, (place[0] * sizes[1] + place[1]) * sizes[2] + place[2]))
    return lax.ppermute(value, axes, pairs)


def bit_of(step, node, obs):
    codes = {"node": node ^ (node >> 1), "obs": obs ^ (obs >> 1)}
    bits = [(codes[axis] >> k) & 1 for axis, k in step]
    return jnp.where(lax.axis_index("mp") % 2 == 0, bits[0], bits[1])


def own_bit(step):
    return bit_of(step, lax.axis_index("node"), lax.axis_index("obs"))


def partner_of(step):
    node, obs, shares = lax.axis_index("node"), lax.axis_index("obs"), lax.axis_size("node")
    owners = []
    for axis, k in step:
        mask = (2 << k) - 1
        owners.append(obs * shares + (node ^ mask) if axis == "node" else (obs ^ mask) * shares + node)
    return jnp.where(lax.axis_index("mp") % 2 == 0, owners[0], owners[1])


def place_of(owner, steps):
    shares = lax.axis_size("node")
    place = 0
    for step in steps:
        place = 2 * place + bit_of(step, lax.rem(owner, shares), lax.div(owner, shares))
    return place


def halves(rows):
    return rows % (2 * SUBLANES) == 0


def half_rows(rows):
    return rows // 2 if halves(rows) else rows


def split_half(total_ref, start, rows, step, tail, keep_ref, send_ref):
    end = start + rows
    half = half_rows(rows) if step else rows
    if half < rows:
        bit = own_bit(step)
        kept, sent = [pl.ds(pl.multiple_of(start + b * half, SUBLANES), half) for b in (bit, 1 - bit)]
        keep_ref[:half, :] = total_ref[kept, :]
        send_ref[:half, :] = total_ref[sent, :].astype(BF16)
    else:
        both = total_ref[start:end, :].astype(BF16)
        keep_ref[:half, :] = both.astype(keep_ref.dtype)
        send_ref[:half, :] = both
    if tail:
        both = total_ref[end : end + tail, :].astype(BF16)
        keep_ref[half:, :] = both.astype(keep_ref.dtype)
        send_ref[half:, :] = both


def weight_kernel(
    step, bundles, tail, hot_ref, act_ref, rows_mine_ref, rows_theirs_ref, state_ref, agg_ref, w_node_ref,
    mine_ref, theirs_ref, *refs
):
    halves_refs, total_ref = refs[:-1], refs[-1]
    width, hidden = w_node_ref.shape
    nodes = state_ref.shape[0]
    sums = dot(hot_ref[...], act_ref[...], 0, 0)
    by_node = sums[:nodes].astype(BF16)
    node_hidden, z_sum = by_node[:, :hidden], by_node[:, hidden:]
    total_ref[:width, :] = dot(state_ref[...], node_hidden, 0, 0)
    begin = width
    for c in range(width // hidden):
        total_ref[begin : begin + hidden, :] = dot(
            z_sum, agg_ref[:, c * hidden : (c + 1) * hidden], 0, 0
        )
        begin += hidden
    g_a = act_ref[:, :hidden]
    core, half = lax.axis_index("mp"), width // 2
    for which, ref in ((core, rows_mine_ref), (1 - core, rows_theirs_ref)):
        total_ref[pl.ds(pl.multiple_of(begin + which * half, SUBLANES), half), :] = dot(ref[...], g_a, 0, 0)
    begin += width
    total_ref[begin:, :] = sums[nodes:, :hidden]
    rows = begin // bundles
    for i in range(bundles):
        split_half(
            total_ref, i * rows, rows, step, tail if i == bundles - 1 else 0,
            halves_refs[2 * i], halves_refs[2 * i + 1],
        )
    mine, theirs = other_half(w_node_ref)
    theirs_ref[...] = dot(node_hidden, theirs, 1, 1).astype(BF16)
    mine_ref[...] = dot(node_hidden, mine, 1, 1)


def obs_kernel(keep_ref, got_ref, w_ref, mine_ref, theirs_ref):
    got = got_ref[got_ref.shape[0] - keep_ref.shape[0] :, :]
    obs_hidden = (keep_ref[...].astype(F32) + got.astype(F32)).astype(BF16)
    mine, theirs = other_half(w_ref)
    theirs_ref[...] = dot(obs_hidden, theirs, 1, 1).astype(BF16)
    mine_ref[...] = dot(obs_hidden, mine, 1, 1)


def add_kernel(step, tail, keep_ref, got_ref, next_ref, send_ref, total_ref):
    total = keep_ref[...].astype(F32) + got_ref[...].astype(F32)
    total_ref[...] = total.astype(total_ref.dtype)
    split_half(total_ref, 0, total_ref.shape[0] - tail, step, tail, next_ref, send_ref)


def unpack_kernel(step, keep_ref, got_ref, pick_ref, next_ref, send_ref, total_ref):
    obs = pick_ref.shape[1]
    blocks = keep_ref.shape[0] // obs
    cap = got_ref.shape[0] // blocks
    for i in range(blocks):
        edges, rows = slice(i * cap, (i + 1) * cap), slice(i * obs, (i + 1) * obs)
        total = keep_ref[rows, :].astype(F32) + dot(pick_ref[edges, :], got_ref[edges, :], 0, 0)
        total_ref[rows, :] = total.astype(BF16)
    split_half(total_ref, 0, total_ref.shape[0], step, 0, next_ref, send_ref)


def add_with_rows_kernel(
    step, tail, keep_ref, got_ref, rows_ref, rows_got_ref, next_ref, send_ref, rows_next_ref, total_ref, rows_total_ref
):
    share = next_ref.shape[0]
    total_ref[...] = keep_ref[...] + got_ref[...].astype(F32)
    split_half(total_ref, 0, share - tail, None, tail, next_ref, send_ref.at[:share])
    rows_total_ref[...] = (rows_ref[...].astype(F32) + rows_got_ref[...].astype(F32)).astype(BF16)
    split_half(
        rows_total_ref, 0, rows_total_ref.shape[0], step, 0, rows_next_ref, send_ref.at[share:]
    )


def last_kernel(keep_ref, got_ref, piece_ref, *slot_refs):
    total = keep_ref[...] + got_ref[: keep_ref.shape[0], :].astype(F32)
    rows = piece_ref.shape[0]
    piece_ref[...] = total[:rows].astype(BF16)
    for slot_ref in slot_refs:
        slot_ref[...] = total[rows : rows + slot_ref.shape[0]]


def join_kernel(step, mine_ref, got_ref, out_ref):
    rows = mine_ref.shape[0]
    bit = own_bit(step)
    out_ref[pl.ds(pl.multiple_of(bit * rows, SUBLANES), rows), :] = mine_ref[...]
    out_ref[pl.ds(pl.multiple_of((1 - bit) * rows, SUBLANES), rows), :] = got_ref[...]


def spread_kernel(step, bundles, *refs):
    low = own_bit(step) == 0
    joined = []
    for i in range(bundles):
        mine, got = refs[2 * i][...], refs[2 * i + 1][...]
        joined += [jnp.where(low, mine, got), jnp.where(low, got, mine)]
    half, hidden = joined[0].shape
    at = 0
    for out_ref in refs[2 * bundles :]:
        for c in range(out_ref.shape[1] // hidden):
            begin = 0
            while begin < out_ref.shape[0]:
                offset = at % half
                count = min(out_ref.shape[0] - begin, half - offset)
                out_ref[begin : begin + count, c * hidden : (c + 1) * hidden] = joined[at // half][
                    offset : offset + count
                ].astype(F32)
                at, begin = at + count, begin + count


def merge_kernel(
    node_ref, node_got_ref, obs_ref, obs_got_ref, slot_ref, grad_node_ref, grad_obs_ref, grad_slot_ref
):
    grad_slot_ref[...] = slot_ref[...]
    grad_node_ref[...] = node_ref[...] + node_got_ref[...].astype(F32)
    grad_obs_ref[...] = (obs_ref[...] + obs_got_ref[...].astype(F32)).astype(BF16)


def summing(steps, halved, tail, keep, got, after):
    hidden = keep.shape[1]
    for at, following in enumerate(steps[1:], 1):
        step = following if at < halved else None
        rows = keep.shape[0] - tail
        rows = (half_rows(rows) if step else rows) + tail
        keep, send = call(
            functools.partial(add_kernel, step, tail),
            [((rows, hidden), keep.dtype), ((rows, hidden), BF16)],
            keep, got,
            scratch=[pltpu.VMEM(keep.shape, keep.dtype)],
            after=after,
        )
        after[:] = [send]
        got = flip(send, following)
        yield
    return keep, got


def halving_used(steps, rows):
    used = []
    for step in steps[:-1]:
        if halves(rows):
            used.append(step)
            rows //= 2
    return used


def weight_chain(steps, rows, tail, slots, keep, got, after, returned=None):
    used = halving_used(steps, rows)
    keep, got = yield from summing(steps[:-1], len(steps) - 1, tail, keep, got, after)
    if returned:
        rows_keep, rows_got = returned
        shape = (half_rows(rows_keep.shape[0]), keep.shape[1])
        keep, send, rows_keep = call(
            functools.partial(add_with_rows_kernel, steps[-1], tail),
            [(keep.shape, F32), ((keep.shape[0] + shape[0], shape[1]), BF16), (shape, BF16)],
            keep, got, rows_keep, rows_got,
            scratch=[pltpu.VMEM(keep.shape, F32), pltpu.VMEM(rows_keep.shape, BF16)],
            after=after,
        )
    else:
        keep, send = call(
            functools.partial(add_kernel, None, tail),
            [(keep.shape, F32), (keep.shape, BF16)],
            keep, got,
            scratch=[pltpu.VMEM(keep.shape, F32)],
            after=after,
        )
    after[:] = [send]
    arrived = got = flip(send, steps[-1])
    yield
    piece, *sums = call(
        last_kernel,
        [((keep.shape[0] - tail, keep.shape[1]), BF16)]
        + ([((slots, keep.shape[1]), F32)] if tail else []),
        keep, got,
        after=after,
    )
    after[:] = [piece]
    got = flip(piece, used[-1])
    yield
    for step, following in zip(used[:0:-1], used[-2::-1]):
        (piece,) = call(
            functools.partial(join_kernel, step),
            [((2 * piece.shape[0], piece.shape[1]), BF16)],
            piece, got,
            after=after,
        )
        after[:] = [piece]
        got = flip(piece, following)
        yield
    return [piece, got], sums, (rows_keep, arrived) if returned else ()


def rows_chain(steps, keep, got, pick, after, out):
    shape = (half_rows(keep.shape[0]), keep.shape[1])
    keep, send = call(
        functools.partial(unpack_kernel, steps[1]),
        [(shape, BF16)] * 2,
        keep, got, pick,
        scratch=[pltpu.VMEM(keep.shape, BF16)],
        after=after,
    )
    after[:] = [send]
    got = flip(send, steps[1])
    yield
    out += yield from summing(steps[1:-1], len(steps), 0, keep, got, after)


def in_turns(chains, turns):
    results = {}
    for key in turns + list(range(len(chains))):
        try:
            next(chains[key])
        except StopIteration as stop:
            results.setdefault(key, stop.value)
    return [results[key] for key in range(len(chains))]


def local(obs_feat, node_state, grad_agg, owner, local_idx, slot, w_obs, w_node, slot_bias, w_out):
    owners = lax.axis_size(OWNER_AXES)
    obs, fanout = owner.shape
    nodes, width = node_state.shape
    hidden = w_obs.shape[1]
    slots = slot_bias.shape[0]
    cap = max(2, 2 * obs * fanout // owners)
    cap = -(-cap // SUBLANES) * SUBLANES
    edges = owners * cap
    half = width // 2
    slot_row = slot.reshape(1, obs)

    steps = halving_steps()
    chunk = cap * half // obs + SUBLANES
    other, *packed = call_staged(
        functools.partial(pack_kernel, cap),
        [((chunk, obs), BF16)] * (owners + 1),
        obs_feat, owner.T, local_idx.T, slot_row,
    )
    received = [shift(packed[j], OWNER_AXES, j) for j in range(1, owners)]
    tail = -(-slots // SUBLANES) * SUBLANES
    table, state_held, agg_held, w_node_held, w_obs_held = call_staged(
        table_kernel,
        [((nodes + tail, 4 * hidden), BF16)],
        node_state, grad_agg, w_node, w_out, slot_bias,
        held=(node_state, grad_agg, w_node, w_obs),
    )
    (mine,) = call(
        join_blocks_kernel, [((owners - 1, chunk, obs), BF16)], *received,
        after=(w_obs_held,),
    )
    theirs = shift(mine, "mp", 1)
    act, hot, rows_mine, rows_theirs, obs_keep, obs_send, obs_pick = call(
        functools.partial(edge_kernel, fanout, nodes, steps),
        [((edges, 2 * hidden), BF16), ((edges, nodes + tail), BF16)]
        + [((edges, half), BF16)] * 2
        + [((owners * obs // 2, hidden), BF16), ((edges // 2, hidden), BF16), ((edges // 2, obs), BF16)],
        packed[0], mine, other, theirs, table, w_obs_held,
        scratch=[
            pltpu.VMEM((owners * obs, hidden), BF16),
            pltpu.VMEM((edges, hidden), BF16),
            pltpu.VMEM((edges, obs), BF16),
        ],
    )

    stack = 2 * width + width // hidden * hidden
    bundles = BUNDLES
    rows = stack // bundles
    obs_got = flip(obs_send, steps[0])
    shapes = []
    for i in range(bundles):
        share = rows // 2 + (tail if i == bundles - 1 else 0)
        shapes += [((share, hidden), F32), ((share, hidden), BF16)]
    node_mine, node_theirs, *shares = call(
        functools.partial(weight_kernel, steps[0], bundles, tail),
        [((nodes, half), F32), ((nodes, half), BF16)] + shapes,
        hot, act, rows_mine, rows_theirs, state_held, agg_held, w_node_held,
        scratch=[pltpu.VMEM((stack + tail, hidden), F32)],
    )
    after = []
    returned = []
    chains = [rows_chain(steps, obs_keep, obs_got, obs_pick, after, returned)]
    got = [flip(send, steps[0]) for send in shares[1::2]]
    for i in range(bundles):
        last = i == bundles - 1
        chains.append(
            weight_chain(
                steps, rows, tail if last else 0, slots, shares[2 * i], got[i], after, returned if last else None
            )
        )
    node_got = shift(node_theirs, "mp", 1)
    everyone = list(range(len(chains)))
    turns = everyone * (len(steps) - 2) + [0] + everyone[1:] * (2 + len(halving_used(steps, rows)) - 1)
    _, *weights = in_turns(chains, turns)
    obs_keep, arrived = weights[-1][2]
    obs_mine, obs_theirs = call(
        obs_kernel, [((obs, half), F32), ((obs, half), BF16)], obs_keep, arrived, w_obs_held
    )
    (slot_sums,) = weights[-1][1]
    grad_node, grad_obs, grad_slot = call(
        merge_kernel, [((nodes, half), F32), ((obs, half), BF16), ((slots, hidden), F32)],
        node_mine, node_got, obs_mine, shift(obs_theirs, "mp", 1), slot_sums,
    )
    ends = [end for pair, *_ in weights for end in pair]
    grad_w_node, grad_w_out, grad_w_obs = call(
        functools.partial(spread_kernel, steps[0], bundles),
        [((width, hidden), F32), ((hidden, width), F32), ((width, hidden), F32)],
        *ends,
        after=[pltpu.with_memory_space_constraint(grad_obs, pltpu.HBM)],
    )
    return grad_obs, grad_node, grad_w_obs, grad_w_node, grad_w_out, grad_slot


def solution(mesh):
    rows = P(("group", "obs", "node"), None)
    return jax.shard_map(
        local,
        mesh=mesh,
        in_specs=(
            rows, rows, rows, rows, rows,
            P(("group", "obs", "node")),
            P(None, "mp"), P(None, "mp"), P(None, "mp"), P("mp", None),
        ),
        out_specs=(
            P(("group", "obs", "node"), "mp"),
            P(("group", "obs", "node"), "mp"),
            P("group", "mp"),
            P("group", "mp"),
            P(("group", "mp"), None),
            P("group", "mp"),
        ),
        check_vma=False,
    )
```

```python
import functools

import jax
import jax.numpy as jnp
from jax import lax
from jax.experimental import pallas as pl
from jax.experimental.pallas import tpu as pltpu
from jax.sharding import PartitionSpec as P

OWNER_AXES = ("obs", "node")
SUBLANES = 16
PARTS = 2
BF16 = jnp.bfloat16
F32 = jnp.float32


def dot(left, right, left_dim=1, right_dim=0):
    return lax.dot_general(
        left, right, (((left_dim,), (right_dim,)), ((), ())), preferred_element_type=F32
    )


def iota(shape, dim):
    return lax.broadcasted_iota(jnp.int32, shape, dim)


def call(kernel, outs, *args, scratch=(), after=()):
    vmem = pl.BlockSpec(memory_space=pltpu.VMEM)
    count = len(args)
    specs = [vmem] * count + [pl.BlockSpec(memory_space=pl.ANY)] * len(after)
    args += tuple(after)
    return pl.pallas_call(
        lambda *refs: kernel(*refs[:count], *refs[len(args) :]),
        out_shape=[jax.ShapeDtypeStruct(shape, dtype) for shape, dtype in outs],
        in_specs=specs,
        out_specs=[vmem] * len(outs),
        scratch_shapes=list(scratch),
        compiler_params=pltpu.CompilerParams(vmem_limit_bytes=40 << 20),
    )(*args)


def call_staged(kernel, outs, *args, held=()):
    count = len(args)
    sources = list(args) + [a for a in held if not any(a is b for b in args)]
    kept = [next(i for i, b in enumerate(sources) if a is b) for a in held]
    rest = [i for i in range(len(sources)) if i not in kept]

    def staged(*refs):
        hbm, refs = refs[: len(sources)], refs[len(sources) :]
        out_refs, refs = refs[: len(outs)], refs[len(outs) :]
        buffers = dict(zip(kept, refs[: len(kept)])) | dict(zip(rest, refs[len(kept) : -1]))
        copies = [
            pltpu.make_async_copy(hbm[i], buffers[i], refs[-1].at[i]) for i in range(len(sources))
        ]
        for copy in copies:
            copy.start()
        for copy in copies:
            copy.wait()
        kernel(*[buffers[i] for i in range(count)], *out_refs)

    return pl.pallas_call(
        staged,
        out_shape=[jax.ShapeDtypeStruct(shape, dtype) for shape, dtype in outs]
        + [jax.ShapeDtypeStruct(a.shape, a.dtype) for a in held],
        in_specs=[pl.BlockSpec(memory_space=pltpu.HBM)] * len(sources),
        out_specs=[pl.BlockSpec(memory_space=pltpu.VMEM)] * (len(outs) + len(held)),
        scratch_shapes=[pltpu.VMEM(sources[i].shape, sources[i].dtype) for i in rest]
        + [pltpu.SemaphoreType.DMA((len(sources),))],
        compiler_params=pltpu.CompilerParams(vmem_limit_bytes=40 << 20),
    )(*[pltpu.with_memory_space_constraint(a, pltpu.HBM) for a in sources])


def exchange(blocks, axes):
    return lax.all_to_all(blocks, axes, split_axis=0, concat_axis=0, tiled=True)


def shift(value, axis, step):
    size = lax.axis_size(axis)
    return lax.ppermute(value, axis, [(i, (i + step) % size) for i in range(size)])


def other_half(ref):
    half = ref.shape[0] // 2
    me = lax.axis_index("mp")
    mine = ref[pl.ds(pl.multiple_of(me * half, half), half), :]
    theirs = ref[pl.ds(pl.multiple_of((1 - me) * half, half), half), :]
    return mine, theirs


def column_half(ref, which):
    half = ref.shape[1] // 2
    return ref[:, pl.ds(pl.multiple_of(which * half, 128), half)]


def pack_kernel(cap, obs_ref, owner_ref, index_ref, slot_ref, other_ref, *outs):
    owners = len(outs)
    chunk, lanes = outs[0].shape
    fanout, obs = owner_ref.shape
    owner, index = owner_ref[...], index_ref[...]
    hits = [iota((owners, obs), 0) == owner[k : k + 1] for k in range(fanout)]
    count = functools.reduce(jnp.add, [h.astype(F32) for h in hits])
    before = dot(count, (iota((obs, obs), 0) < iota((obs, obs), 1)).astype(F32))
    header = jnp.where(iota((SUBLANES, obs), 0) == 4 * fanout, slot_ref[...].astype(F32), 0.0)
    places = []
    for k in range(fanout):
        rank = jnp.sum(jnp.where(hits[k], before, 0.0), axis=0, keepdims=True)
        places.append(owner[k : k + 1] * cap + rank.astype(jnp.int32))
        plus = index[k : k + 1] + 1
        fields = (owner[k : k + 1].astype(F32), rank, (plus // 16).astype(F32), (plus % 16).astype(F32))
        for j, row in enumerate(fields):
            header = jnp.where(iota(header.shape, 0) == 4 * k + j, row, header)
    header = header.astype(BF16)
    me, core = lax.axis_index(OWNER_AXES), lax.axis_index("mp")
    mine, other = column_half(obs_ref, core), column_half(obs_ref, 1 - core)

    def write(ref, pick, rows):
        packed = dot(pick, rows).astype(BF16)
        for c in range(rows.shape[1] // lanes):
            ref[c * cap : (c + 1) * cap, :] = packed[:, c * lanes : (c + 1) * lanes]
        ref[chunk - SUBLANES :, :] = header

    for j, out_ref in enumerate(outs):
        slots = iota((cap, obs), 0) + lax.rem(me + j, owners) * cap
        pick = functools.reduce(jnp.logical_or, [slots == place for place in places]).astype(BF16)
        write(out_ref, pick, mine)
        if j == 0:
            write(other_ref, pick, other)


def table_kernel(state_ref, agg_ref, w_node_ref, w_out_ref, bias_ref, table_ref):
    hidden = w_node_ref.shape[1]
    nodes, slots = state_ref.shape[0], bias_ref.shape[0]
    table_ref[nodes:, :] = jnp.zeros((table_ref.shape[0] - nodes, table_ref.shape[1]), BF16)

    def put(begin, column, part):
        high = part.astype(BF16)
        table_ref[begin : begin + part.shape[0], column : column + hidden] = high
        table_ref[begin : begin + part.shape[0], column + hidden : column + 2 * hidden] = (
            part - high.astype(F32)
        ).astype(BF16)

    put(0, 0, dot(state_ref[...], w_node_ref[...]))
    put(0, 2 * hidden, dot(agg_ref[...], w_out_ref[...], 1, 1))
    put(nodes, 0, bias_ref[...])


def join_blocks_kernel(*refs):
    out_ref = refs[-1]
    for j, ref in enumerate(refs[:-1]):
        out_ref[j] = ref[...]


def edge_kernel(
    fanout, nodes, steps, own_ref, mine_ref, other_ref, theirs_ref, table_ref, w_obs_ref,
    act_ref, hot_ref, rows_mine_ref, rows_theirs_ref, keep_ref, send_ref, pick_ref, total_ref, packed_ref, picks_ref,
):
    owners = mine_ref.shape[0] + 1
    chunk, lanes = own_ref.shape
    half = w_obs_ref.shape[0] // 2
    hidden = w_obs_ref.shape[1]
    cap = (chunk - SUBLANES) * lanes // half
    me = lax.axis_index(OWNER_AXES)
    base = 1 << nodes.bit_length()
    partner = partner_of(steps[0]).astype(F32)
    columns = []
    picks = []
    places = []
    for j in range(owners):
        block, other = (mine_ref.at[j - 1], theirs_ref.at[j - 1]) if j else (own_ref, other_ref)
        header = block[chunk - SUBLANES :, :].astype(F32)
        slot = header[4 * fanout : 4 * fanout + 1] * base
        code = jnp.zeros((cap, lanes), F32)
        pick = partner_pick = jnp.zeros((cap, lanes), jnp.bool_)
        for k in range(fanout):
            row = header[4 * k : 4 * k + 4]
            rank = jnp.where(row[0:1] == me.astype(F32), row[1:2], -1.0).astype(jnp.int32)
            hit = iota((cap, lanes), 0) == rank
            pick = pick | hit
            rank = jnp.where(row[0:1] == partner, row[1:2], -1.0).astype(jnp.int32)
            partner_pick = partner_pick | (iota((cap, lanes), 0) == rank)
            code = code + jnp.where(hit, row[2:3] * 16.0 + row[3:4] + slot, 0.0)
        picks.append(pick.astype(BF16))
        places.append(place_of(lax.rem(me - j + owners, owners), steps))
        begin = pl.multiple_of(places[j] * cap, SUBLANES)
        picks_ref[pl.ds(begin, cap), :] = partner_pick.astype(BF16)
        columns.append(jnp.sum(code, axis=1, keepdims=True).astype(jnp.int32))
        for c in range(half // lanes):
            rows = slice(j * cap, (j + 1) * cap)
            place = slice(c * lanes, (c + 1) * lanes)
            rows_mine_ref[rows, place] = block[c * cap : (c + 1) * cap, :]
            rows_theirs_ref[rows, place] = other[c * cap : (c + 1) * cap, :]
    code = jnp.concatenate(columns, axis=0)
    index, slot = (code & (base - 1)) - 1, (code >> (base.bit_length() - 1)) + nodes
    column = iota(hot_ref.shape, 1)
    hot = ((column == index) | ((column == slot) & (index >= 0))).astype(BF16)
    hot_ref[...] = hot
    rows = dot(hot, table_ref[...])
    w_mine, w_theirs = other_half(w_obs_ref)
    pre = dot(rows_mine_ref[...], w_mine) + dot(rows_theirs_ref[...], w_theirs)
    pre = pre + (rows[:, :hidden] + rows[:, hidden : 2 * hidden])
    g_z = rows[:, 2 * hidden : 3 * hidden] + rows[:, 3 * hidden :]
    sig = jax.nn.sigmoid(pre)
    g_a = (g_z * sig * (1.0 + pre * (1.0 - sig))).astype(BF16)
    act_ref[:, :hidden] = g_a
    act_ref[:, hidden:] = (pre * sig).astype(BF16)
    for j, pick in enumerate(picks):
        rows = g_a[j * cap : (j + 1) * cap]
        begin = pl.multiple_of(places[j] * lanes, SUBLANES)
        total_ref[pl.ds(begin, lanes), :] = dot(pick, rows, 0, 0).astype(BF16)
        packed_ref[pl.ds(pl.multiple_of(places[j] * cap, SUBLANES), cap), :] = rows
    bit = own_bit(steps[0])
    for out_ref, ref, which in (
        (keep_ref, total_ref, bit), (send_ref, packed_ref, 1 - bit), (pick_ref, picks_ref, bit)
    ):
        count = out_ref.shape[0]
        out_ref[...] = ref[pl.ds(pl.multiple_of(which * count, SUBLANES), count), :]


def halving_steps():
    bits = [
        [(axis, k) for k in range(lax.axis_size(axis).bit_length() - 1)] for axis in ("node", "obs")
    ]
    steps = []
    for k in range(max(map(len, bits))):
        both = [line[k] for line in bits if k < len(line)]
        steps += [(both[0], both[-1])] + ([(both[1], both[0])] if len(both) > 1 else [])
    return steps


def flip(value, step):
    axes = ("obs", "node", "mp")
    sizes = [lax.axis_size(axis) for axis in axes]
    pairs = []
    for index in range(sizes[0] * sizes[1] * sizes[2]):
        place = [index // (sizes[1] * sizes[2]), index // sizes[2] % sizes[1], index % sizes[2]]
        axis, k = step[place[2] % 2]
        place[axes.index(axis)] ^= (2 << k) - 1
        pairs.append((index, (place[0] * sizes[1] + place[1]) * sizes[2] + place[2]))
    return lax.ppermute(value, axes, pairs)


def bit_of(step, node, obs):
    codes = {"node": node ^ (node >> 1), "obs": obs ^ (obs >> 1)}
    bits = [(codes[axis] >> k) & 1 for axis, k in step]
    return jnp.where(lax.axis_index("mp") % 2 == 0, bits[0], bits[1])


def own_bit(step):
    return bit_of(step, lax.axis_index("node"), lax.axis_index("obs"))


def partner_of(step):
    node, obs, shares = lax.axis_index("node"), lax.axis_index("obs"), lax.axis_size("node")
    owners = []
    for axis, k in step:
        mask = (2 << k) - 1
        owners.append(obs * shares + (node ^ mask) if axis == "node" else (obs ^ mask) * shares + node)
    return jnp.where(lax.axis_index("mp") % 2 == 0, owners[0], owners[1])


def place_of(owner, steps):
    shares = lax.axis_size("node")
    place = 0
    for step in steps:
        place = 2 * place + bit_of(step, lax.rem(owner, shares), lax.div(owner, shares))
    return place


def halves(rows):
    return rows % (2 * SUBLANES) == 0


def half_rows(rows):
    return rows // 2 if halves(rows) else rows


def split_half(total_ref, start, rows, step, tail, keep_ref, send_ref):
    end = start + rows
    half = half_rows(rows) if step else rows
    if half < rows:
        bit = own_bit(step)
        kept, sent = [pl.ds(pl.multiple_of(start + b * half, SUBLANES), half) for b in (bit, 1 - bit)]
        keep_ref[:half, :] = total_ref[kept, :]
        send_ref[:half, :] = total_ref[sent, :].astype(BF16)
    else:
        both = total_ref[start:end, :].astype(BF16)
        keep_ref[:half, :] = both.astype(keep_ref.dtype)
        send_ref[:half, :] = both
    if tail:
        both = total_ref[end : end + tail, :].astype(BF16)
        keep_ref[half:, :] = both.astype(keep_ref.dtype)
        send_ref[half:, :] = both


def weight_kernel(
    step, tail, hot_ref, act_ref, rows_mine_ref, rows_theirs_ref, state_ref, agg_ref, w_node_ref,
    mine_ref, theirs_ref, keep_ref, send_ref, total_ref,
):
    width, hidden = w_node_ref.shape
    nodes = state_ref.shape[0]
    sums = dot(hot_ref[...], act_ref[...], 0, 0)
    by_node = sums[:nodes].astype(BF16)
    node_hidden, z_sum = by_node[:, :hidden], by_node[:, hidden:]
    total_ref[:width, :] = dot(state_ref[...], node_hidden, 0, 0)
    begin = width
    for c in range(width // hidden):
        total_ref[begin : begin + hidden, :] = dot(
            z_sum, agg_ref[:, c * hidden : (c + 1) * hidden], 0, 0
        )
        begin += hidden
    g_a = act_ref[:, :hidden]
    core, half = lax.axis_index("mp"), width // 2
    for which, ref in ((core, rows_mine_ref), (1 - core, rows_theirs_ref)):
        total_ref[pl.ds(pl.multiple_of(begin + which * half, SUBLANES), half), :] = dot(ref[...], g_a, 0, 0)
    begin += width
    total_ref[begin:, :] = sums[nodes:, :hidden]
    split_half(total_ref, 0, begin, step, tail, keep_ref, send_ref)
    mine, theirs = other_half(w_node_ref)
    theirs_ref[...] = dot(node_hidden, theirs, 1, 1).astype(BF16)
    mine_ref[...] = dot(node_hidden, mine, 1, 1)


def obs_kernel(keep_ref, got_ref, w_ref, mine_ref, theirs_ref):
    got = got_ref[got_ref.shape[0] - keep_ref.shape[0] :, :]
    obs_hidden = (keep_ref[...].astype(F32) + got.astype(F32)).astype(BF16)
    mine, theirs = other_half(w_ref)
    theirs_ref[...] = dot(obs_hidden, theirs, 1, 1).astype(BF16)
    mine_ref[...] = dot(obs_hidden, mine, 1, 1)


def add_kernel(step, tail, keep_ref, got_ref, next_ref, send_ref, total_ref):
    total = keep_ref[...].astype(F32) + got_ref[...].astype(F32)
    total_ref[...] = total.astype(total_ref.dtype)
    split_half(total_ref, 0, total_ref.shape[0] - tail, step, tail, next_ref, send_ref)


def unpack_kernel(step, keep_ref, got_ref, pick_ref, next_ref, send_ref, total_ref):
    obs = pick_ref.shape[1]
    blocks = keep_ref.shape[0] // obs
    cap = got_ref.shape[0] // blocks
    for i in range(blocks):
        edges, rows = slice(i * cap, (i + 1) * cap), slice(i * obs, (i + 1) * obs)
        total = keep_ref[rows, :].astype(F32) + dot(pick_ref[edges, :], got_ref[edges, :], 0, 0)
        total_ref[rows, :] = total.astype(BF16)
    split_half(total_ref, 0, total_ref.shape[0], step, 0, next_ref, send_ref)


def middle_kernel(step, tail, parts, keep_ref, got_ref, rows_ref, rows_got_ref, rows_next_ref, *refs):
    part_refs, (total_ref, rows_total_ref) = refs[: 2 * parts], refs[2 * parts :]
    total_ref[...] = keep_ref[...] + got_ref[...].astype(F32)
    rows = total_ref.shape[0] - tail
    part = rows // parts
    for i in range(parts):
        keep_ref, send_ref = part_refs[2 * i : 2 * i + 2]
        both = total_ref[i * part : (i + 1) * part, :].astype(BF16)
        keep_ref[:part, :] = both.astype(F32)
        send_ref[:part, :] = both
    both = total_ref[rows:, :].astype(BF16)
    part_refs[0][part:, :] = both.astype(F32)
    part_refs[1][part : part + tail, :] = both
    rows_total_ref[...] = (rows_ref[...].astype(F32) + rows_got_ref[...].astype(F32)).astype(BF16)
    split_half(
        rows_total_ref, 0, rows_total_ref.shape[0], step, 0, rows_next_ref, part_refs[1].at[part + tail :]
    )


def last_kernel(keep_ref, got_ref, piece_ref, *slot_refs):
    total = keep_ref[...] + got_ref[: keep_ref.shape[0], :].astype(F32)
    rows = piece_ref.shape[0]
    piece_ref[...] = total[:rows].astype(BF16)
    for slot_ref in slot_refs:
        slot_ref[...] = total[rows : rows + slot_ref.shape[0]]


def join_kernel(step, mine_ref, got_ref, out_ref):
    rows = mine_ref.shape[0]
    bit = own_bit(step)
    out_ref[pl.ds(pl.multiple_of(bit * rows, SUBLANES), rows), :] = mine_ref[...]
    out_ref[pl.ds(pl.multiple_of((1 - bit) * rows, SUBLANES), rows), :] = got_ref[...]


def spread_kernel(step, parts, piece, *refs):
    low = own_bit(step) == 0
    joined = []
    for i in range(parts):
        mine, got = refs[2 * i][...], refs[2 * i + 1][...]
        joined.append([jnp.where(low, mine, got), jnp.where(low, got, mine)])
    half, hidden = joined[0][0].shape
    share = piece // parts
    at = 0
    for out_ref in refs[2 * parts :]:
        for c in range(out_ref.shape[1] // hidden):
            begin = 0
            while begin < out_ref.shape[0]:
                number, offset = divmod(at, share)
                count = min(out_ref.shape[0] - begin, share - offset)
                place, part = divmod(number, parts)
                upper, row = divmod(place * share, half)
                out_ref[begin : begin + count, c * hidden : (c + 1) * hidden] = joined[part][upper][
                    row + offset : row + offset + count
                ].astype(F32)
                at, begin = at + count, begin + count


def merge_kernel(
    node_ref, node_got_ref, obs_ref, obs_got_ref, slot_ref, grad_node_ref, grad_obs_ref, grad_slot_ref
):
    grad_slot_ref[...] = slot_ref[...]
    grad_node_ref[...] = node_ref[...] + node_got_ref[...].astype(F32)
    grad_obs_ref[...] = (obs_ref[...] + obs_got_ref[...].astype(F32)).astype(BF16)


def summing(steps, halved, tail, keep, got, after):
    hidden = keep.shape[1]
    for at, following in enumerate(steps[1:], 1):
        step = following if at < halved else None
        rows = keep.shape[0] - tail
        rows = (half_rows(rows) if step else rows) + tail
        keep, send = call(
            functools.partial(add_kernel, step, tail),
            [((rows, hidden), keep.dtype), ((rows, hidden), BF16)],
            keep, got,
            scratch=[pltpu.VMEM(keep.shape, keep.dtype)],
            after=after,
        )
        after[:] = [send]
        got = flip(send, following)
        yield
    return keep, got


def halving_used(steps, rows):
    used = []
    for step in steps[:-1]:
        if halves(rows):
            used.append(step)
            rows //= 2
    return used


def sum_chain(steps, tail, keep, got, after, out):
    out += yield from summing(steps[:-1], len(steps) - 1, tail, keep, got, after)


def gather_chain(used, rows, slots, keep, got, after):
    hidden = keep.shape[1]
    piece, *sums = call(
        last_kernel,
        [((rows, hidden), BF16)] + ([((slots, hidden), F32)] if keep.shape[0] > rows else []),
        keep, got,
        after=after,
    )
    after[:] = [piece]
    got = flip(piece, used[-1])
    yield
    for step, following in zip(used[:0:-1], used[-2::-1]):
        (piece,) = call(
            functools.partial(join_kernel, step),
            [((2 * piece.shape[0], hidden), BF16)],
            piece, got,
            after=after,
        )
        after[:] = [piece]
        got = flip(piece, following)
        yield
    return [piece, got], sums


def rows_chain(steps, keep, got, pick, after, out):
    shape = (half_rows(keep.shape[0]), keep.shape[1])
    keep, send = call(
        functools.partial(unpack_kernel, steps[1]),
        [(shape, BF16)] * 2,
        keep, got, pick,
        scratch=[pltpu.VMEM(keep.shape, BF16)],
        after=after,
    )
    after[:] = [send]
    got = flip(send, steps[1])
    yield
    out += yield from summing(steps[1:-1], len(steps), 0, keep, got, after)


def in_turns(chains, turns):
    results = {}
    for key in turns + list(range(len(chains))):
        try:
            next(chains[key])
        except StopIteration as stop:
            results.setdefault(key, stop.value)
    return [results[key] for key in range(len(chains))]


def local(obs_feat, node_state, grad_agg, owner, local_idx, slot, w_obs, w_node, slot_bias, w_out):
    owners = lax.axis_size(OWNER_AXES)
    obs, fanout = owner.shape
    nodes, width = node_state.shape
    hidden = w_obs.shape[1]
    slots = slot_bias.shape[0]
    cap = max(2, 2 * obs * fanout // owners)
    cap = -(-cap // SUBLANES) * SUBLANES
    edges = owners * cap
    half = width // 2
    slot_row = slot.reshape(1, obs)

    steps = halving_steps()
    chunk = cap * half // obs + SUBLANES
    other, *packed = call_staged(
        functools.partial(pack_kernel, cap),
        [((chunk, obs), BF16)] * (owners + 1),
        obs_feat, owner.T, local_idx.T, slot_row,
    )
    received = [shift(packed[j], OWNER_AXES, j) for j in range(1, owners)]
    tail = -(-slots // SUBLANES) * SUBLANES
    table, state_held, agg_held, w_node_held, w_obs_held = call_staged(
        table_kernel,
        [((nodes + tail, 4 * hidden), BF16)],
        node_state, grad_agg, w_node, w_out, slot_bias,
        held=(node_state, grad_agg, w_node, w_obs),
    )
    (mine,) = call(
        join_blocks_kernel, [((owners - 1, chunk, obs), BF16)], *received,
        after=(w_obs_held,),
    )
    theirs = shift(mine, "mp", 1)
    act, hot, rows_mine, rows_theirs, obs_keep, obs_send, obs_pick = call(
        functools.partial(edge_kernel, fanout, nodes, steps),
        [((edges, 2 * hidden), BF16), ((edges, nodes + tail), BF16)]
        + [((edges, half), BF16)] * 2
        + [((owners * obs // 2, hidden), BF16), ((edges // 2, hidden), BF16), ((edges // 2, obs), BF16)],
        packed[0], mine, other, theirs, table, w_obs_held,
        scratch=[
            pltpu.VMEM((owners * obs, hidden), BF16),
            pltpu.VMEM((edges, hidden), BF16),
            pltpu.VMEM((edges, obs), BF16),
        ],
    )

    stack = 2 * width + width // hidden * hidden
    obs_got = flip(obs_send, steps[0])
    share = half_rows(stack) + tail
    node_mine, node_theirs, keep, send = call(
        functools.partial(weight_kernel, steps[0], tail),
        [((nodes, half), F32), ((nodes, half), BF16), ((share, hidden), F32), ((share, hidden), BF16)],
        hot, act, rows_mine, rows_theirs, state_held, agg_held, w_node_held,
        scratch=[pltpu.VMEM((stack + tail, hidden), F32)],
    )
    node_got = shift(node_theirs, "mp", 1)
    after, summed, returned = [], [], []
    in_turns(
        [
            sum_chain(steps, tail, keep, flip(send, steps[0]), after, summed),
            rows_chain(steps, obs_keep, obs_got, obs_pick, after, returned),
        ],
        [0, 1] * (len(steps) - 2),
    )

    used = halving_used(steps, stack)
    piece = stack >> len(used)
    parts = PARTS if piece % (PARTS * SUBLANES) == 0 else 1
    shares = [piece // parts + (0 if i else tail) for i in range(parts)]
    shapes = []
    for i, share in enumerate(shares):
        shapes += [((share, hidden), F32), ((share + (0 if i else obs), hidden), BF16)]
    obs_keep, *pieces = call(
        functools.partial(middle_kernel, steps[-1], tail, parts),
        [((obs, hidden), BF16)] + shapes,
        *summed, *returned,
        scratch=[pltpu.VMEM(summed[0].shape, F32), pltpu.VMEM(returned[0].shape, BF16)],
        after=after,
    )
    after[:] = []
    arrived = [flip(send, steps[-1]) for send in pieces[1::2]]
    weights = in_turns(
        [gather_chain(used, piece // parts, slots, pieces[2 * i], arrived[i], after) for i in range(parts)],
        list(range(parts)) * len(used),
    )
    obs_mine, obs_theirs = call(
        obs_kernel, [((obs, half), F32), ((obs, half), BF16)], obs_keep, arrived[0], w_obs_held
    )
    (slot_sums,) = weights[0][1]
    grad_node, grad_obs, grad_slot = call(
        merge_kernel, [((nodes, half), F32), ((obs, half), BF16), ((slots, hidden), F32)],
        node_mine, node_got, obs_mine, shift(obs_theirs, "mp", 1), slot_sums,
    )
    ends = [end for pair, _ in weights for end in pair]
    grad_w_node, grad_w_out, grad_w_obs = call(
        functools.partial(spread_kernel, steps[0], parts, piece),
        [((width, hidden), F32), ((hidden, width), F32), ((width, hidden), F32)],
        *ends,
        after=[pltpu.with_memory_space_constraint(grad_obs, pltpu.HBM)],
    )
    return grad_obs, grad_node, grad_w_obs, grad_w_node, grad_w_out, grad_slot


def solution(mesh):
    rows = P(("group", "obs", "node"), None)
    return jax.shard_map(
        local,
        mesh=mesh,
        in_specs=(
            rows, rows, rows, rows, rows,
            P(("group", "obs", "node")),
            P(None, "mp"), P(None, "mp"), P(None, "mp"), P("mp", None),
        ),
        out_specs=(
            P(("group", "obs", "node"), "mp"),
            P(("group", "obs", "node"), "mp"),
            P("group", "mp"),
            P("group", "mp"),
            P(("group", "mp"), None),
            P("group", "mp"),
        ),
        check_vma=False,
    )
```

```python
import functools

import jax
import jax.numpy as jnp
from jax import lax
from jax.experimental import pallas as pl
from jax.experimental.pallas import tpu as pltpu
from jax.sharding import PartitionSpec as P

OWNER_AXES = ("obs", "node")
SUBLANES = 16
BUNDLES = 2
BF16 = jnp.bfloat16
F32 = jnp.float32


def dot(left, right, left_dim=1, right_dim=0):
    return lax.dot_general(
        left, right, (((left_dim,), (right_dim,)), ((), ())), preferred_element_type=F32
    )


def iota(shape, dim):
    return lax.broadcasted_iota(jnp.int32, shape, dim)


def call(kernel, outs, *args, scratch=(), after=()):
    vmem = pl.BlockSpec(memory_space=pltpu.VMEM)
    count = len(args)
    specs = [vmem] * count + [pl.BlockSpec(memory_space=pl.ANY)] * len(after)
    args += tuple(after)
    return pl.pallas_call(
        lambda *refs: kernel(*refs[:count], *refs[len(args) :]),
        out_shape=[jax.ShapeDtypeStruct(shape, dtype) for shape, dtype in outs],
        in_specs=specs,
        out_specs=[vmem] * len(outs),
        scratch_shapes=list(scratch),
        compiler_params=pltpu.CompilerParams(vmem_limit_bytes=40 << 20),
    )(*args)


def call_staged(kernel, outs, *args, held=()):
    count = len(args)
    sources = list(args) + [a for a in held if not any(a is b for b in args)]
    kept = [next(i for i, b in enumerate(sources) if a is b) for a in held]
    rest = [i for i in range(len(sources)) if i not in kept]

    def staged(*refs):
        hbm, refs = refs[: len(sources)], refs[len(sources) :]
        out_refs, refs = refs[: len(outs)], refs[len(outs) :]
        buffers = dict(zip(kept, refs[: len(kept)])) | dict(zip(rest, refs[len(kept) : -1]))
        copies = [
            pltpu.make_async_copy(hbm[i], buffers[i], refs[-1].at[i]) for i in range(len(sources))
        ]
        for copy in copies:
            copy.start()
        for copy in copies:
            copy.wait()
        kernel(*[buffers[i] for i in range(count)], *out_refs)

    return pl.pallas_call(
        staged,
        out_shape=[jax.ShapeDtypeStruct(shape, dtype) for shape, dtype in outs]
        + [jax.ShapeDtypeStruct(a.shape, a.dtype) for a in held],
        in_specs=[pl.BlockSpec(memory_space=pltpu.HBM)] * len(sources),
        out_specs=[pl.BlockSpec(memory_space=pltpu.VMEM)] * (len(outs) + len(held)),
        scratch_shapes=[pltpu.VMEM(sources[i].shape, sources[i].dtype) for i in rest]
        + [pltpu.SemaphoreType.DMA((len(sources),))],
        compiler_params=pltpu.CompilerParams(vmem_limit_bytes=40 << 20),
    )(*[pltpu.with_memory_space_constraint(a, pltpu.HBM) for a in sources])


def exchange(blocks, axes):
    return lax.all_to_all(blocks, axes, split_axis=0, concat_axis=0, tiled=True)


def shift(value, axis, step):
    size = lax.axis_size(axis)
    return lax.ppermute(value, axis, [(i, (i + step) % size) for i in range(size)])


def other_half(ref):
    half = ref.shape[0] // 2
    me = lax.axis_index("mp")
    mine = ref[pl.ds(pl.multiple_of(me * half, half), half), :]
    theirs = ref[pl.ds(pl.multiple_of((1 - me) * half, half), half), :]
    return mine, theirs


def column_half(ref, which):
    half = ref.shape[1] // 2
    return ref[:, pl.ds(pl.multiple_of(which * half, 128), half)]


def pack_kernel(cap, obs_ref, owner_ref, index_ref, slot_ref, other_ref, *outs):
    owners = len(outs)
    chunk, lanes = outs[0].shape
    fanout, obs = owner_ref.shape
    owner, index = owner_ref[...], index_ref[...]
    hits = [iota((owners, obs), 0) == owner[k : k + 1] for k in range(fanout)]
    count = functools.reduce(jnp.add, [h.astype(F32) for h in hits])
    before = dot(count, (iota((obs, obs), 0) < iota((obs, obs), 1)).astype(F32))
    header = jnp.where(iota((SUBLANES, obs), 0) == 4 * fanout, slot_ref[...].astype(F32), 0.0)
    places = []
    for k in range(fanout):
        rank = jnp.sum(jnp.where(hits[k], before, 0.0), axis=0, keepdims=True)
        places.append(owner[k : k + 1] * cap + rank.astype(jnp.int32))
        plus = index[k : k + 1] + 1
        fields = (owner[k : k + 1].astype(F32), rank, (plus // 16).astype(F32), (plus % 16).astype(F32))
        for j, row in enumerate(fields):
            header = jnp.where(iota(header.shape, 0) == 4 * k + j, row, header)
    header = header.astype(BF16)
    me, core = lax.axis_index(OWNER_AXES), lax.axis_index("mp")
    mine, other = column_half(obs_ref, core), column_half(obs_ref, 1 - core)

    def write(ref, pick, rows):
        packed = dot(pick, rows).astype(BF16)
        for c in range(rows.shape[1] // lanes):
            ref[c * cap : (c + 1) * cap, :] = packed[:, c * lanes : (c + 1) * lanes]
        ref[chunk - SUBLANES :, :] = header

    for j, out_ref in enumerate(outs):
        slots = iota((cap, obs), 0) + lax.rem(me + j, owners) * cap
        pick = functools.reduce(jnp.logical_or, [slots == place for place in places]).astype(BF16)
        write(out_ref, pick, mine)
        if j == 0:
            write(other_ref, pick, other)


def table_kernel(state_ref, agg_ref, w_node_ref, w_out_ref, bias_ref, table_ref):
    hidden = w_node_ref.shape[1]
    nodes, slots = state_ref.shape[0], bias_ref.shape[0]
    table_ref[nodes:, :] = jnp.zeros((table_ref.shape[0] - nodes, table_ref.shape[1]), BF16)

    def put(begin, column, part):
        high = part.astype(BF16)
        table_ref[begin : begin + part.shape[0], column : column + hidden] = high
        table_ref[begin : begin + part.shape[0], column + hidden : column + 2 * hidden] = (
            part - high.astype(F32)
        ).astype(BF16)

    put(0, 0, dot(state_ref[...], w_node_ref[...]))
    put(0, 2 * hidden, dot(agg_ref[...], w_out_ref[...], 1, 1))
    put(nodes, 0, bias_ref[...])


def join_blocks_kernel(*refs):
    out_ref = refs[-1]
    for j, ref in enumerate(refs[:-1]):
        out_ref[j] = ref[...]


def edge_kernel(
    fanout, nodes, steps, own_ref, mine_ref, other_ref, theirs_ref, table_ref, w_obs_ref,
    act_ref, hot_ref, rows_mine_ref, rows_theirs_ref, keep_ref, send_ref, pick_ref, total_ref, packed_ref, picks_ref,
):
    owners = mine_ref.shape[0] + 1
    chunk, lanes = own_ref.shape
    half = w_obs_ref.shape[0] // 2
    hidden = w_obs_ref.shape[1]
    cap = (chunk - SUBLANES) * lanes // half
    me = lax.axis_index(OWNER_AXES)
    base = 1 << nodes.bit_length()
    partner = partner_of(steps[0]).astype(F32)
    columns = []
    picks = []
    places = []
    for j in range(owners):
        block, other = (mine_ref.at[j - 1], theirs_ref.at[j - 1]) if j else (own_ref, other_ref)
        header = block[chunk - SUBLANES :, :].astype(F32)
        slot = header[4 * fanout : 4 * fanout + 1] * base
        code = jnp.zeros((cap, lanes), F32)
        pick = partner_pick = jnp.zeros((cap, lanes), jnp.bool_)
        for k in range(fanout):
            row = header[4 * k : 4 * k + 4]
            rank = jnp.where(row[0:1] == me.astype(F32), row[1:2], -1.0).astype(jnp.int32)
            hit = iota((cap, lanes), 0) == rank
            pick = pick | hit
            rank = jnp.where(row[0:1] == partner, row[1:2], -1.0).astype(jnp.int32)
            partner_pick = partner_pick | (iota((cap, lanes), 0) == rank)
            code = code + jnp.where(hit, row[2:3] * 16.0 + row[3:4] + slot, 0.0)
        picks.append(pick.astype(BF16))
        places.append(place_of(lax.rem(me - j + owners, owners), steps))
        begin = pl.multiple_of(places[j] * cap, SUBLANES)
        picks_ref[pl.ds(begin, cap), :] = partner_pick.astype(BF16)
        columns.append(jnp.sum(code, axis=1, keepdims=True).astype(jnp.int32))
        for c in range(half // lanes):
            rows = slice(j * cap, (j + 1) * cap)
            place = slice(c * lanes, (c + 1) * lanes)
            rows_mine_ref[rows, place] = block[c * cap : (c + 1) * cap, :]
            rows_theirs_ref[rows, place] = other[c * cap : (c + 1) * cap, :]
    code = jnp.concatenate(columns, axis=0)
    index, slot = (code & (base - 1)) - 1, (code >> (base.bit_length() - 1)) + nodes
    column = iota(hot_ref.shape, 1)
    hot = ((column == index) | ((column == slot) & (index >= 0))).astype(BF16)
    hot_ref[...] = hot
    rows = dot(hot, table_ref[...])
    w_mine, w_theirs = other_half(w_obs_ref)
    pre = dot(rows_mine_ref[...], w_mine) + dot(rows_theirs_ref[...], w_theirs)
    pre = pre + (rows[:, :hidden] + rows[:, hidden : 2 * hidden])
    g_z = rows[:, 2 * hidden : 3 * hidden] + rows[:, 3 * hidden :]
    sig = jax.nn.sigmoid(pre)
    g_a = (g_z * sig * (1.0 + pre * (1.0 - sig))).astype(BF16)
    act_ref[:, :hidden] = g_a
    act_ref[:, hidden:] = (pre * sig).astype(BF16)
    for j, pick in enumerate(picks):
        rows = g_a[j * cap : (j + 1) * cap]
        begin = pl.multiple_of(places[j] * lanes, SUBLANES)
        total_ref[pl.ds(begin, lanes), :] = dot(pick, rows, 0, 0).astype(BF16)
        packed_ref[pl.ds(pl.multiple_of(places[j] * cap, SUBLANES), cap), :] = rows
    bit = own_bit(steps[0])
    for out_ref, ref, which in (
        (keep_ref, total_ref, bit), (send_ref, packed_ref, 1 - bit), (pick_ref, picks_ref, bit)
    ):
        count = out_ref.shape[0]
        out_ref[...] = ref[pl.ds(pl.multiple_of(which * count, SUBLANES), count), :]


def halving_steps():
    bits = [
        [(axis, k) for k in range(lax.axis_size(axis).bit_length() - 1)] for axis in ("node", "obs")
    ]
    steps = []
    for k in range(max(map(len, bits))):
        both = [line[k] for line in bits if k < len(line)]
        steps += [(both[0], both[-1])] + ([(both[1], both[0])] if len(both) > 1 else [])
    return steps


def flip(value, step):
    axes = ("obs", "node", "mp")
    sizes = [lax.axis_size(axis) for axis in axes]
    pairs = []
    for index in range(sizes[0] * sizes[1] * sizes[2]):
        place = [index // (sizes[1] * sizes[2]), index // sizes[2] % sizes[1], index % sizes[2]]
        axis, k = step[place[2] % 2]
        place[axes.index(axis)] ^= (2 << k) - 1
        pairs.append((index, (place[0] * sizes[1] + place[1]) * sizes[2] + place[2]))
    return lax.ppermute(value, axes, pairs)


def bit_of(step, node, obs):
    codes = {"node": node ^ (node >> 1), "obs": obs ^ (obs >> 1)}
    bits = [(codes[axis] >> k) & 1 for axis, k in step]
    return jnp.where(lax.axis_index("mp") % 2 == 0, bits[0], bits[1])


def own_bit(step):
    return bit_of(step, lax.axis_index("node"), lax.axis_index("obs"))


def partner_of(step):
    node, obs, shares = lax.axis_index("node"), lax.axis_index("obs"), lax.axis_size("node")
    owners = []
    for axis, k in step:
        mask = (2 << k) - 1
        owners.append(obs * shares + (node ^ mask) if axis == "node" else (obs ^ mask) * shares + node)
    return jnp.where(lax.axis_index("mp") % 2 == 0, owners[0], owners[1])


def place_of(owner, steps):
    shares = lax.axis_size("node")
    place = 0
    for step in steps:
        place = 2 * place + bit_of(step, lax.rem(owner, shares), lax.div(owner, shares))
    return place


def halves(rows):
    return rows % (2 * SUBLANES) == 0


def half_rows(rows):
    return rows // 2 if halves(rows) else rows


def split_half(total_ref, start, rows, step, tail, keep_ref, send_ref):
    end = start + rows
    half = half_rows(rows) if step else rows
    if half < rows:
        bit = own_bit(step)
        kept, sent = [pl.ds(pl.multiple_of(start + b * half, SUBLANES), half) for b in (bit, 1 - bit)]
        keep_ref[:half, :] = total_ref[kept, :]
        send_ref[:half, :] = total_ref[sent, :].astype(BF16)
    else:
        both = total_ref[start:end, :].astype(BF16)
        keep_ref[:half, :] = both.astype(keep_ref.dtype)
        send_ref[:half, :] = both
    if tail:
        both = total_ref[end : end + tail, :].astype(BF16)
        keep_ref[half:, :] = both.astype(keep_ref.dtype)
        send_ref[half:, :] = both


def weight_kernel(
    step, bundles, tail, hot_ref, act_ref, rows_mine_ref, rows_theirs_ref, state_ref, agg_ref, w_node_ref,
    mine_ref, theirs_ref, *refs
):
    halves_refs, total_ref = refs[:-1], refs[-1]
    width, hidden = w_node_ref.shape
    nodes = state_ref.shape[0]
    sums = dot(hot_ref[...], act_ref[...], 0, 0)
    by_node = sums[:nodes].astype(BF16)
    node_hidden, z_sum = by_node[:, :hidden], by_node[:, hidden:]
    total_ref[:width, :] = dot(state_ref[...], node_hidden, 0, 0)
    begin = width
    for c in range(width // hidden):
        total_ref[begin : begin + hidden, :] = dot(
            z_sum, agg_ref[:, c * hidden : (c + 1) * hidden], 0, 0
        )
        begin += hidden
    g_a = act_ref[:, :hidden]
    core, half = lax.axis_index("mp"), width // 2
    for which, ref in ((core, rows_mine_ref), (1 - core, rows_theirs_ref)):
        total_ref[pl.ds(pl.multiple_of(begin + which * half, SUBLANES), half), :] = dot(ref[...], g_a, 0, 0)
    begin += width
    total_ref[begin:, :] = sums[nodes:, :hidden]
    rows = begin // bundles
    for i in range(bundles):
        split_half(
            total_ref, i * rows, rows, step, tail if i == bundles - 1 else 0,
            halves_refs[2 * i], halves_refs[2 * i + 1],
        )
    mine, theirs = other_half(w_node_ref)
    theirs_ref[...] = dot(node_hidden, theirs, 1, 1).astype(BF16)
    mine_ref[...] = dot(node_hidden, mine, 1, 1)


def obs_kernel(keep_ref, got_ref, w_ref, mine_ref, theirs_ref):
    got = got_ref[got_ref.shape[0] - keep_ref.shape[0] :, :]
    obs_hidden = (keep_ref[...].astype(F32) + got.astype(F32)).astype(BF16)
    mine, theirs = other_half(w_ref)
    theirs_ref[...] = dot(obs_hidden, theirs, 1, 1).astype(BF16)
    mine_ref[...] = dot(obs_hidden, mine, 1, 1)


def add_kernel(step, tail, keep_ref, got_ref, next_ref, send_ref, total_ref):
    total = keep_ref[...].astype(F32) + got_ref[...].astype(F32)
    total_ref[...] = total.astype(total_ref.dtype)
    split_half(total_ref, 0, total_ref.shape[0] - tail, step, tail, next_ref, send_ref)


def unpack_kernel(step, keep_ref, got_ref, pick_ref, next_ref, send_ref, total_ref):
    obs = pick_ref.shape[1]
    blocks = keep_ref.shape[0] // obs
    cap = got_ref.shape[0] // blocks
    for i in range(blocks):
        edges, rows = slice(i * cap, (i + 1) * cap), slice(i * obs, (i + 1) * obs)
        total = keep_ref[rows, :].astype(F32) + dot(pick_ref[edges, :], got_ref[edges, :], 0, 0)
        total_ref[rows, :] = total.astype(BF16)
    split_half(total_ref, 0, total_ref.shape[0], step, 0, next_ref, send_ref)


def add_with_rows_kernel(
    step, tail, keep_ref, got_ref, rows_ref, rows_got_ref, next_ref, send_ref, rows_next_ref, total_ref, rows_total_ref
):
    share = next_ref.shape[0]
    total_ref[...] = keep_ref[...] + got_ref[...].astype(F32)
    split_half(total_ref, 0, share - tail, None, tail, next_ref, send_ref.at[:share])
    rows_total_ref[...] = (rows_ref[...].astype(F32) + rows_got_ref[...].astype(F32)).astype(BF16)
    split_half(
        rows_total_ref, 0, rows_total_ref.shape[0], step, 0, rows_next_ref, send_ref.at[share:]
    )


def last_kernel(keep_ref, got_ref, piece_ref, *slot_refs):
    total = keep_ref[...] + got_ref[: keep_ref.shape[0], :].astype(F32)
    rows = piece_ref.shape[0]
    piece_ref[...] = total[:rows].astype(BF16)
    for slot_ref in slot_refs:
        slot_ref[...] = total[rows : rows + slot_ref.shape[0]]


def join_kernel(step, mine_ref, got_ref, out_ref):
    rows = mine_ref.shape[0]
    bit = own_bit(step)
    out_ref[pl.ds(pl.multiple_of(bit * rows, SUBLANES), rows), :] = mine_ref[...]
    out_ref[pl.ds(pl.multiple_of((1 - bit) * rows, SUBLANES), rows), :] = got_ref[...]


def spread_kernel(step, bundles, *refs):
    low = own_bit(step) == 0
    joined = []
    for i in range(bundles):
        mine, got = refs[2 * i][...], refs[2 * i + 1][...]
        joined += [jnp.where(low, mine, got), jnp.where(low, got, mine)]
    half, hidden = joined[0].shape
    at = 0
    for out_ref in refs[2 * bundles :]:
        for c in range(out_ref.shape[1] // hidden):
            begin = 0
            while begin < out_ref.shape[0]:
                offset = at % half
                count = min(out_ref.shape[0] - begin, half - offset)
                out_ref[begin : begin + count, c * hidden : (c + 1) * hidden] = joined[at // half][
                    offset : offset + count
                ].astype(F32)
                at, begin = at + count, begin + count


def merge_kernel(
    node_ref, node_got_ref, obs_ref, obs_got_ref, slot_ref, grad_node_ref, grad_obs_ref, grad_slot_ref
):
    grad_slot_ref[...] = slot_ref[...]
    grad_node_ref[...] = node_ref[...] + node_got_ref[...].astype(F32)
    grad_obs_ref[...] = (obs_ref[...] + obs_got_ref[...].astype(F32)).astype(BF16)


def summing(steps, halved, tail, keep, got, after):
    hidden = keep.shape[1]
    for at, following in enumerate(steps[1:], 1):
        step = following if at < halved else None
        rows = keep.shape[0] - tail
        rows = (half_rows(rows) if step else rows) + tail
        keep, send = call(
            functools.partial(add_kernel, step, tail),
            [((rows, hidden), keep.dtype), ((rows, hidden), BF16)],
            keep, got,
            scratch=[pltpu.VMEM(keep.shape, keep.dtype)],
            after=after,
        )
        after[:] = [send]
        got = flip(send, following)
        yield
    return keep, got


def halving_used(steps, rows):
    used = []
    for step in steps[:-1]:
        if halves(rows):
            used.append(step)
            rows //= 2
    return used


def weight_chain(steps, rows, tail, slots, keep, got, after, returned=None):
    used = halving_used(steps, rows)
    keep, got = yield from summing(steps[:-1], len(steps) - 1, tail, keep, got, after)
    if returned:
        rows_keep, rows_got = returned
        shape = (half_rows(rows_keep.shape[0]), keep.shape[1])
        keep, send, rows_keep = call(
            functools.partial(add_with_rows_kernel, steps[-1], tail),
            [(keep.shape, F32), ((keep.shape[0] + shape[0], shape[1]), BF16), (shape, BF16)],
            keep, got, rows_keep, rows_got,
            scratch=[pltpu.VMEM(keep.shape, F32), pltpu.VMEM(rows_keep.shape, BF16)],
            after=after,
        )
    else:
        keep, send = call(
            functools.partial(add_kernel, None, tail),
            [(keep.shape, F32), (keep.shape, BF16)],
            keep, got,
            scratch=[pltpu.VMEM(keep.shape, F32)],
            after=after,
        )
    after[:] = [send]
    arrived = got = flip(send, steps[-1])
    yield
    piece, *sums = call(
        last_kernel,
        [((keep.shape[0] - tail, keep.shape[1]), BF16)]
        + ([((slots, keep.shape[1]), F32)] if tail else []),
        keep, got,
        after=after,
    )
    after[:] = [piece]
    got = flip(piece, used[-1])
    yield
    for step, following in zip(used[:0:-1], used[-2::-1]):
        (piece,) = call(
            functools.partial(join_kernel, step),
            [((2 * piece.shape[0], piece.shape[1]), BF16)],
            piece, got,
            after=after,
        )
        after[:] = [piece]
        got = flip(piece, following)
        yield
    return [piece, got], sums, (rows_keep, arrived) if returned else ()


def rows_chain(steps, keep, got, pick, after, out):
    shape = (half_rows(keep.shape[0]), keep.shape[1])
    keep, send = call(
        functools.partial(unpack_kernel, steps[1]),
        [(shape, BF16)] * 2,
        keep, got, pick,
        scratch=[pltpu.VMEM(keep.shape, BF16)],
        after=after,
    )
    after[:] = [send]
    got = flip(send, steps[1])
    yield
    out += yield from summing(steps[1:-1], len(steps), 0, keep, got, after)


def in_turns(chains, turns):
    results = {}
    for key in turns + list(range(len(chains))):
        try:
            next(chains[key])
        except StopIteration as stop:
            results.setdefault(key, stop.value)
    return [results[key] for key in range(len(chains))]


def local(obs_feat, node_state, grad_agg, owner, local_idx, slot, w_obs, w_node, slot_bias, w_out):
    owners = lax.axis_size(OWNER_AXES)
    obs, fanout = owner.shape
    nodes, width = node_state.shape
    hidden = w_obs.shape[1]
    slots = slot_bias.shape[0]
    cap = max(2, 2 * obs * fanout // owners)
    cap = -(-cap // SUBLANES) * SUBLANES
    edges = owners * cap
    half = width // 2
    slot_row = slot.reshape(1, obs)

    steps = halving_steps()
    chunk = cap * half // obs + SUBLANES
    other, *packed = call_staged(
        functools.partial(pack_kernel, cap),
        [((chunk, obs), BF16)] * (owners + 1),
        obs_feat, owner.T, local_idx.T, slot_row,
    )
    received = [shift(packed[j], OWNER_AXES, j) for j in range(1, owners)]
    tail = -(-slots // SUBLANES) * SUBLANES
    table, state_held, agg_held, w_node_held, w_obs_held = call_staged(
        table_kernel,
        [((nodes + tail, 4 * hidden), BF16)],
        node_state, grad_agg, w_node, w_out, slot_bias,
        held=(node_state, grad_agg, w_node, w_obs),
    )
    (mine,) = call(
        join_blocks_kernel, [((owners - 1, chunk, obs), BF16)], *received,
        after=(w_obs_held,),
    )
    theirs = shift(mine, "mp", 1)
    act, hot, rows_mine, rows_theirs, obs_keep, obs_send, obs_pick = call(
        functools.partial(edge_kernel, fanout, nodes, steps),
        [((edges, 2 * hidden), BF16), ((edges, nodes + tail), BF16)]
        + [((edges, half), BF16)] * 2
        + [((owners * obs // 2, hidden), BF16), ((edges // 2, hidden), BF16), ((edges // 2, obs), BF16)],
        packed[0], mine, other, theirs, table, w_obs_held,
        scratch=[
            pltpu.VMEM((owners * obs, hidden), BF16),
            pltpu.VMEM((edges, hidden), BF16),
            pltpu.VMEM((edges, obs), BF16),
        ],
    )

    stack = 2 * width + width // hidden * hidden
    bundles = BUNDLES
    rows = stack // bundles
    obs_got = flip(obs_send, steps[0])
    shapes = []
    for i in range(bundles):
        share = rows // 2 + (tail if i == bundles - 1 else 0)
        shapes += [((share, hidden), F32), ((share, hidden), BF16)]
    node_mine, node_theirs, *shares = call(
        functools.partial(weight_kernel, steps[0], bundles, tail),
        [((nodes, half), F32), ((nodes, half), BF16)] + shapes,
        hot, act, rows_mine, rows_theirs, state_held, agg_held, w_node_held,
        scratch=[pltpu.VMEM((stack + tail, hidden), F32)],
    )
    after = []
    returned = []
    chains = [rows_chain(steps, obs_keep, obs_got, obs_pick, after, returned)]
    got = [flip(send, steps[0]) for send in shares[1::2]]
    for i in range(bundles):
        last = i == bundles - 1
        chains.append(
            weight_chain(
                steps, rows, tail if last else 0, slots, shares[2 * i], got[i], after, returned if last else None
            )
        )
    node_got = shift(node_theirs, "mp", 1)
    middle, last = len(steps) - 1, len(steps) + len(halving_used(steps, rows)) - 1
    turns = [1]
    for step in range(1, last):
        turns += [2, 1] if step == middle else [1, 2]
        turns += [0] if step < middle else []
        turns += [0] if step == middle - 1 else []
    turns += [2]
    _, *weights = in_turns(chains, turns)
    obs_keep, arrived = weights[-1][2]
    obs_mine, obs_theirs = call(
        obs_kernel, [((obs, half), F32), ((obs, half), BF16)], obs_keep, arrived, w_obs_held
    )
    (slot_sums,) = weights[-1][1]
    grad_node, grad_obs, grad_slot = call(
        merge_kernel, [((nodes, half), F32), ((obs, half), BF16), ((slots, hidden), F32)],
        node_mine, node_got, obs_mine, shift(obs_theirs, "mp", 1), slot_sums,
    )
    ends = [end for pair, *_ in weights for end in pair]
    grad_w_node, grad_w_out, grad_w_obs = call(
        functools.partial(spread_kernel, steps[0], bundles),
        [((width, hidden), F32), ((hidden, width), F32), ((width, hidden), F32)],
        *ends,
        after=[pltpu.with_memory_space_constraint(grad_obs, pltpu.HBM)],
    )
    return grad_obs, grad_node, grad_w_obs, grad_w_node, grad_w_out, grad_slot


def solution(mesh):
    rows = P(("group", "obs", "node"), None)
    return jax.shard_map(
        local,
        mesh=mesh,
        in_specs=(
            rows, rows, rows, rows, rows,
            P(("group", "obs", "node")),
            P(None, "mp"), P(None, "mp"), P(None, "mp"), P("mp", None),
        ),
        out_specs=(
            P(("group", "obs", "node"), "mp"),
            P(("group", "obs", "node"), "mp"),
            P("group", "mp"),
            P("group", "mp"),
            P(("group", "mp"), None),
            P("group", "mp"),
        ),
        check_vma=False,
    )
```

```python
import functools

import jax
import jax.numpy as jnp
from jax import lax
from jax.experimental import pallas as pl
from jax.experimental.pallas import tpu as pltpu
from jax.sharding import PartitionSpec as P

OWNER_AXES = ("obs", "node")
SUBLANES = 16
BF16 = jnp.bfloat16
F32 = jnp.float32


def dot(left, right, left_dim=1, right_dim=0):
    return lax.dot_general(
        left, right, (((left_dim,), (right_dim,)), ((), ())), preferred_element_type=F32
    )


def iota(shape, dim):
    return lax.broadcasted_iota(jnp.int32, shape, dim)


def call(kernel, outs, *args, scratch=(), after=()):
    vmem = pl.BlockSpec(memory_space=pltpu.VMEM)
    count = len(args)
    specs = [vmem] * count + [pl.BlockSpec(memory_space=pl.ANY)] * len(after)
    args += tuple(after)
    return pl.pallas_call(
        lambda *refs: kernel(*refs[:count], *refs[len(args) :]),
        out_shape=[jax.ShapeDtypeStruct(shape, dtype) for shape, dtype in outs],
        in_specs=specs,
        out_specs=[vmem] * len(outs),
        scratch_shapes=list(scratch),
        compiler_params=pltpu.CompilerParams(vmem_limit_bytes=40 << 20),
    )(*args)


def call_staged(kernel, outs, *args, held=()):
    count = len(args)
    sources = list(args) + [a for a in held if not any(a is b for b in args)]
    kept = [next(i for i, b in enumerate(sources) if a is b) for a in held]
    rest = [i for i in range(len(sources)) if i not in kept]

    def staged(*refs):
        hbm, refs = refs[: len(sources)], refs[len(sources) :]
        out_refs, refs = refs[: len(outs)], refs[len(outs) :]
        buffers = dict(zip(kept, refs[: len(kept)])) | dict(zip(rest, refs[len(kept) : -1]))
        copies = [
            pltpu.make_async_copy(hbm[i], buffers[i], refs[-1].at[i]) for i in range(len(sources))
        ]
        for copy in copies:
            copy.start()
        for copy in copies:
            copy.wait()
        kernel(*[buffers[i] for i in range(count)], *out_refs)

    return pl.pallas_call(
        staged,
        out_shape=[jax.ShapeDtypeStruct(shape, dtype) for shape, dtype in outs]
        + [jax.ShapeDtypeStruct(a.shape, a.dtype) for a in held],
        in_specs=[pl.BlockSpec(memory_space=pltpu.HBM)] * len(sources),
        out_specs=[pl.BlockSpec(memory_space=pltpu.VMEM)] * (len(outs) + len(held)),
        scratch_shapes=[pltpu.VMEM(sources[i].shape, sources[i].dtype) for i in rest]
        + [pltpu.SemaphoreType.DMA((len(sources),))],
        compiler_params=pltpu.CompilerParams(vmem_limit_bytes=40 << 20),
    )(*[pltpu.with_memory_space_constraint(a, pltpu.HBM) for a in sources])


def exchange(blocks, axes):
    return lax.all_to_all(blocks, axes, split_axis=0, concat_axis=0, tiled=True)


def shift(value, axis, step):
    size = lax.axis_size(axis)
    return lax.ppermute(value, axis, [(i, (i + step) % size) for i in range(size)])


def other_half(ref):
    half = ref.shape[0] // 2
    me = lax.axis_index("mp")
    mine = ref[pl.ds(pl.multiple_of(me * half, half), half), :]
    theirs = ref[pl.ds(pl.multiple_of((1 - me) * half, half), half), :]
    return mine, theirs


def column_half(ref, which):
    half = ref.shape[1] // 2
    return ref[:, pl.ds(pl.multiple_of(which * half, 128), half)]


def pack_kernel(cap, obs_ref, owner_ref, index_ref, slot_ref, other_ref, *outs):
    owners = len(outs)
    chunk, lanes = outs[0].shape
    fanout, obs = owner_ref.shape
    owner, index = owner_ref[...], index_ref[...]
    hits = [iota((owners, obs), 0) == owner[k : k + 1] for k in range(fanout)]
    count = functools.reduce(jnp.add, [h.astype(F32) for h in hits])
    before = dot(count, (iota((obs, obs), 0) < iota((obs, obs), 1)).astype(F32))
    header = jnp.where(iota((SUBLANES, obs), 0) == 4 * fanout, slot_ref[...].astype(F32), 0.0)
    places = []
    for k in range(fanout):
        rank = jnp.sum(jnp.where(hits[k], before, 0.0), axis=0, keepdims=True)
        places.append(owner[k : k + 1] * cap + rank.astype(jnp.int32))
        plus = index[k : k + 1] + 1
        fields = (owner[k : k + 1].astype(F32), rank, (plus // 16).astype(F32), (plus % 16).astype(F32))
        for j, row in enumerate(fields):
            header = jnp.where(iota(header.shape, 0) == 4 * k + j, row, header)
    header = header.astype(BF16)
    me, core = lax.axis_index(OWNER_AXES), lax.axis_index("mp")
    mine, other = column_half(obs_ref, core), column_half(obs_ref, 1 - core)

    def write(ref, pick, rows):
        packed = dot(pick, rows).astype(BF16)
        for c in range(rows.shape[1] // lanes):
            ref[c * cap : (c + 1) * cap, :] = packed[:, c * lanes : (c + 1) * lanes]
        ref[chunk - SUBLANES :, :] = header

    for j, out_ref in enumerate(outs):
        slots = iota((cap, obs), 0) + lax.rem(me + j, owners) * cap
        pick = functools.reduce(jnp.logical_or, [slots == place for place in places]).astype(BF16)
        write(out_ref, pick, mine)
        if j == 0:
            write(other_ref, pick, other)


def table_kernel(state_ref, agg_ref, w_node_ref, w_out_ref, bias_ref, table_ref):
    hidden = w_node_ref.shape[1]
    nodes, slots = state_ref.shape[0], bias_ref.shape[0]
    table_ref[nodes:, :] = jnp.zeros((table_ref.shape[0] - nodes, table_ref.shape[1]), BF16)

    def put(begin, column, part):
        high = part.astype(BF16)
        table_ref[begin : begin + part.shape[0], column : column + hidden] = high
        table_ref[begin : begin + part.shape[0], column + hidden : column + 2 * hidden] = (
            part - high.astype(F32)
        ).astype(BF16)

    put(0, 0, dot(state_ref[...], w_node_ref[...]))
    put(0, 2 * hidden, dot(agg_ref[...], w_out_ref[...], 1, 1))
    put(nodes, 0, bias_ref[...])


def join_blocks_kernel(*refs):
    out_ref = refs[-1]
    for j, ref in enumerate(refs[:-1]):
        out_ref[j] = ref[...]


def edge_kernel(
    fanout, nodes, steps, own_ref, mine_ref, other_ref, theirs_ref, table_ref, w_obs_ref,
    act_ref, hot_ref, rows_mine_ref, rows_theirs_ref, keep_ref, send_ref, pick_ref, total_ref, packed_ref, picks_ref,
):
    owners = mine_ref.shape[0] + 1
    chunk, lanes = own_ref.shape
    half = w_obs_ref.shape[0] // 2
    hidden = w_obs_ref.shape[1]
    cap = (chunk - SUBLANES) * lanes // half
    me = lax.axis_index(OWNER_AXES)
    base = 1 << nodes.bit_length()
    partner = partner_of(steps[0]).astype(F32)
    columns = []
    picks = []
    places = []
    for j in range(owners):
        block, other = (mine_ref.at[j - 1], theirs_ref.at[j - 1]) if j else (own_ref, other_ref)
        header = block[chunk - SUBLANES :, :].astype(F32)
        slot = header[4 * fanout : 4 * fanout + 1] * base
        code = jnp.zeros((cap, lanes), F32)
        pick = partner_pick = jnp.zeros((cap, lanes), jnp.bool_)
        for k in range(fanout):
            row = header[4 * k : 4 * k + 4]
            rank = jnp.where(row[0:1] == me.astype(F32), row[1:2], -1.0).astype(jnp.int32)
            hit = iota((cap, lanes), 0) == rank
            pick = pick | hit
            rank = jnp.where(row[0:1] == partner, row[1:2], -1.0).astype(jnp.int32)
            partner_pick = partner_pick | (iota((cap, lanes), 0) == rank)
            code = code + jnp.where(hit, row[2:3] * 16.0 + row[3:4] + slot, 0.0)
        picks.append(pick.astype(BF16))
        places.append(place_of(lax.rem(me - j + owners, owners), steps))
        begin = pl.multiple_of(places[j] * cap, SUBLANES)
        picks_ref[pl.ds(begin, cap), :] = partner_pick.astype(BF16)
        columns.append(jnp.sum(code, axis=1, keepdims=True).astype(jnp.int32))
        for c in range(half // lanes):
            rows = slice(j * cap, (j + 1) * cap)
            place = slice(c * lanes, (c + 1) * lanes)
            rows_mine_ref[rows, place] = block[c * cap : (c + 1) * cap, :]
            rows_theirs_ref[rows, place] = other[c * cap : (c + 1) * cap, :]
    code = jnp.concatenate(columns, axis=0)
    index, slot = (code & (base - 1)) - 1, (code >> (base.bit_length() - 1)) + nodes
    column = iota(hot_ref.shape, 1)
    hot = ((column == index) | ((column == slot) & (index >= 0))).astype(BF16)
    hot_ref[...] = hot
    rows = dot(hot, table_ref[...])
    w_mine, w_theirs = other_half(w_obs_ref)
    pre = dot(rows_mine_ref[...], w_mine) + dot(rows_theirs_ref[...], w_theirs)
    pre = pre + (rows[:, :hidden] + rows[:, hidden : 2 * hidden])
    g_z = rows[:, 2 * hidden : 3 * hidden] + rows[:, 3 * hidden :]
    sig = jax.nn.sigmoid(pre)
    g_a = (g_z * sig * (1.0 + pre * (1.0 - sig))).astype(BF16)
    act_ref[:, :hidden] = g_a
    act_ref[:, hidden:] = (pre * sig).astype(BF16)
    for j, pick in enumerate(picks):
        rows = g_a[j * cap : (j + 1) * cap]
        begin = pl.multiple_of(places[j] * lanes, SUBLANES)
        total_ref[pl.ds(begin, lanes), :] = dot(pick, rows, 0, 0).astype(BF16)
        packed_ref[pl.ds(pl.multiple_of(places[j] * cap, SUBLANES), cap), :] = rows
    bit = own_bit(steps[0])
    for out_ref, ref, which in (
        (keep_ref, total_ref, bit), (send_ref, packed_ref, 1 - bit), (pick_ref, picks_ref, bit)
    ):
        count = out_ref.shape[0]
        out_ref[...] = ref[pl.ds(pl.multiple_of(which * count, SUBLANES), count), :]


def halving_steps():
    bits = [
        [(axis, k) for k in range(lax.axis_size(axis).bit_length() - 1)] for axis in ("node", "obs")
    ]
    steps = []
    for k in range(max(map(len, bits))):
        both = [line[k] for line in bits if k < len(line)]
        steps += [(both[0], both[-1])] + ([(both[1], both[0])] if len(both) > 1 else [])
    return steps


def flip(value, step):
    axes = ("obs", "node", "mp")
    sizes = [lax.axis_size(axis) for axis in axes]
    pairs = []
    for index in range(sizes[0] * sizes[1] * sizes[2]):
        place = [index // (sizes[1] * sizes[2]), index // sizes[2] % sizes[1], index % sizes[2]]
        axis, k = step[place[2] % 2]
        place[axes.index(axis)] ^= (2 << k) - 1
        pairs.append((index, (place[0] * sizes[1] + place[1]) * sizes[2] + place[2]))
    return lax.ppermute(value, axes, pairs)


def bit_of(step, node, obs):
    codes = {"node": node ^ (node >> 1), "obs": obs ^ (obs >> 1)}
    bits = [(codes[axis] >> k) & 1 for axis, k in step]
    return jnp.where(lax.axis_index("mp") % 2 == 0, bits[0], bits[1])


def own_bit(step):
    return bit_of(step, lax.axis_index("node"), lax.axis_index("obs"))


def partner_of(step):
    node, obs, shares = lax.axis_index("node"), lax.axis_index("obs"), lax.axis_size("node")
    owners = []
    for axis, k in step:
        mask = (2 << k) - 1
        owners.append(obs * shares + (node ^ mask) if axis == "node" else (obs ^ mask) * shares + node)
    return jnp.where(lax.axis_index("mp") % 2 == 0, owners[0], owners[1])


def place_of(owner, steps):
    shares = lax.axis_size("node")
    place = 0
    for step in steps:
        place = 2 * place + bit_of(step, lax.rem(owner, shares), lax.div(owner, shares))
    return place


def halves(rows):
    return rows % (2 * SUBLANES) == 0


def half_rows(rows):
    return rows // 2 if halves(rows) else rows


def split_half(total_ref, start, rows, step, tail, keep_ref, send_ref):
    end = start + rows
    half = half_rows(rows) if step else rows
    if half < rows:
        bit = own_bit(step)
        kept, sent = [pl.ds(pl.multiple_of(start + b * half, SUBLANES), half) for b in (bit, 1 - bit)]
        keep_ref[:half, :] = total_ref[kept, :]
        send_ref[:half, :] = total_ref[sent, :].astype(BF16)
    else:
        both = total_ref[start:end, :].astype(BF16)
        keep_ref[:half, :] = both.astype(keep_ref.dtype)
        send_ref[:half, :] = both
    if tail:
        both = total_ref[end : end + tail, :].astype(BF16)
        keep_ref[half:, :] = both.astype(keep_ref.dtype)
        send_ref[half:, :] = both


def weight_kernel(
    step, bundles, tail, hot_ref, act_ref, rows_mine_ref, rows_theirs_ref, state_ref, agg_ref, w_node_ref,
    mine_ref, theirs_ref, *refs
):
    halves_refs, total_ref = refs[:-1], refs[-1]
    width, hidden = w_node_ref.shape
    nodes = state_ref.shape[0]
    sums = dot(hot_ref[...], act_ref[...], 0, 0)
    by_node = sums[:nodes].astype(BF16)
    node_hidden, z_sum = by_node[:, :hidden], by_node[:, hidden:]
    total_ref[:width, :] = dot(state_ref[...], node_hidden, 0, 0)
    begin = width
    for c in range(width // hidden):
        total_ref[begin : begin + hidden, :] = dot(
            z_sum, agg_ref[:, c * hidden : (c + 1) * hidden], 0, 0
        )
        begin += hidden
    g_a = act_ref[:, :hidden]
    core, half = lax.axis_index("mp"), width // 2
    for which, ref in ((core, rows_mine_ref), (1 - core, rows_theirs_ref)):
        total_ref[pl.ds(pl.multiple_of(begin + which * half, SUBLANES), half), :] = dot(ref[...], g_a, 0, 0)
    begin += width
    total_ref[begin:, :] = sums[nodes:, :hidden]
    begin = 0
    for i, rows in enumerate(bundles):
        split_half(
            total_ref, begin, rows, step, tail if i == len(bundles) - 1 else 0,
            halves_refs[2 * i], halves_refs[2 * i + 1],
        )
        begin += rows
    mine, theirs = other_half(w_node_ref)
    theirs_ref[...] = dot(node_hidden, theirs, 1, 1).astype(BF16)
    mine_ref[...] = dot(node_hidden, mine, 1, 1)


def obs_kernel(keep_ref, got_ref, w_ref, mine_ref, theirs_ref):
    got = got_ref[got_ref.shape[0] - keep_ref.shape[0] :, :]
    obs_hidden = (keep_ref[...].astype(F32) + got.astype(F32)).astype(BF16)
    mine, theirs = other_half(w_ref)
    theirs_ref[...] = dot(obs_hidden, theirs, 1, 1).astype(BF16)
    mine_ref[...] = dot(obs_hidden, mine, 1, 1)


def add_kernel(step, tail, keep_ref, got_ref, next_ref, send_ref, total_ref):
    total = keep_ref[...].astype(F32) + got_ref[...].astype(F32)
    total_ref[...] = total.astype(total_ref.dtype)
    split_half(total_ref, 0, total_ref.shape[0] - tail, step, tail, next_ref, send_ref)


def unpack_kernel(step, keep_ref, got_ref, pick_ref, next_ref, send_ref, total_ref):
    obs = pick_ref.shape[1]
    blocks = keep_ref.shape[0] // obs
    cap = got_ref.shape[0] // blocks
    for i in range(blocks):
        edges, rows = slice(i * cap, (i + 1) * cap), slice(i * obs, (i + 1) * obs)
        total = keep_ref[rows, :].astype(F32) + dot(pick_ref[edges, :], got_ref[edges, :], 0, 0)
        total_ref[rows, :] = total.astype(BF16)
    split_half(total_ref, 0, total_ref.shape[0], step, 0, next_ref, send_ref)


def add_with_rows_kernel(
    step, tail, keep_ref, got_ref, rows_ref, rows_got_ref, next_ref, send_ref, rows_next_ref, total_ref, rows_total_ref
):
    share = next_ref.shape[0]
    total_ref[...] = keep_ref[...] + got_ref[...].astype(F32)
    split_half(total_ref, 0, share - tail, None, tail, next_ref, send_ref.at[:share])
    rows_total_ref[...] = (rows_ref[...].astype(F32) + rows_got_ref[...].astype(F32)).astype(BF16)
    split_half(
        rows_total_ref, 0, rows_total_ref.shape[0], step, 0, rows_next_ref, send_ref.at[share:]
    )


def last_kernel(keep_ref, got_ref, piece_ref, *slot_refs):
    total = keep_ref[...] + got_ref[: keep_ref.shape[0], :].astype(F32)
    rows = piece_ref.shape[0]
    piece_ref[...] = total[:rows].astype(BF16)
    for slot_ref in slot_refs:
        slot_ref[...] = total[rows : rows + slot_ref.shape[0]]


def join_kernel(step, mine_ref, got_ref, out_ref):
    rows = mine_ref.shape[0]
    bit = own_bit(step)
    out_ref[pl.ds(pl.multiple_of(bit * rows, SUBLANES), rows), :] = mine_ref[...]
    out_ref[pl.ds(pl.multiple_of((1 - bit) * rows, SUBLANES), rows), :] = got_ref[...]


def spread_kernel(step, mine_ref, got_ref, *out_refs):
    low = own_bit(step) == 0
    mine, got = mine_ref[...], got_ref[...]
    joined = [jnp.where(low, mine, got), jnp.where(low, got, mine)]
    half, hidden = joined[0].shape
    at = 0
    for out_ref in out_refs:
        for c in range(out_ref.shape[1] // hidden):
            begin = 0
            while begin < out_ref.shape[0]:
                offset = at % half
                count = min(out_ref.shape[0] - begin, half - offset)
                out_ref[begin : begin + count, c * hidden : (c + 1) * hidden] = joined[at // half][
                    offset : offset + count
                ].astype(F32)
                at, begin = at + count, begin + count


def merge_kernel(
    node_ref, node_got_ref, obs_ref, obs_got_ref, slot_ref, grad_node_ref, grad_obs_ref, grad_slot_ref
):
    grad_slot_ref[...] = slot_ref[...]
    grad_node_ref[...] = node_ref[...] + node_got_ref[...].astype(F32)
    grad_obs_ref[...] = (obs_ref[...] + obs_got_ref[...].astype(F32)).astype(BF16)


def summing(steps, halved, tail, keep, got, after):
    hidden = keep.shape[1]
    for at, following in enumerate(steps[1:], 1):
        step = following if at < halved else None
        rows = keep.shape[0] - tail
        rows = (half_rows(rows) if step else rows) + tail
        keep, send = call(
            functools.partial(add_kernel, step, tail),
            [((rows, hidden), keep.dtype), ((rows, hidden), BF16)],
            keep, got,
            scratch=[pltpu.VMEM(keep.shape, keep.dtype)],
            after=after,
        )
        after[:] = [send]
        got = flip(send, following)
        yield
    return keep, got


def halving_used(steps, rows):
    used = []
    for step in steps[:-1]:
        if halves(rows):
            used.append(step)
            rows //= 2
    return used


def weight_chain(steps, rows, tail, slots, keep, got, after, returned=None):
    used = halving_used(steps, rows)
    keep, got = yield from summing(steps[:-1], len(steps) - 1, tail, keep, got, after)
    if returned:
        rows_keep, rows_got = returned
        shape = (half_rows(rows_keep.shape[0]), keep.shape[1])
        keep, send, rows_keep = call(
            functools.partial(add_with_rows_kernel, steps[-1], tail),
            [(keep.shape, F32), ((keep.shape[0] + shape[0], shape[1]), BF16), (shape, BF16)],
            keep, got, rows_keep, rows_got,
            scratch=[pltpu.VMEM(keep.shape, F32), pltpu.VMEM(rows_keep.shape, BF16)],
            after=after,
        )
    else:
        keep, send = call(
            functools.partial(add_kernel, None, tail),
            [(keep.shape, F32), (keep.shape, BF16)],
            keep, got,
            scratch=[pltpu.VMEM(keep.shape, F32)],
            after=after,
        )
    after[:] = [send]
    arrived = got = flip(send, steps[-1])
    yield
    piece, *sums = call(
        last_kernel,
        [((keep.shape[0] - tail, keep.shape[1]), BF16)]
        + ([((slots, keep.shape[1]), F32)] if tail else []),
        keep, got,
        after=after,
    )
    after[:] = [piece]
    got = flip(piece, used[-1])
    yield
    for step, following in zip(used[:0:-1], used[-2::-1]):
        (piece,) = call(
            functools.partial(join_kernel, step),
            [((2 * piece.shape[0], piece.shape[1]), BF16)],
            piece, got,
            after=after,
        )
        after[:] = [piece]
        got = flip(piece, following)
        yield
    return [piece, got], sums, (rows_keep, arrived) if returned else ()


def rows_chain(steps, keep, got, pick, after, out):
    shape = (half_rows(keep.shape[0]), keep.shape[1])
    keep, send = call(
        functools.partial(unpack_kernel, steps[1]),
        [(shape, BF16)] * 2,
        keep, got, pick,
        scratch=[pltpu.VMEM(keep.shape, BF16)],
        after=after,
    )
    after[:] = [send]
    got = flip(send, steps[1])
    yield
    out += yield from summing(steps[1:-1], len(steps), 0, keep, got, after)


def in_turns(chains, turns):
    results = {}
    for key in turns + list(range(len(chains))):
        try:
            next(chains[key])
        except StopIteration as stop:
            results.setdefault(key, stop.value)
    return [results[key] for key in range(len(chains))]


def local(obs_feat, node_state, grad_agg, owner, local_idx, slot, w_obs, w_node, slot_bias, w_out):
    owners = lax.axis_size(OWNER_AXES)
    obs, fanout = owner.shape
    nodes, width = node_state.shape
    hidden = w_obs.shape[1]
    slots = slot_bias.shape[0]
    cap = max(2, 2 * obs * fanout // owners)
    cap = -(-cap // SUBLANES) * SUBLANES
    edges = owners * cap
    half = width // 2
    slot_row = slot.reshape(1, obs)

    steps = halving_steps()
    chunk = cap * half // obs + SUBLANES
    other, *packed = call_staged(
        functools.partial(pack_kernel, cap),
        [((chunk, obs), BF16)] * (owners + 1),
        obs_feat, owner.T, local_idx.T, slot_row,
    )
    received = [shift(packed[j], OWNER_AXES, j) for j in range(1, owners)]
    tail = -(-slots // SUBLANES) * SUBLANES
    table, state_held, agg_held, w_node_held, w_obs_held = call_staged(
        table_kernel,
        [((nodes + tail, 4 * hidden), BF16)],
        node_state, grad_agg, w_node, w_out, slot_bias,
        held=(node_state, grad_agg, w_node, w_obs),
    )
    (mine,) = call(
        join_blocks_kernel, [((owners - 1, chunk, obs), BF16)], *received,
        after=(w_obs_held,),
    )
    theirs = shift(mine, "mp", 1)
    act, hot, rows_mine, rows_theirs, obs_keep, obs_send, obs_pick = call(
        functools.partial(edge_kernel, fanout, nodes, steps),
        [((edges, 2 * hidden), BF16), ((edges, nodes + tail), BF16)]
        + [((edges, half), BF16)] * 2
        + [((owners * obs // 2, hidden), BF16), ((edges // 2, hidden), BF16), ((edges // 2, obs), BF16)],
        packed[0], mine, other, theirs, table, w_obs_held,
        scratch=[
            pltpu.VMEM((owners * obs, hidden), BF16),
            pltpu.VMEM((edges, hidden), BF16),
            pltpu.VMEM((edges, obs), BF16),
        ],
    )

    stack = 2 * width + width // hidden * hidden
    bundles = [stack - width, width]
    obs_got = flip(obs_send, steps[0])
    shapes = []
    for i, rows in enumerate(bundles):
        share = half_rows(rows) + (tail if i == len(bundles) - 1 else 0)
        shapes += [((share, hidden), F32), ((share, hidden), BF16)]
    node_mine, node_theirs, *shares = call(
        functools.partial(weight_kernel, steps[0], bundles, tail),
        [((nodes, half), F32), ((nodes, half), BF16)] + shapes,
        hot, act, rows_mine, rows_theirs, state_held, agg_held, w_node_held,
        scratch=[pltpu.VMEM((stack + tail, hidden), F32)],
    )
    after = []
    returned = []
    chains = [rows_chain(steps, obs_keep, obs_got, obs_pick, after, returned)]
    got = [flip(send, steps[0]) for send in shares[1::2]]
    for i, rows in enumerate(bundles):
        last = i == len(bundles) - 1
        chains.append(
            weight_chain(
                steps, rows, tail if last else 0, slots, shares[2 * i], got[i], after, returned if last else None
            )
        )
    node_got = shift(node_theirs, "mp", 1)
    middle, last = len(steps) - 1, len(steps) + len(halving_used(steps, bundles[0])) - 1
    turns = [1]
    for step in range(1, last):
        turns += [2, 1] if step == middle else [1, 2]
        turns += [0] if step < middle else []
        turns += [0] if step == middle - 1 else []
    turns += [2]
    _, *weights = in_turns(chains, turns)
    obs_keep, arrived = weights[-1][2]
    obs_mine, obs_theirs = call(
        obs_kernel, [((obs, half), F32), ((obs, half), BF16)], obs_keep, arrived, w_obs_held
    )
    (slot_sums,) = weights[-1][1]
    grad_node, grad_obs, grad_slot = call(
        merge_kernel, [((nodes, half), F32), ((obs, half), BF16), ((slots, hidden), F32)],
        node_mine, node_got, obs_mine, shift(obs_theirs, "mp", 1), slot_sums,
    )
    grad_w_node, grad_w_out = call(
        functools.partial(spread_kernel, steps[0]),
        [((width, hidden), F32), ((hidden, width), F32)],
        *weights[0][0],
        after=[pltpu.with_memory_space_constraint(grad_obs, pltpu.HBM)],
    )
    (grad_w_obs,) = call(
        functools.partial(spread_kernel, steps[0]),
        [((width, hidden), F32)],
        *weights[1][0],
        after=[pltpu.with_memory_space_constraint(grad_w_node, pltpu.HBM)],
    )
    return grad_obs, grad_node, grad_w_obs, grad_w_node, grad_w_out, grad_slot


def solution(mesh):
    rows = P(("group", "obs", "node"), None)
    return jax.shard_map(
        local,
        mesh=mesh,
        in_specs=(
            rows, rows, rows, rows, rows,
            P(("group", "obs", "node")),
            P(None, "mp"), P(None, "mp"), P(None, "mp"), P("mp", None),
        ),
        out_specs=(
            P(("group", "obs", "node"), "mp"),
            P(("group", "obs", "node"), "mp"),
            P("group", "mp"),
            P("group", "mp"),
            P(("group", "mp"), None),
            P("group", "mp"),
        ),
        check_vma=False,
    )
```

```python
import functools

import jax
import jax.numpy as jnp
from jax import lax
from jax.experimental import pallas as pl
from jax.experimental.pallas import tpu as pltpu
from jax.sharding import PartitionSpec as P

OWNER_AXES = ("obs", "node")
SUBLANES = 16
BUNDLES = 2
BF16 = jnp.bfloat16
F32 = jnp.float32


def dot(left, right, left_dim=1, right_dim=0):
    return lax.dot_general(
        left, right, (((left_dim,), (right_dim,)), ((), ())), preferred_element_type=F32
    )


def iota(shape, dim):
    return lax.broadcasted_iota(jnp.int32, shape, dim)


def call(kernel, outs, *args, scratch=(), after=()):
    vmem = pl.BlockSpec(memory_space=pltpu.VMEM)
    count = len(args)
    specs = [vmem] * count + [pl.BlockSpec(memory_space=pl.ANY)] * len(after)
    args += tuple(after)
    return pl.pallas_call(
        lambda *refs: kernel(*refs[:count], *refs[len(args) :]),
        out_shape=[jax.ShapeDtypeStruct(shape, dtype) for shape, dtype in outs],
        in_specs=specs,
        out_specs=[vmem] * len(outs),
        scratch_shapes=list(scratch),
        compiler_params=pltpu.CompilerParams(vmem_limit_bytes=40 << 20),
    )(*args)


def call_staged(kernel, outs, *args, held=()):
    count = len(args)
    sources = list(args) + [a for a in held if not any(a is b for b in args)]
    kept = [next(i for i, b in enumerate(sources) if a is b) for a in held]
    rest = [i for i in range(len(sources)) if i not in kept]

    def staged(*refs):
        hbm, refs = refs[: len(sources)], refs[len(sources) :]
        out_refs, refs = refs[: len(outs)], refs[len(outs) :]
        buffers = dict(zip(kept, refs[: len(kept)])) | dict(zip(rest, refs[len(kept) : -1]))
        copies = [
            pltpu.make_async_copy(hbm[i], buffers[i], refs[-1].at[i]) for i in range(len(sources))
        ]
        for copy in copies:
            copy.start()
        for copy in copies:
            copy.wait()
        kernel(*[buffers[i] for i in range(count)], *out_refs)

    return pl.pallas_call(
        staged,
        out_shape=[jax.ShapeDtypeStruct(shape, dtype) for shape, dtype in outs]
        + [jax.ShapeDtypeStruct(a.shape, a.dtype) for a in held],
        in_specs=[pl.BlockSpec(memory_space=pltpu.HBM)] * len(sources),
        out_specs=[pl.BlockSpec(memory_space=pltpu.VMEM)] * (len(outs) + len(held)),
        scratch_shapes=[pltpu.VMEM(sources[i].shape, sources[i].dtype) for i in rest]
        + [pltpu.SemaphoreType.DMA((len(sources),))],
        compiler_params=pltpu.CompilerParams(vmem_limit_bytes=40 << 20),
    )(*[pltpu.with_memory_space_constraint(a, pltpu.HBM) for a in sources])


def exchange(blocks, axes):
    return lax.all_to_all(blocks, axes, split_axis=0, concat_axis=0, tiled=True)


def shift(value, axis, step):
    size = lax.axis_size(axis)
    return lax.ppermute(value, axis, [(i, (i + step) % size) for i in range(size)])


def other_half(ref):
    half = ref.shape[0] // 2
    me = lax.axis_index("mp")
    mine = ref[pl.ds(pl.multiple_of(me * half, half), half), :]
    theirs = ref[pl.ds(pl.multiple_of((1 - me) * half, half), half), :]
    return mine, theirs


def column_half(ref, which):
    half = ref.shape[1] // 2
    return ref[:, pl.ds(pl.multiple_of(which * half, 128), half)]


def pack_kernel(cap, obs_ref, owner_ref, index_ref, slot_ref, other_ref, *outs):
    owners = len(outs)
    chunk, lanes = outs[0].shape
    fanout, obs = owner_ref.shape
    owner, index = owner_ref[...], index_ref[...]
    hits = [iota((owners, obs), 0) == owner[k : k + 1] for k in range(fanout)]
    count = functools.reduce(jnp.add, [h.astype(F32) for h in hits])
    before = dot(count, (iota((obs, obs), 0) < iota((obs, obs), 1)).astype(F32))
    header = jnp.where(iota((SUBLANES, obs), 0) == 4 * fanout, slot_ref[...].astype(F32), 0.0)
    places = []
    for k in range(fanout):
        rank = jnp.sum(jnp.where(hits[k], before, 0.0), axis=0, keepdims=True)
        places.append(owner[k : k + 1] * cap + rank.astype(jnp.int32))
        plus = index[k : k + 1] + 1
        fields = (owner[k : k + 1].astype(F32), rank, (plus // 16).astype(F32), (plus % 16).astype(F32))
        for j, row in enumerate(fields):
            header = jnp.where(iota(header.shape, 0) == 4 * k + j, row, header)
    header = header.astype(BF16)
    me, core = lax.axis_index(OWNER_AXES), lax.axis_index("mp")
    mine, other = column_half(obs_ref, core), column_half(obs_ref, 1 - core)

    def write(ref, pick, rows):
        packed = dot(pick, rows).astype(BF16)
        for c in range(rows.shape[1] // lanes):
            ref[c * cap : (c + 1) * cap, :] = packed[:, c * lanes : (c + 1) * lanes]
        ref[chunk - SUBLANES :, :] = header

    for j, out_ref in enumerate(outs):
        slots = iota((cap, obs), 0) + lax.rem(me + j, owners) * cap
        pick = functools.reduce(jnp.logical_or, [slots == place for place in places]).astype(BF16)
        write(out_ref, pick, mine)
        if j == 0:
            write(other_ref, pick, other)


def table_kernel(state_ref, agg_ref, w_node_ref, w_out_ref, bias_ref, table_ref):
    hidden = w_node_ref.shape[1]
    nodes, slots = state_ref.shape[0], bias_ref.shape[0]
    table_ref[nodes:, :] = jnp.zeros((table_ref.shape[0] - nodes, table_ref.shape[1]), BF16)

    def put(begin, column, part):
        high = part.astype(BF16)
        table_ref[begin : begin + part.shape[0], column : column + hidden] = high
        table_ref[begin : begin + part.shape[0], column + hidden : column + 2 * hidden] = (
            part - high.astype(F32)
        ).astype(BF16)

    put(0, 0, dot(state_ref[...], w_node_ref[...]))
    put(0, 2 * hidden, dot(agg_ref[...], w_out_ref[...], 1, 1))
    put(nodes, 0, bias_ref[...])


def join_blocks_kernel(*refs):
    out_ref = refs[-1]
    for j, ref in enumerate(refs[:-1]):
        out_ref[j] = ref[...]


def edge_kernel(
    fanout, nodes, steps, own_ref, mine_ref, other_ref, theirs_ref, table_ref, w_obs_ref,
    act_ref, hot_ref, rows_mine_ref, rows_theirs_ref, keep_ref, send_ref, pick_ref, total_ref, packed_ref, picks_ref,
):
    owners = mine_ref.shape[0] + 1
    chunk, lanes = own_ref.shape
    half = w_obs_ref.shape[0] // 2
    hidden = w_obs_ref.shape[1]
    cap = (chunk - SUBLANES) * lanes // half
    me = lax.axis_index(OWNER_AXES)
    base = 1 << nodes.bit_length()
    partner = partner_of(steps[0]).astype(F32)
    columns = []
    picks = []
    places = []
    for j in range(owners):
        block, other = (mine_ref.at[j - 1], theirs_ref.at[j - 1]) if j else (own_ref, other_ref)
        header = block[chunk - SUBLANES :, :].astype(F32)
        slot = header[4 * fanout : 4 * fanout + 1] * base
        code = jnp.zeros((cap, lanes), F32)
        pick = partner_pick = jnp.zeros((cap, lanes), jnp.bool_)
        for k in range(fanout):
            row = header[4 * k : 4 * k + 4]
            rank = jnp.where(row[0:1] == me.astype(F32), row[1:2], -1.0).astype(jnp.int32)
            hit = iota((cap, lanes), 0) == rank
            pick = pick | hit
            rank = jnp.where(row[0:1] == partner, row[1:2], -1.0).astype(jnp.int32)
            partner_pick = partner_pick | (iota((cap, lanes), 0) == rank)
            code = code + jnp.where(hit, row[2:3] * 16.0 + row[3:4] + slot, 0.0)
        picks.append(pick.astype(BF16))
        places.append(place_of(lax.rem(me - j + owners, owners), steps))
        begin = pl.multiple_of(places[j] * cap, SUBLANES)
        picks_ref[pl.ds(begin, cap), :] = partner_pick.astype(BF16)
        columns.append(jnp.sum(code, axis=1, keepdims=True).astype(jnp.int32))
        for c in range(half // lanes):
            rows = slice(j * cap, (j + 1) * cap)
            place = slice(c * lanes, (c + 1) * lanes)
            rows_mine_ref[rows, place] = block[c * cap : (c + 1) * cap, :]
            rows_theirs_ref[rows, place] = other[c * cap : (c + 1) * cap, :]
    code = jnp.concatenate(columns, axis=0)
    index, slot = (code & (base - 1)) - 1, (code >> (base.bit_length() - 1)) + nodes
    column = iota(hot_ref.shape, 1)
    hot = ((column == index) | ((column == slot) & (index >= 0))).astype(BF16)
    hot_ref[...] = hot
    rows = dot(hot, table_ref[...])
    w_mine, w_theirs = other_half(w_obs_ref)
    pre = dot(rows_mine_ref[...], w_mine) + dot(rows_theirs_ref[...], w_theirs)
    pre = pre + (rows[:, :hidden] + rows[:, hidden : 2 * hidden])
    g_z = rows[:, 2 * hidden : 3 * hidden] + rows[:, 3 * hidden :]
    sig = jax.nn.sigmoid(pre)
    g_a = (g_z * sig * (1.0 + pre * (1.0 - sig))).astype(BF16)
    act_ref[:, :hidden] = g_a
    act_ref[:, hidden:] = (pre * sig).astype(BF16)
    for j, pick in enumerate(picks):
        rows = g_a[j * cap : (j + 1) * cap]
        begin = pl.multiple_of(places[j] * lanes, SUBLANES)
        total_ref[pl.ds(begin, lanes), :] = dot(pick, rows, 0, 0).astype(BF16)
        packed_ref[pl.ds(pl.multiple_of(places[j] * cap, SUBLANES), cap), :] = rows
    bit = own_bit(steps[0])
    for out_ref, ref, which in (
        (keep_ref, total_ref, bit), (send_ref, packed_ref, 1 - bit), (pick_ref, picks_ref, bit)
    ):
        count = out_ref.shape[0]
        out_ref[...] = ref[pl.ds(pl.multiple_of(which * count, SUBLANES), count), :]


def halving_steps():
    bits = [
        [(axis, k) for k in range(lax.axis_size(axis).bit_length() - 1)] for axis in ("node", "obs")
    ]
    steps = []
    for k in range(max(map(len, bits))):
        both = [line[k] for line in bits if k < len(line)]
        steps += [(both[0], both[-1])] + ([(both[1], both[0])] if len(both) > 1 else [])
    return steps


def flip(value, step):
    axes = ("obs", "node", "mp")
    sizes = [lax.axis_size(axis) for axis in axes]
    pairs = []
    for index in range(sizes[0] * sizes[1] * sizes[2]):
        place = [index // (sizes[1] * sizes[2]), index // sizes[2] % sizes[1], index % sizes[2]]
        axis, k = step[place[2] % 2]
        place[axes.index(axis)] ^= (2 << k) - 1
        pairs.append((index, (place[0] * sizes[1] + place[1]) * sizes[2] + place[2]))
    return lax.ppermute(value, axes, pairs)


def bit_of(step, node, obs):
    codes = {"node": node ^ (node >> 1), "obs": obs ^ (obs >> 1)}
    bits = [(codes[axis] >> k) & 1 for axis, k in step]
    return jnp.where(lax.axis_index("mp") % 2 == 0, bits[0], bits[1])


def own_bit(step):
    return bit_of(step, lax.axis_index("node"), lax.axis_index("obs"))


def partner_of(step):
    node, obs, shares = lax.axis_index("node"), lax.axis_index("obs"), lax.axis_size("node")
    owners = []
    for axis, k in step:
        mask = (2 << k) - 1
        owners.append(obs * shares + (node ^ mask) if axis == "node" else (obs ^ mask) * shares + node)
    return jnp.where(lax.axis_index("mp") % 2 == 0, owners[0], owners[1])


def place_of(owner, steps):
    shares = lax.axis_size("node")
    place = 0
    for step in steps:
        place = 2 * place + bit_of(step, lax.rem(owner, shares), lax.div(owner, shares))
    return place


def halves(rows):
    return rows % (2 * SUBLANES) == 0


def half_rows(rows):
    return rows // 2 if halves(rows) else rows


def split_half(total_ref, start, rows, step, tail, keep_ref, send_ref):
    end = start + rows
    half = half_rows(rows) if step else rows
    if half < rows:
        bit = own_bit(step)
        kept, sent = [pl.ds(pl.multiple_of(start + b * half, SUBLANES), half) for b in (bit, 1 - bit)]
        keep_ref[:half, :] = total_ref[kept, :]
        send_ref[:half, :] = total_ref[sent, :].astype(BF16)
    else:
        both = total_ref[start:end, :].astype(BF16)
        keep_ref[:half, :] = both.astype(keep_ref.dtype)
        send_ref[:half, :] = both
    if tail:
        both = total_ref[total_ref.shape[0] - tail :, :].astype(BF16)
        keep_ref[half:, :] = both.astype(keep_ref.dtype)
        send_ref[half:, :] = both


def weight_kernel(
    step, bundles, tail, hot_ref, act_ref, rows_mine_ref, rows_theirs_ref, state_ref, agg_ref, w_node_ref,
    mine_ref, theirs_ref, *refs
):
    halves_refs, total_ref = refs[:-1], refs[-1]
    width, hidden = w_node_ref.shape
    nodes = state_ref.shape[0]
    sums = dot(hot_ref[...], act_ref[...], 0, 0)
    by_node = sums[:nodes].astype(BF16)
    node_hidden, z_sum = by_node[:, :hidden], by_node[:, hidden:]
    total_ref[:width, :] = dot(state_ref[...], node_hidden, 0, 0)
    begin = width
    for c in range(width // hidden):
        total_ref[begin : begin + hidden, :] = dot(
            z_sum, agg_ref[:, c * hidden : (c + 1) * hidden], 0, 0
        )
        begin += hidden
    g_a = act_ref[:, :hidden]
    core, half = lax.axis_index("mp"), width // 2
    for which, ref in ((core, rows_mine_ref), (1 - core, rows_theirs_ref)):
        total_ref[pl.ds(pl.multiple_of(begin + which * half, SUBLANES), half), :] = dot(ref[...], g_a, 0, 0)
    begin += width
    total_ref[begin:, :] = sums[nodes:, :hidden]
    rows = begin // bundles
    for i in range(bundles):
        split_half(
            total_ref, i * rows, rows, step, 0 if i else tail,
            halves_refs[2 * i], halves_refs[2 * i + 1],
        )
    mine, theirs = other_half(w_node_ref)
    theirs_ref[...] = dot(node_hidden, theirs, 1, 1).astype(BF16)
    mine_ref[...] = dot(node_hidden, mine, 1, 1)


def obs_kernel(keep_ref, got_ref, w_ref, mine_ref, theirs_ref):
    got = got_ref[got_ref.shape[0] - keep_ref.shape[0] :, :]
    obs_hidden = (keep_ref[...].astype(F32) + got.astype(F32)).astype(BF16)
    mine, theirs = other_half(w_ref)
    theirs_ref[...] = dot(obs_hidden, theirs, 1, 1).astype(BF16)
    mine_ref[...] = dot(obs_hidden, mine, 1, 1)


def add_kernel(step, tail, keep_ref, got_ref, next_ref, send_ref, total_ref):
    total = keep_ref[...].astype(F32) + got_ref[...].astype(F32)
    total_ref[...] = total.astype(total_ref.dtype)
    split_half(total_ref, 0, total_ref.shape[0] - tail, step, tail, next_ref, send_ref)


def unpack_kernel(step, keep_ref, got_ref, pick_ref, next_ref, send_ref, total_ref):
    obs = pick_ref.shape[1]
    blocks = keep_ref.shape[0] // obs
    cap = got_ref.shape[0] // blocks
    for i in range(blocks):
        edges, rows = slice(i * cap, (i + 1) * cap), slice(i * obs, (i + 1) * obs)
        total = keep_ref[rows, :].astype(F32) + dot(pick_ref[edges, :], got_ref[edges, :], 0, 0)
        total_ref[rows, :] = total.astype(BF16)
    split_half(total_ref, 0, total_ref.shape[0], step, 0, next_ref, send_ref)


def add_with_rows_kernel(
    step, tail, keep_ref, got_ref, rows_ref, rows_got_ref, next_ref, send_ref, rows_next_ref, total_ref, rows_total_ref
):
    share = next_ref.shape[0]
    total_ref[...] = keep_ref[...] + got_ref[...].astype(F32)
    split_half(total_ref, 0, share - tail, None, tail, next_ref, send_ref.at[:share])
    rows_total_ref[...] = (rows_ref[...].astype(F32) + rows_got_ref[...].astype(F32)).astype(BF16)
    split_half(
        rows_total_ref, 0, rows_total_ref.shape[0], step, 0, rows_next_ref, send_ref.at[share:]
    )


def last_kernel(keep_ref, got_ref, piece_ref, *slot_refs):
    total = keep_ref[...] + got_ref[: keep_ref.shape[0], :].astype(F32)
    rows = piece_ref.shape[0]
    piece_ref[...] = total[:rows].astype(BF16)
    for slot_ref in slot_refs:
        slot_ref[...] = total[rows : rows + slot_ref.shape[0]]


def join_kernel(step, mine_ref, got_ref, out_ref):
    rows = mine_ref.shape[0]
    bit = own_bit(step)
    out_ref[pl.ds(pl.multiple_of(bit * rows, SUBLANES), rows), :] = mine_ref[...]
    out_ref[pl.ds(pl.multiple_of((1 - bit) * rows, SUBLANES), rows), :] = got_ref[...]


def spread_kernel(step, bundles, *refs):
    low = own_bit(step) == 0
    joined = []
    for i in range(bundles):
        mine, got = refs[2 * i][...], refs[2 * i + 1][...]
        joined += [jnp.where(low, mine, got), jnp.where(low, got, mine)]
    half, hidden = joined[0].shape
    at = 0
    for out_ref in refs[2 * bundles :]:
        for c in range(out_ref.shape[1] // hidden):
            begin = 0
            while begin < out_ref.shape[0]:
                offset = at % half
                count = min(out_ref.shape[0] - begin, half - offset)
                out_ref[begin : begin + count, c * hidden : (c + 1) * hidden] = joined[at // half][
                    offset : offset + count
                ].astype(F32)
                at, begin = at + count, begin + count


def merge_kernel(
    node_ref, node_got_ref, obs_ref, obs_got_ref, slot_ref, grad_node_ref, grad_obs_ref, grad_slot_ref
):
    grad_slot_ref[...] = slot_ref[...]
    grad_node_ref[...] = node_ref[...] + node_got_ref[...].astype(F32)
    grad_obs_ref[...] = (obs_ref[...] + obs_got_ref[...].astype(F32)).astype(BF16)


def summing(steps, halved, tail, keep, got, after):
    hidden = keep.shape[1]
    for at, following in enumerate(steps[1:], 1):
        step = following if at < halved else None
        rows = keep.shape[0] - tail
        rows = (half_rows(rows) if step else rows) + tail
        keep, send = call(
            functools.partial(add_kernel, step, tail),
            [((rows, hidden), keep.dtype), ((rows, hidden), BF16)],
            keep, got,
            scratch=[pltpu.VMEM(keep.shape, keep.dtype)],
            after=after,
        )
        after[:] = [send]
        got = flip(send, following)
        yield
    return keep, got


def halving_used(steps, rows):
    used = []
    for step in steps[:-1]:
        if halves(rows):
            used.append(step)
            rows //= 2
    return used


def weight_chain(steps, rows, tail, slots, keep, got, after, returned=None):
    used = halving_used(steps, rows)
    keep, got = yield from summing(steps[:-1], len(steps) - 1, tail, keep, got, after)
    if returned:
        rows_keep, rows_got = returned
        shape = (half_rows(rows_keep.shape[0]), keep.shape[1])
        keep, send, rows_keep = call(
            functools.partial(add_with_rows_kernel, steps[-1], tail),
            [(keep.shape, F32), ((keep.shape[0] + shape[0], shape[1]), BF16), (shape, BF16)],
            keep, got, rows_keep, rows_got,
            scratch=[pltpu.VMEM(keep.shape, F32), pltpu.VMEM(rows_keep.shape, BF16)],
            after=after,
        )
    else:
        keep, send = call(
            functools.partial(add_kernel, None, tail),
            [(keep.shape, F32), (keep.shape, BF16)],
            keep, got,
            scratch=[pltpu.VMEM(keep.shape, F32)],
            after=after,
        )
    after[:] = [send]
    arrived = got = flip(send, steps[-1])
    yield
    piece, *sums = call(
        last_kernel,
        [((keep.shape[0] - tail, keep.shape[1]), BF16)]
        + ([((slots, keep.shape[1]), F32)] if tail else []),
        keep, got,
        after=after,
    )
    after[:] = [piece]
    got = flip(piece, used[-1])
    yield
    for step, following in zip(used[:0:-1], used[-2::-1]):
        (piece,) = call(
            functools.partial(join_kernel, step),
            [((2 * piece.shape[0], piece.shape[1]), BF16)],
            piece, got,
            after=after,
        )
        after[:] = [piece]
        got = flip(piece, following)
        yield
    return [piece, got], sums, (rows_keep, arrived) if returned else ()


def rows_chain(steps, keep, got, pick, after, out):
    shape = (half_rows(keep.shape[0]), keep.shape[1])
    keep, send = call(
        functools.partial(unpack_kernel, steps[1]),
        [(shape, BF16)] * 2,
        keep, got, pick,
        scratch=[pltpu.VMEM(keep.shape, BF16)],
        after=after,
    )
    after[:] = [send]
    got = flip(send, steps[1])
    yield
    out += yield from summing(steps[1:-1], len(steps), 0, keep, got, after)


def in_turns(chains, turns):
    results = {}
    for key in turns + list(range(len(chains))):
        try:
            next(chains[key])
        except StopIteration as stop:
            results.setdefault(key, stop.value)
    return [results[key] for key in range(len(chains))]


def local(obs_feat, node_state, grad_agg, owner, local_idx, slot, w_obs, w_node, slot_bias, w_out):
    owners = lax.axis_size(OWNER_AXES)
    obs, fanout = owner.shape
    nodes, width = node_state.shape
    hidden = w_obs.shape[1]
    slots = slot_bias.shape[0]
    cap = max(2, 2 * obs * fanout // owners)
    cap = -(-cap // SUBLANES) * SUBLANES
    edges = owners * cap
    half = width // 2
    slot_row = slot.reshape(1, obs)

    steps = halving_steps()
    chunk = cap * half // obs + SUBLANES
    other, *packed = call_staged(
        functools.partial(pack_kernel, cap),
        [((chunk, obs), BF16)] * (owners + 1),
        obs_feat, owner.T, local_idx.T, slot_row,
    )
    received = [shift(packed[j], OWNER_AXES, j) for j in range(1, owners)]
    tail = -(-slots // SUBLANES) * SUBLANES
    table, state_held, agg_held, w_node_held, w_obs_held = call_staged(
        table_kernel,
        [((nodes + tail, 4 * hidden), BF16)],
        node_state, grad_agg, w_node, w_out, slot_bias,
        held=(node_state, grad_agg, w_node, w_obs),
    )
    (mine,) = call(
        join_blocks_kernel, [((owners - 1, chunk, obs), BF16)], *received,
        after=(w_obs_held,),
    )
    theirs = shift(mine, "mp", 1)
    act, hot, rows_mine, rows_theirs, obs_keep, obs_send, obs_pick = call(
        functools.partial(edge_kernel, fanout, nodes, steps),
        [((edges, 2 * hidden), BF16), ((edges, nodes + tail), BF16)]
        + [((edges, half), BF16)] * 2
        + [((owners * obs // 2, hidden), BF16), ((edges // 2, hidden), BF16), ((edges // 2, obs), BF16)],
        packed[0], mine, other, theirs, table, w_obs_held,
        scratch=[
            pltpu.VMEM((owners * obs, hidden), BF16),
            pltpu.VMEM((edges, hidden), BF16),
            pltpu.VMEM((edges, obs), BF16),
        ],
    )

    stack = 2 * width + width // hidden * hidden
    bundles = BUNDLES
    rows = stack // bundles
    obs_got = flip(obs_send, steps[0])
    shapes = []
    for i in range(bundles):
        share = rows // 2 + (0 if i else tail)
        shapes += [((share, hidden), F32), ((share, hidden), BF16)]
    node_mine, node_theirs, *shares = call(
        functools.partial(weight_kernel, steps[0], bundles, tail),
        [((nodes, half), F32), ((nodes, half), BF16)] + shapes,
        hot, act, rows_mine, rows_theirs, state_held, agg_held, w_node_held,
        scratch=[pltpu.VMEM((stack + tail, hidden), F32)],
    )
    after = []
    returned = []
    chains = [rows_chain(steps, obs_keep, obs_got, obs_pick, after, returned)]
    got = [flip(send, steps[0]) for send in shares[1::2]]
    for i in range(bundles):
        last = i == bundles - 1
        chains.append(
            weight_chain(
                steps, rows, 0 if i else tail, slots, shares[2 * i], got[i], after, returned if last else None
            )
        )
    node_got = shift(node_theirs, "mp", 1)
    middle, last = len(steps) - 1, len(steps) + len(halving_used(steps, rows)) - 1
    turns = [1]
    for step in range(1, last):
        turns += [0] if step < middle else []
        turns += [0] if step == middle - 1 else []
        turns += [2, 1] if step == middle else [1, 2]
    turns += [2]
    _, *weights = in_turns(chains, turns)
    obs_keep, arrived = weights[-1][2]
    obs_mine, obs_theirs = call(
        obs_kernel, [((obs, half), F32), ((obs, half), BF16)], obs_keep, arrived, w_obs_held
    )
    (slot_sums,) = weights[0][1]
    grad_node, grad_obs, grad_slot = call(
        merge_kernel, [((nodes, half), F32), ((obs, half), BF16), ((slots, hidden), F32)],
        node_mine, node_got, obs_mine, shift(obs_theirs, "mp", 1), slot_sums,
    )
    ends = [end for pair, *_ in weights for end in pair]
    grad_w_node, grad_w_out, grad_w_obs = call(
        functools.partial(spread_kernel, steps[0], bundles),
        [((width, hidden), F32), ((hidden, width), F32), ((width, hidden), F32)],
        *ends,
        after=[pltpu.with_memory_space_constraint(grad_obs, pltpu.HBM)],
    )
    return grad_obs, grad_node, grad_w_obs, grad_w_node, grad_w_out, grad_slot


def solution(mesh):
    rows = P(("group", "obs", "node"), None)
    return jax.shard_map(
        local,
        mesh=mesh,
        in_specs=(
            rows, rows, rows, rows, rows,
            P(("group", "obs", "node")),
            P(None, "mp"), P(None, "mp"), P(None, "mp"), P("mp", None),
        ),
        out_specs=(
            P(("group", "obs", "node"), "mp"),
            P(("group", "obs", "node"), "mp"),
            P("group", "mp"),
            P("group", "mp"),
            P(("group", "mp"), None),
            P("group", "mp"),
        ),
        check_vma=False,
    )
```

```python
import functools

import jax
import jax.numpy as jnp
from jax import lax
from jax.experimental import pallas as pl
from jax.experimental.pallas import tpu as pltpu
from jax.sharding import PartitionSpec as P

OWNER_AXES = ("obs", "node")
SUBLANES = 16
BUNDLES = 2
BF16 = jnp.bfloat16
F32 = jnp.float32


def dot(left, right, left_dim=1, right_dim=0):
    return lax.dot_general(
        left, right, (((left_dim,), (right_dim,)), ((), ())), preferred_element_type=F32
    )


def iota(shape, dim):
    return lax.broadcasted_iota(jnp.int32, shape, dim)


def call(kernel, outs, *args, scratch=(), after=()):
    vmem = pl.BlockSpec(memory_space=pltpu.VMEM)
    count = len(args)
    specs = [vmem] * count + [pl.BlockSpec(memory_space=pl.ANY)] * len(after)
    args += tuple(after)
    return pl.pallas_call(
        lambda *refs: kernel(*refs[:count], *refs[len(args) :]),
        out_shape=[jax.ShapeDtypeStruct(shape, dtype) for shape, dtype in outs],
        in_specs=specs,
        out_specs=[vmem] * len(outs),
        scratch_shapes=list(scratch),
        compiler_params=pltpu.CompilerParams(vmem_limit_bytes=40 << 20),
    )(*args)


def call_staged(kernel, outs, *args, held=()):
    count = len(args)
    sources = list(args) + [a for a in held if not any(a is b for b in args)]
    kept = [next(i for i, b in enumerate(sources) if a is b) for a in held]
    rest = [i for i in range(len(sources)) if i not in kept]

    def staged(*refs):
        hbm, refs = refs[: len(sources)], refs[len(sources) :]
        out_refs, refs = refs[: len(outs)], refs[len(outs) :]
        buffers = dict(zip(kept, refs[: len(kept)])) | dict(zip(rest, refs[len(kept) : -1]))
        copies = [
            pltpu.make_async_copy(hbm[i], buffers[i], refs[-1].at[i]) for i in range(len(sources))
        ]
        for copy in copies:
            copy.start()
        for copy in copies:
            copy.wait()
        kernel(*[buffers[i] for i in range(count)], *out_refs)

    return pl.pallas_call(
        staged,
        out_shape=[jax.ShapeDtypeStruct(shape, dtype) for shape, dtype in outs]
        + [jax.ShapeDtypeStruct(a.shape, a.dtype) for a in held],
        in_specs=[pl.BlockSpec(memory_space=pltpu.HBM)] * len(sources),
        out_specs=[pl.BlockSpec(memory_space=pltpu.VMEM)] * (len(outs) + len(held)),
        scratch_shapes=[pltpu.VMEM(sources[i].shape, sources[i].dtype) for i in rest]
        + [pltpu.SemaphoreType.DMA((len(sources),))],
        compiler_params=pltpu.CompilerParams(vmem_limit_bytes=40 << 20),
    )(*[pltpu.with_memory_space_constraint(a, pltpu.HBM) for a in sources])


def exchange(blocks, axes):
    return lax.all_to_all(blocks, axes, split_axis=0, concat_axis=0, tiled=True)


def shift(value, axis, step):
    size = lax.axis_size(axis)
    return lax.ppermute(value, axis, [(i, (i + step) % size) for i in range(size)])


def other_half(ref):
    half = ref.shape[0] // 2
    me = lax.axis_index("mp")
    mine = ref[pl.ds(pl.multiple_of(me * half, half), half), :]
    theirs = ref[pl.ds(pl.multiple_of((1 - me) * half, half), half), :]
    return mine, theirs


def column_half(ref, which):
    half = ref.shape[1] // 2
    return ref[:, pl.ds(pl.multiple_of(which * half, 128), half)]


def pack_kernel(cap, obs_ref, owner_ref, index_ref, slot_ref, other_ref, *outs):
    owners = len(outs)
    chunk, lanes = outs[0].shape
    fanout, obs = owner_ref.shape
    owner, index = owner_ref[...], index_ref[...]
    hits = [iota((owners, obs), 0) == owner[k : k + 1] for k in range(fanout)]
    count = functools.reduce(jnp.add, [h.astype(F32) for h in hits])
    before = dot(count, (iota((obs, obs), 0) < iota((obs, obs), 1)).astype(F32))
    header = jnp.where(iota((SUBLANES, obs), 0) == 4 * fanout, slot_ref[...].astype(F32), 0.0)
    places = []
    for k in range(fanout):
        rank = jnp.sum(jnp.where(hits[k], before, 0.0), axis=0, keepdims=True)
        places.append(owner[k : k + 1] * cap + rank.astype(jnp.int32))
        plus = index[k : k + 1] + 1
        fields = (owner[k : k + 1].astype(F32), rank, (plus // 16).astype(F32), (plus % 16).astype(F32))
        for j, row in enumerate(fields):
            header = jnp.where(iota(header.shape, 0) == 4 * k + j, row, header)
    header = header.astype(BF16)
    me, core = lax.axis_index(OWNER_AXES), lax.axis_index("mp")
    mine, other = column_half(obs_ref, core), column_half(obs_ref, 1 - core)

    def write(ref, pick, rows):
        packed = dot(pick, rows).astype(BF16)
        for c in range(rows.shape[1] // lanes):
            ref[c * cap : (c + 1) * cap, :] = packed[:, c * lanes : (c + 1) * lanes]
        ref[chunk - SUBLANES :, :] = header

    for j, out_ref in enumerate(outs):
        slots = iota((cap, obs), 0) + lax.rem(me + j, owners) * cap
        pick = functools.reduce(jnp.logical_or, [slots == place for place in places]).astype(BF16)
        write(out_ref, pick, mine)
        if j == 0:
            write(other_ref, pick, other)


def table_kernel(state_ref, agg_ref, w_node_ref, w_out_ref, bias_ref, table_ref):
    hidden = w_node_ref.shape[1]
    nodes, slots = state_ref.shape[0], bias_ref.shape[0]
    table_ref[nodes:, :] = jnp.zeros((table_ref.shape[0] - nodes, table_ref.shape[1]), BF16)

    def put(begin, column, part):
        high = part.astype(BF16)
        table_ref[begin : begin + part.shape[0], column : column + hidden] = high
        table_ref[begin : begin + part.shape[0], column + hidden : column + 2 * hidden] = (
            part - high.astype(F32)
        ).astype(BF16)

    put(0, 0, dot(state_ref[...], w_node_ref[...]))
    put(0, 2 * hidden, dot(agg_ref[...], w_out_ref[...], 1, 1))
    put(nodes, 0, bias_ref[...])


def join_blocks_kernel(*refs):
    out_ref = refs[-1]
    for j, ref in enumerate(refs[:-1]):
        out_ref[j] = ref[...]


def edge_kernel(
    fanout, nodes, steps, own_ref, mine_ref, other_ref, theirs_ref, table_ref, w_obs_ref,
    act_ref, hot_ref, rows_mine_ref, rows_theirs_ref, keep_ref, send_ref, pick_ref, total_ref, packed_ref, picks_ref,
):
    owners = mine_ref.shape[0] + 1
    chunk, lanes = own_ref.shape
    half = w_obs_ref.shape[0] // 2
    hidden = w_obs_ref.shape[1]
    cap = (chunk - SUBLANES) * lanes // half
    me = lax.axis_index(OWNER_AXES)
    base = 1 << nodes.bit_length()
    partner = partner_of(steps[0]).astype(F32)
    columns = []
    picks = []
    places = []
    for j in range(owners):
        block, other = (mine_ref.at[j - 1], theirs_ref.at[j - 1]) if j else (own_ref, other_ref)
        header = block[chunk - SUBLANES :, :].astype(F32)
        slot = header[4 * fanout : 4 * fanout + 1] * base
        code = jnp.zeros((cap, lanes), F32)
        pick = partner_pick = jnp.zeros((cap, lanes), jnp.bool_)
        for k in range(fanout):
            row = header[4 * k : 4 * k + 4]
            rank = jnp.where(row[0:1] == me.astype(F32), row[1:2], -1.0).astype(jnp.int32)
            hit = iota((cap, lanes), 0) == rank
            pick = pick | hit
            rank = jnp.where(row[0:1] == partner, row[1:2], -1.0).astype(jnp.int32)
            partner_pick = partner_pick | (iota((cap, lanes), 0) == rank)
            code = code + jnp.where(hit, row[2:3] * 16.0 + row[3:4] + slot, 0.0)
        picks.append(pick.astype(BF16))
        places.append(place_of(lax.rem(me - j + owners, owners), steps))
        begin = pl.multiple_of(places[j] * cap, SUBLANES)
        picks_ref[pl.ds(begin, cap), :] = partner_pick.astype(BF16)
        columns.append(jnp.sum(code, axis=1, keepdims=True).astype(jnp.int32))
        for c in range(half // lanes):
            rows = slice(j * cap, (j + 1) * cap)
            place = slice(c * lanes, (c + 1) * lanes)
            rows_mine_ref[rows, place] = block[c * cap : (c + 1) * cap, :]
            rows_theirs_ref[rows, place] = other[c * cap : (c + 1) * cap, :]
    code = jnp.concatenate(columns, axis=0)
    index, slot = (code & (base - 1)) - 1, (code >> (base.bit_length() - 1)) + nodes
    column = iota(hot_ref.shape, 1)
    hot = ((column == index) | ((column == slot) & (index >= 0))).astype(BF16)
    hot_ref[...] = hot
    rows = dot(hot, table_ref[...])
    w_mine, w_theirs = other_half(w_obs_ref)
    pre = dot(rows_mine_ref[...], w_mine) + dot(rows_theirs_ref[...], w_theirs)
    pre = pre + (rows[:, :hidden] + rows[:, hidden : 2 * hidden])
    g_z = rows[:, 2 * hidden : 3 * hidden] + rows[:, 3 * hidden :]
    sig = jax.nn.sigmoid(pre)
    g_a = (g_z * sig * (1.0 + pre * (1.0 - sig))).astype(BF16)
    act_ref[:, :hidden] = g_a
    act_ref[:, hidden:] = (pre * sig).astype(BF16)
    for j, pick in enumerate(picks):
        rows = g_a[j * cap : (j + 1) * cap]
        begin = pl.multiple_of(places[j] * lanes, SUBLANES)
        total_ref[pl.ds(begin, lanes), :] = dot(pick, rows, 0, 0).astype(BF16)
        packed_ref[pl.ds(pl.multiple_of(places[j] * cap, SUBLANES), cap), :] = rows
    bit = own_bit(steps[0])
    for out_ref, ref, which in (
        (keep_ref, total_ref, bit), (send_ref, packed_ref, 1 - bit), (pick_ref, picks_ref, bit)
    ):
        count = out_ref.shape[0]
        out_ref[...] = ref[pl.ds(pl.multiple_of(which * count, SUBLANES), count), :]


def halving_steps():
    bits = [
        [(axis, k) for k in range(lax.axis_size(axis).bit_length() - 1)] for axis in ("node", "obs")
    ]
    steps = []
    for k in range(max(map(len, bits))):
        both = [line[k] for line in bits if k < len(line)]
        steps += [(both[0], both[-1])] + ([(both[1], both[0])] if len(both) > 1 else [])
    return steps


def flip(value, step):
    axes = ("obs", "node", "mp")
    sizes = [lax.axis_size(axis) for axis in axes]
    pairs = []
    for index in range(sizes[0] * sizes[1] * sizes[2]):
        place = [index // (sizes[1] * sizes[2]), index // sizes[2] % sizes[1], index % sizes[2]]
        axis, k = step[place[2] % 2]
        place[axes.index(axis)] ^= (2 << k) - 1
        pairs.append((index, (place[0] * sizes[1] + place[1]) * sizes[2] + place[2]))
    return lax.ppermute(value, axes, pairs)


def bit_of(step, node, obs):
    codes = {"node": node ^ (node >> 1), "obs": obs ^ (obs >> 1)}
    bits = [(codes[axis] >> k) & 1 for axis, k in step]
    return jnp.where(lax.axis_index("mp") % 2 == 0, bits[0], bits[1])


def own_bit(step):
    return bit_of(step, lax.axis_index("node"), lax.axis_index("obs"))


def partner_of(step):
    node, obs, shares = lax.axis_index("node"), lax.axis_index("obs"), lax.axis_size("node")
    owners = []
    for axis, k in step:
        mask = (2 << k) - 1
        owners.append(obs * shares + (node ^ mask) if axis == "node" else (obs ^ mask) * shares + node)
    return jnp.where(lax.axis_index("mp") % 2 == 0, owners[0], owners[1])


def place_of(owner, steps):
    shares = lax.axis_size("node")
    place = 0
    for step in steps:
        place = 2 * place + bit_of(step, lax.rem(owner, shares), lax.div(owner, shares))
    return place


def halves(rows):
    return rows % (2 * SUBLANES) == 0


def half_rows(rows):
    return rows // 2 if halves(rows) else rows


def split_half(total_ref, start, rows, step, tail, keep_ref, send_ref):
    end = start + rows
    half = half_rows(rows) if step else rows
    if half < rows:
        bit = own_bit(step)
        kept, sent = [pl.ds(pl.multiple_of(start + b * half, SUBLANES), half) for b in (bit, 1 - bit)]
        keep_ref[:half, :] = total_ref[kept, :]
        send_ref[:half, :] = total_ref[sent, :].astype(BF16)
    else:
        both = total_ref[start:end, :].astype(BF16)
        keep_ref[:half, :] = both.astype(keep_ref.dtype)
        send_ref[:half, :] = both
    if tail:
        both = total_ref[total_ref.shape[0] - tail :, :].astype(BF16)
        keep_ref[half:, :] = both.astype(keep_ref.dtype)
        send_ref[half:, :] = both


def weight_kernel(
    step, bundles, tail, hot_ref, act_ref, rows_mine_ref, rows_theirs_ref, state_ref, agg_ref, w_node_ref,
    mine_ref, theirs_ref, *refs
):
    halves_refs, total_ref = refs[:-1], refs[-1]
    width, hidden = w_node_ref.shape
    nodes = state_ref.shape[0]
    sums = dot(hot_ref[...], act_ref[...], 0, 0)
    by_node = sums[:nodes].astype(BF16)
    node_hidden, z_sum = by_node[:, :hidden], by_node[:, hidden:]
    total_ref[:width, :] = dot(state_ref[...], node_hidden, 0, 0)
    begin = width
    for c in range(width // hidden):
        total_ref[begin : begin + hidden, :] = dot(
            z_sum, agg_ref[:, c * hidden : (c + 1) * hidden], 0, 0
        )
        begin += hidden
    g_a = act_ref[:, :hidden]
    core, half = lax.axis_index("mp"), width // 2
    for which, ref in ((core, rows_mine_ref), (1 - core, rows_theirs_ref)):
        total_ref[pl.ds(pl.multiple_of(begin + which * half, SUBLANES), half), :] = dot(ref[...], g_a, 0, 0)
    begin += width
    total_ref[begin:, :] = sums[nodes:, :hidden]
    rows = begin // bundles
    for i in range(bundles):
        split_half(
            total_ref, i * rows, rows, step, 0 if i else tail,
            halves_refs[2 * i], halves_refs[2 * i + 1],
        )
    mine, theirs = other_half(w_node_ref)
    theirs_ref[...] = dot(node_hidden, theirs, 1, 1).astype(BF16)
    mine_ref[...] = dot(node_hidden, mine, 1, 1)


def obs_kernel(keep_ref, got_ref, w_ref, mine_ref, theirs_ref):
    got = got_ref[got_ref.shape[0] - keep_ref.shape[0] :, :]
    obs_hidden = (keep_ref[...].astype(F32) + got.astype(F32)).astype(BF16)
    mine, theirs = other_half(w_ref)
    theirs_ref[...] = dot(obs_hidden, theirs, 1, 1).astype(BF16)
    mine_ref[...] = dot(obs_hidden, mine, 1, 1)


def add_kernel(step, tail, keep_ref, got_ref, next_ref, send_ref, total_ref):
    total = keep_ref[...].astype(F32) + got_ref[...].astype(F32)
    total_ref[...] = total.astype(total_ref.dtype)
    split_half(total_ref, 0, total_ref.shape[0] - tail, step, tail, next_ref, send_ref)


def unpack_kernel(step, keep_ref, got_ref, pick_ref, next_ref, send_ref, total_ref):
    obs = pick_ref.shape[1]
    blocks = keep_ref.shape[0] // obs
    cap = got_ref.shape[0] // blocks
    for i in range(blocks):
        edges, rows = slice(i * cap, (i + 1) * cap), slice(i * obs, (i + 1) * obs)
        total = keep_ref[rows, :].astype(F32) + dot(pick_ref[edges, :], got_ref[edges, :], 0, 0)
        total_ref[rows, :] = total.astype(BF16)
    split_half(total_ref, 0, total_ref.shape[0], step, 0, next_ref, send_ref)


def add_with_rows_kernel(
    step, tail, keep_ref, got_ref, rows_ref, rows_got_ref, next_ref, send_ref, rows_next_ref, total_ref, rows_total_ref
):
    share = next_ref.shape[0]
    total_ref[...] = keep_ref[...] + got_ref[...].astype(F32)
    split_half(total_ref, 0, share - tail, None, tail, next_ref, send_ref.at[:share])
    rows_total_ref[...] = (rows_ref[...].astype(F32) + rows_got_ref[...].astype(F32)).astype(BF16)
    split_half(
        rows_total_ref, 0, rows_total_ref.shape[0], step, 0, rows_next_ref, send_ref.at[share:]
    )


def last_kernel(keep_ref, got_ref, piece_ref, *slot_refs):
    total = keep_ref[...] + got_ref[: keep_ref.shape[0], :].astype(F32)
    rows = piece_ref.shape[0]
    piece_ref[...] = total[:rows].astype(BF16)
    for slot_ref in slot_refs:
        slot_ref[...] = total[rows : rows + slot_ref.shape[0]]


def join_kernel(step, mine_ref, got_ref, out_ref):
    rows = mine_ref.shape[0]
    bit = own_bit(step)
    out_ref[pl.ds(pl.multiple_of(bit * rows, SUBLANES), rows), :] = mine_ref[...]
    out_ref[pl.ds(pl.multiple_of((1 - bit) * rows, SUBLANES), rows), :] = got_ref[...]


def spread_kernel(step, bundles, at, *refs):
    low = own_bit(step) == 0
    joined = []
    for i in range(bundles):
        mine, got = refs[2 * i][...], refs[2 * i + 1][...]
        joined += [jnp.where(low, mine, got), jnp.where(low, got, mine)]
    half, hidden = joined[0].shape
    for out_ref in refs[2 * bundles :]:
        for c in range(out_ref.shape[1] // hidden):
            begin = 0
            while begin < out_ref.shape[0]:
                offset = at % half
                count = min(out_ref.shape[0] - begin, half - offset)
                out_ref[begin : begin + count, c * hidden : (c + 1) * hidden] = joined[at // half][
                    offset : offset + count
                ].astype(F32)
                at, begin = at + count, begin + count


def merge_kernel(
    node_ref, node_got_ref, obs_ref, obs_got_ref, slot_ref, grad_node_ref, grad_obs_ref, grad_slot_ref
):
    grad_slot_ref[...] = slot_ref[...]
    grad_node_ref[...] = node_ref[...] + node_got_ref[...].astype(F32)
    grad_obs_ref[...] = (obs_ref[...] + obs_got_ref[...].astype(F32)).astype(BF16)


def summing(steps, halved, tail, keep, got, after):
    hidden = keep.shape[1]
    for at, following in enumerate(steps[1:], 1):
        step = following if at < halved else None
        rows = keep.shape[0] - tail
        rows = (half_rows(rows) if step else rows) + tail
        keep, send = call(
            functools.partial(add_kernel, step, tail),
            [((rows, hidden), keep.dtype), ((rows, hidden), BF16)],
            keep, got,
            scratch=[pltpu.VMEM(keep.shape, keep.dtype)],
            after=after,
        )
        after[:] = [send]
        got = flip(send, following)
        yield
    return keep, got


def halving_used(steps, rows):
    used = []
    for step in steps[:-1]:
        if halves(rows):
            used.append(step)
            rows //= 2
    return used


def weight_chain(steps, rows, tail, slots, keep, got, after, returned=None):
    used = halving_used(steps, rows)
    keep, got = yield from summing(steps[:-1], len(steps) - 1, tail, keep, got, after)
    if returned:
        rows_keep, rows_got = returned
        shape = (half_rows(rows_keep.shape[0]), keep.shape[1])
        keep, send, rows_keep = call(
            functools.partial(add_with_rows_kernel, steps[-1], tail),
            [(keep.shape, F32), ((keep.shape[0] + shape[0], shape[1]), BF16), (shape, BF16)],
            keep, got, rows_keep, rows_got,
            scratch=[pltpu.VMEM(keep.shape, F32), pltpu.VMEM(rows_keep.shape, BF16)],
            after=after,
        )
    else:
        keep, send = call(
            functools.partial(add_kernel, None, tail),
            [(keep.shape, F32), (keep.shape, BF16)],
            keep, got,
            scratch=[pltpu.VMEM(keep.shape, F32)],
            after=after,
        )
    after[:] = [send]
    arrived = got = flip(send, steps[-1])
    yield
    piece, *sums = call(
        last_kernel,
        [((keep.shape[0] - tail, keep.shape[1]), BF16)]
        + ([((slots, keep.shape[1]), F32)] if tail else []),
        keep, got,
        after=after,
    )
    after[:] = [piece]
    got = flip(piece, used[-1])
    yield
    for step, following in zip(used[:0:-1], used[-2::-1]):
        (piece,) = call(
            functools.partial(join_kernel, step),
            [((2 * piece.shape[0], piece.shape[1]), BF16)],
            piece, got,
            after=after,
        )
        after[:] = [piece]
        got = flip(piece, following)
        yield
    return [piece, got], sums, (rows_keep, arrived) if returned else ()


def rows_chain(steps, keep, got, pick, after, out):
    shape = (half_rows(keep.shape[0]), keep.shape[1])
    keep, send = call(
        functools.partial(unpack_kernel, steps[1]),
        [(shape, BF16)] * 2,
        keep, got, pick,
        scratch=[pltpu.VMEM(keep.shape, BF16)],
        after=after,
    )
    after[:] = [send]
    got = flip(send, steps[1])
    yield
    out += yield from summing(steps[1:-1], len(steps), 0, keep, got, after)


def in_turns(chains, turns):
    results = {}
    for key in turns + list(range(len(chains))):
        try:
            next(chains[key])
        except StopIteration as stop:
            results.setdefault(key, stop.value)
    return [results[key] for key in range(len(chains))]


def local(obs_feat, node_state, grad_agg, owner, local_idx, slot, w_obs, w_node, slot_bias, w_out):
    owners = lax.axis_size(OWNER_AXES)
    obs, fanout = owner.shape
    nodes, width = node_state.shape
    hidden = w_obs.shape[1]
    slots = slot_bias.shape[0]
    cap = max(2, 2 * obs * fanout // owners)
    cap = -(-cap // SUBLANES) * SUBLANES
    edges = owners * cap
    half = width // 2
    slot_row = slot.reshape(1, obs)

    steps = halving_steps()
    chunk = cap * half // obs + SUBLANES
    other, *packed = call_staged(
        functools.partial(pack_kernel, cap),
        [((chunk, obs), BF16)] * (owners + 1),
        obs_feat, owner.T, local_idx.T, slot_row,
    )
    received = [shift(packed[j], OWNER_AXES, j) for j in range(1, owners)]
    tail = -(-slots // SUBLANES) * SUBLANES
    table, state_held, agg_held, w_node_held, w_obs_held = call_staged(
        table_kernel,
        [((nodes + tail, 4 * hidden), BF16)],
        node_state, grad_agg, w_node, w_out, slot_bias,
        held=(node_state, grad_agg, w_node, w_obs),
    )
    (mine,) = call(
        join_blocks_kernel, [((owners - 1, chunk, obs), BF16)], *received,
        after=(w_obs_held,),
    )
    theirs = shift(mine, "mp", 1)
    act, hot, rows_mine, rows_theirs, obs_keep, obs_send, obs_pick = call(
        functools.partial(edge_kernel, fanout, nodes, steps),
        [((edges, 2 * hidden), BF16), ((edges, nodes + tail), BF16)]
        + [((edges, half), BF16)] * 2
        + [((owners * obs // 2, hidden), BF16), ((edges // 2, hidden), BF16), ((edges // 2, obs), BF16)],
        packed[0], mine, other, theirs, table, w_obs_held,
        scratch=[
            pltpu.VMEM((owners * obs, hidden), BF16),
            pltpu.VMEM((edges, hidden), BF16),
            pltpu.VMEM((edges, obs), BF16),
        ],
    )

    stack = 2 * width + width // hidden * hidden
    bundles = BUNDLES
    rows = stack // bundles
    obs_got = flip(obs_send, steps[0])
    shapes = []
    for i in range(bundles):
        share = rows // 2 + (0 if i else tail)
        shapes += [((share, hidden), F32), ((share, hidden), BF16)]
    node_mine, node_theirs, *shares = call(
        functools.partial(weight_kernel, steps[0], bundles, tail),
        [((nodes, half), F32), ((nodes, half), BF16)] + shapes,
        hot, act, rows_mine, rows_theirs, state_held, agg_held, w_node_held,
        scratch=[pltpu.VMEM((stack + tail, hidden), F32)],
    )
    after = []
    returned = []
    chains = [rows_chain(steps, obs_keep, obs_got, obs_pick, after, returned)]
    got = [flip(send, steps[0]) for send in shares[1::2]]
    for i in range(bundles):
        last = i == bundles - 1
        chains.append(
            weight_chain(
                steps, rows, 0 if i else tail, slots, shares[2 * i], got[i], after, returned if last else None
            )
        )
    node_got = shift(node_theirs, "mp", 1)
    middle, last = len(steps) - 1, len(steps) + len(halving_used(steps, rows)) - 1
    turns = [1]
    for step in range(1, last):
        turns += [0] if step < middle else []
        turns += [0] if step == middle - 1 else []
        turns += [2, 1] if step == middle else [1, 2]
    turns += [2]
    _, *weights = in_turns(chains, turns)
    obs_keep, arrived = weights[-1][2]
    obs_mine, obs_theirs = call(
        obs_kernel, [((obs, half), F32), ((obs, half), BF16)], obs_keep, arrived, w_obs_held
    )
    (slot_sums,) = weights[0][1]
    grad_node, grad_obs, grad_slot = call(
        merge_kernel, [((nodes, half), F32), ((obs, half), BF16), ((slots, hidden), F32)],
        node_mine, node_got, obs_mine, shift(obs_theirs, "mp", 1), slot_sums,
    )
    ends = [end for pair, *_ in weights for end in pair]
    (grad_w_node,) = call(
        functools.partial(spread_kernel, steps[0], 1, 0),
        [((width, hidden), F32)],
        *ends[:2],
        after=[pltpu.with_memory_space_constraint(grad_obs, pltpu.HBM)],
    )
    grad_w_out, grad_w_obs = call(
        functools.partial(spread_kernel, steps[0], bundles, width),
        [((hidden, width), F32), ((width, hidden), F32)],
        *ends,
        after=[pltpu.with_memory_space_constraint(grad_w_node, pltpu.HBM)],
    )
    return grad_obs, grad_node, grad_w_obs, grad_w_node, grad_w_out, grad_slot


def solution(mesh):
    rows = P(("group", "obs", "node"), None)
    return jax.shard_map(
        local,
        mesh=mesh,
        in_specs=(
            rows, rows, rows, rows, rows,
            P(("group", "obs", "node")),
            P(None, "mp"), P(None, "mp"), P(None, "mp"), P("mp", None),
        ),
        out_specs=(
            P(("group", "obs", "node"), "mp"),
            P(("group", "obs", "node"), "mp"),
            P("group", "mp"),
            P("group", "mp"),
            P(("group", "mp"), None),
            P("group", "mp"),
        ),
        check_vma=False,
    )
```
